32 devices in a mesh: ctx: 8 (over z, y), fsdp: 4 (over x, core).
Axes of the slice: x: 2, y: 2, z: 4, core: 2. Of those that a mesh axis runs over, the one named last changes fastest.
Arguments:
- query_rows: bfloat16 [4096, 8192], P(('fsdp', 'ctx')), may hold values from -6 to 6
- key_rows: bfloat16 [4096, 1024], P(('fsdp', 'ctx')), may hold values from -6 to 6
- value_rows: bfloat16 [4096, 1024], P(('fsdp', 'ctx')), may hold values from -6 to 6
- grad_out: bfloat16 [4096, 8192], P(('fsdp', 'ctx')), may hold values from -384 to 384
- query_map: bfloat16 [64, 128, 64], P('ctx', 'fsdp'), may hold values from -1.5 to 1.5
- key_map: bfloat16 [64, 128, 64], P('ctx', 'fsdp'), may hold values from -1.5 to 1.5
- prefix_state: float32 [64, 128, 128], P('ctx'), may hold values from -24 to 24
- prefix_norm: float32 [64, 128], P('ctx'), may hold values from 16 to 256
Outputs:
- grad_queries: bfloat16 [4096, 8192], P(('fsdp', 'ctx'))
- grad_keys: bfloat16 [4096, 1024], P(('fsdp', 'ctx'))
- grad_values: bfloat16 [4096, 1024], P(('fsdp', 'ctx'))
- grad_query_map: float32 [64, 128, 64], P('ctx', 'fsdp')
- grad_key_map: float32 [64, 128, 64], P('ctx', 'fsdp')
- grad_prefix_state: float32 [64, 128, 128], P('ctx', 'fsdp')
The draws below stay inside these ranges and needn't reach their ends.
All inputs are finite; a program needn't handle non-finite values.
Results may differ from the reference program's by a relative error of at most 0.014.
The reference program's roundings to bfloat16 on the way (of `query_logits`, `key_logits`, `state_low`, `scores_low`, `scaled_low`, `dscores` and `suffix_low`) count: a program that leaves them out, or rounds other values in their place, can miss the bound.
Values may be sent and summed in bfloat16 or wider, within the bound.
No kernel may reach another device: no remote copies, remote signals or barrier semaphores. Data moves between devices by JAX's collectives and lax.ppermute only.
A program may use at most 128 MiB of HBM per device.

```python
import math
import jax
import jax.numpy as jnp
from jax import lax

H = 64
KVH = 8
HD = 128
FH = 64
BLK = 512
GROUP = 8
TOKENS = 4096


def levels(own_key, dims, cuts, smallest, largest):
    factor_of, own = 1.0, jax.random.fold_in(own_key, 6)
    for axis_at, blocks in cuts:
        heights = jnp.exp(jax.random.uniform(jax.random.fold_in(own, axis_at), (blocks,), jnp.float32, smallest / len(cuts), largest / len(cuts)))
        factor_of = factor_of * jnp.repeat(heights, dims[axis_at] // blocks).reshape([-1 if axis == axis_at else 1 for axis in range(len(dims))])
    return factor_of


def normal_values(key, shape, width, most, shards=(), kind=jnp.bfloat16):
    gain = levels(key, shape, shards, -0.22, 0.18) if shards else 1.0
    result = jax.random.normal(key, shape, jnp.float32) * width * gain
    return jnp.minimum(jnp.maximum(result, -most), most).astype(kind)


def setup_inputs(seed: int = 0) -> dict:
    keys = jax.random.split(jax.random.key(seed), 9)
    return {
        "query_rows": normal_values(keys[0], (TOKENS, H * HD), 1.0, 6.0, ((0, 32),)),
        "key_rows": normal_values(keys[1], (TOKENS, KVH * HD), 1.0, 6.0, ((0, 32),)),
        "value_rows": normal_values(keys[2], (TOKENS, KVH * HD), 1.0, 6.0, ((0, 32),)),
        "grad_out": normal_values(keys[3], (TOKENS, H * HD), (HD // 2), 384.0, ((0, 32),)),
        "query_map": normal_values(keys[4], (H, HD, FH), (HD // 8) ** -0.5, 1.5, ((0, 8), (1, 4))),
        "key_map": normal_values(keys[5], (H, HD, FH), (HD // 8) ** -0.5, 1.5, ((0, 8), (1, 4))),
        "prefix_state": normal_values(keys[6], (H, 2 * FH, HD), 4.0, 24.0, ((0, 8),), jnp.float32),
        "prefix_norm": jnp.clip(jnp.exp(math.log(256.0) - 2.7725887 * jax.random.uniform(keys[7], (H, 2 * FH), jnp.float32) ** levels(keys[7], (H, 2 * FH), ((0, 8),), -0.2, 0.2)), 16.0, 256.0),
    }


precise = lax.Precision.HIGHEST


def round_low(array):
    return lax.optimization_barrier(array.astype(jnp.bfloat16))


def to_wide(array):
    return array.astype(jnp.float32)


def feature_pair(logits):
    widened = logits.astype(jnp.float32)
    upper_exp = jnp.exp(widened)
    lower_exp = jnp.exp(-widened)
    return upper_exp / jnp.sum(upper_exp, axis=-1, keepdims=True), lower_exp / jnp.sum(lower_exp, axis=-1, keepdims=True)


def feature_back(positive, negative, upstream):
    half_width = positive.shape[-1]
    first_half = upstream[..., :half_width]
    second_half = upstream[..., half_width:]
    first_term = positive * (first_half - jnp.sum(positive * first_half, axis=-1, keepdims=True))
    second_term = negative * (second_half - jnp.sum(negative * second_half, axis=-1, keepdims=True))
    return first_term - second_term


def causal_mask(length):
    position = jnp.arange(length)
    return (position[:, None] >= position[None, :]).astype(jnp.float32)


def recompute(state_sum, norm_sum, queries, key_part, value_part, grad_part, query_map, key_map):
    key_wide = jnp.repeat(key_part, GROUP, axis=1)
    value_wide = jnp.repeat(value_part, GROUP, axis=1)
    query_logits = round_low(jnp.einsum("thd,hdf->thf", to_wide(queries), to_wide(query_map)))
    key_logits = round_low(jnp.einsum("thd,hdf->thf", to_wide(key_wide), to_wide(key_map)))
    query_pos, query_neg = feature_pair(query_logits)
    key_pos, key_neg = feature_pair(key_logits)
    query_feat = to_wide(round_low(jnp.concatenate((query_pos, query_neg), axis=-1)))
    key_feat = to_wide(round_low(jnp.concatenate((key_pos, key_neg), axis=-1)))
    state_low = to_wide(round_low(state_sum))
    scores = jnp.einsum("thf,shf->hts", query_feat, key_feat) * causal_mask(BLK)
    scores_low = to_wide(round_low(scores))
    numerator = jnp.einsum("thf,hfd->thd", query_feat, state_low) + jnp.einsum("hts,shd->thd", scores_low, to_wide(value_wide))
    denominator = jnp.einsum("thf,hf->th", query_feat, norm_sum, precision=precise) + jnp.sum(scores, axis=-1).T
    attended = numerator / denominator[..., None]
    scaled = to_wide(grad_part) / denominator[..., None]
    scaled_low = to_wide(round_low(scaled))
    norm_grad = -jnp.sum(scaled * attended, axis=-1)
    return (key_wide, value_wide, query_pos, query_neg, key_pos, key_neg, query_feat, key_feat, state_low, scores_low, scaled_low, norm_grad)


def advance(state_sum, norm_sum, key_feat, value_wide):
    new_state = state_sum + jnp.einsum("shf,shd->hfd", key_feat, to_wide(value_wide))
    new_norm = norm_sum + jnp.sum(key_feat, axis=0)
    return new_state, new_norm


def reference(query_rows, key_rows, value_rows, grad_out, query_map, key_map, prefix_state, prefix_norm):
    blocks = TOKENS // BLK
    block_inputs = (query_rows.reshape(blocks, BLK, H, HD), key_rows.reshape(blocks, BLK, KVH, HD), value_rows.reshape(blocks, BLK, KVH, HD), grad_out.reshape(blocks, BLK, H, HD))

    def forward_step(carried, block_items):
        state_sum, norm_sum = carried
        queries, key_part, value_part, grad_part = block_items
        pieces = recompute(state_sum, norm_sum, queries, key_part, value_part, grad_part, query_map, key_map)
        value_wide = pieces[1]
        query_feat = pieces[6]
        key_feat = pieces[7]
        scaled_low = pieces[10]
        norm_grad = pieces[11]
        suffix_part = jnp.einsum("thf,thd->hfd", query_feat, scaled_low)
        suffix_norm_part = jnp.einsum("thf,th->hf", query_feat, norm_grad, precision=precise)
        return advance(state_sum, norm_sum, key_feat, value_wide), (suffix_part, suffix_norm_part)

    final_state, (suffix_parts, suffix_norms) = lax.scan(forward_step, (prefix_state, prefix_norm), block_inputs)
    suffix_next = jnp.flip(jnp.cumsum(jnp.flip(suffix_parts, 0), axis=0), 0) - suffix_parts
    suffix_norm_next = jnp.flip(jnp.cumsum(jnp.flip(suffix_norms, 0), axis=0), 0) - suffix_norms
    mask = causal_mask(BLK)

    def backward_step(carried, block_items):
        state_sum, norm_sum, query_map_acc, key_map_acc = carried
        queries, key_part, value_part, grad_part, suffix_after, suffix_norm_after = block_items
        (key_wide, value_wide, query_pos, query_neg, key_pos, key_neg, query_feat, key_feat, state_low, scores_low, scaled_low, norm_grad) = recompute(state_sum, norm_sum, queries, key_part, value_part, grad_part, query_map, key_map)
        dscores = (jnp.einsum("thd,shd->hts", scaled_low, to_wide(value_wide)) + norm_grad.T[:, :, None]) * mask
        dscores_low = to_wide(round_low(dscores))
        suffix_low = to_wide(round_low(suffix_after))
        dfeat_query = jnp.einsum("thd,hfd->thf", scaled_low, state_low) + norm_grad[..., None] * norm_sum[None] + jnp.einsum("hts,shf->thf", dscores_low, key_feat)
        dfeat_key = jnp.einsum("hts,thf->shf", dscores_low, query_feat) + jnp.einsum("shd,hfd->shf", to_wide(value_wide), suffix_low) + suffix_norm_after[None]
        dvalue = jnp.einsum("hts,thd->shd", scores_low, scaled_low) + jnp.einsum("shf,hfd->shd", key_feat, suffix_low)
        dlog_query = to_wide(round_low(feature_back(query_pos, query_neg, dfeat_query)))
        dlog_key = to_wide(round_low(feature_back(key_pos, key_neg, dfeat_key)))
        query_grad = jnp.einsum("thf,hdf->thd", dlog_query, to_wide(query_map)).astype(jnp.bfloat16)
        key_heads_grad = jnp.einsum("shf,hdf->shd", dlog_key, to_wide(key_map))
        key_grad = jnp.sum(key_heads_grad.reshape(BLK, KVH, GROUP, HD), axis=2).astype(jnp.bfloat16)
        value_grad = jnp.sum(dvalue.reshape(BLK, KVH, GROUP, HD), axis=2).astype(jnp.bfloat16)
        query_map_acc = query_map_acc + jnp.einsum("thd,thf->hdf", to_wide(queries), dlog_query)
        key_map_acc = key_map_acc + jnp.einsum("thd,thf->hdf", to_wide(key_wide), dlog_key)
        new_state, new_norm = advance(state_sum, norm_sum, key_feat, value_wide)
        return (new_state, new_norm, query_map_acc, key_map_acc), (query_grad, key_grad, value_grad)

    start = (prefix_state, prefix_norm, jnp.zeros((H, HD, FH), jnp.float32), jnp.zeros((H, HD, FH), jnp.float32))
    finals, outputs = lax.scan(backward_step, start, block_inputs + (suffix_next, suffix_norm_next))
    grad_queries = outputs[0].reshape(TOKENS, H * HD)
    grad_keys = outputs[1].reshape(TOKENS, KVH * HD)
    grad_values = outputs[2].reshape(TOKENS, KVH * HD)
    grad_prefix_state = jnp.sum(suffix_parts, axis=0)
    return (grad_queries, grad_keys, grad_values, finals[2], finals[3], grad_prefix_state)
```

```python
import functools

import jax
import jax.numpy as jnp
from jax import lax
from jax.experimental import pallas as pl
from jax.experimental.pallas import tpu as pltpu
from jax.sharding import PartitionSpec as P

BLK = 512
TILE = 256
PAIR = 2
EXT = 16
LIMIT = 40 * 1024 * 1024

F32 = jnp.float32
BF16 = jnp.bfloat16
SMEM = pltpu.SMEM


def nn(left, right):
    return lax.dot_general(left, right, (((1,), (0,)), ((), ())), preferred_element_type=F32)


def nt(left, right):
    return lax.dot_general(left, right, (((1,), (1,)), ((), ())), preferred_element_type=F32)


def turned(array):
    return array.astype(F32).T.astype(array.dtype)


def column(row, width):
    n = row.shape[1]
    square = jnp.broadcast_to(row, (n, n)).T
    return jnp.concatenate([square] * (width // n), axis=1)


def thirds(row):
    rows = jnp.broadcast_to(row, (EXT, row.shape[1]))
    high = rows.astype(BF16).astype(F32)
    middle = (rows - high).astype(BF16).astype(F32)
    low = rows - high - middle
    place = lax.broadcasted_iota(jnp.int32, rows.shape, 0)
    picked = jnp.where(place == 0, high, jnp.where(place == 1, middle, low))
    return jnp.where(place < 3, picked, 0.0).astype(BF16)


def whole_row(block):
    return jnp.sum(block.astype(F32), axis=0, keepdims=True)


def weight_rows(ref, u):
    whole = jnp.concatenate([ref[i, u] for i in range(ref.shape[0])], axis=0)
    return turned(whole)


def features(weight, rows):
    logits = nt(weight, rows).astype(BF16).astype(F32)
    upper = jnp.exp(logits)
    lower = jnp.exp(-logits)
    upper = upper * (1.0 / jnp.sum(upper, axis=0, keepdims=True))
    lower = lower * (1.0 / jnp.sum(lower, axis=0, keepdims=True))
    return jnp.concatenate([upper, lower], axis=0)


def feature_back(feats, upstream):
    half = feats.shape[0] // 2
    weighted = feats * upstream
    first, second = weighted[:half], weighted[half:]
    first = first - feats[:half] * jnp.sum(first, axis=0, keepdims=True)
    second = second - feats[half:] * jnp.sum(second, axis=0, keepdims=True)
    return (first - second).astype(BF16)


def gather(offsets, refs, out):
    rows = refs[0].shape[0]
    for r, ref in enumerate(refs):
        out[pl.ds(pl.multiple_of(offsets[r], rows), rows), :] = ref[...]


def scatter(offsets, source, refs):
    rows = refs[0].shape[0]
    for r, ref in enumerate(refs):
        ref[...] = source[pl.ds(pl.multiple_of(offsets[r], rows), rows), :].astype(ref.dtype)


def pack_kernel(columns, inputs, width, table, *refs):
    sources, outs, sems = refs[:inputs], refs[inputs:-1], refs[-1]
    copies = []
    for r, out in enumerate(outs):
        for s in range(columns):
            at = pl.multiple_of(table[r * columns + s] * width, width)
            for i, source in enumerate(sources):
                to = (s * inputs + i) * width
                copies.append(
                    pltpu.make_async_copy(
                        source.at[:, pl.ds(at, width)],
                        out.at[:, pl.ds(to, width)],
                        sems.at[len(copies)],
                    )
                )
    for copy in copies:
        copy.start()
    for copy in copies:
        copy.wait()


def pack(table, sources, pieces, columns, width):
    rows = sources[0].shape[0]
    total = columns * len(sources) * width
    return pl.pallas_call(
        functools.partial(pack_kernel, columns, len(sources), width),
        out_shape=[jax.ShapeDtypeStruct((rows, total), sources[0].dtype)] * pieces,
        in_specs=[pl.BlockSpec(memory_space=SMEM)]
        + [pl.BlockSpec(memory_space=pl.ANY)] * len(sources),
        out_specs=[pl.BlockSpec(memory_space=pl.ANY)] * pieces,
        scratch_shapes=[pltpu.SemaphoreType.DMA((pieces * columns * len(sources),))],
        cost_estimate=pl.CostEstimate(
            flops=0, bytes_accessed=4 * pieces * rows * total, transcendentals=0
        ),
        name="pack",
    )(table, *sources)


def unpack_kernel(outputs, width, table, *refs):
    pieces, outs, sems = refs[: -outputs - 1], refs[-outputs - 1 : -1], refs[-1]
    copies = []
    for r, piece in enumerate(pieces):
        at = pl.multiple_of(table[r] * width, width)
        for i, out in enumerate(outs):
            copies.append(
                pltpu.make_async_copy(
                    piece.at[:, pl.ds(i * width, width)],
                    out.at[:, pl.ds(at, width)],
                    sems.at[len(copies)],
                )
            )
    for copy in copies:
        copy.start()
    for copy in copies:
        copy.wait()


def unpack(table, pieces, outputs, width):
    rows = pieces[0].shape[0]
    total = len(pieces) * width
    return pl.pallas_call(
        functools.partial(unpack_kernel, outputs, width),
        out_shape=[jax.ShapeDtypeStruct((rows, total), pieces[0].dtype)] * outputs,
        in_specs=[pl.BlockSpec(memory_space=SMEM)]
        + [pl.BlockSpec(memory_space=pl.ANY)] * len(pieces),
        out_specs=[pl.BlockSpec(memory_space=pl.ANY)] * outputs,
        scratch_shapes=[pltpu.SemaphoreType.DMA((len(pieces) * outputs,))],
        cost_estimate=pl.CostEstimate(
            flops=0, bytes_accessed=4 * rows * total * outputs, transcendentals=0
        ),
        name="unpack",
    )(table, *pieces)


def state_kernel(part, offsets, *refs):
    k_refs, v_refs, (w_ref, out, k_all, v_all) = refs[:part], refs[part : 2 * part], refs[2 * part :]
    hd = k_all.shape[1]

    @pl.when(pl.program_id(0) == 0)
    def _():
        gather(offsets, k_refs, k_all)
        gather(offsets, v_refs, v_all)

    for u in range(out.shape[0]):
        weight = weight_rows(w_ref, u)
        feats = features(weight[weight.shape[0] // 2 :], k_all[...]).astype(BF16)
        out[u, :hd, :] = nn(feats, v_all[...]).astype(BF16)
        ones = jnp.ones((EXT, feats.shape[1]), BF16)
        out[u, hd:, :] = thirds(nt(ones, feats)[:1])


def block_kernel(part, offsets, *refs):
    k_refs, v_refs = refs[:part], refs[part : 2 * part]
    q_refs, g_refs = refs[2 * part : 3 * part], refs[3 * part : 4 * part]
    w_ref, st_ref = refs[4 * part : 4 * part + 2]
    gq_refs = refs[4 * part + 2 : 5 * part + 2]
    dk_ref, dv_ref, sx_ref, gm_ref, k_all, v_all, vt_all, q_all, g_all, gq_all = refs[5 * part + 2 :]
    hd = k_all.shape[1]

    @pl.when(pl.program_id(0) == 0)
    def _():
        gather(offsets, k_refs, k_all)
        gather(offsets, v_refs, v_all)
        vt_all[...] = turned(v_all[...])
        dv_ref[...] = jnp.zeros_like(dv_ref)

    gather(offsets, q_refs, q_all)
    gather(offsets, g_refs, g_all)
    maps = []
    earlier = lax.broadcasted_iota(jnp.int32, (TILE, TILE), 0) <= lax.broadcasted_iota(
        jnp.int32, (TILE, TILE), 1
    )

    def causal(array, begin):
        masked = jnp.where(earlier, array[begin:], 0.0)
        return masked if begin == 0 else jnp.concatenate([array[:begin], masked], axis=0)

    for u in range(PAIR):
        weight = weight_rows(w_ref, u)
        half = weight.shape[0] // 2
        lanes = slice(u * hd, (u + 1) * hd)
        q_feat = features(weight[:half], q_all[:, lanes])
        k_low = features(weight[half:], k_all[...]).astype(BF16)
        q_low = q_feat.astype(BF16)
        k_turned = turned(k_low)
        state = st_ref[u, :hd, :]
        state_turned = turned(state)
        norm = column(whole_row(st_ref[u, hd:, :]), TILE)
        g_turned = g_all[:, lanes].astype(F32).T
        back = []
        dkey = [jnp.zeros((2 * half, TILE), F32) for _ in range(BLK // TILE)]
        dvalue = [jnp.zeros((hd, TILE), F32) for _ in range(BLK // TILE)]
        suffix = jnp.zeros((2 * half, hd), F32)
        suffix_norm = jnp.zeros((2 * half, 1), F32)
        for j in range(BLK // TILE):
            begin, end = j * TILE, (j + 1) * TILE
            own = q_low[:, begin:end]
            own_wide = own.astype(F32)
            scores = causal(nn(k_turned[:end], own), begin)
            scores_low = scores.astype(BF16)
            numerator = nn(state_turned, own) + nn(vt_all[:, :end], scores_low)
            denominator = jnp.sum(own_wide * norm, axis=0, keepdims=True) + jnp.sum(
                scores, axis=0, keepdims=True
            )
            inverse = 1.0 / denominator
            scaled = g_turned[:, begin:end] * inverse
            scaled_low = scaled.astype(BF16)
            norm_grad = -jnp.sum(scaled * (numerator * inverse), axis=0, keepdims=True)
            dscores = causal(nn(v_all[:end, :], scaled_low) + norm_grad, begin).astype(BF16)
            dquery = nn(state, scaled_low) + norm * norm_grad + nn(k_low[:, :end], dscores)
            back.append(feature_back(q_feat[:, begin:end], dquery))
            for i in range(j + 1):
                rows = slice(i * TILE, (i + 1) * TILE)
                dkey[i] = dkey[i] + nt(own, dscores[rows])
                dvalue[i] = dvalue[i] + nt(scaled_low, scores_low[rows])
            suffix = suffix + nt(own, scaled_low)
            suffix_norm = suffix_norm + jnp.sum(own_wide * norm_grad, axis=1, keepdims=True)
        dlog = jnp.concatenate(back, axis=1)
        gq_all[:, lanes] = nn(turned(dlog), weight[:half])
        maps.append(nn(dlog, q_all[:, lanes]))
        dk_ref[u] = jnp.concatenate(dkey, axis=1)
        dv_ref[...] += jnp.concatenate(dvalue, axis=1)
        sx_ref[u, :hd, :] = suffix.astype(BF16)
        sx_ref[u, hd:, :] = thirds(jnp.broadcast_to(suffix_norm, (2 * half, 2 * half)).T[:1])
    gm_ref[0] = jnp.concatenate(maps, axis=0).T.astype(gm_ref.dtype)
    scatter(offsets, gq_all, gq_refs)


def key_kernel(part, offsets, *refs):
    k_refs, v_refs = refs[:part], refs[part : 2 * part]
    w_ref, sx_ref, dk_ref, dv_ref = refs[2 * part : 2 * part + 4]
    outs = refs[2 * part + 4 : 3 * part + 4]
    gm_ref, k_all, v_all, vt_all, total, logs, weights, pair = refs[3 * part + 4 :]
    hd = k_all.shape[1]
    step = pl.program_id(0)

    @pl.when(step == 0)
    def _():
        gather(offsets, k_refs, k_all)
        gather(offsets, v_refs, v_all)
        vt_all[...] = turned(v_all[...])
        total[...] = dv_ref[...]

    maps = []
    for u in range(PAIR):
        weight = weight_rows(w_ref, u)
        half = weight.shape[0] // 2
        weight = weight[half:]
        feats = features(weight, k_all[...])
        suffix = sx_ref[u, :hd, :]
        norm = column(whole_row(sx_ref[u, hd:, :]), BLK)
        dlog = feature_back(feats, dk_ref[u] + nn(suffix, vt_all[...]) + norm)
        at = pl.ds(pl.multiple_of((step * PAIR + u) * half, half), half)
        logs[at, :] = dlog
        weights[at, :] = weight
        maps.append(nn(dlog, k_all[...]))
        total[...] += nn(turned(suffix), feats.astype(BF16))
    gm_ref[0] = jnp.concatenate(maps, axis=0).T.astype(gm_ref.dtype)

    @pl.when(step == pl.num_programs(0) - 1)
    def _():
        pair[:, :hd] = nn(turned(logs[...]), weights[...])
        pair[:, hd:] = total[...].T
        scatter(offsets, pair, outs)


def total_kernel(*refs):
    out = refs[-1]
    heads, hd = out.shape[0], out.shape[2]
    for h in range(heads):
        out[h, :hd, :] = sum(ref[h, :hd, :].astype(F32) for ref in refs[:-1]).astype(BF16)
        out[h, hd:, :] = thirds(sum(whole_row(ref[h, hd:, :]) for ref in refs[:-1]))


def spread_kernel(grp, others, closing, block_weight, total_weight, place, *refs):
    parts, totals, refs = refs[:grp], refs[grp : grp + others], refs[grp + others :]
    if closing:
        outs, grad, scratch = refs[:grp], refs[grp], refs[grp + 1]
    else:
        state_ref, norm_ref, outs = refs[0], refs[1], refs[2:]
    heads, hd = parts[0].shape[0], parts[0].shape[2]
    for h in range(heads):
        states = [ref[h, :hd, :].astype(F32) for ref in parts]
        norms = [whole_row(ref[h, hd:, :]) for ref in parts]
        others_state = [ref[h, :hd, :].astype(F32) for ref in totals]
        others_norm = [whole_row(ref[h, hd:, :]) for ref in totals]
        if closing:
            base, base_norm = jnp.zeros_like(states[0]), jnp.zeros_like(norms[0])
            scratch[...] = sum(states) + sum(others_state)
            rows = grad.shape[1]
            grad[h] = scratch[pl.ds(pl.multiple_of(place[0] * rows, rows), rows), :]
        else:
            base, base_norm = state_ref[h], norm_ref[pl.ds(h, 1), :]
        for i, (state, norm) in enumerate(zip(others_state, others_norm)):
            base = base + total_weight[i] * state
            base_norm = base_norm + total_weight[i] * norm
        for r, out in enumerate(outs):
            state, norm = base, base_norm
            for i in range(grp):
                if i != r:
                    state = state + block_weight[r * grp + i] * states[i]
                    norm = norm + block_weight[r * grp + i] * norms[i]
            out[h, :hd, :] = state.astype(BF16)
            out[h, hd:, :] = thirds(norm)


def whole_call(kernel, outs, smem, arrays, name, scratch=()):
    total = sum(a.size * a.dtype.itemsize for a in (*arrays, *outs))
    return pl.pallas_call(
        kernel,
        out_shape=outs,
        in_specs=[pl.BlockSpec(memory_space=SMEM)] * len(smem)
        + [pl.BlockSpec(memory_space=pltpu.VMEM)] * len(arrays),
        out_specs=[pl.BlockSpec(memory_space=pltpu.VMEM)] * len(outs),
        scratch_shapes=list(scratch),
        compiler_params=pltpu.CompilerParams(vmem_limit_bytes=LIMIT),
        cost_estimate=pl.CostEstimate(flops=total, bytes_accessed=total, transcendentals=0),
        name=name,
    )(*smem, *arrays)


def shards(
    query_rows, key_rows, value_rows, grad_out, query_map, key_map, prefix_state, prefix_norm
):
    ctx, fsdp = lax.axis_size("ctx"), lax.axis_size("fsdp")
    tok = query_rows.shape[0]
    heads, map_rows, half = query_map.shape
    hd = map_rows * fsdp
    kv_heads = key_rows.shape[1] // hd
    replicas = ctx // kv_heads
    part = BLK // tok
    grp = ctx // part
    mine = lax.axis_index("ctx")
    at, block, seq = mine % part, mine // part, lax.axis_index("fsdp")

    def within(array, shift):
        return lax.ppermute(
            array, "ctx", [(d, d // part * part + (d + shift) % part) for d in range(ctx)]
        )

    def across(array, shift):
        return lax.ppermute(array, "ctx", [(d, (d + shift * part) % ctx) for d in range(ctx)])

    def along(array, shift):
        return lax.ppermute(array, "fsdp", [(d, (d + shift) % fsdp) for d in range(fsdp)])

    def owner(shift, slot):
        return (block + slot) % grp * part + (at + shift) % part

    def ints(values):
        return jnp.stack([jnp.asarray(v, jnp.int32) for v in values])

    shifts, slots = range(part), range(grp)
    order = list(reversed(slots))
    offsets = ints([(at - r) % part * tok for r in shifts])

    own_maps = jnp.concatenate((query_map, key_map), axis=-1)
    kv_table = ints([owner(r, s) // replicas for r in shifts for s in slots])
    kv_sent = pack(kv_table, (key_rows, value_rows), part, grp, hd)
    kv = [kv_sent[0]] + [within(kv_sent[r], r) for r in shifts[1:]]
    maps = jnp.stack([own_maps] + [across(own_maps, -s) for s in slots[1:]])
    maps = lax.all_gather(maps, "fsdp")

    rows = {}
    for s in order:
        table = ints([owner(r, s) for r in shifts])
        sent = pack(table, (query_rows, grad_out), part, 1, heads * hd)
        rows[s] = [sent[0]] + [within(sent[r], r) for r in shifts[1:]]

    grid = (heads // PAIR,)
    params = pltpu.CompilerParams(
        dimension_semantics=("arbitrary",), vmem_limit_bytes=LIMIT
    )
    in_smem = pl.BlockSpec(memory_space=SMEM)

    def piece_specs(column, count):
        return [pl.BlockSpec((tok, count * hd), column)] * part

    def kv_specs(s):
        return piece_specs(lambda h: (0, 2 * s), 1) + piece_specs(lambda h: (0, 2 * s + 1), 1)

    def map_spec(s):
        return pl.BlockSpec((fsdp, None, PAIR, map_rows, 2 * half), lambda h: (0, s, h, 0, 0))

    ext_spec = pl.BlockSpec((PAIR, hd + EXT, hd), lambda h: (h, 0, 0))
    ext_shape = jax.ShapeDtypeStruct((heads, hd + EXT, hd), BF16)
    gm_spec = pl.BlockSpec((1, hd, PAIR * half), lambda h: (h, 0, 0))
    gm_shape = jax.ShapeDtypeStruct((heads // PAIR, hd, PAIR * half), BF16)
    dk_spec = pl.BlockSpec((PAIR, 2 * half, BLK), lambda h: (h, 0, 0))
    dv_spec = pl.BlockSpec((hd, BLK), lambda h: (0, 0))
    unit = 2 * heads * BLK * hd

    def states_of(s):
        return pl.pallas_call(
            functools.partial(state_kernel, part),
            out_shape=ext_shape,
            grid=grid,
            in_specs=[in_smem] + kv_specs(s) + [map_spec(s)],
            out_specs=ext_spec,
            scratch_shapes=[pltpu.VMEM((BLK, hd), BF16)] * 2,
            compiler_params=params,
            cost_estimate=pl.CostEstimate(
                flops=unit * 2 * hd, bytes_accessed=2 * heads * hd * hd, transcendentals=0
            ),
            name="states",
        )(offsets, *kv, *kv, maps)

    def scan(partial, before, extra, closing):
        parts = [partial[0]] + [across(partial[s], s) for s in slots[1:]]
        (total,) = whole_call(total_kernel, [ext_shape], [], parts, "totals")
        others = [along(total, r) for r in range(1, fsdp)]
        result = whole_call(
            functools.partial(spread_kernel, grp, fsdp - 1, closing),
            [ext_shape] * grp
            + [jax.ShapeDtypeStruct((heads, map_rows, hd), F32)] * closing,
            [*weights(before), ints([seq])],
            parts + others + extra,
            "spread",
            [pltpu.VMEM((hd, hd), F32)] * closing,
        )
        return [result[0]] + [across(result[s], -s) for s in slots[1:]], result[grp:]

    def weights(before):
        seqs = [(seq - r) % fsdp for r in range(1, fsdp)]
        blocks = [(block - r) % grp for r in slots]
        return (
            jnp.stack([before(b, a).astype(F32) for a in blocks for b in blocks]),
            jnp.stack([before(other, seq).astype(F32) for other in seqs]),
        )

    partial = {s: states_of(s) for s in order}
    state, _ = scan(partial, lambda a, b: a < b, [prefix_state, prefix_norm], False)

    def block_of(s):
        half_specs = piece_specs(lambda h: (0, h), PAIR) + piece_specs(
            lambda h: (0, grid[0] + h), PAIR
        )
        return pl.pallas_call(
            functools.partial(block_kernel, part),
            out_shape=[jax.ShapeDtypeStruct((tok, heads * hd), BF16)] * part
            + [
                jax.ShapeDtypeStruct((heads, 2 * half, BLK), F32),
                jax.ShapeDtypeStruct((hd, BLK), F32),
                ext_shape,
                gm_shape,
            ],
            grid=grid,
            in_specs=[in_smem] + kv_specs(s) + half_specs + [map_spec(s), ext_spec],
            out_specs=piece_specs(lambda h: (0, h), PAIR) + [dk_spec, dv_spec, ext_spec, gm_spec],
            scratch_shapes=[
                pltpu.VMEM((BLK, hd), BF16),
                pltpu.VMEM((BLK, hd), BF16),
                pltpu.VMEM((hd, BLK), BF16),
                pltpu.VMEM((BLK, PAIR * hd), BF16),
                pltpu.VMEM((BLK, PAIR * hd), BF16),
                pltpu.VMEM((BLK, PAIR * hd), F32),
            ],
            compiler_params=params,
            cost_estimate=pl.CostEstimate(
                flops=unit * 8 * BLK, bytes_accessed=16 * heads * BLK * hd, transcendentals=0
            ),
            name="blocks",
        )(offsets, *kv, *kv, *rows[s], *rows[s], maps, state[s])

    blocks = {}
    for s in order:
        result = block_of(s)
        blocks[s] = (result[:part], *result[part:])
    partial = {s: blocks[s][3] for s in slots}
    suffix, (grad_prefix,) = scan(partial, lambda a, b: a > b, [], True)

    kv_type = BF16 if replicas == 1 else F32

    def keys_of(s):
        return pl.pallas_call(
            functools.partial(key_kernel, part),
            out_shape=[jax.ShapeDtypeStruct((tok, 2 * hd), kv_type)] * part + [gm_shape],
            grid=grid,
            in_specs=[in_smem] + kv_specs(s) + [map_spec(s), ext_spec, dk_spec, dv_spec],
            out_specs=piece_specs(lambda h: (0, 0), 2) + [gm_spec],
            scratch_shapes=[
                pltpu.VMEM((BLK, hd), BF16),
                pltpu.VMEM((BLK, hd), BF16),
                pltpu.VMEM((hd, BLK), BF16),
                pltpu.VMEM((hd, BLK), F32),
                pltpu.VMEM((heads * half, BLK), BF16),
                pltpu.VMEM((heads * half, hd), BF16),
                pltpu.VMEM((BLK, 2 * hd), F32),
            ],
            compiler_params=params,
            cost_estimate=pl.CostEstimate(
                flops=unit * 4 * hd, bytes_accessed=4 * heads * BLK * hd, transcendentals=0
            ),
            name="keys",
        )(offsets, *kv, *kv, maps, suffix[s], blocks[s][1], blocks[s][2])

    def returned(pieces):
        return [pieces[0]] + [within(pieces[r], -r) for r in shifts[1:]]

    def fold(parts):
        stacked = jnp.stack([parts[s] for s in slots])
        pieces = stacked.reshape(grp, heads // PAIR, fsdp, map_rows, PAIR * half)

        def rows_for(device):
            return lax.dynamic_index_in_dim(pieces, device, 2, keepdims=False)

        summed = rows_for(seq).astype(F32)
        for r in range(1, fsdp):
            summed = summed + along(rows_for((seq + r) % fsdp), r).astype(F32)
        sent = summed.astype(BF16)
        result = summed[0]
        for s in slots[1:]:
            result = result + across(sent[s], s).astype(F32)
        result = result.reshape(heads // PAIR, map_rows, PAIR, half)
        return jnp.swapaxes(result, 1, 2).reshape(heads, map_rows, half)

    table = ints([owner(r, s) for s in order for r in shifts])
    back = [piece for s in order for piece in returned(blocks[s][0])]
    (grad_queries,) = unpack(table, back, 1, heads * hd)
    query_map_grad = fold({s: blocks[s][4] for s in slots})

    keys = {s: keys_of(s) for s in slots}
    back = [piece for s in order for piece in returned(keys[s][:part])]
    grad_keys, grad_values = unpack(table, back, 2, hd)
    if replicas > 1:
        grad_keys, grad_values = (
            jnp.sum(a.reshape(tok, kv_heads, replicas, hd), axis=2)
            .astype(BF16)
            .reshape(tok, kv_heads * hd)
            for a in (grad_keys, grad_values)
        )
    key_map_grad = fold({s: keys[s][part] for s in slots})
    return grad_queries, grad_keys, grad_values, query_map_grad, key_map_grad, grad_prefix


def solution(mesh):
    rows, maps = P(("fsdp", "ctx"), None), P("ctx", "fsdp", None)
    return jax.shard_map(
        shards,
        mesh=mesh,
        in_specs=(rows,) * 4 + (maps, maps, P("ctx", None, None), P("ctx", None)),
        out_specs=(rows,) * 3 + (maps,) * 3,
        check_vma=False,
    )
```

```python
import functools

import jax
import jax.numpy as jnp
from jax import lax
from jax.experimental import pallas as pl
from jax.experimental.pallas import tpu as pltpu
from jax.sharding import PartitionSpec as P

BLK = 512
TILE = 256
PAIR = 2
EXT = 16
LIMIT = 40 * 1024 * 1024

F32 = jnp.float32
BF16 = jnp.bfloat16
SMEM = pltpu.SMEM


def nn(left, right):
    return lax.dot_general(left, right, (((1,), (0,)), ((), ())), preferred_element_type=F32)


def nt(left, right):
    return lax.dot_general(left, right, (((1,), (1,)), ((), ())), preferred_element_type=F32)


def turned(array):
    return array.astype(F32).T.astype(array.dtype)


def column(row, width):
    n = row.shape[1]
    square = jnp.broadcast_to(row, (n, n)).T
    return jnp.concatenate([square] * (width // n), axis=1)


def thirds(row):
    rows = jnp.broadcast_to(row, (EXT, row.shape[1]))
    high = rows.astype(BF16).astype(F32)
    middle = (rows - high).astype(BF16).astype(F32)
    low = rows - high - middle
    place = lax.broadcasted_iota(jnp.int32, rows.shape, 0)
    picked = jnp.where(place == 0, high, jnp.where(place == 1, middle, low))
    return jnp.where(place < 3, picked, 0.0).astype(BF16)


def whole_row(block):
    return jnp.sum(block.astype(F32), axis=0, keepdims=True)


def weight_rows(ref, u):
    whole = jnp.concatenate([ref[i, u] for i in range(ref.shape[0])], axis=0)
    return turned(whole)


def features(weight, rows):
    logits = nt(weight, rows).astype(BF16).astype(F32)
    upper = jnp.exp(logits)
    lower = jnp.exp(-logits)
    upper = upper * (1.0 / jnp.sum(upper, axis=0, keepdims=True))
    lower = lower * (1.0 / jnp.sum(lower, axis=0, keepdims=True))
    return jnp.concatenate([upper, lower], axis=0)


def feature_back(feats, upstream):
    half = feats.shape[0] // 2
    weighted = feats * upstream
    first, second = weighted[:half], weighted[half:]
    first = first - feats[:half] * jnp.sum(first, axis=0, keepdims=True)
    second = second - feats[half:] * jnp.sum(second, axis=0, keepdims=True)
    return (first - second).astype(BF16)


def gather(offsets, refs, out):
    rows = refs[0].shape[0]
    for r, ref in enumerate(refs):
        out[pl.ds(pl.multiple_of(offsets[r], rows), rows), :] = ref[...]


def scatter(offsets, source, refs):
    rows = refs[0].shape[0]
    for r, ref in enumerate(refs):
        ref[...] = source[pl.ds(pl.multiple_of(offsets[r], rows), rows), :].astype(ref.dtype)


def pack_kernel(columns, inputs, table, *refs):
    count = columns * inputs
    for r, out in enumerate(refs[-(len(refs) // (count + 1)) :]):
        width = out.shape[1] // count
        for i in range(count):
            out[:, i * width : (i + 1) * width] = refs[r * count + i][...]


def pack(table, sources, pieces, columns, width):
    rows = sources[0].shape[0]
    count = columns * len(sources)
    step = rows // 2

    def take(at):
        return pl.BlockSpec((step, width), lambda i, t: (i, t[at]))

    return pl.pallas_call(
        functools.partial(pack_kernel, columns, len(sources)),
        out_shape=[jax.ShapeDtypeStruct((rows, count * width), sources[0].dtype)] * pieces,
        grid_spec=pltpu.PrefetchScalarGridSpec(
            num_scalar_prefetch=1,
            grid=(rows // step,),
            in_specs=[
                take(r * columns + s)
                for r in range(pieces)
                for s in range(columns)
                for _ in sources
            ],
            out_specs=[pl.BlockSpec((step, count * width), lambda i, t: (i, 0))] * pieces,
        ),
        compiler_params=pltpu.CompilerParams(vmem_limit_bytes=LIMIT),
        cost_estimate=pl.CostEstimate(
            flops=0, bytes_accessed=4 * pieces * rows * count * width, transcendentals=0
        ),
        name="pack",
    )(table, *(list(sources) * (pieces * columns)))


def unpack_kernel(outputs, table, *refs):
    pieces, outs = refs[:-outputs], refs[-outputs:]
    for r, piece in enumerate(pieces):
        width = piece.shape[1] // outputs
        at = pl.ds(pl.multiple_of(table[r] * width, width), width)
        for i, out in enumerate(outs):
            out[:, at] = piece[:, i * width : (i + 1) * width]


def unpack(table, pieces, outputs, width):
    rows = pieces[0].shape[0]
    total = len(pieces) * width
    step = rows // 2
    return pl.pallas_call(
        functools.partial(unpack_kernel, outputs),
        out_shape=[jax.ShapeDtypeStruct((rows, total), pieces[0].dtype)] * outputs,
        grid=(rows // step,),
        in_specs=[pl.BlockSpec(memory_space=SMEM)]
        + [pl.BlockSpec((step, outputs * width), lambda i: (i, 0))] * len(pieces),
        out_specs=[pl.BlockSpec((step, total), lambda i: (i, 0))] * outputs,
        compiler_params=pltpu.CompilerParams(vmem_limit_bytes=LIMIT),
        cost_estimate=pl.CostEstimate(
            flops=0, bytes_accessed=4 * rows * total * outputs, transcendentals=0
        ),
        name="unpack",
    )(table, *pieces)


def state_kernel(part, offsets, *refs):
    k_refs, v_refs, (w_ref, out, k_all, v_all) = refs[:part], refs[part : 2 * part], refs[2 * part :]
    hd = k_all.shape[1]

    @pl.when(pl.program_id(0) == 0)
    def _():
        gather(offsets, k_refs, k_all)
        gather(offsets, v_refs, v_all)

    for u in range(out.shape[0]):
        weight = weight_rows(w_ref, u)
        feats = features(weight[weight.shape[0] // 2 :], k_all[...]).astype(BF16)
        out[u, :hd, :] = nn(feats, v_all[...]).astype(BF16)
        ones = jnp.ones((EXT, feats.shape[1]), BF16)
        out[u, hd:, :] = thirds(nt(ones, feats)[:1])


def block_kernel(part, offsets, *refs):
    k_refs, v_refs = refs[:part], refs[part : 2 * part]
    q_refs, g_refs = refs[2 * part : 3 * part], refs[3 * part : 4 * part]
    w_ref, st_ref = refs[4 * part : 4 * part + 2]
    gq_refs = refs[4 * part + 2 : 5 * part + 2]
    dk_ref, dv_ref, sx_ref, gm_ref, k_all, v_all, vt_all, q_all, g_all, gq_all = refs[5 * part + 2 :]
    hd = k_all.shape[1]

    @pl.when(pl.program_id(0) == 0)
    def _():
        gather(offsets, k_refs, k_all)
        gather(offsets, v_refs, v_all)
        vt_all[...] = turned(v_all[...])
        dv_ref[...] = jnp.zeros_like(dv_ref)

    gather(offsets, q_refs, q_all)
    gather(offsets, g_refs, g_all)
    maps = []
    earlier = lax.broadcasted_iota(jnp.int32, (TILE, TILE), 0) <= lax.broadcasted_iota(
        jnp.int32, (TILE, TILE), 1
    )

    def causal(array, begin):
        masked = jnp.where(earlier, array[begin:], 0.0)
        return masked if begin == 0 else jnp.concatenate([array[:begin], masked], axis=0)

    for u in range(PAIR):
        weight = weight_rows(w_ref, u)
        half = weight.shape[0] // 2
        lanes = slice(u * hd, (u + 1) * hd)
        q_feat = features(weight[:half], q_all[:, lanes])
        k_low = features(weight[half:], k_all[...]).astype(BF16)
        q_low = q_feat.astype(BF16)
        k_turned = turned(k_low)
        state = st_ref[u, :hd, :]
        state_turned = turned(state)
        norm = column(whole_row(st_ref[u, hd:, :]), TILE)
        g_turned = g_all[:, lanes].astype(F32).T
        back = []
        dkey = [jnp.zeros((2 * half, TILE), F32) for _ in range(BLK // TILE)]
        dvalue = [jnp.zeros((hd, TILE), F32) for _ in range(BLK // TILE)]
        suffix = jnp.zeros((2 * half, hd), F32)
        suffix_norm = jnp.zeros((2 * half, 1), F32)
        for j in range(BLK // TILE):
            begin, end = j * TILE, (j + 1) * TILE
            own = q_low[:, begin:end]
            own_wide = own.astype(F32)
            scores = causal(nn(k_turned[:end], own), begin)
            scores_low = scores.astype(BF16)
            numerator = nn(state_turned, own) + nn(vt_all[:, :end], scores_low)
            denominator = jnp.sum(own_wide * norm, axis=0, keepdims=True) + jnp.sum(
                scores, axis=0, keepdims=True
            )
            inverse = 1.0 / denominator
            scaled = g_turned[:, begin:end] * inverse
            scaled_low = scaled.astype(BF16)
            norm_grad = -jnp.sum(scaled * (numerator * inverse), axis=0, keepdims=True)
            dscores = causal(nn(v_all[:end, :], scaled_low) + norm_grad, begin).astype(BF16)
            dquery = nn(state, scaled_low) + norm * norm_grad + nn(k_low[:, :end], dscores)
            back.append(feature_back(q_feat[:, begin:end], dquery))
            for i in range(j + 1):
                rows = slice(i * TILE, (i + 1) * TILE)
                dkey[i] = dkey[i] + nt(own, dscores[rows])
                dvalue[i] = dvalue[i] + nt(scaled_low, scores_low[rows])
            suffix = suffix + nt(own, scaled_low)
            suffix_norm = suffix_norm + jnp.sum(own_wide * norm_grad, axis=1, keepdims=True)
        dlog = jnp.concatenate(back, axis=1)
        gq_all[:, lanes] = nn(turned(dlog), weight[:half])
        maps.append(nn(dlog, q_all[:, lanes]))
        dk_ref[u] = jnp.concatenate(dkey, axis=1)
        dv_ref[...] += jnp.concatenate(dvalue, axis=1)
        sx_ref[u, :hd, :] = suffix.astype(BF16)
        sx_ref[u, hd:, :] = thirds(jnp.broadcast_to(suffix_norm, (2 * half, 2 * half)).T[:1])
    gm_ref[0] = jnp.concatenate(maps, axis=0).T.astype(gm_ref.dtype)
    scatter(offsets, gq_all, gq_refs)


def key_kernel(part, offsets, *refs):
    k_refs, v_refs = refs[:part], refs[part : 2 * part]
    w_ref, sx_ref, dk_ref, dv_ref = refs[2 * part : 2 * part + 4]
    outs = refs[2 * part + 4 : 3 * part + 4]
    gm_ref, k_all, v_all, vt_all, total, logs, weights, pair = refs[3 * part + 4 :]
    hd = k_all.shape[1]
    step = pl.program_id(0)

    @pl.when(step == 0)
    def _():
        gather(offsets, k_refs, k_all)
        gather(offsets, v_refs, v_all)
        vt_all[...] = turned(v_all[...])
        total[...] = dv_ref[...]

    maps = []
    for u in range(PAIR):
        weight = weight_rows(w_ref, u)
        half = weight.shape[0] // 2
        weight = weight[half:]
        feats = features(weight, k_all[...])
        suffix = sx_ref[u, :hd, :]
        norm = column(whole_row(sx_ref[u, hd:, :]), BLK)
        dlog = feature_back(feats, dk_ref[u] + nn(suffix, vt_all[...]) + norm)
        at = pl.ds(pl.multiple_of((step * PAIR + u) * half, half), half)
        logs[at, :] = dlog
        weights[at, :] = weight
        maps.append(nn(dlog, k_all[...]))
        total[...] += nn(turned(suffix), feats.astype(BF16))
    gm_ref[0] = jnp.concatenate(maps, axis=0).T.astype(gm_ref.dtype)

    @pl.when(step == pl.num_programs(0) - 1)
    def _():
        pair[:, :hd] = nn(turned(logs[...]), weights[...])
        pair[:, hd:] = total[...].T
        scatter(offsets, pair, outs)


def total_kernel(*refs):
    out = refs[-1]
    heads, hd = out.shape[0], out.shape[2]
    for h in range(heads):
        out[h, :hd, :] = sum(ref[h, :hd, :].astype(F32) for ref in refs[:-1]).astype(BF16)
        out[h, hd:, :] = thirds(sum(whole_row(ref[h, hd:, :]) for ref in refs[:-1]))


def spread_kernel(grp, others, closing, block_weight, total_weight, place, *refs):
    parts, totals, refs = refs[:grp], refs[grp : grp + others], refs[grp + others :]
    if closing:
        outs, grad, scratch = refs[:grp], refs[grp], refs[grp + 1]
    else:
        state_ref, norm_ref, outs = refs[0], refs[1], refs[2:]
    heads, hd = parts[0].shape[0], parts[0].shape[2]
    for h in range(heads):
        states = [ref[h, :hd, :].astype(F32) for ref in parts]
        norms = [whole_row(ref[h, hd:, :]) for ref in parts]
        others_state = [ref[h, :hd, :].astype(F32) for ref in totals]
        others_norm = [whole_row(ref[h, hd:, :]) for ref in totals]
        if closing:
            base, base_norm = jnp.zeros_like(states[0]), jnp.zeros_like(norms[0])
            scratch[...] = sum(states) + sum(others_state)
            rows = grad.shape[1]
            grad[h] = scratch[pl.ds(pl.multiple_of(place[0] * rows, rows), rows), :]
        else:
            base, base_norm = state_ref[h], norm_ref[pl.ds(h, 1), :]
        for i, (state, norm) in enumerate(zip(others_state, others_norm)):
            base = base + total_weight[i] * state
            base_norm = base_norm + total_weight[i] * norm
        for r, out in enumerate(outs):
            state, norm = base, base_norm
            for i in range(grp):
                if i != r:
                    state = state + block_weight[r * grp + i] * states[i]
                    norm = norm + block_weight[r * grp + i] * norms[i]
            out[h, :hd, :] = state.astype(BF16)
            out[h, hd:, :] = thirds(norm)


def whole_call(kernel, outs, smem, arrays, name, scratch=()):
    total = sum(a.size * a.dtype.itemsize for a in (*arrays, *outs))
    return pl.pallas_call(
        kernel,
        out_shape=outs,
        in_specs=[pl.BlockSpec(memory_space=SMEM)] * len(smem)
        + [pl.BlockSpec(memory_space=pltpu.VMEM)] * len(arrays),
        out_specs=[pl.BlockSpec(memory_space=pltpu.VMEM)] * len(outs),
        scratch_shapes=list(scratch),
        compiler_params=pltpu.CompilerParams(vmem_limit_bytes=LIMIT),
        cost_estimate=pl.CostEstimate(flops=total, bytes_accessed=total, transcendentals=0),
        name=name,
    )(*smem, *arrays)


def shards(
    query_rows, key_rows, value_rows, grad_out, query_map, key_map, prefix_state, prefix_norm
):
    ctx, fsdp = lax.axis_size("ctx"), lax.axis_size("fsdp")
    tok = query_rows.shape[0]
    heads, map_rows, half = query_map.shape
    hd = map_rows * fsdp
    kv_heads = key_rows.shape[1] // hd
    replicas = ctx // kv_heads
    part = BLK // tok
    grp = ctx // part
    mine = lax.axis_index("ctx")
    at, block, seq = mine % part, mine // part, lax.axis_index("fsdp")

    def within(array, shift):
        return lax.ppermute(
            array, "ctx", [(d, d // part * part + (d + shift) % part) for d in range(ctx)]
        )

    def across(array, shift):
        return lax.ppermute(array, "ctx", [(d, (d + shift * part) % ctx) for d in range(ctx)])

    def along(array, shift):
        return lax.ppermute(array, "fsdp", [(d, (d + shift) % fsdp) for d in range(fsdp)])

    def owner(shift, slot):
        return (block + slot) % grp * part + (at + shift) % part

    def ints(values):
        return jnp.stack([jnp.asarray(v, jnp.int32) for v in values])

    shifts, slots = range(part), range(grp)
    order = list(reversed(slots))
    offsets = ints([(at - r) % part * tok for r in shifts])

    own_maps = jnp.concatenate((query_map, key_map), axis=-1)
    kv_table = ints([owner(r, s) // replicas for r in shifts for s in slots])
    kv_sent = pack(kv_table, (key_rows, value_rows), part, grp, hd)
    kv = [kv_sent[0]] + [within(kv_sent[r], r) for r in shifts[1:]]
    maps = jnp.stack([own_maps] + [across(own_maps, -s) for s in slots[1:]])
    maps = lax.all_gather(maps, "fsdp")

    rows = {}
    for s in order:
        table = ints([owner(r, s) for r in shifts])
        sent = pack(table, (query_rows, grad_out), part, 1, heads * hd)
        rows[s] = [sent[0]] + [within(sent[r], r) for r in shifts[1:]]

    grid = (heads // PAIR,)
    params = pltpu.CompilerParams(
        dimension_semantics=("arbitrary",), vmem_limit_bytes=LIMIT
    )
    in_smem = pl.BlockSpec(memory_space=SMEM)

    def piece_specs(column, count):
        return [pl.BlockSpec((tok, count * hd), column)] * part

    def kv_specs(s):
        return piece_specs(lambda h: (0, 2 * s), 1) + piece_specs(lambda h: (0, 2 * s + 1), 1)

    def map_spec(s):
        return pl.BlockSpec((fsdp, None, PAIR, map_rows, 2 * half), lambda h: (0, s, h, 0, 0))

    ext_spec = pl.BlockSpec((PAIR, hd + EXT, hd), lambda h: (h, 0, 0))
    ext_shape = jax.ShapeDtypeStruct((heads, hd + EXT, hd), BF16)
    gm_spec = pl.BlockSpec((1, hd, PAIR * half), lambda h: (h, 0, 0))
    gm_shape = jax.ShapeDtypeStruct((heads // PAIR, hd, PAIR * half), BF16)
    dk_spec = pl.BlockSpec((PAIR, 2 * half, BLK), lambda h: (h, 0, 0))
    dv_spec = pl.BlockSpec((hd, BLK), lambda h: (0, 0))
    unit = 2 * heads * BLK * hd

    def states_of(s):
        return pl.pallas_call(
            functools.partial(state_kernel, part),
            out_shape=ext_shape,
            grid=grid,
            in_specs=[in_smem] + kv_specs(s) + [map_spec(s)],
            out_specs=ext_spec,
            scratch_shapes=[pltpu.VMEM((BLK, hd), BF16)] * 2,
            compiler_params=params,
            cost_estimate=pl.CostEstimate(
                flops=unit * 2 * hd, bytes_accessed=2 * heads * hd * hd, transcendentals=0
            ),
            name="states",
        )(offsets, *kv, *kv, maps)

    def scan(partial, before, extra, closing):
        parts = [partial[0]] + [across(partial[s], s) for s in slots[1:]]
        (total,) = whole_call(total_kernel, [ext_shape], [], parts, "totals")
        others = [along(total, r) for r in range(1, fsdp)]
        result = whole_call(
            functools.partial(spread_kernel, grp, fsdp - 1, closing),
            [ext_shape] * grp
            + [jax.ShapeDtypeStruct((heads, map_rows, hd), F32)] * closing,
            [*weights(before), ints([seq])],
            parts + others + extra,
            "spread",
            [pltpu.VMEM((hd, hd), F32)] * closing,
        )
        return [result[0]] + [across(result[s], -s) for s in slots[1:]], result[grp:]

    def weights(before):
        seqs = [(seq - r) % fsdp for r in range(1, fsdp)]
        blocks = [(block - r) % grp for r in slots]
        return (
            jnp.stack([before(b, a).astype(F32) for a in blocks for b in blocks]),
            jnp.stack([before(other, seq).astype(F32) for other in seqs]),
        )

    partial = {s: states_of(s) for s in order}
    state, _ = scan(partial, lambda a, b: a < b, [prefix_state, prefix_norm], False)

    def block_of(s):
        half_specs = piece_specs(lambda h: (0, h), PAIR) + piece_specs(
            lambda h: (0, grid[0] + h), PAIR
        )
        return pl.pallas_call(
            functools.partial(block_kernel, part),
            out_shape=[jax.ShapeDtypeStruct((tok, heads * hd), BF16)] * part
            + [
                jax.ShapeDtypeStruct((heads, 2 * half, BLK), F32),
                jax.ShapeDtypeStruct((hd, BLK), F32),
                ext_shape,
                gm_shape,
            ],
            grid=grid,
            in_specs=[in_smem] + kv_specs(s) + half_specs + [map_spec(s), ext_spec],
            out_specs=piece_specs(lambda h: (0, h), PAIR) + [dk_spec, dv_spec, ext_spec, gm_spec],
            scratch_shapes=[
                pltpu.VMEM((BLK, hd), BF16),
                pltpu.VMEM((BLK, hd), BF16),
                pltpu.VMEM((hd, BLK), BF16),
                pltpu.VMEM((BLK, PAIR * hd), BF16),
                pltpu.VMEM((BLK, PAIR * hd), BF16),
                pltpu.VMEM((BLK, PAIR * hd), F32),
            ],
            compiler_params=params,
            cost_estimate=pl.CostEstimate(
                flops=unit * 8 * BLK, bytes_accessed=16 * heads * BLK * hd, transcendentals=0
            ),
            name="blocks",
        )(offsets, *kv, *kv, *rows[s], *rows[s], maps, state[s])

    blocks = {}
    for s in order:
        result = block_of(s)
        blocks[s] = (result[:part], *result[part:])
    partial = {s: blocks[s][3] for s in slots}
    suffix, (grad_prefix,) = scan(partial, lambda a, b: a > b, [], True)

    kv_type = BF16 if replicas == 1 else F32

    def keys_of(s):
        return pl.pallas_call(
            functools.partial(key_kernel, part),
            out_shape=[jax.ShapeDtypeStruct((tok, 2 * hd), kv_type)] * part + [gm_shape],
            grid=grid,
            in_specs=[in_smem] + kv_specs(s) + [map_spec(s), ext_spec, dk_spec, dv_spec],
            out_specs=piece_specs(lambda h: (0, 0), 2) + [gm_spec],
            scratch_shapes=[
                pltpu.VMEM((BLK, hd), BF16),
                pltpu.VMEM((BLK, hd), BF16),
                pltpu.VMEM((hd, BLK), BF16),
                pltpu.VMEM((hd, BLK), F32),
                pltpu.VMEM((heads * half, BLK), BF16),
                pltpu.VMEM((heads * half, hd), BF16),
                pltpu.VMEM((BLK, 2 * hd), F32),
            ],
            compiler_params=params,
            cost_estimate=pl.CostEstimate(
                flops=unit * 4 * hd, bytes_accessed=4 * heads * BLK * hd, transcendentals=0
            ),
            name="keys",
        )(offsets, *kv, *kv, maps, suffix[s], blocks[s][1], blocks[s][2])

    def returned(pieces):
        return [pieces[0]] + [within(pieces[r], -r) for r in shifts[1:]]

    def fold(parts):
        stacked = jnp.stack([parts[s] for s in slots])
        pieces = stacked.reshape(grp, heads // PAIR, fsdp, map_rows, PAIR * half)

        def rows_for(device):
            return lax.dynamic_index_in_dim(pieces, device, 2, keepdims=False)

        summed = rows_for(seq).astype(F32)
        for r in range(1, fsdp):
            summed = summed + along(rows_for((seq + r) % fsdp), r).astype(F32)
        sent = summed.astype(BF16)
        result = summed[0]
        for s in slots[1:]:
            result = result + across(sent[s], s).astype(F32)
        result = result.reshape(heads // PAIR, map_rows, PAIR, half)
        return jnp.swapaxes(result, 1, 2).reshape(heads, map_rows, half)

    table = ints([owner(r, s) for s in order for r in shifts])
    back = [piece for s in order for piece in returned(blocks[s][0])]
    (grad_queries,) = unpack(table, back, 1, heads * hd)
    query_map_grad = fold({s: blocks[s][4] for s in slots})

    keys = {s: keys_of(s) for s in slots}
    back = [piece for s in order for piece in returned(keys[s][:part])]
    grad_keys, grad_values = unpack(table, back, 2, hd)
    if replicas > 1:
        grad_keys, grad_values = (
            jnp.sum(a.reshape(tok, kv_heads, replicas, hd), axis=2)
            .astype(BF16)
            .reshape(tok, kv_heads * hd)
            for a in (grad_keys, grad_values)
        )
    key_map_grad = fold({s: keys[s][part] for s in slots})
    return grad_queries, grad_keys, grad_values, query_map_grad, key_map_grad, grad_prefix


def solution(mesh):
    rows, maps = P(("fsdp", "ctx"), None), P("ctx", "fsdp", None)
    return jax.shard_map(
        shards,
        mesh=mesh,
        in_specs=(rows,) * 4 + (maps, maps, P("ctx", None, None), P("ctx", None)),
        out_specs=(rows,) * 3 + (maps,) * 3,
        check_vma=False,
    )
```

```python
import functools

import jax
import jax.numpy as jnp
from jax import lax
from jax.experimental import pallas as pl
from jax.experimental.pallas import tpu as pltpu
from jax.sharding import PartitionSpec as P

BLK = 512
TILE = 256
PAIR = 2
EXT = 16
LIMIT = 40 * 1024 * 1024

F32 = jnp.float32
BF16 = jnp.bfloat16
SMEM = pltpu.SMEM


def nn(left, right):
    return lax.dot_general(left, right, (((1,), (0,)), ((), ())), preferred_element_type=F32)


def nt(left, right):
    return lax.dot_general(left, right, (((1,), (1,)), ((), ())), preferred_element_type=F32)


def turned(array):
    return array.astype(F32).T.astype(array.dtype)


def column(row, width):
    n = row.shape[1]
    square = jnp.broadcast_to(row, (n, n)).T
    return jnp.concatenate([square] * (width // n), axis=1)


def thirds(row):
    rows = jnp.broadcast_to(row, (EXT, row.shape[1]))
    high = rows.astype(BF16).astype(F32)
    middle = (rows - high).astype(BF16).astype(F32)
    low = rows - high - middle
    place = lax.broadcasted_iota(jnp.int32, rows.shape, 0)
    picked = jnp.where(place == 0, high, jnp.where(place == 1, middle, low))
    return jnp.where(place < 3, picked, 0.0).astype(BF16)


def whole_row(block):
    return jnp.sum(block.astype(F32), axis=0, keepdims=True)


def weight_rows(ref, u):
    whole = jnp.concatenate([ref[i, u] for i in range(ref.shape[0])], axis=0)
    return turned(whole)


def features(weight, rows):
    logits = nt(weight, rows).astype(BF16).astype(F32)
    upper = jnp.exp(logits)
    lower = jnp.exp(-logits)
    upper = upper * (1.0 / jnp.sum(upper, axis=0, keepdims=True))
    lower = lower * (1.0 / jnp.sum(lower, axis=0, keepdims=True))
    return jnp.concatenate([upper, lower], axis=0)


def feature_back(feats, upstream):
    half = feats.shape[0] // 2
    weighted = feats * upstream
    first, second = weighted[:half], weighted[half:]
    first = first - feats[:half] * jnp.sum(first, axis=0, keepdims=True)
    second = second - feats[half:] * jnp.sum(second, axis=0, keepdims=True)
    return (first - second).astype(BF16)


def flat(ref):
    return ref[...].reshape(-1, ref.shape[-1])


def pack_kernel(columns, table, *refs):
    sources, out = refs[:-1], refs[-1]
    width = sources[0].shape[1]
    for i, source in enumerate(sources):
        out[0, :, i * width : (i + 1) * width] = source[...]


def pack(table, sources, pieces, columns, width):
    rows = sources[0].shape[0]
    count = columns * len(sources)

    def take(s):
        return pl.BlockSpec((rows, width), lambda i, t: (0, t[s * pieces + i]))

    return pl.pallas_call(
        functools.partial(pack_kernel, columns),
        out_shape=jax.ShapeDtypeStruct((pieces, rows, count * width), sources[0].dtype),
        grid_spec=pltpu.PrefetchScalarGridSpec(
            num_scalar_prefetch=1,
            grid=(pieces,),
            in_specs=[take(s) for s in range(columns) for _ in sources],
            out_specs=pl.BlockSpec((1, rows, count * width), lambda i, t: (i, 0, 0)),
        ),
        compiler_params=pltpu.CompilerParams(vmem_limit_bytes=LIMIT),
        cost_estimate=pl.CostEstimate(
            flops=0, bytes_accessed=4 * pieces * rows * count * width, transcendentals=0
        ),
        name="pack",
    )(table, *(list(sources) * columns))


def unpack_kernel(outputs, table, *refs):
    sources, outs = refs[:-outputs], refs[-outputs:]
    for s, source in enumerate(sources):
        pieces = source.shape[0]
        width = source.shape[2] // outputs
        for r in range(pieces):
            at = pl.ds(pl.multiple_of(table[s * pieces + r] * width, width), width)
            for i, out in enumerate(outs):
                out[:, at] = source[r, :, i * width : (i + 1) * width]


def unpack(table, sources, outputs, width):
    pieces, rows = sources[0].shape[:2]
    total = len(sources) * pieces * width
    step = rows // 2
    return pl.pallas_call(
        functools.partial(unpack_kernel, outputs),
        out_shape=[jax.ShapeDtypeStruct((rows, total), sources[0].dtype)] * outputs,
        grid=(rows // step,),
        in_specs=[pl.BlockSpec(memory_space=SMEM)]
        + [pl.BlockSpec((pieces, step, outputs * width), lambda i: (0, i, 0))] * len(sources),
        out_specs=[pl.BlockSpec((step, total), lambda i: (i, 0))] * outputs,
        compiler_params=pltpu.CompilerParams(vmem_limit_bytes=LIMIT),
        cost_estimate=pl.CostEstimate(
            flops=0, bytes_accessed=4 * rows * total * outputs, transcendentals=0
        ),
        name="unpack",
    )(table, *sources)


def state_kernel(slot, k_ref, v_ref, w_ref, out):
    k_all, v_all = flat(k_ref), flat(v_ref)
    hd = k_all.shape[1]
    for u in range(out.shape[0]):
        weight = weight_rows(w_ref, u)
        feats = features(weight[weight.shape[0] // 2 :], k_all).astype(BF16)
        out[u, :hd, :] = nn(feats, v_all).astype(BF16)
        ones = jnp.ones((EXT, feats.shape[1]), BF16)
        out[u, hd:, :] = thirds(nt(ones, feats)[:1])


def block_kernel(
    slot, k_ref, v_ref, q_ref, g_ref, w_ref, st_ref, gq_ref, dk_ref, dv_ref, sx_ref, gm_ref, vt_all
):
    k_all, v_all, q_all, g_all = flat(k_ref), flat(v_ref), flat(q_ref), flat(g_ref)
    hd = k_all.shape[1]

    @pl.when(pl.program_id(0) == 0)
    def _():
        vt_all[...] = turned(v_all)
        dv_ref[...] = jnp.zeros_like(dv_ref)

    maps = []
    earlier = lax.broadcasted_iota(jnp.int32, (TILE, TILE), 0) <= lax.broadcasted_iota(
        jnp.int32, (TILE, TILE), 1
    )

    def causal(array, begin):
        masked = jnp.where(earlier, array[begin:], 0.0)
        return masked if begin == 0 else jnp.concatenate([array[:begin], masked], axis=0)

    for u in range(PAIR):
        weight = weight_rows(w_ref, u)
        half = weight.shape[0] // 2
        lanes = slice(u * hd, (u + 1) * hd)
        q_feat = features(weight[:half], q_all[:, lanes])
        k_low = features(weight[half:], k_all).astype(BF16)
        q_low = q_feat.astype(BF16)
        k_turned = turned(k_low)
        state = st_ref[u, :hd, :]
        state_turned = turned(state)
        norm = column(whole_row(st_ref[u, hd:, :]), TILE)
        g_turned = g_all[:, lanes].astype(F32).T
        back = []
        dkey = [jnp.zeros((2 * half, TILE), F32) for _ in range(BLK // TILE)]
        dvalue = [jnp.zeros((hd, TILE), F32) for _ in range(BLK // TILE)]
        suffix = jnp.zeros((2 * half, hd), F32)
        suffix_norm = jnp.zeros((2 * half, 1), F32)
        for j in range(BLK // TILE):
            begin, end = j * TILE, (j + 1) * TILE
            own = q_low[:, begin:end]
            own_wide = own.astype(F32)
            scores = causal(nn(k_turned[:end], own), begin)
            scores_low = scores.astype(BF16)
            numerator = nn(state_turned, own) + nn(vt_all[:, :end], scores_low)
            denominator = jnp.sum(own_wide * norm, axis=0, keepdims=True) + jnp.sum(
                scores, axis=0, keepdims=True
            )
            inverse = 1.0 / denominator
            scaled = g_turned[:, begin:end] * inverse
            scaled_low = scaled.astype(BF16)
            norm_grad = -jnp.sum(scaled * (numerator * inverse), axis=0, keepdims=True)
            dscores = causal(nn(v_all[:end], scaled_low) + norm_grad, begin).astype(BF16)
            dquery = nn(state, scaled_low) + norm * norm_grad + nn(k_low[:, :end], dscores)
            back.append(feature_back(q_feat[:, begin:end], dquery))
            for i in range(j + 1):
                rows = slice(i * TILE, (i + 1) * TILE)
                dkey[i] = dkey[i] + nt(own, dscores[rows])
                dvalue[i] = dvalue[i] + nt(scaled_low, scores_low[rows])
            suffix = suffix + nt(own, scaled_low)
            suffix_norm = suffix_norm + jnp.sum(own_wide * norm_grad, axis=1, keepdims=True)
        dlog = jnp.concatenate(back, axis=1)
        back = nn(turned(dlog), weight[:half]).astype(BF16)
        gq_ref[:, :, lanes] = back.reshape(gq_ref.shape[0], -1, hd)
        maps.append(nn(dlog, q_all[:, lanes]))
        dk_ref[u] = jnp.concatenate(dkey, axis=1)
        dv_ref[...] += jnp.concatenate(dvalue, axis=1)
        sx_ref[u, :hd, :] = suffix.astype(BF16)
        sx_ref[u, hd:, :] = thirds(jnp.broadcast_to(suffix_norm, (2 * half, 2 * half)).T[:1])
    gm_ref[0] = jnp.concatenate(maps, axis=0).T.astype(gm_ref.dtype)


def key_kernel(
    slot, k_ref, v_ref, w_ref, sx_ref, dk_ref, dv_ref, out, gm_ref, vt_all, total, logs, weights
):
    k_all, v_all = flat(k_ref), flat(v_ref)
    hd = k_all.shape[1]
    step = pl.program_id(0)

    @pl.when(step == 0)
    def _():
        vt_all[...] = turned(v_all)
        total[...] = dv_ref[...]

    maps = []
    for u in range(PAIR):
        weight = weight_rows(w_ref, u)
        half = weight.shape[0] // 2
        weight = weight[half:]
        feats = features(weight, k_all)
        suffix = sx_ref[u, :hd, :]
        norm = column(whole_row(sx_ref[u, hd:, :]), BLK)
        dlog = feature_back(feats, dk_ref[u] + nn(suffix, vt_all[...]) + norm)
        at = pl.ds(pl.multiple_of((step * PAIR + u) * half, half), half)
        logs[at, :] = dlog
        weights[at, :] = weight
        maps.append(nn(dlog, k_all))
        total[...] += nn(turned(suffix), feats.astype(BF16))
    gm_ref[0] = jnp.concatenate(maps, axis=0).T.astype(gm_ref.dtype)

    @pl.when(step == pl.num_programs(0) - 1)
    def _():
        pair = jnp.concatenate([nn(turned(logs[...]), weights[...]), total[...].T], axis=1)
        out[...] = pair.astype(out.dtype).reshape(out.shape)


def total_kernel(*refs):
    out = refs[-1]
    heads, hd = out.shape[0], out.shape[2]
    for h in range(heads):
        out[h, :hd, :] = sum(ref[h, :hd, :].astype(F32) for ref in refs[:-1]).astype(BF16)
        out[h, hd:, :] = thirds(sum(whole_row(ref[h, hd:, :]) for ref in refs[:-1]))


def spread_kernel(grp, others, closing, block_weight, total_weight, place, *refs):
    parts, totals, refs = refs[:grp], refs[grp : grp + others], refs[grp + others :]
    if closing:
        outs, grad, scratch = refs[:grp], refs[grp], refs[grp + 1]
    else:
        state_ref, norm_ref, outs = refs[0], refs[1], refs[2:]
    heads, hd = parts[0].shape[0], parts[0].shape[2]
    for h in range(heads):
        states = [ref[h, :hd, :].astype(F32) for ref in parts]
        norms = [whole_row(ref[h, hd:, :]) for ref in parts]
        others_state = [ref[h, :hd, :].astype(F32) for ref in totals]
        others_norm = [whole_row(ref[h, hd:, :]) for ref in totals]
        if closing:
            base, base_norm = jnp.zeros_like(states[0]), jnp.zeros_like(norms[0])
            scratch[...] = sum(states) + sum(others_state)
            rows = grad.shape[1]
            grad[h] = scratch[pl.ds(pl.multiple_of(place[0] * rows, rows), rows), :]
        else:
            base, base_norm = state_ref[h], norm_ref[pl.ds(h, 1), :]
        for i, (state, norm) in enumerate(zip(others_state, others_norm)):
            base = base + total_weight[i] * state
            base_norm = base_norm + total_weight[i] * norm
        for r, out in enumerate(outs):
            state, norm = base, base_norm
            for i in range(grp):
                if i != r:
                    state = state + block_weight[r * grp + i] * states[i]
                    norm = norm + block_weight[r * grp + i] * norms[i]
            out[h, :hd, :] = state.astype(BF16)
            out[h, hd:, :] = thirds(norm)


def whole_call(kernel, outs, smem, arrays, name, scratch=()):
    total = sum(a.size * a.dtype.itemsize for a in (*arrays, *outs))
    return pl.pallas_call(
        kernel,
        out_shape=outs,
        in_specs=[pl.BlockSpec(memory_space=SMEM)] * len(smem)
        + [pl.BlockSpec(memory_space=pltpu.VMEM)] * len(arrays),
        out_specs=[pl.BlockSpec(memory_space=pltpu.VMEM)] * len(outs),
        scratch_shapes=list(scratch),
        compiler_params=pltpu.CompilerParams(vmem_limit_bytes=LIMIT),
        cost_estimate=pl.CostEstimate(flops=total, bytes_accessed=total, transcendentals=0),
        name=name,
    )(*smem, *arrays)


def shards(
    query_rows, key_rows, value_rows, grad_out, query_map, key_map, prefix_state, prefix_norm
):
    ctx, fsdp = lax.axis_size("ctx"), lax.axis_size("fsdp")
    tok = query_rows.shape[0]
    heads, map_rows, half = query_map.shape
    hd = map_rows * fsdp
    kv_heads = key_rows.shape[1] // hd
    replicas = ctx // kv_heads
    part = BLK // tok
    grp = ctx // part
    mine = lax.axis_index("ctx")
    block, seq = mine // part, lax.axis_index("fsdp")

    blocks_of = [[g * part + p for p in range(part)] for g in range(grp)]
    owners_of = [
        [(g * part + p) * fsdp + i for g in range(grp) for i in range(fsdp)] for p in range(part)
    ]

    def within(array):
        return lax.all_to_all(array, "ctx", 0, 0, axis_index_groups=blocks_of, tiled=True)

    def across(array, shift):
        return lax.ppermute(array, "ctx", [(d, (d + shift * part) % ctx) for d in range(ctx)])

    def along(array, shift):
        return lax.ppermute(array, "fsdp", [(d, (d + shift) % fsdp) for d in range(fsdp)])

    def ints(values):
        return jnp.stack([jnp.asarray(v, jnp.int32) for v in values])

    slots = range(grp)
    order = list(reversed(slots))
    slot = {s: (block + s) % grp for s in slots}
    owner = {s: [slot[s] * part + p for p in range(part)] for s in slots}

    kv_table = ints([c // replicas for s in slots for c in owner[s]])
    kv = within(pack(kv_table, (key_rows, value_rows), part, grp, hd))
    own_maps = jnp.concatenate((query_map, key_map), axis=-1)
    maps = lax.all_gather(own_maps, ("ctx", "fsdp"), axis_index_groups=owners_of)
    rows = {
        s: within(pack(ints(owner[s]), (query_rows, grad_out), part, 1, heads * hd))
        for s in order
    }

    grid = (heads // PAIR,)
    params = pltpu.CompilerParams(
        dimension_semantics=("arbitrary",), vmem_limit_bytes=LIMIT
    )

    def piece_spec(column, count):
        return pl.BlockSpec((part, tok, count * hd), lambda h, t: (0, 0, column(h)))

    def kv_specs(s):
        return [piece_spec(lambda h: 2 * s, 1), piece_spec(lambda h: 2 * s + 1, 1)]

    map_spec = pl.BlockSpec((fsdp, PAIR, map_rows, 2 * half), lambda h, t: (t[0], h, 0, 0))

    def call(kernel, s, outs, specs, out_specs, arrays, scratch, name, flops):
        moved = sum(a.size * a.dtype.itemsize for a in (*arrays, *outs))
        return pl.pallas_call(
            kernel,
            out_shape=outs,
            grid_spec=pltpu.PrefetchScalarGridSpec(
                num_scalar_prefetch=1,
                grid=grid,
                in_specs=specs,
                out_specs=out_specs,
                scratch_shapes=scratch,
            ),
            compiler_params=params,
            cost_estimate=pl.CostEstimate(flops=flops, bytes_accessed=moved, transcendentals=0),
            name=name,
        )(ints([slot[s]]), *arrays)

    ext_spec = pl.BlockSpec((PAIR, hd + EXT, hd), lambda h, t: (h, 0, 0))
    ext_shape = jax.ShapeDtypeStruct((heads, hd + EXT, hd), BF16)
    gm_spec = pl.BlockSpec((1, hd, PAIR * half), lambda h, t: (h, 0, 0))
    gm_shape = jax.ShapeDtypeStruct((heads // PAIR, hd, PAIR * half), BF16)
    dk_spec = pl.BlockSpec((PAIR, 2 * half, BLK), lambda h, t: (h, 0, 0))
    dv_spec = pl.BlockSpec((hd, BLK), lambda h, t: (0, 0))
    unit = 2 * heads * BLK * hd

    def states_of(s):
        return call(
            state_kernel,
            s,
            [ext_shape],
            kv_specs(s) + [map_spec],
            [ext_spec],
            [kv, kv, maps],
            [],
            "states",
            unit * 2 * hd,
        )[0]

    def scan(partial, before, extra, closing):
        parts = [partial[0]] + [across(partial[s], s) for s in slots[1:]]
        (total,) = whole_call(total_kernel, [ext_shape], [], parts, "totals")
        others = [along(total, r) for r in range(1, fsdp)]
        result = whole_call(
            functools.partial(spread_kernel, grp, fsdp - 1, closing),
            [ext_shape] * grp
            + [jax.ShapeDtypeStruct((heads, map_rows, hd), F32)] * closing,
            [*weights(before), ints([seq])],
            parts + others + extra,
            "spread",
            [pltpu.VMEM((hd, hd), F32)] * closing,
        )
        return [result[0]] + [across(result[s], -s) for s in slots[1:]], result[grp:]

    def weights(before):
        seqs = [(seq - r) % fsdp for r in range(1, fsdp)]
        blocks = [(block - r) % grp for r in slots]
        return (
            jnp.stack([before(b, a).astype(F32) for a in blocks for b in blocks]),
            jnp.stack([before(other, seq).astype(F32) for other in seqs]),
        )

    partial = {s: states_of(s) for s in order}
    state, _ = scan(partial, lambda a, b: a < b, [prefix_state, prefix_norm], False)

    def block_of(s):
        return call(
            block_kernel,
            s,
            [
                jax.ShapeDtypeStruct((part, tok, heads * hd), BF16),
                jax.ShapeDtypeStruct((heads, 2 * half, BLK), F32),
                jax.ShapeDtypeStruct((hd, BLK), F32),
                ext_shape,
                gm_shape,
            ],
            kv_specs(s)
            + [piece_spec(lambda h: h, PAIR), piece_spec(lambda h: grid[0] + h, PAIR)]
            + [map_spec, ext_spec],
            [piece_spec(lambda h: h, PAIR), dk_spec, dv_spec, ext_spec, gm_spec],
            [kv, kv, rows[s], rows[s], maps, state[s]],
            [pltpu.VMEM((hd, BLK), BF16)],
            "blocks",
            unit * 8 * BLK,
        )

    blocks = {s: block_of(s) for s in order}
    partial = {s: blocks[s][3] for s in slots}
    suffix, (grad_prefix,) = scan(partial, lambda a, b: a > b, [], True)

    kv_type = BF16 if replicas == 1 else F32

    def keys_of(s):
        return call(
            key_kernel,
            s,
            [jax.ShapeDtypeStruct((part, tok, 2 * hd), kv_type), gm_shape],
            kv_specs(s) + [map_spec, ext_spec, dk_spec, dv_spec],
            [piece_spec(lambda h: 0, 2), gm_spec],
            [kv, kv, maps, suffix[s], blocks[s][1], blocks[s][2]],
            [
                pltpu.VMEM((hd, BLK), BF16),
                pltpu.VMEM((hd, BLK), F32),
                pltpu.VMEM((heads * half, BLK), BF16),
                pltpu.VMEM((heads * half, hd), BF16),
            ],
            "keys",
            unit * 4 * hd,
        )

    def fold(parts):
        stacked = jnp.stack([parts[s] for s in slots])
        pieces = stacked.reshape(grp, heads // PAIR, fsdp, map_rows, PAIR * half)

        def rows_for(device):
            return lax.dynamic_index_in_dim(pieces, device, 2, keepdims=False)

        summed = rows_for(seq).astype(F32)
        for r in range(1, fsdp):
            summed = summed + along(rows_for((seq + r) % fsdp), r).astype(F32)
        sent = summed.astype(BF16)
        result = summed[0]
        for s in slots[1:]:
            result = result + across(sent[s], s).astype(F32)
        result = result.reshape(heads // PAIR, map_rows, PAIR, half)
        return jnp.swapaxes(result, 1, 2).reshape(heads, map_rows, half)

    table = ints([c for s in slots for c in owner[s]])
    back = {s: within(blocks[s][0]) for s in order}
    (grad_queries,) = unpack(table, [back[s] for s in slots], 1, heads * hd)
    query_map_grad = fold({s: blocks[s][4] for s in slots})

    keys = {s: keys_of(s) for s in slots}
    back = {s: within(keys[s][0]) for s in slots}
    grad_keys, grad_values = unpack(table, [back[s] for s in slots], 2, hd)
    if replicas > 1:
        grad_keys, grad_values = (
            jnp.sum(a.reshape(tok, kv_heads, replicas, hd), axis=2)
            .astype(BF16)
            .reshape(tok, kv_heads * hd)
            for a in (grad_keys, grad_values)
        )
    key_map_grad = fold({s: keys[s][1] for s in slots})
    return grad_queries, grad_keys, grad_values, query_map_grad, key_map_grad, grad_prefix


def solution(mesh):
    rows, maps = P(("fsdp", "ctx"), None), P("ctx", "fsdp", None)
    return jax.shard_map(
        shards,
        mesh=mesh,
        in_specs=(rows,) * 4 + (maps, maps, P("ctx", None, None), P("ctx", None)),
        out_specs=(rows,) * 3 + (maps,) * 3,
        check_vma=False,
    )
```

```python
import functools

import jax
import jax.numpy as jnp
from jax import lax
from jax.experimental import pallas as pl
from jax.experimental.pallas import tpu as pltpu
from jax.sharding import PartitionSpec as P

BLK = 512
TILE = 256
PAIR = 2
LIMIT = 40 * 1024 * 1024

F32 = jnp.float32
BF16 = jnp.bfloat16
SMEM = pltpu.SMEM


def nn(left, right):
    return lax.dot_general(left, right, (((1,), (0,)), ((), ())), preferred_element_type=F32)


def nt(left, right):
    return lax.dot_general(left, right, (((1,), (1,)), ((), ())), preferred_element_type=F32)


def turned(array):
    return array.astype(F32).T.astype(array.dtype)


def column(row, width):
    n = row.shape[1]
    square = jnp.broadcast_to(row, (n, n)).T
    return jnp.concatenate([square] * (width // n), axis=1)


def pick(ref, weights, slot, blocks, before):
    heads = ref.shape[1] // (ref.shape[0] // blocks + 1 if before else ref.shape[0] // blocks)
    groups = ref.shape[0] // blocks
    total = jnp.zeros((heads, ref.shape[2]), F32)
    for i in range(ref.shape[0]):
        at = lax.rem(slot + groups - i // blocks, groups) * heads
        total = total + weights[i] * ref[i, pl.ds(pl.multiple_of(at, heads), heads), :]
    if before:
        total = total + ref[slot * blocks, groups * heads :, :]
    return total


def weight_rows(ref, u):
    whole = jnp.concatenate([ref[i, u] for i in range(ref.shape[0])], axis=0)
    return turned(whole)


def features(weight, rows):
    logits = nt(weight, rows).astype(BF16).astype(F32)
    upper = jnp.exp(logits)
    lower = jnp.exp(-logits)
    upper = upper * (1.0 / jnp.sum(upper, axis=0, keepdims=True))
    lower = lower * (1.0 / jnp.sum(lower, axis=0, keepdims=True))
    return jnp.concatenate([upper, lower], axis=0)


def feature_back(feats, upstream):
    half = feats.shape[0] // 2
    weighted = feats * upstream
    first, second = weighted[:half], weighted[half:]
    first = first - feats[:half] * jnp.sum(first, axis=0, keepdims=True)
    second = second - feats[half:] * jnp.sum(second, axis=0, keepdims=True)
    return (first - second).astype(BF16)


def flat(ref):
    return ref[...].reshape(-1, ref.shape[-1])


def pack_kernel(columns, table, *refs):
    sources, out = refs[:-1], refs[-1]
    width = sources[0].shape[1]
    for i, source in enumerate(sources):
        out[0, :, i * width : (i + 1) * width] = source[...]


def pack(table, sources, pieces, columns, width):
    rows = sources[0].shape[0]
    count = columns * len(sources)

    def take(s):
        return pl.BlockSpec((rows, width), lambda i, t: (0, t[s * pieces + i]))

    return pl.pallas_call(
        functools.partial(pack_kernel, columns),
        out_shape=jax.ShapeDtypeStruct((pieces, rows, count * width), sources[0].dtype),
        grid_spec=pltpu.PrefetchScalarGridSpec(
            num_scalar_prefetch=1,
            grid=(pieces,),
            in_specs=[take(s) for s in range(columns) for _ in sources],
            out_specs=pl.BlockSpec((1, rows, count * width), lambda i, t: (i, 0, 0)),
        ),
        compiler_params=pltpu.CompilerParams(vmem_limit_bytes=LIMIT),
        cost_estimate=pl.CostEstimate(
            flops=0, bytes_accessed=4 * pieces * rows * count * width, transcendentals=0
        ),
        name="pack",
    )(table, *(list(sources) * columns))


def unpack_kernel(outputs, table, *refs):
    sources, outs = refs[:-outputs], refs[-outputs:]
    for s, source in enumerate(sources):
        pieces = source.shape[0]
        width = source.shape[2] // outputs
        for r in range(pieces):
            at = pl.ds(pl.multiple_of(table[s * pieces + r] * width, width), width)
            for i, out in enumerate(outs):
                out[:, at] = source[r, :, i * width : (i + 1) * width]


def unpack(table, sources, outputs, width):
    pieces, rows = sources[0].shape[:2]
    total = len(sources) * pieces * width
    step = rows // 2
    return pl.pallas_call(
        functools.partial(unpack_kernel, outputs),
        out_shape=[jax.ShapeDtypeStruct((rows, total), sources[0].dtype)] * outputs,
        grid=(rows // step,),
        in_specs=[pl.BlockSpec(memory_space=SMEM)]
        + [pl.BlockSpec((pieces, step, outputs * width), lambda i: (0, i, 0))] * len(sources),
        out_specs=[pl.BlockSpec((step, total), lambda i: (i, 0))] * outputs,
        compiler_params=pltpu.CompilerParams(vmem_limit_bytes=LIMIT),
        cost_estimate=pl.CostEstimate(
            flops=0, bytes_accessed=4 * rows * total * outputs, transcendentals=0
        ),
        name="unpack",
    )(table, *sources)


def place(step, u):
    return pl.ds(step * PAIR + u, 1)


def state_kernel(slot, k_ref, v_ref, w_ref, out, norm_ref):
    k_all, v_all = flat(k_ref), flat(v_ref)
    step = pl.program_id(0)
    for u in range(PAIR):
        weight = weight_rows(w_ref, u)
        feats = features(weight[weight.shape[0] // 2 :], k_all).astype(BF16)
        out[u] = nn(feats, v_all).astype(BF16)
        ones = jnp.ones((8, feats.shape[1]), BF16)
        norm_ref[place(step, u), :] = nt(ones, feats)[:1]


def tiles_of(j):
    return range(j * (j + 1) // 2, (j + 1) * (j + 2) // 2)


def causal(array, begin):
    earlier = lax.broadcasted_iota(jnp.int32, (TILE, TILE), 0) <= lax.broadcasted_iota(
        jnp.int32, (TILE, TILE), 1
    )
    masked = jnp.where(earlier, array[begin:], 0.0)
    return masked if begin == 0 else jnp.concatenate([array[:begin], masked], axis=0)


def front_kernel(
    fsdp, slot, k_ref, q_ref, g_ref, w_ref, norms_ref, weights,
    qf_ref, kf_ref, scaled_ref, sc_ref, inv_ref, norm_ref, sx_ref,
):
    k_all, q_all, g_all = flat(k_ref), flat(q_ref), flat(g_ref)
    hd = k_all.shape[1]
    step = pl.program_id(0)

    @pl.when(step == 0)
    def _():
        norm_ref[...] = pick(norms_ref, weights, slot[0], fsdp, True)

    for u in range(PAIR):
        weight = weight_rows(w_ref, u)
        half = weight.shape[0] // 2
        lanes = slice(u * hd, (u + 1) * hd)
        q_feat = features(weight[:half], q_all[:, lanes])
        k_low = features(weight[half:], k_all).astype(BF16)
        qf_ref[u] = q_feat
        kf_ref[u] = k_low
        q_low = q_feat.astype(BF16)
        k_turned = turned(k_low)
        norm = column(norm_ref[place(step, u), :], TILE)
        g_turned = g_all[:, lanes].astype(F32).T
        suffix = jnp.zeros((2 * half, hd), F32)
        for j in range(BLK // TILE):
            begin, end = j * TILE, (j + 1) * TILE
            own = q_low[:, begin:end]
            scores = causal(nn(k_turned[:end], own), begin)
            for i, tile in enumerate(tiles_of(j)):
                sc_ref[u, tile] = scores[i * TILE : (i + 1) * TILE].astype(BF16)
            denominator = jnp.sum(own.astype(F32) * norm, axis=0, keepdims=True) + jnp.sum(
                scores, axis=0, keepdims=True
            )
            inverse = 1.0 / denominator
            inv_ref[place(step, u), begin:end] = inverse
            scaled = g_turned[:, begin:end] * inverse
            scaled_ref[u, :, begin:end] = scaled
            suffix = suffix + nt(own, scaled.astype(BF16))
        sx_ref[u] = suffix.astype(BF16)


def back_kernel(
    slot, k_ref, v_ref, q_ref, w_ref, qf_ref, kf_ref, scaled_ref, sc_ref, inv_ref, norm_ref, st_ref,
    gq_ref, dk_ref, dv_ref, sn_ref, gm_ref, vt_all,
):
    v_all, q_all = flat(v_ref), flat(q_ref)
    hd = v_all.shape[1]
    step = pl.program_id(0)

    @pl.when(step == 0)
    def _():
        vt_all[...] = turned(v_all)
        dv_ref[...] = jnp.zeros_like(dv_ref)

    maps = []
    for u in range(PAIR):
        half = w_ref.shape[3] // 2
        weight = weight_rows(w_ref, u)
        lanes = slice(u * hd, (u + 1) * hd)
        q_feat = qf_ref[u]
        k_low = kf_ref[u]
        state = st_ref[u]
        state_turned = turned(state)
        norm = column(norm_ref[place(step, u), :], TILE)
        back = []
        dkey = [jnp.zeros((2 * half, TILE), F32) for _ in range(BLK // TILE)]
        dvalue = [jnp.zeros((hd, TILE), F32) for _ in range(BLK // TILE)]
        suffix_norm = jnp.zeros((2 * half, 1), F32)
        for j in range(BLK // TILE):
            begin, end = j * TILE, (j + 1) * TILE
            own = q_feat[:, begin:end].astype(BF16)
            scores_low = [sc_ref[u, tile] for tile in tiles_of(j)]
            numerator = nn(state_turned, own) + nn(
                vt_all[:, :end], jnp.concatenate(scores_low, axis=0)
            )
            inverse = inv_ref[place(step, u), begin:end]
            scaled = scaled_ref[u, :, begin:end]
            scaled_low = scaled.astype(BF16)
            norm_grad = -jnp.sum(scaled * (numerator * inverse), axis=0, keepdims=True)
            dscores = causal(nn(v_all[:end], scaled_low) + norm_grad, begin).astype(BF16)
            dquery = nn(state, scaled_low) + norm * norm_grad + nn(k_low[:, :end], dscores)
            back.append(feature_back(q_feat[:, begin:end], dquery))
            for i in range(j + 1):
                dkey[i] = dkey[i] + nt(own, dscores[i * TILE : (i + 1) * TILE])
                dvalue[i] = dvalue[i] + nt(scaled_low, scores_low[i])
            suffix_norm = suffix_norm + jnp.sum(
                own.astype(F32) * norm_grad, axis=1, keepdims=True
            )
        dlog = jnp.concatenate(back, axis=1)
        grads = nn(turned(dlog), weight[:half]).astype(BF16)
        gq_ref[:, :, lanes] = grads.reshape(gq_ref.shape[0], -1, hd)
        maps.append(nn(dlog, q_all[:, lanes]))
        dk_ref[u] = jnp.concatenate(dkey, axis=1)
        dv_ref[...] += jnp.concatenate(dvalue, axis=1)
        sn_ref[place(step, u), :] = jnp.broadcast_to(suffix_norm, (2 * half, 2 * half)).T[:1]
    gm_ref[0] = jnp.concatenate(maps, axis=0).T.astype(gm_ref.dtype)


def key_kernel(
    fsdp, slot, k_ref, v_ref, w_ref, sx_ref, dk_ref, dv_ref, norms_ref, weights, _,
    out, gm_ref, vt_all, total, logs, all_weights, norm_all,
):
    k_all, v_all = flat(k_ref), flat(v_ref)
    hd = k_all.shape[1]
    step = pl.program_id(0)

    @pl.when(step == 0)
    def _():
        vt_all[...] = turned(v_all)
        total[...] = dv_ref[...]
        norm_all[...] = pick(norms_ref, weights, slot[0], fsdp, False)

    maps = []
    for u in range(PAIR):
        weight = weight_rows(w_ref, u)
        half = weight.shape[0] // 2
        weight = weight[half:]
        feats = features(weight, k_all)
        suffix = sx_ref[u]
        norm = column(norm_all[place(step, u), :], BLK)
        dlog = feature_back(feats, dk_ref[u] + nn(suffix, vt_all[...]) + norm)
        at = pl.ds(pl.multiple_of((step * PAIR + u) * half, half), half)
        logs[at, :] = dlog
        all_weights[at, :] = weight
        maps.append(nn(dlog, k_all))
        total[...] += nn(turned(suffix), feats.astype(BF16))
    gm_ref[0] = jnp.concatenate(maps, axis=0).T.astype(gm_ref.dtype)

    @pl.when(step == pl.num_programs(0) - 1)
    def _():
        pair = jnp.concatenate([nn(turned(logs[...]), all_weights[...]), total[...].T], axis=1)
        out[...] = pair.astype(out.dtype).reshape(out.shape)


def total_kernel(*refs):
    for h in range(refs[-1].shape[0]):
        refs[-1][h] = sum(ref[h].astype(F32) for ref in refs[:-1]).astype(BF16)


def spread_kernel(grp, others, closing, block_weight, total_weight, at, *refs):
    parts, totals, refs = refs[:grp], refs[grp : grp + others], refs[grp + others :]
    if closing:
        outs, grad, scratch = refs[:grp], refs[grp], refs[grp + 1]
    else:
        state_ref, outs = refs[0], refs[1:]
    for h in range(parts[0].shape[0]):
        states = [ref[h].astype(F32) for ref in parts]
        others_state = [ref[h].astype(F32) for ref in totals]
        if closing:
            base = jnp.zeros_like(states[0])
            scratch[...] = sum(states) + sum(others_state)
            rows = grad.shape[1]
            grad[h] = scratch[pl.ds(pl.multiple_of(at[0] * rows, rows), rows), :]
        else:
            base = state_ref[h]
        for i, state in enumerate(others_state):
            base = base + total_weight[i] * state
        for r, out in enumerate(outs):
            state = base
            for i in range(grp):
                if i != r:
                    state = state + block_weight[r * grp + i] * states[i]
            out[h] = state.astype(BF16)


def close_kernel(pairs, singles, at, q_ref, k_ref, *refs):
    both, q_parts, k_parts = (
        refs[:pairs],
        refs[pairs : pairs + singles],
        refs[pairs + singles : pairs + 2 * singles],
    )
    for i, (own, parts, out) in enumerate(
        ((q_ref, q_parts, refs[-2]), (k_ref, k_parts, refs[-1]))
    ):
        rows, half = out.shape[1:]
        mine = pl.ds(pl.multiple_of(at[0] * rows, rows), rows)
        for h in range(own.shape[0]):
            total = own[h, mine, :].astype(F32)
            for ref in both:
                total = total + ref[i, h].astype(F32)
            for ref in parts:
                total = total + ref[h].astype(F32)
            for u in range(PAIR):
                out[h * PAIR + u] = total[:, u * half : (u + 1) * half]


def whole_call(kernel, outs, smem, arrays, name, scratch=()):
    total = sum(a.size * a.dtype.itemsize for a in (*arrays, *outs))
    return pl.pallas_call(
        kernel,
        out_shape=outs,
        in_specs=[pl.BlockSpec(memory_space=SMEM)] * len(smem)
        + [pl.BlockSpec(memory_space=pltpu.VMEM)] * len(arrays),
        out_specs=[pl.BlockSpec(memory_space=pltpu.VMEM)] * len(outs),
        scratch_shapes=list(scratch),
        compiler_params=pltpu.CompilerParams(vmem_limit_bytes=LIMIT),
        cost_estimate=pl.CostEstimate(flops=total, bytes_accessed=total, transcendentals=0),
        name=name,
    )(*smem, *arrays)


def after(value, *others):
    return lax.optimization_barrier((value, *others))[0]


def shards(
    query_rows, key_rows, value_rows, grad_out, query_map, key_map, prefix_state, prefix_norm
):
    ctx, fsdp = lax.axis_size("ctx"), lax.axis_size("fsdp")
    tok = query_rows.shape[0]
    heads, map_rows, half = query_map.shape
    hd = map_rows * fsdp
    kv_heads = key_rows.shape[1] // hd
    replicas = ctx // kv_heads
    part = BLK // tok
    grp = ctx // part
    mine = lax.axis_index("ctx")
    block, seq = mine // part, lax.axis_index("fsdp")
    slots = range(grp)
    order = list(reversed(slots))
    grid = (heads // PAIR,)

    blocks_of = [[g * part + p for p in range(part)] for g in slots]
    owners_of = [
        [(g * part + p) * fsdp + i for g in slots for i in range(fsdp)] for p in range(part)
    ]

    def within(array):
        return lax.all_to_all(array, "ctx", 0, 0, axis_index_groups=blocks_of, tiled=True)

    def across(array, shift):
        return lax.ppermute(array, "ctx", [(d, (d + shift * part) % ctx) for d in range(ctx)])

    def along(array, shift):
        return lax.ppermute(array, "fsdp", [(d, (d + shift) % fsdp) for d in range(fsdp)])

    def apart(array, s, r):
        moves = [
            (d * fsdp + i, (d + s * part) % ctx * fsdp + (i + r) % fsdp)
            for d in range(ctx)
            for i in range(fsdp)
        ]
        return lax.ppermute(array, ("ctx", "fsdp"), moves)

    def gathered(array):
        return lax.all_gather(array, ("ctx", "fsdp"), axis_index_groups=owners_of)

    def ints(values):
        return jnp.stack([jnp.asarray(v, jnp.int32) for v in values])

    def flags(values):
        return jnp.stack([v.astype(F32) for v in values])

    slot = {s: (block + s) % grp for s in slots}
    owner = {s: [slot[s] * part + p for p in range(part)] for s in slots}
    place_of = [(g, i) for g in slots for i in range(fsdp)]
    earlier = flags([i * grp + g < seq * grp + block for g, i in place_of])
    later = flags([i * grp + g > seq * grp + block for g, i in place_of])

    own_maps = jnp.concatenate((query_map, key_map), axis=-1)
    maps = jnp.stack([own_maps] + [across(own_maps, -s) for s in slots[1:]])
    kv_table = ints([c // replicas for s in slots for c in owner[s]])
    kv = within(pack(kv_table, (key_rows, value_rows), part, grp, hd))
    maps = lax.all_gather(maps, "fsdp")

    params = pltpu.CompilerParams(
        dimension_semantics=("arbitrary",), vmem_limit_bytes=LIMIT
    )
    in_smem = pl.BlockSpec(memory_space=SMEM)
    anywhere = pl.BlockSpec(memory_space=pl.ANY)

    def piece_spec(column, count):
        return pl.BlockSpec((part, tok, count * hd), lambda h, t: (0, 0, column(h)))

    def head_spec(*shape):
        return pl.BlockSpec((PAIR, *shape), lambda h, t: (h,) + (0,) * len(shape))

    def fixed_spec(*shape):
        return pl.BlockSpec(shape, lambda h, t: (0,) * len(shape))

    def of(dtype, *shape):
        return jax.ShapeDtypeStruct(shape, dtype)

    def k_spec(s):
        return piece_spec(lambda h: 2 * s, 1)

    def v_spec(s):
        return piece_spec(lambda h: 2 * s + 1, 1)

    def map_spec(s):
        return pl.BlockSpec((fsdp, None, PAIR, map_rows, 2 * half), lambda h, t: (0, s, h, 0, 0))

    q_spec, g_spec = piece_spec(lambda h: h, PAIR), piece_spec(lambda h: grid[0] + h, PAIR)
    state_spec, state_shape = head_spec(hd, hd), of(BF16, heads, hd, hd)
    row_spec, row_shape = fixed_spec(heads, hd), of(F32, heads, hd)
    wide_spec, wide_shape = head_spec(2 * half, BLK), of(F32, heads, 2 * half, BLK)
    gm_spec = pl.BlockSpec((1, hd, PAIR * half), lambda h, t: (h, 0, 0))
    gm_shape = of(BF16, heads // PAIR, hd, PAIR * half)
    dv_spec, dv_shape = fixed_spec(hd, BLK), of(F32, hd, BLK)
    count = tiles_of(BLK // TILE - 1)[-1] + 1
    unit = 2 * heads * BLK * hd

    def call(kernel, s, outs, specs, out_specs, arrays, scratch, name, flops, alias=()):
        moved = sum(a.size * a.dtype.itemsize for a in (*arrays, *outs))
        return pl.pallas_call(
            kernel,
            out_shape=outs,
            grid_spec=pltpu.PrefetchScalarGridSpec(
                num_scalar_prefetch=1,
                grid=grid,
                in_specs=specs,
                out_specs=out_specs,
                scratch_shapes=scratch,
            ),
            compiler_params=params,
            cost_estimate=pl.CostEstimate(flops=flops, bytes_accessed=moved, transcendentals=0),
            input_output_aliases=dict(alias),
            name=name,
        )(ints([slot[s]]), *arrays)

    def scan(partial, before, extra, closing):
        parts = [partial[0]] + [across(partial[s], s) for s in slots[1:]]
        (total,) = whole_call(total_kernel, [state_shape], [], parts, "totals")
        others = [along(total, r) for r in range(1, fsdp)]
        blocks = [(block - r) % grp for r in slots]
        block_weight = flags([before(b, a) for a in blocks for b in blocks])
        total_weight = flags([before((seq - r) % fsdp, seq) for r in range(1, fsdp)])
        result = whole_call(
            functools.partial(spread_kernel, grp, fsdp - 1, closing),
            [state_shape] * grp + [of(F32, heads, map_rows, hd)] * closing,
            [block_weight, total_weight, ints([seq])],
            parts + others + extra,
            "spread",
            [pltpu.VMEM((hd, hd), F32)] * closing,
        )
        return [result[0]] + [across(result[s], -s) for s in slots[1:]], result[grp:]

    rows, partial, norm = {}, {}, {}
    for s in order:
        table, sources = ints(owner[s]), (query_rows, grad_out)
        if s != order[0]:
            table = after(table, *partial.values())
        else:
            table = after(table, kv)
        rows[s] = within(pack(table, sources, part, 1, heads * hd))
        if s == order[0]:
            for i in order:
                partial[i], norm[i] = call(
                    state_kernel,
                    i,
                    [state_shape, row_shape],
                    [k_spec(i), v_spec(i), map_spec(i)],
                    [state_spec, row_spec],
                    [kv, kv, maps],
                    [],
                    "states",
                    unit * 2 * hd,
                )
            norms = gathered(jnp.concatenate([norm[i] for i in slots] + [prefix_norm], axis=0))
    state, _ = scan(partial, lambda a, b: a < b, [prefix_state], False)

    def front_of(s):
        return call(
            functools.partial(front_kernel, fsdp),
            s,
            [
                wide_shape,
                of(BF16, heads, 2 * half, BLK),
                of(F32, heads, hd, BLK),
                of(BF16, heads, count, TILE, TILE),
                of(F32, heads, BLK),
                row_shape,
                state_shape,
            ],
            [k_spec(s), q_spec, g_spec, map_spec(s), fixed_spec(*norms.shape), in_smem],
            [
                wide_spec,
                wide_spec,
                wide_spec,
                head_spec(count, TILE, TILE),
                fixed_spec(heads, BLK),
                row_spec,
                state_spec,
            ],
            [kv, rows[s], rows[s], maps, norms, earlier],
            [],
            "front",
            unit * 3 * BLK,
        )

    def back_of(s):
        return call(
            back_kernel,
            s,
            [of(BF16, part, tok, heads * hd), wide_shape, dv_shape, row_shape, gm_shape],
            [
                k_spec(s),
                v_spec(s),
                q_spec,
                map_spec(s),
                wide_spec,
                wide_spec,
                wide_spec,
                head_spec(count, TILE, TILE),
                fixed_spec(heads, BLK),
                row_spec,
                state_spec,
            ],
            [q_spec, wide_spec, dv_spec, row_spec, gm_spec],
            [kv, kv, rows[s], maps, *fronts[s][:6], state[s]],
            [pltpu.VMEM((hd, BLK), BF16)],
            "back",
            unit * 6 * BLK,
        )

    def rows_for(array, device):
        pieces = array.reshape(*array.shape[:-2], fsdp, map_rows, array.shape[-1])
        return lax.dynamic_index_in_dim(pieces, device % fsdp, array.ndim - 2, keepdims=False)

    fronts = {s: front_of(s) for s in order}
    suffix, (grad_prefix,) = scan(
        {s: fronts[s][6] for s in slots}, lambda a, b: a > b, [], True
    )
    backs, returned, q_maps = {}, {}, []
    for s in order:
        backs[s] = back_of(s)
        returned[s] = within(backs[s][0])
        if s:
            q_maps += [apart(rows_for(backs[s][4], seq + r), s, r) for r in range(fsdp)]
    suffix_norms = gathered(jnp.concatenate([backs[s][3] for s in slots], axis=0))

    kv_type = BF16 if replicas == 1 else F32
    pairs = jnp.zeros((part, tok, grp * 2 * hd), kv_type)
    k_maps, both_maps, key_gm = [], [], {}
    for s in slots:
        if s == 0:
            suffix[s] = after(suffix[s], *[returned[i] for i in slots[1:]], *q_maps)
        pairs, key_gm[s] = call(
            functools.partial(key_kernel, fsdp),
            s,
            [of(kv_type, *pairs.shape), gm_shape],
            [k_spec(s), v_spec(s), map_spec(s), state_spec, wide_spec, dv_spec]
            + [fixed_spec(*suffix_norms.shape), in_smem, anywhere],
            [piece_spec(lambda h: s, 2), gm_spec],
            [kv, kv, maps, suffix[s], backs[s][1], backs[s][2], suffix_norms, later, pairs],
            [
                pltpu.VMEM((hd, BLK), BF16),
                pltpu.VMEM((hd, BLK), F32),
                pltpu.VMEM((heads * half, BLK), BF16),
                pltpu.VMEM((heads * half, hd), BF16),
                pltpu.VMEM((heads, hd), F32),
            ],
            "keys",
            unit * 4 * hd,
            {9: 0},
        )
        if s == 0:
            two = jnp.stack([backs[s][4], key_gm[s]])
            both_maps = [along(rows_for(two, seq + r), r) for r in range(1, fsdp)]
        else:
            k_maps += [apart(rows_for(key_gm[s], seq + r), s, r) for r in range(fsdp)]

    table = ints([c for s in slots for c in owner[s]])
    pairs = after(pairs, *returned.values())
    pairs = within(pairs)
    (grad_queries,) = unpack(table, [returned[s] for s in slots], 1, heads * hd)
    pairs = [pairs[:, :, s * 2 * hd : (s + 1) * 2 * hd] for s in slots]
    grad_keys, grad_values = unpack(table, pairs, 2, hd)
    if replicas > 1:
        grad_keys, grad_values = (
            jnp.sum(a.reshape(tok, kv_heads, replicas, hd), axis=2)
            .astype(BF16)
            .reshape(tok, kv_heads * hd)
            for a in (grad_keys, grad_values)
        )
    query_map_grad, key_map_grad = whole_call(
        functools.partial(close_kernel, len(both_maps), len(q_maps)),
        [of(F32, heads, map_rows, half)] * 2,
        [ints([seq])],
        [backs[0][4], key_gm[0]] + both_maps + q_maps + k_maps,
        "close",
    )
    return grad_queries, grad_keys, grad_values, query_map_grad, key_map_grad, grad_prefix


def solution(mesh):
    rows, maps = P(("fsdp", "ctx"), None), P("ctx", "fsdp", None)
    return jax.shard_map(
        shards,
        mesh=mesh,
        in_specs=(rows,) * 4 + (maps, maps, P("ctx", None, None), P("ctx", None)),
        out_specs=(rows,) * 3 + (maps,) * 3,
        check_vma=False,
    )
```

```python
import functools

import jax
import jax.numpy as jnp
from jax import lax
from jax.experimental import pallas as pl
from jax.experimental.pallas import tpu as pltpu
from jax.sharding import PartitionSpec as P

BLK = 512
TILE = 256
PAIR = 2
LIMIT = 56 * 1024 * 1024

LITTLE = pl.CostEstimate(flops=1000, bytes_accessed=1000, transcendentals=0)

F32 = jnp.float32
BF16 = jnp.bfloat16
SMEM = pltpu.SMEM


def nn(left, right):
    return lax.dot_general(left, right, (((1,), (0,)), ((), ())), preferred_element_type=F32)


def nt(left, right):
    return lax.dot_general(left, right, (((1,), (1,)), ((), ())), preferred_element_type=F32)


def turned(array):
    return array.astype(F32).T.astype(array.dtype)


def column(row, width):
    n = row.shape[1]
    square = jnp.broadcast_to(row, (n, n)).T
    return jnp.concatenate([square] * (width // n), axis=1)


def pick(ref, weights, slot, block, before):
    blocks, groups = ref.shape[:2]
    heads = ref.shape[2] // (groups + before)
    total = jnp.zeros((heads, ref.shape[3]), F32)
    for r in range(groups):
        at = lax.rem(slot - block + r + groups, groups) * heads
        rows = pl.ds(pl.multiple_of(at, heads), heads)
        for i in range(blocks):
            total = total + weights[i * groups + r] * ref[i, r, rows, :]
    if before:
        total = total + ref[0, lax.rem(block - slot + groups, groups), groups * heads :, :]
    return total


def weight_rows(ref, u):
    whole = jnp.concatenate([ref[i, u] for i in range(ref.shape[0])], axis=0)
    return turned(whole)


def features(weight, rows):
    logits = nt(weight, rows).astype(BF16).astype(F32)
    upper = jnp.exp(logits)
    lower = jnp.exp(-logits)
    upper = upper * (1.0 / jnp.sum(upper, axis=0, keepdims=True))
    lower = lower * (1.0 / jnp.sum(lower, axis=0, keepdims=True))
    return jnp.concatenate([upper, lower], axis=0)


def feature_back(feats, upstream):
    half = feats.shape[0] // 2
    weighted = feats * upstream
    first, second = weighted[:half], weighted[half:]
    first = first - feats[:half] * jnp.sum(first, axis=0, keepdims=True)
    second = second - feats[half:] * jnp.sum(second, axis=0, keepdims=True)
    return (first - second).astype(BF16)


def flat(ref):
    return ref[...].reshape(-1, ref.shape[-1])


def pack_kernel(columns, table, *refs):
    sources, out = refs[:-1], refs[-1]
    width = sources[0].shape[1]
    for i, source in enumerate(sources):
        out[0, :, i * width : (i + 1) * width] = source[...]


def pack(table, sources, pieces, columns, width):
    rows = sources[0].shape[0]
    count = columns * len(sources)

    def take(s):
        return pl.BlockSpec((rows, width), lambda i, t: (0, t[s * pieces + i]))

    return pl.pallas_call(
        functools.partial(pack_kernel, columns),
        out_shape=jax.ShapeDtypeStruct((pieces, rows, count * width), sources[0].dtype),
        grid_spec=pltpu.PrefetchScalarGridSpec(
            num_scalar_prefetch=1,
            grid=(pieces,),
            in_specs=[take(s) for s in range(columns) for _ in sources],
            out_specs=pl.BlockSpec((1, rows, count * width), lambda i, t: (i, 0, 0)),
        ),
        compiler_params=pltpu.CompilerParams(vmem_limit_bytes=LIMIT),
        cost_estimate=LITTLE,
        name="pack",
    )(table, *(list(sources) * columns))


def deal_kernel(columns, inputs, table, *refs):
    count = columns * inputs
    for r, out in enumerate(refs[-(len(refs) // (count + 1)) :]):
        width = out.shape[1] // count
        for i in range(count):
            out[:, i * width : (i + 1) * width] = refs[r * count + i][...]


def deal(table, sources, pieces, columns, width):
    rows = sources[0].shape[0]
    count = columns * len(sources)

    def take(at):
        return pl.BlockSpec((rows, width), lambda i, t: (0, t[at]))

    return pl.pallas_call(
        functools.partial(deal_kernel, columns, len(sources)),
        out_shape=[jax.ShapeDtypeStruct((rows, count * width), sources[0].dtype)] * pieces,
        grid_spec=pltpu.PrefetchScalarGridSpec(
            num_scalar_prefetch=1,
            grid=(1,),
            in_specs=[
                take(r * columns + s)
                for r in range(pieces)
                for s in range(columns)
                for _ in sources
            ],
            out_specs=[pl.BlockSpec((rows, count * width), lambda i, t: (0, 0))] * pieces,
        ),
        compiler_params=pltpu.CompilerParams(vmem_limit_bytes=LIMIT),
        cost_estimate=LITTLE,
        name="deal",
    )(table, *(list(sources) * (pieces * columns)))


def sort_kernel(table, *refs):
    for r, ref in enumerate(refs[:-1]):
        refs[-1][table[r]] = ref[...]


def unpack_kernel(outputs, table, *refs):
    sources, outs = refs[:-outputs], refs[-outputs:]
    for s, source in enumerate(sources):
        pieces = source.shape[0]
        width = source.shape[2] // outputs
        for r in range(pieces):
            at = pl.ds(pl.multiple_of(table[s * pieces + r] * width, width), width)
            for i, out in enumerate(outs):
                out[:, at] = source[r, :, i * width : (i + 1) * width]


def unpack(table, sources, outputs, width):
    pieces, rows = sources[0].shape[:2]
    total = len(sources) * pieces * width
    step = rows // 2
    return pl.pallas_call(
        functools.partial(unpack_kernel, outputs),
        out_shape=[jax.ShapeDtypeStruct((rows, total), sources[0].dtype)] * outputs,
        grid=(rows // step,),
        in_specs=[pl.BlockSpec(memory_space=SMEM)]
        + [pl.BlockSpec((pieces, step, outputs * width), lambda i: (0, i, 0))] * len(sources),
        out_specs=[pl.BlockSpec((step, total), lambda i: (i, 0))] * outputs,
        compiler_params=pltpu.CompilerParams(vmem_limit_bytes=LIMIT),
        cost_estimate=LITTLE,
        name="unpack",
    )(table, *sources)


def place(step, u):
    return pl.ds(step * PAIR + u, 1)


def state_kernel(slot, k_ref, v_ref, w_ref, out, norm_ref):
    k_all, v_all = flat(k_ref), flat(v_ref)
    step = pl.program_id(0)
    for u in range(PAIR):
        weight = weight_rows(w_ref, u)
        feats = features(weight[weight.shape[0] // 2 :], k_all).astype(BF16)
        out[u] = nn(feats, v_all).astype(BF16)
        ones = jnp.ones((8, feats.shape[1]), BF16)
        norm_ref[place(step, u), :] = nt(ones, feats)[:1]


def tiles_of(j):
    return range(j * (j + 1) // 2, (j + 1) * (j + 2) // 2)


def causal(array, begin):
    earlier = lax.broadcasted_iota(jnp.int32, (TILE, TILE), 0) <= lax.broadcasted_iota(
        jnp.int32, (TILE, TILE), 1
    )
    masked = jnp.where(earlier, array[begin:], 0.0)
    return masked if begin == 0 else jnp.concatenate([array[:begin], masked], axis=0)


def front_kernel(
    slot, k_ref, q_ref, g_ref, w_ref, norms_ref, weights,
    qf_ref, kf_ref, scaled_ref, sc_ref, inv_ref, norm_ref, sx_ref,
):
    k_all, q_all, g_all = flat(k_ref), flat(q_ref), flat(g_ref)
    hd = k_all.shape[1]
    step = pl.program_id(0)

    @pl.when(step == 0)
    def _():
        norm_ref[...] = pick(norms_ref, weights, slot[0], slot[1], True)

    for u in range(PAIR):
        weight = weight_rows(w_ref, u)
        half = weight.shape[0] // 2
        lanes = slice(u * hd, (u + 1) * hd)
        q_feat = features(weight[:half], q_all[:, lanes])
        k_low = features(weight[half:], k_all).astype(BF16)
        qf_ref[u] = q_feat
        kf_ref[u] = k_low
        q_low = q_feat.astype(BF16)
        k_turned = turned(k_low)
        norm = column(norm_ref[place(step, u), :], TILE)
        g_turned = g_all[:, lanes].astype(F32).T
        suffix = jnp.zeros((2 * half, hd), F32)
        for j in range(BLK // TILE):
            begin, end = j * TILE, (j + 1) * TILE
            own = q_low[:, begin:end]
            scores = causal(nn(k_turned[:end], own), begin)
            for i, tile in enumerate(tiles_of(j)):
                sc_ref[u, tile] = scores[i * TILE : (i + 1) * TILE].astype(BF16)
            denominator = jnp.sum(own.astype(F32) * norm, axis=0, keepdims=True) + jnp.sum(
                scores, axis=0, keepdims=True
            )
            inverse = 1.0 / denominator
            inv_ref[place(step, u), begin:end] = inverse
            scaled = g_turned[:, begin:end] * inverse
            scaled_ref[u, :, begin:end] = scaled
            suffix = suffix + nt(own, scaled.astype(BF16))
        sx_ref[u] = suffix.astype(BF16)


def back_kernel(
    slot, k_ref, v_ref, q_ref, w_ref, qf_ref, kf_ref, scaled_ref, sc_ref, inv_ref, norm_ref, st_ref,
    gq_ref, dk_ref, dv_ref, sn_ref, gm_ref, vt_all,
):
    v_all, q_all = flat(v_ref), flat(q_ref)
    hd = v_all.shape[1]
    step = pl.program_id(0)

    @pl.when(step == 0)
    def _():
        vt_all[...] = turned(v_all)
        dv_ref[...] = jnp.zeros_like(dv_ref)

    maps = []
    for u in range(PAIR):
        half = w_ref.shape[3] // 2
        weight = weight_rows(w_ref, u)
        lanes = slice(u * hd, (u + 1) * hd)
        q_feat = qf_ref[u]
        k_low = kf_ref[u]
        state = st_ref[u]
        state_turned = turned(state)
        norm = column(norm_ref[place(step, u), :], TILE)
        back = []
        dkey = [jnp.zeros((2 * half, TILE), F32) for _ in range(BLK // TILE)]
        dvalue = [jnp.zeros((hd, TILE), F32) for _ in range(BLK // TILE)]
        suffix_norm = jnp.zeros((2 * half, 1), F32)
        for j in range(BLK // TILE):
            begin, end = j * TILE, (j + 1) * TILE
            own = q_feat[:, begin:end].astype(BF16)
            scores_low = [sc_ref[u, tile] for tile in tiles_of(j)]
            numerator = nn(state_turned, own) + nn(
                vt_all[:, :end], jnp.concatenate(scores_low, axis=0)
            )
            inverse = inv_ref[place(step, u), begin:end]
            scaled = scaled_ref[u, :, begin:end]
            scaled_low = scaled.astype(BF16)
            norm_grad = -jnp.sum(scaled * (numerator * inverse), axis=0, keepdims=True)
            dscores = causal(nn(v_all[:end], scaled_low) + norm_grad, begin).astype(BF16)
            dquery = nn(state, scaled_low) + norm * norm_grad + nn(k_low[:, :end], dscores)
            back.append(feature_back(q_feat[:, begin:end], dquery))
            for i in range(j + 1):
                dkey[i] = dkey[i] + nt(own, dscores[i * TILE : (i + 1) * TILE])
                dvalue[i] = dvalue[i] + nt(scaled_low, scores_low[i])
            suffix_norm = suffix_norm + jnp.sum(
                own.astype(F32) * norm_grad, axis=1, keepdims=True
            )
        dlog = jnp.concatenate(back, axis=1)
        grads = nn(turned(dlog), weight[:half]).astype(BF16)
        gq_ref[:, :, lanes] = grads.reshape(gq_ref.shape[0], -1, hd)
        maps.append(nn(dlog, q_all[:, lanes]))
        dk_ref[u] = jnp.concatenate(dkey, axis=1)
        dv_ref[...] += jnp.concatenate(dvalue, axis=1)
        sn_ref[place(step, u), :] = jnp.broadcast_to(suffix_norm, (2 * half, 2 * half)).T[:1]
    gm_ref[0] = jnp.concatenate(maps, axis=0).T.astype(gm_ref.dtype)


def key_kernel(
    slot, k_ref, v_ref, w_ref, sx_ref, dk_ref, dv_ref, norms_ref, weights, _,
    out, gm_ref, vt_all, total, logs, all_weights, norm_all,
):
    k_all, v_all = flat(k_ref), flat(v_ref)
    hd = k_all.shape[1]
    step = pl.program_id(0)

    @pl.when(step == 0)
    def _():
        vt_all[...] = turned(v_all)
        total[...] = dv_ref[...]
        norm_all[...] = pick(norms_ref, weights, slot[0], slot[1], False)

    maps = []
    for u in range(PAIR):
        weight = weight_rows(w_ref, u)
        half = weight.shape[0] // 2
        weight = weight[half:]
        feats = features(weight, k_all)
        suffix = sx_ref[u]
        norm = column(norm_all[place(step, u), :], BLK)
        dlog = feature_back(feats, dk_ref[u] + nn(suffix, vt_all[...]) + norm)
        at = pl.ds(pl.multiple_of((step * PAIR + u) * half, half), half)
        logs[at, :] = dlog
        all_weights[at, :] = weight
        maps.append(nn(dlog, k_all))
        total[...] += nn(turned(suffix), feats.astype(BF16))
    gm_ref[0] = jnp.concatenate(maps, axis=0).T.astype(gm_ref.dtype)

    @pl.when(step == pl.num_programs(0) - 1)
    def _():
        pair = jnp.concatenate([nn(turned(logs[...]), all_weights[...]), total[...].T], axis=1)
        out[...] = pair.astype(out.dtype).reshape(out.shape)


def total_kernel(*refs):
    for h in range(refs[-1].shape[0]):
        refs[-1][h] = sum(ref[h].astype(F32) for ref in refs[:-1]).astype(BF16)


def spread_kernel(grp, others, closing, block_weight, total_weight, at, *refs):
    parts, totals, refs = refs[:grp], refs[grp : grp + others], refs[grp + others :]
    if closing:
        outs, grad, scratch = refs[:grp], refs[grp], refs[grp + 1]
    else:
        state_ref, outs = refs[0], refs[1:]
    for h in range(parts[0].shape[0]):
        states = [ref[h].astype(F32) for ref in parts]
        others_state = [ref[h].astype(F32) for ref in totals]
        if closing:
            base = jnp.zeros_like(states[0])
            scratch[...] = sum(states) + sum(others_state)
            rows = grad.shape[1]
            grad[h] = scratch[pl.ds(pl.multiple_of(at[0] * rows, rows), rows), :]
        else:
            base = state_ref[h]
        for i, state in enumerate(others_state):
            base = base + total_weight[i] * state
        for r, out in enumerate(outs):
            state = base
            for i in range(grp):
                if i != r:
                    state = state + block_weight[r * grp + i] * states[i]
            out[h] = state.astype(BF16)


def close_kernel(pairs, singles, at, q_ref, k_ref, *refs):
    both, q_parts, k_parts = (
        refs[:pairs],
        refs[pairs : pairs + singles],
        refs[pairs + singles : pairs + 2 * singles],
    )
    for i, (own, parts, out) in enumerate(
        ((q_ref, q_parts, refs[-2]), (k_ref, k_parts, refs[-1]))
    ):
        rows, half = out.shape[1:]
        mine = pl.ds(pl.multiple_of(at[0] * rows, rows), rows)
        for h in range(own.shape[0]):
            total = own[h, mine, :].astype(F32)
            for ref in both:
                total = total + ref[i, h].astype(F32)
            for ref in parts:
                total = total + ref[h].astype(F32)
            for u in range(PAIR):
                out[h * PAIR + u] = total[:, u * half : (u + 1) * half]


def whole_call(kernel, outs, smem, arrays, name, scratch=()):
    total = sum(a.size * a.dtype.itemsize for a in (*arrays, *outs))
    return pl.pallas_call(
        kernel,
        out_shape=outs,
        in_specs=[pl.BlockSpec(memory_space=SMEM)] * len(smem)
        + [pl.BlockSpec(memory_space=pltpu.VMEM)] * len(arrays),
        out_specs=[pl.BlockSpec(memory_space=pltpu.VMEM)] * len(outs),
        scratch_shapes=list(scratch),
        compiler_params=pltpu.CompilerParams(vmem_limit_bytes=LIMIT),
        cost_estimate=LITTLE,
        name=name,
    )(*smem, *arrays)


def after(value, *others):
    return lax.optimization_barrier((value, *others))[0]


def shards(
    query_rows, key_rows, value_rows, grad_out, query_map, key_map, prefix_state, prefix_norm
):
    ctx, fsdp = lax.axis_size("ctx"), lax.axis_size("fsdp")
    tok = query_rows.shape[0]
    heads, map_rows, half = query_map.shape
    hd = map_rows * fsdp
    kv_heads = key_rows.shape[1] // hd
    replicas = ctx // kv_heads
    part = BLK // tok
    grp = ctx // part
    mine = lax.axis_index("ctx")
    block, seq = mine // part, lax.axis_index("fsdp")
    slots = range(grp)
    order = list(reversed(slots))
    grid = (heads // PAIR,)

    blocks_of = [[g * part + p for p in range(part)] for g in slots]

    def within(array):
        return lax.all_to_all(array, "ctx", 0, 0, axis_index_groups=blocks_of, tiled=True)

    def across(array, shift):
        return lax.ppermute(array, "ctx", [(d, (d + shift * part) % ctx) for d in range(ctx)])

    def along(array, shift):
        return lax.ppermute(array, "fsdp", [(d, (d + shift) % fsdp) for d in range(fsdp)])

    def apart(array, s, r):
        moves = [
            (d * fsdp + i, (d + s * part) % ctx * fsdp + (i + r) % fsdp)
            for d in range(ctx)
            for i in range(fsdp)
        ]
        return lax.ppermute(array, ("ctx", "fsdp"), moves)

    def gathered(array):
        pieces = jnp.stack([array] + [across(array, s) for s in slots[1:]])
        return lax.all_gather(pieces, "fsdp")

    def ints(values):
        return jnp.stack([jnp.asarray(v, jnp.int32) for v in values])

    def flags(values):
        return jnp.stack([v.astype(F32) for v in values])

    slot = {s: (block + s) % grp for s in slots}
    owner = {s: [slot[s] * part + p for p in range(part)] for s in slots}
    place_of = [i * grp + (block - r) % grp for i in range(fsdp) for r in slots]
    earlier = flags([other < seq * grp + block for other in place_of])
    later = flags([other > seq * grp + block for other in place_of])

    own_maps = jnp.concatenate((query_map, key_map), axis=-1)
    maps = jnp.stack([own_maps] + [across(own_maps, -s) for s in slots[1:]])
    maps = lax.all_gather(maps, "fsdp")
    at = mine % part
    kv_table = ints(
        [(slot[s] * part + (at + r) % part) // replicas for r in range(part) for s in slots]
    )
    dealt = deal(kv_table, (key_rows, value_rows), part, grp, hd)
    moves = [[(d, d // part * part + (d + r) % part) for d in range(ctx)] for r in range(part)]
    kv = [dealt[0]] + [lax.ppermute(dealt[r], "ctx", moves[r]) for r in range(1, part)]
    (kv,) = whole_call(
        sort_kernel,
        [jax.ShapeDtypeStruct((part, *dealt[0].shape), BF16)],
        [ints([(at - r) % part for r in range(part)])],
        kv,
        "sort",
    )

    params = pltpu.CompilerParams(
        dimension_semantics=("arbitrary",), vmem_limit_bytes=LIMIT
    )
    in_smem = pl.BlockSpec(memory_space=SMEM)
    anywhere = pl.BlockSpec(memory_space=pl.ANY)

    def piece_spec(column, count):
        return pl.BlockSpec((part, tok, count * hd), lambda h, t: (0, 0, column(h)))

    def head_spec(*shape):
        return pl.BlockSpec((PAIR, *shape), lambda h, t: (h,) + (0,) * len(shape))

    def fixed_spec(*shape):
        return pl.BlockSpec(shape, lambda h, t: (0,) * len(shape))

    def of(dtype, *shape):
        return jax.ShapeDtypeStruct(shape, dtype)

    def k_spec(s):
        return piece_spec(lambda h: 2 * s, 1)

    def v_spec(s):
        return piece_spec(lambda h: 2 * s + 1, 1)

    def map_spec(s):
        return pl.BlockSpec((fsdp, None, PAIR, map_rows, 2 * half), lambda h, t: (0, s, h, 0, 0))

    q_spec, g_spec = piece_spec(lambda h: h, PAIR), piece_spec(lambda h: grid[0] + h, PAIR)
    state_spec, state_shape = head_spec(hd, hd), of(BF16, heads, hd, hd)
    row_spec, row_shape = fixed_spec(heads, hd), of(F32, heads, hd)
    wide_spec, wide_shape = head_spec(2 * half, BLK), of(F32, heads, 2 * half, BLK)
    gm_spec = pl.BlockSpec((1, hd, PAIR * half), lambda h, t: (h, 0, 0))
    gm_shape = of(BF16, heads // PAIR, hd, PAIR * half)
    dv_spec, dv_shape = fixed_spec(hd, BLK), of(F32, hd, BLK)
    count = tiles_of(BLK // TILE - 1)[-1] + 1
    unit = 2 * heads * BLK * hd

    def call(kernel, s, outs, specs, out_specs, arrays, scratch, name, flops, alias=()):
        moved = sum(a.size * a.dtype.itemsize for a in (*arrays, *outs))
        return pl.pallas_call(
            kernel,
            out_shape=outs,
            grid_spec=pltpu.PrefetchScalarGridSpec(
                num_scalar_prefetch=1,
                grid=grid,
                in_specs=specs,
                out_specs=out_specs,
                scratch_shapes=scratch,
            ),
            compiler_params=params,
            cost_estimate=LITTLE,
            input_output_aliases=dict(alias),
            name=name,
        )(ints([slot[s], block]), *arrays)

    def totals_of(partial, sent=()):
        sent = dict(sent)
        parts = [partial[0]] + [
            sent[s] if s in sent else across(partial[s], s) for s in slots[1:]
        ]
        return parts, whole_call(total_kernel, [state_shape], [], parts, "totals")[0]

    def spread(parts, total, before, extra, closing):
        others = [along(total, r) for r in range(1, fsdp)]
        blocks = [(block - r) % grp for r in slots]
        block_weight = flags([before(b, a) for a in blocks for b in blocks])
        total_weight = flags([before((seq - r) % fsdp, seq) for r in range(1, fsdp)])
        result = whole_call(
            functools.partial(spread_kernel, grp, fsdp - 1, closing),
            [state_shape] * grp + [of(F32, heads, map_rows, hd)] * closing,
            [block_weight, total_weight, ints([seq])],
            parts + others + extra,
            "spread",
            [pltpu.VMEM((hd, hd), F32)] * closing,
        )
        return [result[0]] + [across(result[s], -s) for s in slots[1:]], result[grp:]

    def sent_rows(s, table):
        return within(pack(table, (query_rows, grad_out), part, 1, heads * hd))

    first, others = order[0], order[1:]
    rows = {first: sent_rows(first, ints(owner[first]))}
    partial, norm = {}, {}
    for s in order:
        partial[s], norm[s] = call(
            state_kernel,
            s,
            [state_shape, row_shape],
            [k_spec(s), v_spec(s), map_spec(s)],
            [state_spec, row_spec],
            [kv, kv, maps],
            [],
            "states",
            unit * 2 * hd,
        )
    norms = gathered(jnp.concatenate([norm[i] for i in slots] + [prefix_norm], axis=0))
    parts, total = totals_of(partial)
    for s in others:
        rows[s] = sent_rows(s, after(ints(owner[s]), *parts))
    state, _ = spread(parts, total, lambda a, b: a < b, [prefix_state], False)

    def front_of(s, norms):
        return call(
            front_kernel,
            s,
            [
                wide_shape,
                of(BF16, heads, 2 * half, BLK),
                of(F32, heads, hd, BLK),
                of(BF16, heads, count, TILE, TILE),
                of(F32, heads, BLK),
                row_shape,
                state_shape,
            ],
            [k_spec(s), q_spec, g_spec, map_spec(s), fixed_spec(*norms.shape), in_smem],
            [
                wide_spec,
                wide_spec,
                wide_spec,
                head_spec(count, TILE, TILE),
                fixed_spec(heads, BLK),
                row_spec,
                state_spec,
            ],
            [kv, rows[s], rows[s], maps, norms, earlier],
            [],
            "front",
            unit * 3 * BLK,
        )

    def back_of(s):
        return call(
            back_kernel,
            s,
            [of(BF16, part, tok, heads * hd), wide_shape, dv_shape, row_shape, gm_shape],
            [
                k_spec(s),
                v_spec(s),
                q_spec,
                map_spec(s),
                wide_spec,
                wide_spec,
                wide_spec,
                head_spec(count, TILE, TILE),
                fixed_spec(heads, BLK),
                row_spec,
                state_spec,
            ],
            [q_spec, wide_spec, dv_spec, row_spec, gm_spec],
            [kv, kv, rows[s], maps, *fronts[s][:6], state[s]],
            [pltpu.VMEM((hd, BLK), BF16)],
            "back",
            unit * 6 * BLK,
        )

    def rows_for(array, device):
        pieces = array.reshape(*array.shape[:-2], fsdp, map_rows, array.shape[-1])
        return lax.dynamic_index_in_dim(pieces, device % fsdp, array.ndim - 2, keepdims=False)

    fronts = {first: front_of(first, norms)}
    sent = {s: across(fronts[first][6], s) for s in (first,) if s}
    for s in others:
        fronts[s] = front_of(s, after(norms, state[0], *sent.values()))
    parts, total = totals_of({s: fronts[s][6] for s in slots}, sent)
    state[0] = after(state[0], total)
    suffix, (grad_prefix,) = spread(parts, total, lambda a, b: a > b, [], True)
    backs, returned, q_maps = {}, {}, []
    for s in slots:
        if s:
            state[s] = after(state[s], suffix[0])
        backs[s] = back_of(s)
        returned[s] = within(backs[s][0])
        if s:
            q_maps += [apart(rows_for(backs[s][4], seq + r), s, r) for r in range(fsdp)]
    suffix_norms = gathered(jnp.concatenate([backs[s][3] for s in slots], axis=0))

    kv_type = BF16 if replicas == 1 else F32
    pairs = jnp.zeros((part, tok, grp * 2 * hd), kv_type)
    k_maps, both_maps, key_gm = [], [], {}
    for s in slots:
        if s:
            suffix[s] = after(suffix[s], returned[0], *q_maps, *both_maps)
        pairs, key_gm[s] = call(
            key_kernel,
            s,
            [of(kv_type, *pairs.shape), gm_shape],
            [k_spec(s), v_spec(s), map_spec(s), state_spec, wide_spec, dv_spec]
            + [fixed_spec(*suffix_norms.shape), in_smem, anywhere],
            [piece_spec(lambda h: s, 2), gm_spec],
            [kv, kv, maps, suffix[s], backs[s][1], backs[s][2], suffix_norms, later, pairs],
            [
                pltpu.VMEM((hd, BLK), BF16),
                pltpu.VMEM((hd, BLK), F32),
                pltpu.VMEM((heads * half, BLK), BF16),
                pltpu.VMEM((heads * half, hd), BF16),
                pltpu.VMEM((heads, hd), F32),
            ],
            "keys",
            unit * 4 * hd,
            {9: 0},
        )
        if s == 0:
            two = jnp.stack([backs[s][4], key_gm[s]])
            both_maps = [along(rows_for(two, seq + r), r) for r in range(1, fsdp)]
        else:
            k_maps += [apart(rows_for(key_gm[s], seq + r), s, r) for r in range(fsdp)]

    table = ints([c for s in slots for c in owner[s]])
    pairs = after(pairs, *returned.values())
    pairs = within(pairs)
    (grad_queries,) = unpack(table, [returned[s] for s in slots], 1, heads * hd)
    pairs = [pairs[:, :, s * 2 * hd : (s + 1) * 2 * hd] for s in slots]
    grad_keys, grad_values = unpack(table, pairs, 2, hd)
    if replicas > 1:
        grad_keys, grad_values = (
            jnp.sum(a.reshape(tok, kv_heads, replicas, hd), axis=2)
            .astype(BF16)
            .reshape(tok, kv_heads * hd)
            for a in (grad_keys, grad_values)
        )
    query_map_grad, key_map_grad = whole_call(
        functools.partial(close_kernel, len(both_maps), len(q_maps)),
        [of(F32, heads, map_rows, half)] * 2,
        [ints([seq])],
        [backs[0][4], key_gm[0]] + both_maps + q_maps + k_maps,
        "close",
    )
    return grad_queries, grad_keys, grad_values, query_map_grad, key_map_grad, grad_prefix


def solution(mesh):
    rows, maps = P(("fsdp", "ctx"), None), P("ctx", "fsdp", None)
    return jax.shard_map(
        shards,
        mesh=mesh,
        in_specs=(rows,) * 4 + (maps, maps, P("ctx", None, None), P("ctx", None)),
        out_specs=(rows,) * 3 + (maps,) * 3,
        check_vma=False,
    )
```

```python
import functools

import jax
import jax.numpy as jnp
from jax import lax
from jax.experimental import pallas as pl
from jax.experimental.pallas import tpu as pltpu
from jax.sharding import PartitionSpec as P

BLK = 512
TILE = 256
PAIR = 2
LIMIT = 40 * 1024 * 1024

LITTLE = pl.CostEstimate(flops=1000, bytes_accessed=1000, transcendentals=0)

F32 = jnp.float32
BF16 = jnp.bfloat16
SMEM = pltpu.SMEM


def nn(left, right):
    return lax.dot_general(left, right, (((1,), (0,)), ((), ())), preferred_element_type=F32)


def nt(left, right):
    return lax.dot_general(left, right, (((1,), (1,)), ((), ())), preferred_element_type=F32)


def turned(array):
    return array.astype(F32).T.astype(array.dtype)


def column(row, width):
    n = row.shape[1]
    square = jnp.broadcast_to(row, (n, n)).T
    return jnp.concatenate([square] * (width // n), axis=1)


def pick(ref, table, slot, block, weights, before):
    blocks, groups = ref.shape[:2]
    heads = ref.shape[2] // (groups + before)
    total = jnp.zeros((heads, ref.shape[3]), F32)
    slot, block = table[slot], table[block]
    for r in range(groups):
        at = lax.rem(slot - block + r + groups, groups) * heads
        rows = pl.ds(pl.multiple_of(at, heads), heads)
        for i in range(blocks):
            total = total + table[weights + i * groups + r].astype(F32) * ref[i, r, rows, :]
    if before:
        total = total + ref[0, lax.rem(block - slot + groups, groups), groups * heads :, :]
    return total


def weight_rows(ref, u):
    whole = jnp.concatenate([ref[i, u] for i in range(ref.shape[0])], axis=0)
    return turned(whole)


def features(weight, rows):
    logits = nt(weight, rows).astype(BF16).astype(F32)
    upper = jnp.exp(logits)
    lower = jnp.exp(-logits)
    upper = upper * (1.0 / jnp.sum(upper, axis=0, keepdims=True))
    lower = lower * (1.0 / jnp.sum(lower, axis=0, keepdims=True))
    return jnp.concatenate([upper, lower], axis=0)


def feature_back(feats, upstream):
    half = feats.shape[0] // 2
    weighted = feats * upstream
    first, second = weighted[:half], weighted[half:]
    first = first - feats[:half] * jnp.sum(first, axis=0, keepdims=True)
    second = second - feats[half:] * jnp.sum(second, axis=0, keepdims=True)
    return (first - second).astype(BF16)


def flat(ref):
    return ref[...].reshape(-1, ref.shape[-1])


def pack_kernel(columns, table, *refs):
    sources, out = refs[:-1], refs[-1]
    width = sources[0].shape[1]
    for i, source in enumerate(sources):
        out[0, :, i * width : (i + 1) * width] = source[...]


def pack(table, base, sources, pieces, columns, width):
    rows = sources[0].shape[0]
    count = columns * len(sources)

    def take(s):
        return pl.BlockSpec((rows, width), lambda i, t: (0, t[base + s * pieces + i]))

    return pl.pallas_call(
        functools.partial(pack_kernel, columns),
        out_shape=jax.ShapeDtypeStruct((pieces, rows, count * width), sources[0].dtype),
        grid_spec=pltpu.PrefetchScalarGridSpec(
            num_scalar_prefetch=1,
            grid=(pieces,),
            in_specs=[take(s) for s in range(columns) for _ in sources],
            out_specs=pl.BlockSpec((1, rows, count * width), lambda i, t: (i, 0, 0)),
        ),
        compiler_params=pltpu.CompilerParams(vmem_limit_bytes=LIMIT),
        cost_estimate=LITTLE,
        name="pack",
    )(table, *(list(sources) * columns))


def deal_kernel(columns, inputs, table, *refs):
    count = columns * inputs
    for r, out in enumerate(refs[-(len(refs) // (count + 1)) :]):
        width = out.shape[1] // count
        for i in range(count):
            out[:, i * width : (i + 1) * width] = refs[r * count + i][...]


def deal(table, base, sources, pieces, columns, width):
    rows = sources[0].shape[0]
    count = columns * len(sources)

    def take(at):
        return pl.BlockSpec((rows, width), lambda i, t: (0, t[base + at]))

    return pl.pallas_call(
        functools.partial(deal_kernel, columns, len(sources)),
        out_shape=[jax.ShapeDtypeStruct((rows, count * width), sources[0].dtype)] * pieces,
        grid_spec=pltpu.PrefetchScalarGridSpec(
            num_scalar_prefetch=1,
            grid=(1,),
            in_specs=[
                take(r * columns + s)
                for r in range(pieces)
                for s in range(columns)
                for _ in sources
            ],
            out_specs=[pl.BlockSpec((rows, count * width), lambda i, t: (0, 0))] * pieces,
        ),
        compiler_params=pltpu.CompilerParams(vmem_limit_bytes=LIMIT),
        cost_estimate=LITTLE,
        name="deal",
    )(table, *(list(sources) * (pieces * columns)))


def sort_kernel(base, table, *refs):
    for r, ref in enumerate(refs[:-1]):
        refs[-1][table[base + r]] = ref[...]


def unpack_kernel(outputs, base, table, *refs):
    sources, outs = refs[:-outputs], refs[-outputs:]
    for s, source in enumerate(sources):
        pieces = source.shape[0]
        width = source.shape[2] // outputs
        for r in range(pieces):
            at = pl.ds(pl.multiple_of(table[base + s * pieces + r] * width, width), width)
            for i, out in enumerate(outs):
                out[:, at] = source[r, :, i * width : (i + 1) * width]


def unpack(table, base, sources, outputs, width):
    pieces, rows = sources[0].shape[:2]
    total = len(sources) * pieces * width
    step = rows // 2
    return pl.pallas_call(
        functools.partial(unpack_kernel, outputs, base),
        out_shape=[jax.ShapeDtypeStruct((rows, total), sources[0].dtype)] * outputs,
        grid=(rows // step,),
        in_specs=[pl.BlockSpec(memory_space=SMEM)]
        + [pl.BlockSpec((pieces, step, outputs * width), lambda i: (0, i, 0))] * len(sources),
        out_specs=[pl.BlockSpec((step, total), lambda i: (i, 0))] * outputs,
        compiler_params=pltpu.CompilerParams(vmem_limit_bytes=LIMIT),
        cost_estimate=LITTLE,
        name="unpack",
    )(table, *sources)


def place(step, u):
    return pl.ds(step * PAIR + u, 1)


def state_kernel(slot, k_ref, v_ref, w_ref, out, norm_ref):
    k_all, v_all = flat(k_ref), flat(v_ref)
    step = pl.program_id(0)
    for u in range(PAIR):
        weight = weight_rows(w_ref, u)
        feats = features(weight[weight.shape[0] // 2 :], k_all).astype(BF16)
        out[u] = nn(feats, v_all).astype(BF16)
        ones = jnp.ones((8, feats.shape[1]), BF16)
        norm_ref[place(step, u), :] = nt(ones, feats)[:1]


def tiles_of(j):
    return range(j * (j + 1) // 2, (j + 1) * (j + 2) // 2)


def causal(array, begin):
    earlier = lax.broadcasted_iota(jnp.int32, (TILE, TILE), 0) <= lax.broadcasted_iota(
        jnp.int32, (TILE, TILE), 1
    )
    masked = jnp.where(earlier, array[begin:], 0.0)
    return masked if begin == 0 else jnp.concatenate([array[:begin], masked], axis=0)


def front_kernel(
    where, table, k_ref, q_ref, g_ref, w_ref, norms_ref,
    qf_ref, kf_ref, scaled_ref, sc_ref, inv_ref, norm_ref, sx_ref,
):
    k_all, q_all, g_all = flat(k_ref), flat(q_ref), flat(g_ref)
    hd = k_all.shape[1]
    step = pl.program_id(0)

    @pl.when(step == 0)
    def _():
        norm_ref[...] = pick(norms_ref, table, *where, True)

    for u in range(PAIR):
        weight = weight_rows(w_ref, u)
        half = weight.shape[0] // 2
        lanes = slice(u * hd, (u + 1) * hd)
        q_feat = features(weight[:half], q_all[:, lanes])
        k_low = features(weight[half:], k_all).astype(BF16)
        qf_ref[u] = q_feat
        kf_ref[u] = k_low
        q_low = q_feat.astype(BF16)
        k_turned = turned(k_low)
        norm = column(norm_ref[place(step, u), :], TILE)
        g_turned = g_all[:, lanes].astype(F32).T
        suffix = jnp.zeros((2 * half, hd), F32)
        for j in range(BLK // TILE):
            begin, end = j * TILE, (j + 1) * TILE
            own = q_low[:, begin:end]
            scores = causal(nn(k_turned[:end], own), begin)
            for i, tile in enumerate(tiles_of(j)):
                sc_ref[u, tile] = scores[i * TILE : (i + 1) * TILE].astype(BF16)
            denominator = jnp.sum(own.astype(F32) * norm, axis=0, keepdims=True) + jnp.sum(
                scores, axis=0, keepdims=True
            )
            inverse = 1.0 / denominator
            inv_ref[place(step, u), begin:end] = inverse
            scaled = g_turned[:, begin:end] * inverse
            scaled_ref[u, :, begin:end] = scaled
            suffix = suffix + nt(own, scaled.astype(BF16))
        sx_ref[u] = suffix.astype(BF16)


def back_kernel(
    slot, k_ref, v_ref, q_ref, w_ref, qf_ref, kf_ref, scaled_ref, sc_ref, inv_ref, norm_ref, st_ref,
    gq_ref, dk_ref, dv_ref, sn_ref, gm_ref, vt_all,
):
    v_all, q_all = flat(v_ref), flat(q_ref)
    hd = v_all.shape[1]
    step = pl.program_id(0)

    @pl.when(step == 0)
    def _():
        vt_all[...] = turned(v_all)
        dv_ref[...] = jnp.zeros_like(dv_ref)

    maps = []
    for u in range(PAIR):
        half = w_ref.shape[3] // 2
        weight = weight_rows(w_ref, u)
        lanes = slice(u * hd, (u + 1) * hd)
        q_feat = qf_ref[u]
        k_low = kf_ref[u]
        state = st_ref[u]
        state_turned = turned(state)
        norm = column(norm_ref[place(step, u), :], TILE)
        back = []
        dkey = [jnp.zeros((2 * half, TILE), F32) for _ in range(BLK // TILE)]
        dvalue = [jnp.zeros((hd, TILE), F32) for _ in range(BLK // TILE)]
        suffix_norm = jnp.zeros((2 * half, 1), F32)
        for j in range(BLK // TILE):
            begin, end = j * TILE, (j + 1) * TILE
            own = q_feat[:, begin:end].astype(BF16)
            scores_low = [sc_ref[u, tile] for tile in tiles_of(j)]
            numerator = nn(state_turned, own) + nn(
                vt_all[:, :end], jnp.concatenate(scores_low, axis=0)
            )
            inverse = inv_ref[place(step, u), begin:end]
            scaled = scaled_ref[u, :, begin:end]
            scaled_low = scaled.astype(BF16)
            norm_grad = -jnp.sum(scaled * (numerator * inverse), axis=0, keepdims=True)
            dscores = causal(nn(v_all[:end], scaled_low) + norm_grad, begin).astype(BF16)
            dquery = nn(state, scaled_low) + norm * norm_grad + nn(k_low[:, :end], dscores)
            back.append(feature_back(q_feat[:, begin:end], dquery))
            for i in range(j + 1):
                dkey[i] = dkey[i] + nt(own, dscores[i * TILE : (i + 1) * TILE])
                dvalue[i] = dvalue[i] + nt(scaled_low, scores_low[i])
            suffix_norm = suffix_norm + jnp.sum(
                own.astype(F32) * norm_grad, axis=1, keepdims=True
            )
        dlog = jnp.concatenate(back, axis=1)
        grads = nn(turned(dlog), weight[:half]).astype(BF16)
        gq_ref[:, :, lanes] = grads.reshape(gq_ref.shape[0], -1, hd)
        maps.append(nn(dlog, q_all[:, lanes]))
        dk_ref[u] = jnp.concatenate(dkey, axis=1)
        dv_ref[...] += jnp.concatenate(dvalue, axis=1)
        sn_ref[place(step, u), :] = jnp.broadcast_to(suffix_norm, (2 * half, 2 * half)).T[:1]
    gm_ref[0] = jnp.concatenate(maps, axis=0).T.astype(gm_ref.dtype)


def key_kernel(
    where, table, k_ref, v_ref, w_ref, sx_ref, dk_ref, dv_ref, norms_ref, _,
    out, gm_ref, vt_all, total, logs, all_weights, norm_all,
):
    k_all, v_all = flat(k_ref), flat(v_ref)
    hd = k_all.shape[1]
    step = pl.program_id(0)

    @pl.when(step == 0)
    def _():
        vt_all[...] = turned(v_all)
        total[...] = dv_ref[...]
        norm_all[...] = pick(norms_ref, table, *where, False)

    maps = []
    for u in range(PAIR):
        weight = weight_rows(w_ref, u)
        half = weight.shape[0] // 2
        weight = weight[half:]
        feats = features(weight, k_all)
        suffix = sx_ref[u]
        norm = column(norm_all[place(step, u), :], BLK)
        dlog = feature_back(feats, dk_ref[u] + nn(suffix, vt_all[...]) + norm)
        at = pl.ds(pl.multiple_of((step * PAIR + u) * half, half), half)
        logs[at, :] = dlog
        all_weights[at, :] = weight
        maps.append(nn(dlog, k_all))
        total[...] += nn(turned(suffix), feats.astype(BF16))
    gm_ref[0] = jnp.concatenate(maps, axis=0).T.astype(gm_ref.dtype)

    @pl.when(step == pl.num_programs(0) - 1)
    def _():
        pair = jnp.concatenate([nn(turned(logs[...]), all_weights[...]), total[...].T], axis=1)
        out[...] = pair.astype(out.dtype).reshape(out.shape)


def total_kernel(table, *refs):
    for h in range(refs[-1].shape[0]):
        refs[-1][h] = sum(ref[h].astype(F32) for ref in refs[:-1]).astype(BF16)


def spread_kernel(grp, others, closing, block_weight, total_weight, at, table, *refs):
    parts, totals, refs = refs[:grp], refs[grp : grp + others], refs[grp + others :]
    if closing:
        outs, grad, scratch = refs[:grp], refs[grp], refs[grp + 1]
    else:
        state_ref, outs = refs[0], refs[1:]
    for h in range(parts[0].shape[0]):
        states = [ref[h].astype(F32) for ref in parts]
        others_state = [ref[h].astype(F32) for ref in totals]
        if closing:
            base = jnp.zeros_like(states[0])
            scratch[...] = sum(states) + sum(others_state)
            rows = grad.shape[1]
            grad[h] = scratch[pl.ds(pl.multiple_of(table[at] * rows, rows), rows), :]
        else:
            base = state_ref[h]
        for i, state in enumerate(others_state):
            base = base + table[total_weight + i].astype(F32) * state
        for r, out in enumerate(outs):
            state = base
            for i in range(grp):
                if i != r:
                    state = state + table[block_weight + r * grp + i].astype(F32) * states[i]
            out[h] = state.astype(BF16)


def close_kernel(pairs, singles, at, table, q_ref, k_ref, *refs):
    both, q_parts, k_parts = (
        refs[:pairs],
        refs[pairs : pairs + singles],
        refs[pairs + singles : pairs + 2 * singles],
    )
    for i, (own, parts, out) in enumerate(
        ((q_ref, q_parts, refs[-2]), (k_ref, k_parts, refs[-1]))
    ):
        rows, half = out.shape[1:]
        mine = pl.ds(pl.multiple_of(table[at] * rows, rows), rows)
        for h in range(own.shape[0]):
            total = own[h, mine, :].astype(F32)
            for ref in both:
                total = total + ref[i, h].astype(F32)
            for ref in parts:
                total = total + ref[h].astype(F32)
            for u in range(PAIR):
                out[h * PAIR + u] = total[:, u * half : (u + 1) * half]


def whole_call(kernel, outs, table, arrays, name, scratch=()):
    return pl.pallas_call(
        kernel,
        out_shape=outs,
        in_specs=[pl.BlockSpec(memory_space=SMEM)]
        + [pl.BlockSpec(memory_space=pltpu.VMEM)] * len(arrays),
        out_specs=[pl.BlockSpec(memory_space=pltpu.VMEM)] * len(outs),
        scratch_shapes=list(scratch),
        compiler_params=pltpu.CompilerParams(vmem_limit_bytes=LIMIT),
        cost_estimate=LITTLE,
        name=name,
    )(table, *arrays)


def after(value, *others):
    return lax.optimization_barrier((value, *others))[0]


def shards(
    query_rows, key_rows, value_rows, grad_out, query_map, key_map, prefix_state, prefix_norm
):
    ctx, fsdp = lax.axis_size("ctx"), lax.axis_size("fsdp")
    tok = query_rows.shape[0]
    heads, map_rows, half = query_map.shape
    hd = map_rows * fsdp
    kv_heads = key_rows.shape[1] // hd
    replicas = ctx // kv_heads
    part = BLK // tok
    grp = ctx // part
    mine = lax.axis_index("ctx")
    block, seq = mine // part, lax.axis_index("fsdp")
    slots = range(grp)
    order = list(reversed(slots))
    grid = (heads // PAIR,)

    blocks_of = [[g * part + p for p in range(part)] for g in slots]

    def within(array):
        return lax.all_to_all(array, "ctx", 0, 0, axis_index_groups=blocks_of, tiled=True)

    def across(array, shift):
        return lax.ppermute(array, "ctx", [(d, (d + shift * part) % ctx) for d in range(ctx)])

    def along(array, shift):
        return lax.ppermute(array, "fsdp", [(d, (d + shift) % fsdp) for d in range(fsdp)])

    def apart(array, s, r):
        moves = [
            (d * fsdp + i, (d + s * part) % ctx * fsdp + (i + r) % fsdp)
            for d in range(ctx)
            for i in range(fsdp)
        ]
        return lax.ppermute(array, ("ctx", "fsdp"), moves)

    def both_halves(array):
        return jnp.stack([array] + [across(array, s) for s in slots[1:]])

    def ints(values):
        return jnp.stack([jnp.asarray(v, jnp.int32) for v in values])

    slot = [(block + s) % grp for s in slots]
    owner = [slot[s] * part + p for s in slots for p in range(part)]
    at = mine % part
    here = seq * grp + block
    places = [i * grp + (block - r) % grp for i in range(fsdp) for r in slots]
    near = [(block - r) % grp for r in slots]
    far = [(seq - r) % fsdp for r in range(1, fsdp)]
    lists = {
        "slot": slot,
        "block": [block],
        "seq": [seq],
        "owner": owner,
        "kv": [
            (slot[s] * part + (at + r) % part) // replicas for r in range(part) for s in slots
        ],
        "sorted": [(at - r) % part for r in range(part)],
        "places before": [other < here for other in places],
        "places after": [other > here for other in places],
        "near before": [b < a for a in near for b in near],
        "near after": [b > a for a in near for b in near],
        "far before": [other < seq for other in far],
        "far after": [other > seq for other in far],
    }
    base, values = {}, []
    for name, entries in lists.items():
        base[name] = len(values)
        values += entries
    table = ints(values)

    own_maps = jnp.concatenate((query_map, key_map), axis=-1)
    maps = jnp.stack([own_maps] + [across(own_maps, -s) for s in slots[1:]])
    maps = lax.all_gather(maps, "fsdp")
    dealt = deal(table, base["kv"], (key_rows, value_rows), part, grp, hd)
    moves = [[(d, d // part * part + (d + r) % part) for d in range(ctx)] for r in range(part)]
    kv = [dealt[0]] + [lax.ppermute(dealt[r], "ctx", moves[r]) for r in range(1, part)]
    (kv,) = whole_call(
        functools.partial(sort_kernel, base["sorted"]),
        [jax.ShapeDtypeStruct((part, *dealt[0].shape), BF16)],
        table,
        kv,
        "sort",
    )

    params = pltpu.CompilerParams(
        dimension_semantics=("arbitrary",), vmem_limit_bytes=LIMIT
    )
    anywhere = pl.BlockSpec(memory_space=pl.ANY)

    def piece_spec(column, count):
        return pl.BlockSpec((part, tok, count * hd), lambda h, t: (0, 0, column(h)))

    def head_spec(*shape):
        return pl.BlockSpec((PAIR, *shape), lambda h, t: (h,) + (0,) * len(shape))

    def fixed_spec(*shape):
        return pl.BlockSpec(shape, lambda h, t: (0,) * len(shape))

    def of(dtype, *shape):
        return jax.ShapeDtypeStruct(shape, dtype)

    def k_spec(s):
        return piece_spec(lambda h: 2 * s, 1)

    def v_spec(s):
        return piece_spec(lambda h: 2 * s + 1, 1)

    def map_spec(s):
        return pl.BlockSpec((fsdp, None, PAIR, map_rows, 2 * half), lambda h, t: (0, s, h, 0, 0))

    q_spec, g_spec = piece_spec(lambda h: h, PAIR), piece_spec(lambda h: grid[0] + h, PAIR)
    state_spec, state_shape = head_spec(hd, hd), of(BF16, heads, hd, hd)
    row_spec, row_shape = fixed_spec(heads, hd), of(F32, heads, hd)
    wide_spec, wide_shape = head_spec(2 * half, BLK), of(F32, heads, 2 * half, BLK)
    gm_spec = pl.BlockSpec((1, hd, PAIR * half), lambda h, t: (h, 0, 0))
    gm_shape = of(BF16, heads // PAIR, hd, PAIR * half)
    dv_spec, dv_shape = fixed_spec(hd, BLK), of(F32, hd, BLK)
    count = tiles_of(BLK // TILE - 1)[-1] + 1
    unit = 2 * heads * BLK * hd

    def call(kernel, s, outs, specs, out_specs, arrays, scratch, name, flops, alias=()):
        return pl.pallas_call(
            kernel,
            out_shape=outs,
            grid_spec=pltpu.PrefetchScalarGridSpec(
                num_scalar_prefetch=1,
                grid=grid,
                in_specs=specs,
                out_specs=out_specs,
                scratch_shapes=scratch,
            ),
            compiler_params=params,
            cost_estimate=LITTLE,
            input_output_aliases=dict(alias),
            name=name,
        )(table, *arrays)

    def totals_of(partial, sent=()):
        sent = dict(sent)
        parts = [partial[0]] + [
            sent[s] if s in sent else across(partial[s], s) for s in slots[1:]
        ]
        return parts, whole_call(total_kernel, [state_shape], table, parts, "totals")[0]

    def spread(parts, total, when, extra, closing):
        others = [along(total, r) for r in range(1, fsdp)]
        weights = [base["near " + when], base["far " + when], base["seq"]]
        result = whole_call(
            functools.partial(spread_kernel, grp, fsdp - 1, closing, *weights),
            [state_shape] * grp + [of(F32, heads, map_rows, hd)] * closing,
            table,
            parts + others + extra,
            "spread",
            [pltpu.VMEM((hd, hd), F32)] * closing,
        )
        return [result[0]] + [across(result[s], -s) for s in slots[1:]], result[grp:]

    def sent_rows(s, *earlier):
        packed = pack(
            after(table, *earlier),
            base["owner"] + s * part,
            (query_rows, grad_out),
            part,
            1,
            heads * hd,
        )
        return within(packed)

    first, others = order[0], order[1:]
    rows = {first: sent_rows(first, kv)}
    partial, norm = {}, {}
    for s in order:
        partial[s], norm[s] = call(
            state_kernel,
            s,
            [state_shape, row_shape],
            [k_spec(s), v_spec(s), map_spec(s)],
            [state_spec, row_spec],
            [kv, kv, maps],
            [],
            "states",
            unit * 2 * hd,
        )
    halves = both_halves(jnp.concatenate([norm[i] for i in slots] + [prefix_norm], axis=0))
    parts, total = totals_of(partial)
    for s in others:
        rows[s] = sent_rows(s, halves, *parts)
    norms = lax.all_gather(halves, "fsdp")
    state, _ = spread(parts, total, "before", [prefix_state], False)

    def front_of(s, norms):
        return call(
            functools.partial(front_kernel, (s, base["block"], base["places before"])),
            s,
            [
                wide_shape,
                of(BF16, heads, 2 * half, BLK),
                of(F32, heads, hd, BLK),
                of(BF16, heads, count, TILE, TILE),
                of(F32, heads, BLK),
                row_shape,
                state_shape,
            ],
            [k_spec(s), q_spec, g_spec, map_spec(s), fixed_spec(*norms.shape)],
            [
                wide_spec,
                wide_spec,
                wide_spec,
                head_spec(count, TILE, TILE),
                fixed_spec(heads, BLK),
                row_spec,
                state_spec,
            ],
            [kv, rows[s], rows[s], maps, norms],
            [],
            "front",
            unit * 3 * BLK,
        )

    def back_of(s):
        return call(
            back_kernel,
            s,
            [of(BF16, part, tok, heads * hd), wide_shape, dv_shape, row_shape, gm_shape],
            [
                k_spec(s),
                v_spec(s),
                q_spec,
                map_spec(s),
                wide_spec,
                wide_spec,
                wide_spec,
                head_spec(count, TILE, TILE),
                fixed_spec(heads, BLK),
                row_spec,
                state_spec,
            ],
            [q_spec, wide_spec, dv_spec, row_spec, gm_spec],
            [kv, kv, rows[s], maps, *fronts[s][:6], state[s]],
            [pltpu.VMEM((hd, BLK), BF16)],
            "back",
            unit * 6 * BLK,
        )

    def rows_for(array, device):
        pieces = array.reshape(*array.shape[:-2], fsdp, map_rows, array.shape[-1])
        return lax.dynamic_index_in_dim(pieces, device % fsdp, array.ndim - 2, keepdims=False)

    fronts = {first: front_of(first, norms)}
    sent = {s: across(fronts[first][6], s) for s in (first,) if s}
    for s in others:
        fronts[s] = front_of(s, after(norms, state[0], *sent.values()))
    sent = {s: after(sent[s], *state[1:]) for s in sent}
    parts, total = totals_of({s: fronts[s][6] for s in slots}, sent)
    state[0] = after(state[0], total)
    backs = {0: back_of(0)}
    parts[0] = after(parts[0], backs[0][3])
    suffix, (grad_prefix,) = spread(parts, total, "after", [], True)
    returned, q_maps = {}, []
    for s in slots:
        if s:
            state[s] = after(state[s], suffix[0])
            backs[s] = back_of(s)
            q_maps += [apart(rows_for(backs[s][4], seq + r), s, r) for r in range(fsdp)]
        returned[s] = within(after(backs[s][0], suffix[0]))
    suffix_norms = jnp.concatenate([backs[s][3] for s in slots], axis=0)
    suffix_norms = both_halves(after(suffix_norms, *suffix[1:]))
    suffix_norms = lax.all_gather(suffix_norms, "fsdp")

    kv_type = BF16 if replicas == 1 else F32
    pairs = jnp.zeros((part, tok, grp * 2 * hd), kv_type)
    k_maps, both_maps, key_gm = [], [], {}
    for s in slots:
        if s:
            suffix[s] = after(suffix[s], returned[0], *q_maps, *both_maps)
        pairs, key_gm[s] = call(
            functools.partial(key_kernel, (s, base["block"], base["places after"])),
            s,
            [of(kv_type, *pairs.shape), gm_shape],
            [k_spec(s), v_spec(s), map_spec(s), state_spec, wide_spec, dv_spec]
            + [fixed_spec(*suffix_norms.shape), anywhere],
            [piece_spec(lambda h: s, 2), gm_spec],
            [kv, kv, maps, suffix[s], backs[s][1], backs[s][2], suffix_norms, pairs],
            [
                pltpu.VMEM((hd, BLK), BF16),
                pltpu.VMEM((hd, BLK), F32),
                pltpu.VMEM((heads * half, BLK), BF16),
                pltpu.VMEM((heads * half, hd), BF16),
                pltpu.VMEM((heads, hd), F32),
            ],
            "keys",
            unit * 4 * hd,
            {8: 0},
        )
        if s == 0:
            two = jnp.stack([backs[s][4], key_gm[s]])
            both_maps = [along(rows_for(two, seq + r), r) for r in range(1, fsdp)]
        else:
            k_maps += [apart(rows_for(key_gm[s], seq + r), s, r) for r in range(fsdp)]

    pairs = after(pairs, *returned.values())
    pairs = within(pairs)
    (grad_queries,) = unpack(table, base["owner"], [returned[s] for s in slots], 1, heads * hd)
    pairs = [pairs[:, :, s * 2 * hd : (s + 1) * 2 * hd] for s in slots]
    grad_keys, grad_values = unpack(table, base["owner"], pairs, 2, hd)
    if replicas > 1:
        grad_keys, grad_values = (
            jnp.sum(a.reshape(tok, kv_heads, replicas, hd), axis=2)
            .astype(BF16)
            .reshape(tok, kv_heads * hd)
            for a in (grad_keys, grad_values)
        )
    query_map_grad, key_map_grad = whole_call(
        functools.partial(close_kernel, len(both_maps), len(q_maps), base["seq"]),
        [of(F32, heads, map_rows, half)] * 2,
        table,
        [backs[0][4], key_gm[0]] + both_maps + q_maps + k_maps,
        "close",
    )
    return grad_queries, grad_keys, grad_values, query_map_grad, key_map_grad, grad_prefix


def solution(mesh):
    rows, maps = P(("fsdp", "ctx"), None), P("ctx", "fsdp", None)
    return jax.shard_map(
        shards,
        mesh=mesh,
        in_specs=(rows,) * 4 + (maps, maps, P("ctx", None, None), P("ctx", None)),
        out_specs=(rows,) * 3 + (maps,) * 3,
        check_vma=False,
    )
```

```python
import functools

import jax
import jax.numpy as jnp
from jax import lax
from jax.experimental import pallas as pl
from jax.experimental.pallas import tpu as pltpu
from jax.sharding import PartitionSpec as P

BLK = 512
TILE = 256
PAIR = 2
LIMIT = 24 * 1024 * 1024

LITTLE = pl.CostEstimate(flops=1000, bytes_accessed=1000, transcendentals=0)

F32 = jnp.float32
BF16 = jnp.bfloat16
SMEM = pltpu.SMEM


def nn(left, right):
    return lax.dot_general(left, right, (((1,), (0,)), ((), ())), preferred_element_type=F32)


def nt(left, right):
    return lax.dot_general(left, right, (((1,), (1,)), ((), ())), preferred_element_type=F32)


def turned(array):
    return array.astype(F32).T.astype(array.dtype)


def column(row, width):
    n = row.shape[1]
    square = jnp.broadcast_to(row, (n, n)).T
    return jnp.concatenate([square] * (width // n), axis=1)


def pick(ref, table, slot, block, weights):
    blocks, groups = ref.shape[:2]
    heads = ref.shape[2] // groups
    total = jnp.zeros((heads, ref.shape[3]), F32)
    slot, block = table[slot], table[block]
    for r in range(groups):
        at = lax.rem(slot - block + r + groups, groups) * heads
        rows = pl.ds(pl.multiple_of(at, heads), heads)
        for i in range(blocks):
            total = total + table[weights + i * groups + r].astype(F32) * ref[i, r, rows, :]
    return total


def weight_rows(ref, u):
    whole = jnp.concatenate([ref[i, u] for i in range(ref.shape[0])], axis=0)
    return turned(whole)


def features(weight, rows):
    logits = nt(weight, rows).astype(BF16).astype(F32)
    upper = jnp.exp(logits)
    lower = jnp.exp(-logits)
    upper = upper * (1.0 / jnp.sum(upper, axis=0, keepdims=True))
    lower = lower * (1.0 / jnp.sum(lower, axis=0, keepdims=True))
    return jnp.concatenate([upper, lower], axis=0)


def feature_back(feats, upstream):
    half = feats.shape[0] // 2
    weighted = feats * upstream
    first, second = weighted[:half], weighted[half:]
    first = first - feats[:half] * jnp.sum(first, axis=0, keepdims=True)
    second = second - feats[half:] * jnp.sum(second, axis=0, keepdims=True)
    return (first - second).astype(BF16)


def flat(ref):
    return ref[...].reshape(-1, ref.shape[-1])


def pack_kernel(columns, table, *refs):
    sources, out = refs[:-1], refs[-1]
    width = sources[0].shape[1]
    for i, source in enumerate(sources):
        out[0, :, i * width : (i + 1) * width] = source[...]


def pack(table, base, sources, pieces, columns, width):
    rows = sources[0].shape[0]
    count = columns * len(sources)

    def take(s):
        return pl.BlockSpec((rows, width), lambda i, t: (0, t[base + s * pieces + i]))

    return pl.pallas_call(
        functools.partial(pack_kernel, columns),
        out_shape=jax.ShapeDtypeStruct((pieces, rows, count * width), sources[0].dtype),
        grid_spec=pltpu.PrefetchScalarGridSpec(
            num_scalar_prefetch=1,
            grid=(pieces,),
            in_specs=[take(s) for s in range(columns) for _ in sources],
            out_specs=pl.BlockSpec((1, rows, count * width), lambda i, t: (i, 0, 0)),
        ),
        compiler_params=pltpu.CompilerParams(vmem_limit_bytes=LIMIT),
        cost_estimate=LITTLE,
        name="pack",
    )(table, *(list(sources) * columns))


def unpack_kernel(outputs, base, table, *refs):
    sources, outs = refs[:-outputs], refs[-outputs:]
    for s, source in enumerate(sources):
        pieces = source.shape[0]
        width = source.shape[2] // outputs
        for r in range(pieces):
            at = pl.ds(pl.multiple_of(table[base + s * pieces + r] * width, width), width)
            for i, out in enumerate(outs):
                out[:, at] = source[r, :, i * width : (i + 1) * width]


def unpack(table, base, sources, outputs, width):
    pieces, rows = sources[0].shape[:2]
    total = len(sources) * pieces * width
    step = rows // 2
    return pl.pallas_call(
        functools.partial(unpack_kernel, outputs, base),
        out_shape=[jax.ShapeDtypeStruct((rows, total), sources[0].dtype)] * outputs,
        grid=(rows // step,),
        in_specs=[pl.BlockSpec(memory_space=SMEM)]
        + [pl.BlockSpec((pieces, step, outputs * width), lambda i: (0, i, 0))] * len(sources),
        out_specs=[pl.BlockSpec((step, total), lambda i: (i, 0))] * outputs,
        compiler_params=pltpu.CompilerParams(vmem_limit_bytes=LIMIT),
        cost_estimate=LITTLE,
        name="unpack",
    )(table, *sources)


def place(step, u):
    return pl.ds(step * PAIR + u, 1)


def state_kernel(
    near, table, k_ref, v_ref, w_ref, total_ref, before_ref, norm_ref, norm_before_ref
):
    k_all, v_all = flat(k_ref), flat(v_ref)
    step = pl.program_id(0)
    for u in range(PAIR):
        weight = weight_rows(w_ref, u)
        feats = features(weight[weight.shape[0] // 2 :], k_all).astype(BF16)
        ones = jnp.ones((8, BLK), BF16)
        sums = [jnp.zeros((feats.shape[0], v_all.shape[1]), F32)] * 2
        norms = [jnp.zeros((1, feats.shape[0]), F32)] * 2
        for g in range(k_all.shape[0] // BLK):
            rows = slice(g * BLK, (g + 1) * BLK)
            part = nn(feats[:, rows], v_all[rows])
            norm = nt(ones, feats[:, rows])[:1]
            weight = table[near + g].astype(F32)
            sums = [sums[0] + part, sums[1] + weight * part]
            norms = [norms[0] + norm, norms[1] + weight * norm]
        total_ref[u] = sums[0].astype(BF16)
        before_ref[u] = sums[1]
        norm_ref[place(step, u), :] = norms[0]
        norm_before_ref[place(step, u), :] = norms[1]


def tiles_of(j):
    return range(j * (j + 1) // 2, (j + 1) * (j + 2) // 2)


def causal(array, begin):
    earlier = lax.broadcasted_iota(jnp.int32, (TILE, TILE), 0) <= lax.broadcasted_iota(
        jnp.int32, (TILE, TILE), 1
    )
    masked = jnp.where(earlier, array[begin:], 0.0)
    return masked if begin == 0 else jnp.concatenate([array[:begin], masked], axis=0)


def front_kernel(
    far, slot, table, k_ref, q_ref, g_ref, w_ref, norms_ref, before_ref, prefix_ref,
    qf_ref, kf_ref, scaled_ref, sc_ref, inv_ref, norm_ref, sx_ref,
):
    k_all, q_all, g_all = flat(k_ref), flat(q_ref), flat(g_ref)
    hd = k_all.shape[1]
    step = pl.program_id(0)

    @pl.when(step == 0)
    def _():
        norm = prefix_ref[...] + before_ref[...]
        for i in range(norms_ref.shape[0]):
            norm = norm + table[far + i].astype(F32) * norms_ref[i, slot]
        norm_ref[...] = norm

    for u in range(PAIR):
        weight = weight_rows(w_ref, u)
        half = weight.shape[0] // 2
        lanes = slice(u * hd, (u + 1) * hd)
        q_feat = features(weight[:half], q_all[:, lanes])
        k_low = features(weight[half:], k_all).astype(BF16)
        qf_ref[u] = q_feat
        kf_ref[u] = k_low
        q_low = q_feat.astype(BF16)
        k_turned = turned(k_low)
        norm = column(norm_ref[place(step, u), :], TILE)
        g_turned = g_all[:, lanes].astype(F32).T
        suffix = jnp.zeros((2 * half, hd), F32)
        for j in range(BLK // TILE):
            begin, end = j * TILE, (j + 1) * TILE
            own = q_low[:, begin:end]
            scores = causal(nn(k_turned[:end], own), begin)
            for i, tile in enumerate(tiles_of(j)):
                sc_ref[u, tile] = scores[i * TILE : (i + 1) * TILE].astype(BF16)
            denominator = jnp.sum(own.astype(F32) * norm, axis=0, keepdims=True) + jnp.sum(
                scores, axis=0, keepdims=True
            )
            inverse = 1.0 / denominator
            inv_ref[place(step, u), begin:end] = inverse
            scaled = g_turned[:, begin:end] * inverse
            scaled_ref[u, :, begin:end] = scaled
            suffix = suffix + nt(own, scaled.astype(BF16))
        sx_ref[u] = suffix.astype(BF16)


def back_kernel(
    slot, k_ref, v_ref, q_ref, w_ref, qf_ref, kf_ref, scaled_ref, sc_ref, inv_ref, norm_ref, st_ref,
    gq_ref, dk_ref, dv_ref, sn_ref, gm_ref, vt_all,
):
    v_all, q_all = flat(v_ref), flat(q_ref)
    hd = v_all.shape[1]
    step = pl.program_id(0)

    @pl.when(step == 0)
    def _():
        vt_all[...] = turned(v_all)
        dv_ref[...] = jnp.zeros_like(dv_ref)

    maps = []
    for u in range(PAIR):
        half = w_ref.shape[3] // 2
        weight = weight_rows(w_ref, u)
        lanes = slice(u * hd, (u + 1) * hd)
        q_feat = qf_ref[u]
        k_low = kf_ref[u]
        state = st_ref[u]
        state_turned = turned(state)
        norm = column(norm_ref[place(step, u), :], TILE)
        back = []
        dkey = [jnp.zeros((2 * half, TILE), F32) for _ in range(BLK // TILE)]
        dvalue = [jnp.zeros((hd, TILE), F32) for _ in range(BLK // TILE)]
        suffix_norm = jnp.zeros((2 * half, 1), F32)
        for j in range(BLK // TILE):
            begin, end = j * TILE, (j + 1) * TILE
            own = q_feat[:, begin:end].astype(BF16)
            scores_low = [sc_ref[u, tile] for tile in tiles_of(j)]
            numerator = nn(state_turned, own) + nn(
                vt_all[:, :end], jnp.concatenate(scores_low, axis=0)
            )
            inverse = inv_ref[place(step, u), begin:end]
            scaled = scaled_ref[u, :, begin:end]
            scaled_low = scaled.astype(BF16)
            norm_grad = -jnp.sum(scaled * (numerator * inverse), axis=0, keepdims=True)
            dscores = causal(nn(v_all[:end], scaled_low) + norm_grad, begin).astype(BF16)
            dquery = nn(state, scaled_low) + norm * norm_grad + nn(k_low[:, :end], dscores)
            back.append(feature_back(q_feat[:, begin:end], dquery))
            for i in range(j + 1):
                dkey[i] = dkey[i] + nt(own, dscores[i * TILE : (i + 1) * TILE])
                dvalue[i] = dvalue[i] + nt(scaled_low, scores_low[i])
            suffix_norm = suffix_norm + jnp.sum(
                own.astype(F32) * norm_grad, axis=1, keepdims=True
            )
        dlog = jnp.concatenate(back, axis=1)
        grads = nn(turned(dlog), weight[:half]).astype(BF16)
        gq_ref[:, :, lanes] = grads.reshape(gq_ref.shape[0], -1, hd)
        maps.append(nn(dlog, q_all[:, lanes]))
        dk_ref[u] = jnp.concatenate(dkey, axis=1)
        dv_ref[...] += jnp.concatenate(dvalue, axis=1)
        sn_ref[place(step, u), :] = jnp.broadcast_to(suffix_norm, (2 * half, 2 * half)).T[:1]
    gm_ref[0] = jnp.concatenate(maps, axis=0).T.astype(gm_ref.dtype)


def key_kernel(
    where, table, k_ref, v_ref, w_ref, sx_ref, dk_ref, dv_ref, norms_ref, _,
    out, gm_ref, vt_all, total, logs, all_weights, norm_all,
):
    k_all, v_all = flat(k_ref), flat(v_ref)
    hd = k_all.shape[1]
    step = pl.program_id(0)

    @pl.when(step == 0)
    def _():
        vt_all[...] = turned(v_all)
        total[...] = dv_ref[...]
        norm_all[...] = pick(norms_ref, table, *where)

    maps = []
    for u in range(PAIR):
        weight = weight_rows(w_ref, u)
        half = weight.shape[0] // 2
        weight = weight[half:]
        feats = features(weight, k_all)
        suffix = sx_ref[u]
        norm = column(norm_all[place(step, u), :], BLK)
        dlog = feature_back(feats, dk_ref[u] + nn(suffix, vt_all[...]) + norm)
        at = pl.ds(pl.multiple_of((step * PAIR + u) * half, half), half)
        logs[at, :] = dlog
        all_weights[at, :] = weight
        maps.append(nn(dlog, k_all))
        total[...] += nn(turned(suffix), feats.astype(BF16))
    gm_ref[0] = jnp.concatenate(maps, axis=0).T.astype(gm_ref.dtype)

    @pl.when(step == pl.num_programs(0) - 1)
    def _():
        pair = jnp.concatenate([nn(turned(logs[...]), all_weights[...]), total[...].T], axis=1)
        out[...] = pair.astype(out.dtype).reshape(out.shape)


def total_kernel(table, *refs):
    for h in range(refs[-1].shape[0]):
        refs[-1][h] = sum(ref[h].astype(F32) for ref in refs[:-1]).astype(BF16)


def prefix_kernel(others, total_weight, table, *refs):
    totals, (before_ref, state_ref, out) = refs[:others], refs[others:]
    for h in range(out.shape[0]):
        state = state_ref[h].astype(F32) + before_ref[h]
        for i, ref in enumerate(totals):
            state = state + table[total_weight + i].astype(F32) * ref[h].astype(F32)
        out[h] = state.astype(BF16)


def suffix_kernel(grp, others, block_weight, total_weight, at, table, *refs):
    parts, totals, refs = refs[:grp], refs[grp : grp + others], refs[grp + others :]
    outs, grad, scratch = refs[:grp], refs[grp], refs[grp + 1]
    rows = grad.shape[1]
    for h in range(parts[0].shape[0]):
        states = [ref[h].astype(F32) for ref in parts]
        others_state = [ref[h].astype(F32) for ref in totals]
        scratch[...] = sum(states) + sum(others_state)
        grad[h] = scratch[pl.ds(pl.multiple_of(table[at] * rows, rows), rows), :]
        base = jnp.zeros_like(states[0])
        for i, state in enumerate(others_state):
            base = base + table[total_weight + i].astype(F32) * state
        for r, out in enumerate(outs):
            state = base
            for i in range(grp):
                if i != r:
                    state = state + table[block_weight + r * grp + i].astype(F32) * states[i]
            out[h] = state.astype(BF16)


def close_kernel(pairs, singles, at, table, q_ref, k_ref, *refs):
    both, q_parts, k_parts = (
        refs[:pairs],
        refs[pairs : pairs + singles],
        refs[pairs + singles : pairs + 2 * singles],
    )
    for i, (own, parts, out) in enumerate(
        ((q_ref, q_parts, refs[-2]), (k_ref, k_parts, refs[-1]))
    ):
        rows, half = out.shape[1:]
        mine = pl.ds(pl.multiple_of(table[at] * rows, rows), rows)
        for h in range(own.shape[0]):
            total = own[h, mine, :].astype(F32)
            for ref in both:
                total = total + ref[i, h].astype(F32)
            for ref in parts:
                total = total + ref[h].astype(F32)
            for u in range(PAIR):
                out[h * PAIR + u] = total[:, u * half : (u + 1) * half]


def whole_call(kernel, outs, table, arrays, name, scratch=()):
    return pl.pallas_call(
        kernel,
        out_shape=outs,
        in_specs=[pl.BlockSpec(memory_space=SMEM)]
        + [pl.BlockSpec(memory_space=pltpu.VMEM)] * len(arrays),
        out_specs=[pl.BlockSpec(memory_space=pltpu.VMEM)] * len(outs),
        scratch_shapes=list(scratch),
        compiler_params=pltpu.CompilerParams(vmem_limit_bytes=LIMIT),
        cost_estimate=LITTLE,
        name=name,
    )(table, *arrays)


def after(value, *others):
    return lax.optimization_barrier((value, *others))[0]


def shards(
    query_rows, key_rows, value_rows, grad_out, query_map, key_map, prefix_state, prefix_norm
):
    ctx, fsdp = lax.axis_size("ctx"), lax.axis_size("fsdp")
    tok = query_rows.shape[0]
    heads, map_rows, half = query_map.shape
    hd = map_rows * fsdp
    kv_heads = key_rows.shape[1] // hd
    replicas = ctx // kv_heads
    part = BLK // tok
    grp = ctx // part
    mine = lax.axis_index("ctx")
    block, seq = mine // part, lax.axis_index("fsdp")
    slots = range(grp)
    order = list(reversed(slots))
    grid = (heads // PAIR,)

    blocks_of = [[g * part + p for p in range(part)] for g in slots]

    def within(array):
        return lax.all_to_all(array, "ctx", 0, 0, axis_index_groups=blocks_of, tiled=True)

    def across(array, shift):
        return lax.ppermute(array, "ctx", [(d, (d + shift * part) % ctx) for d in range(ctx)])

    def along(array, shift):
        return lax.ppermute(array, "fsdp", [(d, (d + shift) % fsdp) for d in range(fsdp)])

    def apart(array, s, r):
        moves = [
            (d * fsdp + i, (d + s * part) % ctx * fsdp + (i + r) % fsdp)
            for d in range(ctx)
            for i in range(fsdp)
        ]
        return lax.ppermute(array, ("ctx", "fsdp"), moves)

    def both_halves(array):
        return jnp.stack([array] + [across(array, s) for s in slots[1:]])

    def ints(values):
        return jnp.stack([jnp.asarray(v, jnp.int32) for v in values])

    slot = [(block + s) % grp for s in slots]
    owner = [slot[s] * part + p for s in slots for p in range(part)]
    here = seq * grp + block
    places = [i * grp + (block - r) % grp for i in range(fsdp) for r in slots]
    near = [(block - r) % grp for r in slots]
    far = [(seq - r) % fsdp for r in range(1, fsdp)]
    lists = {
        "slot": slot,
        "block": [block],
        "seq": [seq],
        "owner": owner,
        "kv": [
            ((g + s) % grp * part + p) // replicas
            for s in slots
            for g in slots
            for p in range(part)
        ],
        "places after": [other > here for other in places],
        "before": [g < block for g in slots],
        "seq before": [i < seq for i in range(fsdp)],
        "near after": [b > a for a in near for b in near],
        "far before": [other < seq for other in far],
        "far after": [other > seq for other in far],
    }
    base, values = {}, []
    for name, entries in lists.items():
        base[name] = len(values)
        values += entries
    table = ints(values)

    own_maps = jnp.concatenate((query_map, key_map), axis=-1)
    maps = jnp.stack([own_maps] + [across(own_maps, -s) for s in slots[1:]])
    kv = pack(
        after(table, maps), base["kv"], (key_rows, value_rows), ctx, grp, hd
    )
    kv = lax.all_to_all(kv, "ctx", 0, 0, tiled=True)
    maps = lax.all_gather(maps, "fsdp")
    prefix_states = [prefix_state] + [
        across(prefix_state.astype(BF16), -s) for s in slots[1:]
    ]
    prefix_norms = [prefix_norm] + [across(prefix_norm, -s) for s in slots[1:]]

    params = pltpu.CompilerParams(
        dimension_semantics=("arbitrary",), vmem_limit_bytes=LIMIT
    )
    anywhere = pl.BlockSpec(memory_space=pl.ANY)

    def piece_spec(column, count):
        return pl.BlockSpec((part, tok, count * hd), lambda h, t: (0, 0, column(h)))

    def head_spec(*shape):
        return pl.BlockSpec((PAIR, *shape), lambda h, t: (h,) + (0,) * len(shape))

    def fixed_spec(*shape):
        return pl.BlockSpec(shape, lambda h, t: (0,) * len(shape))

    def of(dtype, *shape):
        return jax.ShapeDtypeStruct(shape, dtype)

    def k_spec(s):
        return pl.BlockSpec((part, tok, hd), lambda h, t: (t[base["block"]], 0, 2 * s))

    def v_spec(s):
        return pl.BlockSpec((part, tok, hd), lambda h, t: (t[base["block"]], 0, 2 * s + 1))

    def all_spec(column):
        return pl.BlockSpec((ctx, tok, hd), lambda h, t: (0, 0, column))

    def map_spec(s):
        return pl.BlockSpec((fsdp, None, PAIR, map_rows, 2 * half), lambda h, t: (0, s, h, 0, 0))

    q_spec, g_spec = piece_spec(lambda h: h, PAIR), piece_spec(lambda h: grid[0] + h, PAIR)
    state_spec, state_shape = head_spec(hd, hd), of(BF16, heads, hd, hd)
    row_spec, row_shape = fixed_spec(heads, hd), of(F32, heads, hd)
    wide_spec, wide_shape = head_spec(2 * half, BLK), of(F32, heads, 2 * half, BLK)
    gm_spec = pl.BlockSpec((1, hd, PAIR * half), lambda h, t: (h, 0, 0))
    gm_shape = of(BF16, heads // PAIR, hd, PAIR * half)
    dv_spec, dv_shape = fixed_spec(hd, BLK), of(F32, hd, BLK)
    count = tiles_of(BLK // TILE - 1)[-1] + 1
    unit = 2 * heads * BLK * hd

    def call(kernel, s, outs, specs, out_specs, arrays, scratch, name, flops, alias=()):
        return pl.pallas_call(
            kernel,
            out_shape=outs,
            grid_spec=pltpu.PrefetchScalarGridSpec(
                num_scalar_prefetch=1,
                grid=grid,
                in_specs=specs,
                out_specs=out_specs,
                scratch_shapes=scratch,
            ),
            compiler_params=params,
            cost_estimate=LITTLE,
            input_output_aliases=dict(alias),
            name=name,
        )(table, *arrays)

    def totals_of(partial, sent=()):
        sent = dict(sent)
        parts = [partial[0]] + [
            sent[s] if s in sent else across(partial[s], s) for s in slots[1:]
        ]
        return parts, whole_call(total_kernel, [state_shape], table, parts, "totals")[0]

    def prefix_of(s, total, before):
        others = [along(total, r) for r in range(1, fsdp)]
        return whole_call(
            functools.partial(prefix_kernel, fsdp - 1, base["far before"]),
            [state_shape],
            table,
            [*others, before, prefix_states[s]],
            "prefix",
        )[0]

    def suffixes_of(parts, total):
        others = [along(total, r) for r in range(1, fsdp)]
        weights = [base["near after"], base["far after"], base["seq"]]
        result = whole_call(
            functools.partial(suffix_kernel, grp, fsdp - 1, *weights),
            [state_shape] * grp + [of(F32, heads, map_rows, hd)],
            table,
            parts + others,
            "suffix",
            [pltpu.VMEM((hd, hd), F32)],
        )
        return [result[0]] + [across(result[s], -s) for s in slots[1:]], result[grp]

    def sent_rows(s, *earlier):
        packed = pack(
            after(table, *earlier),
            base["owner"] + s * part,
            (query_rows, grad_out),
            part,
            1,
            heads * hd,
        )
        return within(packed)

    first, others = order[0], order[1:]
    rows = {first: sent_rows(first, kv)}
    partial = {}
    for s in order:
        partial[s] = call(
            functools.partial(state_kernel, base["before"]),
            s,
            [state_shape, of(F32, heads, hd, hd), row_shape, row_shape],
            [all_spec(2 * s), all_spec(2 * s + 1), map_spec(s)],
            [state_spec, head_spec(hd, hd), row_spec, row_spec],
            [kv, kv, maps],
            [],
            "states",
            unit * 2 * hd,
        )
    norms = lax.all_gather(jnp.stack([partial[s][2] for s in slots]), "fsdp")
    state = {s: prefix_of(s, after(partial[s][0], norms), partial[s][1]) for s in order}
    for s in others:
        rows[s] = sent_rows(s, norms)

    def front_of(s, norms):
        return call(
            functools.partial(front_kernel, base["seq before"], s),
            s,
            [
                wide_shape,
                of(BF16, heads, 2 * half, BLK),
                of(F32, heads, hd, BLK),
                of(BF16, heads, count, TILE, TILE),
                of(F32, heads, BLK),
                row_shape,
                state_shape,
            ],
            [k_spec(s), q_spec, g_spec, map_spec(s), fixed_spec(*norms.shape), row_spec, row_spec],
            [
                wide_spec,
                wide_spec,
                wide_spec,
                head_spec(count, TILE, TILE),
                fixed_spec(heads, BLK),
                row_spec,
                state_spec,
            ],
            [kv, rows[s], rows[s], maps, norms, partial[s][3], prefix_norms[s]],
            [],
            "front",
            unit * 3 * BLK,
        )

    def back_of(s):
        return call(
            back_kernel,
            s,
            [of(BF16, part, tok, heads * hd), wide_shape, dv_shape, row_shape, gm_shape],
            [
                k_spec(s),
                v_spec(s),
                q_spec,
                map_spec(s),
                wide_spec,
                wide_spec,
                wide_spec,
                head_spec(count, TILE, TILE),
                fixed_spec(heads, BLK),
                row_spec,
                state_spec,
            ],
            [q_spec, wide_spec, dv_spec, row_spec, gm_spec],
            [kv, kv, rows[s], maps, *fronts[s][:6], state[s]],
            [pltpu.VMEM((hd, BLK), BF16)],
            "back",
            unit * 6 * BLK,
        )

    def rows_for(array, device):
        pieces = array.reshape(*array.shape[:-2], fsdp, map_rows, array.shape[-1])
        return lax.dynamic_index_in_dim(pieces, device % fsdp, array.ndim - 2, keepdims=False)

    fronts, backs, sent, returned, q_maps = {}, {}, {}, {}, []
    for s in order:
        fronts[s] = front_of(s, after(norms, *q_maps))
        if s:
            sent[s] = across(fronts[s][6], s)
            backs[s] = back_of(s)
            q_maps += [apart(rows_for(backs[s][4], seq + r), s, r) for r in range(fsdp)]
    parts, total = totals_of({s: fronts[s][6] for s in slots}, sent)
    state[0] = after(state[0], total)
    backs[0] = back_of(0)
    parts[0] = after(parts[0], backs[0][3])
    suffix, grad_prefix = suffixes_of(parts, total)
    for s in order:
        returned[s] = within(after(backs[s][0], total if s else suffix[0]))
    suffix_norms = jnp.concatenate([backs[s][3] for s in slots], axis=0)
    suffix_norms = both_halves(suffix_norms)
    suffix_norms = lax.all_gather(suffix_norms, "fsdp")

    kv_type = BF16 if replicas == 1 else F32
    pairs = jnp.zeros((part, tok, grp * 2 * hd), kv_type)
    k_maps, both_maps, key_gm = [], [], {}
    for s in slots:
        if s:
            suffix[s] = after(suffix[s], *both_maps)
        pairs, key_gm[s] = call(
            functools.partial(key_kernel, (s, base["block"], base["places after"])),
            s,
            [of(kv_type, *pairs.shape), gm_shape],
            [k_spec(s), v_spec(s), map_spec(s), state_spec, wide_spec, dv_spec]
            + [fixed_spec(*suffix_norms.shape), anywhere],
            [piece_spec(lambda h: s, 2), gm_spec],
            [kv, kv, maps, suffix[s], backs[s][1], backs[s][2], suffix_norms, pairs],
            [
                pltpu.VMEM((hd, BLK), BF16),
                pltpu.VMEM((hd, BLK), F32),
                pltpu.VMEM((heads * half, BLK), BF16),
                pltpu.VMEM((heads * half, hd), BF16),
                pltpu.VMEM((heads, hd), F32),
            ],
            "keys",
            unit * 4 * hd,
            {8: 0},
        )
        if s == 0:
            two = jnp.stack([backs[s][4], key_gm[s]])
            both_maps = [along(rows_for(two, seq + r), r) for r in range(1, fsdp)]
        else:
            k_maps += [apart(rows_for(key_gm[s], seq + r), s, r) for r in range(fsdp)]

    pairs = after(pairs, *returned.values())
    pairs = within(pairs)
    (grad_queries,) = unpack(table, base["owner"], [returned[s] for s in slots], 1, heads * hd)
    pairs = [pairs[:, :, s * 2 * hd : (s + 1) * 2 * hd] for s in slots]
    grad_keys, grad_values = unpack(table, base["owner"], pairs, 2, hd)
    if replicas > 1:
        grad_keys, grad_values = (
            jnp.sum(a.reshape(tok, kv_heads, replicas, hd), axis=2)
            .astype(BF16)
            .reshape(tok, kv_heads * hd)
            for a in (grad_keys, grad_values)
        )
    query_map_grad, key_map_grad = whole_call(
        functools.partial(close_kernel, len(both_maps), len(q_maps), base["seq"]),
        [of(F32, heads, map_rows, half)] * 2,
        table,
        [backs[0][4], key_gm[0]] + both_maps + q_maps + k_maps,
        "close",
    )
    return grad_queries, grad_keys, grad_values, query_map_grad, key_map_grad, grad_prefix


def solution(mesh):
    rows, maps = P(("fsdp", "ctx"), None), P("ctx", "fsdp", None)
    return jax.shard_map(
        shards,
        mesh=mesh,
        in_specs=(rows,) * 4 + (maps, maps, P("ctx", None, None), P("ctx", None)),
        out_specs=(rows,) * 3 + (maps,) * 3,
        check_vma=False,
    )
```

```python
import functools

import jax
import jax.numpy as jnp
from jax import lax
from jax.experimental import pallas as pl
from jax.experimental.pallas import tpu as pltpu
from jax.sharding import PartitionSpec as P

BLK = 512
TILE = 256
PAIR = 2
EXT = 16
LIMIT = 40 * 1024 * 1024

LITTLE = pl.CostEstimate(flops=1000, bytes_accessed=1000, transcendentals=0)

F32 = jnp.float32
BF16 = jnp.bfloat16
SMEM = pltpu.SMEM


def nn(left, right):
    return lax.dot_general(left, right, (((1,), (0,)), ((), ())), preferred_element_type=F32)


def nt(left, right):
    return lax.dot_general(left, right, (((1,), (1,)), ((), ())), preferred_element_type=F32)


def turned(array):
    return array.astype(F32).T.astype(array.dtype)


def column(row, width):
    n = row.shape[1]
    square = jnp.broadcast_to(row, (n, n)).T
    return jnp.concatenate([square] * (width // n), axis=1)


def thirds(row):
    rows = jnp.broadcast_to(row, (EXT, row.shape[1]))
    high = rows.astype(BF16).astype(F32)
    middle = (rows - high).astype(BF16).astype(F32)
    low = rows - high - middle
    place = lax.broadcasted_iota(jnp.int32, rows.shape, 0)
    picked = jnp.where(place == 0, high, jnp.where(place == 1, middle, low))
    return jnp.where(place < 3, picked, 0.0).astype(BF16)


def whole_row(block):
    return jnp.sum(block.astype(F32), axis=0, keepdims=True)


def weight_rows(ref, u):
    whole = jnp.concatenate([ref[i, u] for i in range(ref.shape[0])], axis=0)
    return turned(whole)


def features(weight, rows):
    logits = nt(weight, rows).astype(BF16).astype(F32)
    upper = jnp.exp(logits)
    lower = jnp.exp(-logits)
    upper = upper * (1.0 / jnp.sum(upper, axis=0, keepdims=True))
    lower = lower * (1.0 / jnp.sum(lower, axis=0, keepdims=True))
    return jnp.concatenate([upper, lower], axis=0)


def feature_back(feats, upstream):
    half = feats.shape[0] // 2
    weighted = feats * upstream
    first, second = weighted[:half], weighted[half:]
    first = first - feats[:half] * jnp.sum(first, axis=0, keepdims=True)
    second = second - feats[half:] * jnp.sum(second, axis=0, keepdims=True)
    return (first - second).astype(BF16)


def gather(table, base, refs, out):
    rows = refs[0].shape[0]
    for r, ref in enumerate(refs):
        out[pl.ds(pl.multiple_of(table[base + r] * rows, rows), rows), :] = ref[...]


def pack_kernel(columns, inputs, table, *refs):
    count = columns * inputs
    for r, out in enumerate(refs[-(len(refs) // (count + 1)) :]):
        width = out.shape[1] // count
        for i in range(count):
            out[:, i * width : (i + 1) * width] = refs[r * count + i][...]


def pack(table, base, sources, pieces, columns, width):
    rows = sources[0].shape[0]
    count = columns * len(sources)
    step = rows // 2

    def take(at):
        return pl.BlockSpec((step, width), lambda i, t: (i, t[base + at]))

    return pl.pallas_call(
        functools.partial(pack_kernel, columns, len(sources)),
        out_shape=[jax.ShapeDtypeStruct((rows, count * width), sources[0].dtype)] * pieces,
        grid_spec=pltpu.PrefetchScalarGridSpec(
            num_scalar_prefetch=1,
            grid=(rows // step,),
            in_specs=[
                take(r * columns + s)
                for r in range(pieces)
                for s in range(columns)
                for _ in sources
            ],
            out_specs=[pl.BlockSpec((step, count * width), lambda i, t: (i, 0))] * pieces,
        ),
        compiler_params=pltpu.CompilerParams(vmem_limit_bytes=LIMIT),
        cost_estimate=LITTLE,
        name="pack",
    )(table, *(list(sources) * (pieces * columns)))


def unpack_kernel(outputs, base, table, *refs):
    sources, outs = refs[:-outputs], refs[-outputs:]
    for s, source in enumerate(sources):
        pieces = source.shape[0]
        width = source.shape[2] // outputs
        for r in range(pieces):
            at = pl.ds(pl.multiple_of(table[base + s * pieces + r] * width, width), width)
            for i, out in enumerate(outs):
                out[:, at] = source[r, :, i * width : (i + 1) * width]


def unpack(table, base, sources, outputs, width):
    pieces, rows = sources[0].shape[:2]
    total = len(sources) * pieces * width
    step = rows // 2
    return pl.pallas_call(
        functools.partial(unpack_kernel, outputs, base),
        out_shape=[jax.ShapeDtypeStruct((rows, total), sources[0].dtype)] * outputs,
        grid=(rows // step,),
        in_specs=[pl.BlockSpec(memory_space=SMEM)]
        + [pl.BlockSpec((pieces, step, outputs * width), lambda i: (0, i, 0))] * len(sources),
        out_specs=[pl.BlockSpec((step, total), lambda i: (i, 0))] * outputs,
        compiler_params=pltpu.CompilerParams(vmem_limit_bytes=LIMIT),
        cost_estimate=LITTLE,
        name="unpack",
    )(table, *sources)


def state_kernel(part, base, table, *refs):
    k_refs, v_refs, (w_ref, out, k_all, v_all) = refs[:part], refs[part : 2 * part], refs[2 * part :]
    hd = k_all.shape[1]

    @pl.when(pl.program_id(0) == 0)
    def _():
        gather(table, base, k_refs, k_all)
        gather(table, base, v_refs, v_all)

    for u in range(out.shape[0]):
        weight = weight_rows(w_ref, u)
        feats = features(weight[weight.shape[0] // 2 :], k_all[...]).astype(BF16)
        out[u, :hd, :] = nn(feats, v_all[...]).astype(BF16)
        ones = jnp.ones((EXT, feats.shape[1]), BF16)
        out[u, hd:, :] = thirds(nt(ones, feats)[:1])


def block_kernel(part, base, table, *refs):
    k_refs, v_refs = refs[:part], refs[part : 2 * part]
    q_refs, g_refs = refs[2 * part : 3 * part], refs[3 * part : 4 * part]
    w_ref, st_ref = refs[4 * part : 4 * part + 2]
    gq_ref, dk_ref, dv_ref, sx_ref, gm_ref, k_all, v_all, vt_all, q_all, g_all = refs[4 * part + 2 :]
    hd = k_all.shape[1]

    @pl.when(pl.program_id(0) == 0)
    def _():
        gather(table, base, k_refs, k_all)
        gather(table, base, v_refs, v_all)
        vt_all[...] = turned(v_all[...])
        dv_ref[...] = jnp.zeros_like(dv_ref)

    gather(table, base, q_refs, q_all)
    gather(table, base, g_refs, g_all)
    maps = []
    earlier = lax.broadcasted_iota(jnp.int32, (TILE, TILE), 0) <= lax.broadcasted_iota(
        jnp.int32, (TILE, TILE), 1
    )

    def causal(array, begin):
        masked = jnp.where(earlier, array[begin:], 0.0)
        return masked if begin == 0 else jnp.concatenate([array[:begin], masked], axis=0)

    for u in range(PAIR):
        weight = weight_rows(w_ref, u)
        half = weight.shape[0] // 2
        lanes = slice(u * hd, (u + 1) * hd)
        q_feat = features(weight[:half], q_all[:, lanes])
        k_low = features(weight[half:], k_all[...]).astype(BF16)
        q_low = q_feat.astype(BF16)
        k_turned = turned(k_low)
        state = st_ref[u, :hd, :]
        state_turned = turned(state)
        norm = column(whole_row(st_ref[u, hd:, :]), TILE)
        g_turned = g_all[:, lanes].astype(F32).T
        back = []
        dkey = [jnp.zeros((2 * half, TILE), F32) for _ in range(BLK // TILE)]
        dvalue = [jnp.zeros((hd, TILE), F32) for _ in range(BLK // TILE)]
        suffix = jnp.zeros((2 * half, hd), F32)
        suffix_norm = jnp.zeros((2 * half, 1), F32)
        for j in range(BLK // TILE):
            begin, end = j * TILE, (j + 1) * TILE
            own = q_low[:, begin:end]
            own_wide = own.astype(F32)
            scores = causal(nn(k_turned[:end], own), begin)
            scores_low = scores.astype(BF16)
            numerator = nn(state_turned, own) + nn(vt_all[:, :end], scores_low)
            denominator = jnp.sum(own_wide * norm, axis=0, keepdims=True) + jnp.sum(
                scores, axis=0, keepdims=True
            )
            inverse = 1.0 / denominator
            scaled = g_turned[:, begin:end] * inverse
            scaled_low = scaled.astype(BF16)
            norm_grad = -jnp.sum(scaled * (numerator * inverse), axis=0, keepdims=True)
            dscores = causal(nn(v_all[:end, :], scaled_low) + norm_grad, begin).astype(BF16)
            dquery = nn(state, scaled_low) + norm * norm_grad + nn(k_low[:, :end], dscores)
            back.append(feature_back(q_feat[:, begin:end], dquery))
            for i in range(j + 1):
                rows = slice(i * TILE, (i + 1) * TILE)
                dkey[i] = dkey[i] + nt(own, dscores[rows])
                dvalue[i] = dvalue[i] + nt(scaled_low, scores_low[rows])
            suffix = suffix + nt(own, scaled_low)
            suffix_norm = suffix_norm + jnp.sum(own_wide * norm_grad, axis=1, keepdims=True)
        dlog = jnp.concatenate(back, axis=1)
        grads = nn(turned(dlog), weight[:half]).astype(BF16)
        gq_ref[:, :, lanes] = grads.reshape(gq_ref.shape[0], -1, hd)
        maps.append(nn(dlog, q_all[:, lanes]))
        dk_ref[u] = jnp.concatenate(dkey, axis=1)
        dv_ref[...] += jnp.concatenate(dvalue, axis=1)
        sx_ref[u, :hd, :] = suffix.astype(BF16)
        sx_ref[u, hd:, :] = thirds(jnp.broadcast_to(suffix_norm, (2 * half, 2 * half)).T[:1])
    gm_ref[0] = jnp.concatenate(maps, axis=0).T.astype(gm_ref.dtype)


def key_kernel(part, base, table, *refs):
    k_refs, v_refs = refs[:part], refs[part : 2 * part]
    w_ref, sx_ref, dk_ref, dv_ref = refs[2 * part : 2 * part + 4]
    out, gm_ref, k_all, v_all, vt_all, total, logs, weights = refs[2 * part + 5 :]
    hd = k_all.shape[1]
    step = pl.program_id(0)

    @pl.when(step == 0)
    def _():
        gather(table, base, k_refs, k_all)
        gather(table, base, v_refs, v_all)
        vt_all[...] = turned(v_all[...])
        total[...] = dv_ref[...]

    maps = []
    for u in range(PAIR):
        weight = weight_rows(w_ref, u)
        half = weight.shape[0] // 2
        weight = weight[half:]
        feats = features(weight, k_all[...])
        suffix = sx_ref[u, :hd, :]
        norm = column(whole_row(sx_ref[u, hd:, :]), BLK)
        dlog = feature_back(feats, dk_ref[u] + nn(suffix, vt_all[...]) + norm)
        at = pl.ds(pl.multiple_of((step * PAIR + u) * half, half), half)
        logs[at, :] = dlog
        weights[at, :] = weight
        maps.append(nn(dlog, k_all[...]))
        total[...] += nn(turned(suffix), feats.astype(BF16))
    gm_ref[0] = jnp.concatenate(maps, axis=0).T.astype(gm_ref.dtype)

    @pl.when(step == pl.num_programs(0) - 1)
    def _():
        pair = jnp.concatenate([nn(turned(logs[...]), weights[...]), total[...].T], axis=1)
        out[...] = pair.astype(out.dtype).reshape(out.shape)


def total_kernel(table, *refs):
    out = refs[-1]
    heads, hd = out.shape[0], out.shape[2]
    for h in range(heads):
        out[h, :hd, :] = sum(ref[h, :hd, :].astype(F32) for ref in refs[:-1]).astype(BF16)
        out[h, hd:, :] = thirds(sum(whole_row(ref[h, hd:, :]) for ref in refs[:-1]))


def spread_kernel(grp, others, closing, block_weight, total_weight, at, table, *refs):
    parts, totals, refs = refs[:grp], refs[grp : grp + others], refs[grp + others :]
    if closing:
        outs, grad, scratch = refs[:grp], refs[grp], refs[grp + 1]
    else:
        state_ref, norm_ref, outs = refs[0], refs[1], refs[2:]
    heads, hd = parts[0].shape[0], parts[0].shape[2]
    for h in range(heads):
        states = [ref[h, :hd, :].astype(F32) for ref in parts]
        norms = [whole_row(ref[h, hd:, :]) for ref in parts]
        others_state = [ref[h, :hd, :].astype(F32) for ref in totals]
        others_norm = [whole_row(ref[h, hd:, :]) for ref in totals]
        if closing:
            base, base_norm = jnp.zeros_like(states[0]), jnp.zeros_like(norms[0])
            scratch[...] = sum(states) + sum(others_state)
            rows = grad.shape[1]
            grad[h] = scratch[pl.ds(pl.multiple_of(table[at] * rows, rows), rows), :]
        else:
            base, base_norm = state_ref[h], norm_ref[pl.ds(h, 1), :]
        for i, (state, norm) in enumerate(zip(others_state, others_norm)):
            base = base + table[total_weight + i].astype(F32) * state
            base_norm = base_norm + table[total_weight + i].astype(F32) * norm
        for r, out in enumerate(outs):
            state, norm = base, base_norm
            for i in range(grp):
                if i != r:
                    state = state + table[block_weight + r * grp + i].astype(F32) * states[i]
                    norm = norm + table[block_weight + r * grp + i].astype(F32) * norms[i]
            out[h, :hd, :] = state.astype(BF16)
            out[h, hd:, :] = thirds(norm)


def close_kernel(pairs, singles, at, table, q_ref, k_ref, *refs):
    both, q_parts, k_parts = (
        refs[:pairs],
        refs[pairs : pairs + singles],
        refs[pairs + singles : pairs + 2 * singles],
    )
    for i, (own, parts, out) in enumerate(
        ((q_ref, q_parts, refs[-2]), (k_ref, k_parts, refs[-1]))
    ):
        rows, half = out.shape[1:]
        mine = pl.ds(pl.multiple_of(table[at] * rows, rows), rows)
        for h in range(own.shape[0]):
            total = own[h, mine, :].astype(F32)
            for ref in both:
                total = total + ref[i, h].astype(F32)
            for ref in parts:
                total = total + ref[h].astype(F32)
            for u in range(PAIR):
                out[h * PAIR + u] = total[:, u * half : (u + 1) * half]


def whole_call(kernel, outs, table, arrays, name, scratch=()):
    return pl.pallas_call(
        kernel,
        out_shape=outs,
        in_specs=[pl.BlockSpec(memory_space=SMEM)]
        + [pl.BlockSpec(memory_space=pltpu.VMEM)] * len(arrays),
        out_specs=[pl.BlockSpec(memory_space=pltpu.VMEM)] * len(outs),
        scratch_shapes=list(scratch),
        compiler_params=pltpu.CompilerParams(vmem_limit_bytes=LIMIT),
        cost_estimate=LITTLE,
        name=name,
    )(table, *arrays)


def after(value, *others):
    return lax.optimization_barrier((value, *others))[0]


def shards(
    query_rows, key_rows, value_rows, grad_out, query_map, key_map, prefix_state, prefix_norm
):
    ctx, fsdp = lax.axis_size("ctx"), lax.axis_size("fsdp")
    tok = query_rows.shape[0]
    heads, map_rows, half = query_map.shape
    hd = map_rows * fsdp
    kv_heads = key_rows.shape[1] // hd
    replicas = ctx // kv_heads
    part = BLK // tok
    grp = ctx // part
    mine = lax.axis_index("ctx")
    at, block, seq = mine % part, mine // part, lax.axis_index("fsdp")
    shifts, slots = range(part), range(grp)
    order = list(reversed(slots))
    grid = (heads // PAIR,)
    blocks_of = [[g * part + p for p in range(part)] for g in slots]

    def within(array):
        return lax.all_to_all(array, "ctx", 0, 0, axis_index_groups=blocks_of, tiled=True)

    def around(array, shift):
        return lax.ppermute(
            array, "ctx", [(d, d // part * part + (d + shift) % part) for d in range(ctx)]
        )

    def across(array, shift):
        return lax.ppermute(array, "ctx", [(d, (d + shift * part) % ctx) for d in range(ctx)])

    def along(array, shift):
        return lax.ppermute(array, "fsdp", [(d, (d + shift) % fsdp) for d in range(fsdp)])

    def apart(array, s, r):
        moves = [
            (d * fsdp + i, (d + s * part) % ctx * fsdp + (i + r) % fsdp)
            for d in range(ctx)
            for i in range(fsdp)
        ]
        return lax.ppermute(array, ("ctx", "fsdp"), moves)

    slot = [(block + s) % grp for s in slots]
    near = [(block - r) % grp for r in slots]
    far = [(seq - r) % fsdp for r in range(1, fsdp)]
    lists = {
        "seq": [seq],
        "owner": [slot[s] * part + p for s in slots for p in range(part)],
        "sent": [slot[s] * part + (at + r) % part for s in slots for r in shifts],
        "kv": [
            (slot[s] * part + (at + r) % part) // replicas for r in shifts for s in slots
        ],
        "sorted": [(at - r) % part for r in shifts],
        "near before": [b < a for a in near for b in near],
        "near after": [b > a for a in near for b in near],
        "far before": [other < seq for other in far],
        "far after": [other > seq for other in far],
    }
    base, values = {}, []
    for name, entries in lists.items():
        base[name] = len(values)
        values += entries
    table = jnp.stack([jnp.asarray(v, jnp.int32) for v in values])

    own_maps = jnp.concatenate((query_map, key_map), axis=-1)
    maps = jnp.stack([own_maps] + [across(own_maps, -s) for s in slots[1:]])
    kv_sent = pack(table, base["kv"], (key_rows, value_rows), part, grp, hd)
    kv = [kv_sent[0]] + [around(kv_sent[r], r) for r in shifts[1:]]
    maps = lax.all_gather(maps, "fsdp")

    rows = {}
    for s in order:
        sent = pack(
            after(table, maps),
            base["sent"] + s * part,
            (query_rows, grad_out),
            part,
            1,
            heads * hd,
        )
        rows[s] = [sent[0]] + [around(sent[r], r) for r in shifts[1:]]

    params = pltpu.CompilerParams(
        dimension_semantics=("arbitrary",), vmem_limit_bytes=LIMIT
    )

    def piece_specs(column, count):
        return [pl.BlockSpec((tok, count * hd), lambda h, t: (0, column(h)))] * part

    def kv_specs(s):
        return piece_specs(lambda h: 2 * s, 1) + piece_specs(lambda h: 2 * s + 1, 1)

    def map_spec(s):
        return pl.BlockSpec((fsdp, None, PAIR, map_rows, 2 * half), lambda h, t: (0, s, h, 0, 0))

    def head_spec(*shape):
        return pl.BlockSpec((PAIR, *shape), lambda h, t: (h,) + (0,) * len(shape))

    def of(dtype, *shape):
        return jax.ShapeDtypeStruct(shape, dtype)

    ext_spec, ext_shape = head_spec(hd + EXT, hd), of(BF16, heads, hd + EXT, hd)
    gm_spec = pl.BlockSpec((1, hd, PAIR * half), lambda h, t: (h, 0, 0))
    gm_shape = of(BF16, heads // PAIR, hd, PAIR * half)
    dk_spec, dk_shape = head_spec(2 * half, BLK), of(F32, heads, 2 * half, BLK)
    dv_spec, dv_shape = pl.BlockSpec((hd, BLK), lambda h, t: (0, 0)), of(F32, hd, BLK)
    low, wide = pltpu.VMEM((BLK, hd), BF16), pltpu.VMEM((BLK, PAIR * hd), BF16)

    def call(kernel, outs, specs, out_specs, arrays, scratch, name, alias=()):
        return pl.pallas_call(
            functools.partial(kernel, part, base["sorted"]),
            out_shape=outs,
            grid_spec=pltpu.PrefetchScalarGridSpec(
                num_scalar_prefetch=1,
                grid=grid,
                in_specs=specs,
                out_specs=out_specs,
                scratch_shapes=scratch,
            ),
            compiler_params=params,
            cost_estimate=LITTLE,
            input_output_aliases=dict(alias),
            name=name,
        )(table, *arrays)

    def states_of(s):
        return call(
            state_kernel,
            [ext_shape],
            kv_specs(s) + [map_spec(s)],
            [ext_spec],
            [*kv, *kv, maps],
            [low, low],
            "states",
        )[0]

    def spread(parts, total, when, extra, closing):
        others = [along(total, r) for r in range(1, fsdp)]
        weights = [base["near " + when], base["far " + when], base["seq"]]
        result = whole_call(
            functools.partial(spread_kernel, grp, fsdp - 1, closing, *weights),
            [ext_shape] * grp + [of(F32, heads, map_rows, hd)] * closing,
            table,
            parts + others + extra,
            "spread",
            [pltpu.VMEM((hd, hd), F32)] * closing,
        )
        return [result[0]] + [across(result[s], -s) for s in slots[1:]], result[grp:]

    def totals_of(parts):
        return whole_call(total_kernel, [ext_shape], table, parts, "totals")[0]

    partial = {s: states_of(s) for s in order}
    parts = [after(partial[0], *rows[order[0]])] + [across(partial[s], s) for s in slots[1:]]
    state, _ = spread(parts, totals_of(parts), "before", [prefix_state, prefix_norm], False)

    def block_of(s):
        return call(
            block_kernel,
            [of(BF16, part, tok, heads * hd), dk_shape, dv_shape, ext_shape, gm_shape],
            kv_specs(s)
            + piece_specs(lambda h: h, PAIR)
            + piece_specs(lambda h: grid[0] + h, PAIR)
            + [map_spec(s), ext_spec],
            [
                pl.BlockSpec((part, tok, PAIR * hd), lambda h, t: (0, 0, h)),
                dk_spec,
                dv_spec,
                ext_spec,
                gm_spec,
            ],
            [*kv, *kv, *rows[s], *rows[s], maps, state[s]],
            [low, low, pltpu.VMEM((hd, BLK), BF16), wide, wide],
            "blocks",
        )

    def rows_for(array, device):
        pieces = array.reshape(*array.shape[:-2], fsdp, map_rows, array.shape[-1])
        return lax.dynamic_index_in_dim(pieces, device % fsdp, array.ndim - 2, keepdims=False)

    blocks, parts, q_maps = {}, {}, []
    for s in order:
        blocks[s] = block_of(s)
        parts[s] = across(blocks[s][3], s) if s else blocks[s][3]
        if s:
            q_maps += [apart(rows_for(blocks[s][4], seq + r), s, r) for r in range(fsdp)]
    parts = [after(parts[0], *q_maps)] + [parts[s] for s in slots[1:]]
    total = totals_of(parts)
    suffix, (grad_prefix,) = spread(parts, total, "after", [], True)
    returned = {s: within(after(blocks[s][0], total if s else suffix[0])) for s in order}

    kv_type = BF16 if replicas == 1 else F32
    pairs = jnp.zeros((part, tok, grp * 2 * hd), kv_type)
    k_maps, both_maps, key_gm = [], [], {}
    for s in slots:
        pairs, key_gm[s] = call(
            key_kernel,
            [of(kv_type, *pairs.shape), gm_shape],
            kv_specs(s)
            + [map_spec(s), ext_spec, dk_spec, dv_spec, pl.BlockSpec(memory_space=pl.ANY)],
            [pl.BlockSpec((part, tok, 2 * hd), lambda h, t: (0, 0, s)), gm_spec],
            [*kv, *kv, maps, suffix[s], blocks[s][1], blocks[s][2], pairs],
            [
                low,
                low,
                pltpu.VMEM((hd, BLK), BF16),
                pltpu.VMEM((hd, BLK), F32),
                pltpu.VMEM((heads * half, BLK), BF16),
                pltpu.VMEM((heads * half, hd), BF16),
            ],
            "keys",
            {2 * part + 5: 0},
        )
        if s == 0:
            two = after(jnp.stack([blocks[s][4], key_gm[s]]), *suffix[1:])
            both_maps = [along(rows_for(two, seq + r), r) for r in range(1, fsdp)]
        else:
            k_maps += [apart(rows_for(key_gm[s], seq + r), s, r) for r in range(fsdp)]

    pairs = within(after(pairs, *returned.values()))
    (grad_queries,) = unpack(table, base["owner"], [returned[s] for s in slots], 1, heads * hd)
    pairs = [pairs[:, :, s * 2 * hd : (s + 1) * 2 * hd] for s in slots]
    grad_keys, grad_values = unpack(table, base["owner"], pairs, 2, hd)
    if replicas > 1:
        grad_keys, grad_values = (
            jnp.sum(a.reshape(tok, kv_heads, replicas, hd), axis=2)
            .astype(BF16)
            .reshape(tok, kv_heads * hd)
            for a in (grad_keys, grad_values)
        )
    query_map_grad, key_map_grad = whole_call(
        functools.partial(close_kernel, len(both_maps), len(q_maps), base["seq"]),
        [of(F32, heads, map_rows, half)] * 2,
        table,
        [blocks[0][4], key_gm[0]] + both_maps + q_maps + k_maps,
        "close",
    )
    return grad_queries, grad_keys, grad_values, query_map_grad, key_map_grad, grad_prefix


def solution(mesh):
    rows, maps = P(("fsdp", "ctx"), None), P("ctx", "fsdp", None)
    return jax.shard_map(
        shards,
        mesh=mesh,
        in_specs=(rows,) * 4 + (maps, maps, P("ctx", None, None), P("ctx", None)),
        out_specs=(rows,) * 3 + (maps,) * 3,
        check_vma=False,
    )
```

```python
import functools

import jax
import jax.numpy as jnp
from jax import lax
from jax.experimental import pallas as pl
from jax.experimental.pallas import tpu as pltpu
from jax.sharding import PartitionSpec as P

BLK = 512
TILE = 256
PAIR = 2
EXT = 16
LIMIT = 40 * 1024 * 1024
LARGE = 56 * 1024 * 1024

LITTLE = pl.CostEstimate(flops=1000, bytes_accessed=1000, transcendentals=0)

F32 = jnp.float32
BF16 = jnp.bfloat16
SMEM = pltpu.SMEM


def nn(left, right):
    return lax.dot_general(left, right, (((1,), (0,)), ((), ())), preferred_element_type=F32)


def nt(left, right):
    return lax.dot_general(left, right, (((1,), (1,)), ((), ())), preferred_element_type=F32)


def turned(array):
    return array.astype(F32).T.astype(array.dtype)


def column(row, width):
    n = row.shape[1]
    square = jnp.broadcast_to(row, (n, n)).T
    return jnp.concatenate([square] * (width // n), axis=1)


def thirds(row):
    rows = jnp.broadcast_to(row, (EXT, row.shape[1]))
    high = rows.astype(BF16).astype(F32)
    middle = (rows - high).astype(BF16).astype(F32)
    low = rows - high - middle
    place = lax.broadcasted_iota(jnp.int32, rows.shape, 0)
    picked = jnp.where(place == 0, high, jnp.where(place == 1, middle, low))
    return jnp.where(place < 3, picked, 0.0).astype(BF16)


def whole_row(block):
    return jnp.sum(block.astype(F32), axis=0, keepdims=True)


def weight_rows(ref, u):
    whole = jnp.concatenate([ref[i, u] for i in range(ref.shape[0])], axis=0)
    return turned(whole)


def features(weight, rows):
    logits = nt(weight, rows).astype(BF16).astype(F32)
    upper = jnp.exp(logits)
    lower = jnp.exp(-logits)
    upper = upper * (1.0 / jnp.sum(upper, axis=0, keepdims=True))
    lower = lower * (1.0 / jnp.sum(lower, axis=0, keepdims=True))
    return jnp.concatenate([upper, lower], axis=0)


def feature_back(feats, upstream):
    half = feats.shape[0] // 2
    weighted = feats * upstream
    first, second = weighted[:half], weighted[half:]
    first = first - feats[:half] * jnp.sum(first, axis=0, keepdims=True)
    second = second - feats[half:] * jnp.sum(second, axis=0, keepdims=True)
    return (first - second).astype(BF16)


def gather(table, base, refs, out):
    rows = refs[0].shape[0]
    for r, ref in enumerate(refs):
        out[pl.ds(pl.multiple_of(table[base + r] * rows, rows), rows), :] = ref[...]


def pack_kernel(columns, inputs, table, *refs):
    count = columns * inputs
    for r, out in enumerate(refs[-(len(refs) // (count + 1)) :]):
        width = out.shape[1] // count
        for i in range(count):
            out[:, i * width : (i + 1) * width] = refs[r * count + i][...]


def pack(table, base, sources, pieces, columns, width):
    rows = sources[0].shape[0]
    count = columns * len(sources)
    step = rows // 2

    def take(at):
        return pl.BlockSpec((step, width), lambda i, t: (i, t[base + at]))

    return pl.pallas_call(
        functools.partial(pack_kernel, columns, len(sources)),
        out_shape=[jax.ShapeDtypeStruct((rows, count * width), sources[0].dtype)] * pieces,
        grid_spec=pltpu.PrefetchScalarGridSpec(
            num_scalar_prefetch=1,
            grid=(rows // step,),
            in_specs=[
                take(r * columns + s)
                for r in range(pieces)
                for s in range(columns)
                for _ in sources
            ],
            out_specs=[pl.BlockSpec((step, count * width), lambda i, t: (i, 0))] * pieces,
        ),
        compiler_params=pltpu.CompilerParams(vmem_limit_bytes=LIMIT),
        cost_estimate=LITTLE,
        name="pack",
    )(table, *(list(sources) * (pieces * columns)))


def unpack_kernel(outputs, inner, base, table, *refs):
    sources, outs = refs[:-outputs], refs[-outputs:]
    for s, source in enumerate(sources):
        pieces = source.shape[0]
        width = source.shape[2] // (outputs * inner)
        for r in range(pieces):
            for j in range(inner):
                slot = s * inner + j
                at = table[base + slot * pieces + r] * width
                for i, out in enumerate(outs):
                    lanes = slice((j * outputs + i) * width, (j * outputs + i + 1) * width)
                    out[:, pl.ds(pl.multiple_of(at, width), width)] = source[r, :, lanes]


def unpack(table, base, sources, inner, outputs, width):
    pieces, rows = sources[0].shape[:2]
    total = len(sources) * inner * pieces * width
    step = rows // 2
    taken = pl.BlockSpec((pieces, step, inner * outputs * width), lambda i: (0, i, 0))
    return pl.pallas_call(
        functools.partial(unpack_kernel, outputs, inner, base),
        out_shape=[jax.ShapeDtypeStruct((rows, total), sources[0].dtype)] * outputs,
        grid=(rows // step,),
        in_specs=[pl.BlockSpec(memory_space=SMEM)] + [taken] * len(sources),
        out_specs=[pl.BlockSpec((step, total), lambda i: (i, 0))] * outputs,
        compiler_params=pltpu.CompilerParams(vmem_limit_bytes=LIMIT),
        cost_estimate=LITTLE,
        name="unpack",
    )(table, *sources)


def state_kernel(part, base, table, *refs):
    k_refs, v_refs, (w_ref, out, k_all, v_all) = refs[:part], refs[part : 2 * part], refs[2 * part :]
    hd = k_all.shape[1]

    @pl.when(pl.program_id(0) == 0)
    def _():
        gather(table, base, k_refs, k_all)
        gather(table, base, v_refs, v_all)

    for u in range(out.shape[0]):
        weight = weight_rows(w_ref, u)
        feats = features(weight[weight.shape[0] // 2 :], k_all[...]).astype(BF16)
        out[u, :hd, :] = nn(feats, v_all[...]).astype(BF16)
        ones = jnp.ones((EXT, feats.shape[1]), BF16)
        out[u, hd:, :] = thirds(nt(ones, feats)[:1])


def block_kernel(part, base, table, *refs):
    k_refs, v_refs = refs[:part], refs[part : 2 * part]
    q_refs, g_refs = refs[2 * part : 3 * part], refs[3 * part : 4 * part]
    w_ref, st_ref = refs[4 * part : 4 * part + 2]
    gq_ref, dk_ref, dv_ref, sx_ref, gm_ref, k_all, v_all, vt_all, q_all, g_all = refs[4 * part + 2 :]
    hd = k_all.shape[1]

    @pl.when(pl.program_id(0) == 0)
    def _():
        gather(table, base, k_refs, k_all)
        gather(table, base, v_refs, v_all)
        vt_all[...] = turned(v_all[...])
        dv_ref[...] = jnp.zeros_like(dv_ref)

    gather(table, base, q_refs, q_all)
    gather(table, base, g_refs, g_all)
    maps = []
    earlier = lax.broadcasted_iota(jnp.int32, (TILE, TILE), 0) <= lax.broadcasted_iota(
        jnp.int32, (TILE, TILE), 1
    )

    def causal(array, begin):
        masked = jnp.where(earlier, array[begin:], 0.0)
        return masked if begin == 0 else jnp.concatenate([array[:begin], masked], axis=0)

    for u in range(PAIR):
        weight = weight_rows(w_ref, u)
        half = weight.shape[0] // 2
        lanes = slice(u * hd, (u + 1) * hd)
        q_feat = features(weight[:half], q_all[:, lanes])
        k_low = features(weight[half:], k_all[...]).astype(BF16)
        q_low = q_feat.astype(BF16)
        k_turned = turned(k_low)
        state = st_ref[u, :hd, :]
        state_turned = turned(state)
        norm = column(whole_row(st_ref[u, hd:, :]), TILE)
        g_turned = g_all[:, lanes].astype(F32).T
        back = []
        dkey = [jnp.zeros((2 * half, TILE), F32) for _ in range(BLK // TILE)]
        dvalue = [jnp.zeros((hd, TILE), F32) for _ in range(BLK // TILE)]
        suffix = jnp.zeros((2 * half, hd), F32)
        suffix_norm = jnp.zeros((2 * half, 1), F32)
        for j in range(BLK // TILE):
            begin, end = j * TILE, (j + 1) * TILE
            own = q_low[:, begin:end]
            own_wide = own.astype(F32)
            scores = causal(nn(k_turned[:end], own), begin)
            scores_low = scores.astype(BF16)
            numerator = nn(state_turned, own) + nn(vt_all[:, :end], scores_low)
            denominator = jnp.sum(own_wide * norm, axis=0, keepdims=True) + jnp.sum(
                scores, axis=0, keepdims=True
            )
            inverse = 1.0 / denominator
            scaled = g_turned[:, begin:end] * inverse
            scaled_low = scaled.astype(BF16)
            norm_grad = -jnp.sum(scaled * (numerator * inverse), axis=0, keepdims=True)
            dscores = causal(nn(v_all[:end, :], scaled_low) + norm_grad, begin).astype(BF16)
            dquery = nn(state, scaled_low) + norm * norm_grad + nn(k_low[:, :end], dscores)
            back.append(feature_back(q_feat[:, begin:end], dquery))
            for i in range(j + 1):
                rows = slice(i * TILE, (i + 1) * TILE)
                dkey[i] = dkey[i] + nt(own, dscores[rows])
                dvalue[i] = dvalue[i] + nt(scaled_low, scores_low[rows])
            suffix = suffix + nt(own, scaled_low)
            suffix_norm = suffix_norm + jnp.sum(own_wide * norm_grad, axis=1, keepdims=True)
        dlog = jnp.concatenate(back, axis=1)
        grads = nn(turned(dlog), weight[:half]).astype(BF16)
        gq_ref[:, :, lanes] = grads.reshape(gq_ref.shape[0], -1, hd)
        maps.append(nn(dlog, q_all[:, lanes]))
        dk_ref[u] = jnp.concatenate(dkey, axis=1)
        dv_ref[...] += jnp.concatenate(dvalue, axis=1)
        sx_ref[u, :hd, :] = suffix.astype(BF16)
        sx_ref[u, hd:, :] = thirds(jnp.broadcast_to(suffix_norm, (2 * half, 2 * half)).T[:1])
    gm_ref[0] = jnp.concatenate(maps, axis=0).T.astype(gm_ref.dtype)


def key_kernel(begun, part, base, table, *refs):
    k_refs, v_refs = refs[:part], refs[part : 2 * part]
    w_ref, sx_ref, dk_ref, dv_ref = refs[2 * part : 2 * part + 4]
    out, gm_ref, k_all, v_all, vt_all, total, logs, weights = refs[2 * part + 4 + begun :]
    hd = k_all.shape[1]
    step = pl.program_id(0)

    @pl.when(step == 0)
    def _():
        gather(table, base, k_refs, k_all)
        gather(table, base, v_refs, v_all)
        vt_all[...] = turned(v_all[...])
        total[...] = dv_ref[...]

    maps = []
    for u in range(PAIR):
        weight = weight_rows(w_ref, u)
        half = weight.shape[0] // 2
        weight = weight[half:]
        feats = features(weight, k_all[...])
        suffix = sx_ref[u, :hd, :]
        norm = column(whole_row(sx_ref[u, hd:, :]), BLK)
        dlog = feature_back(feats, dk_ref[u] + nn(suffix, vt_all[...]) + norm)
        at = pl.ds(pl.multiple_of((step * PAIR + u) * half, half), half)
        logs[at, :] = dlog
        weights[at, :] = weight
        maps.append(nn(dlog, k_all[...]))
        total[...] += nn(turned(suffix), feats.astype(BF16))
    gm_ref[0] = jnp.concatenate(maps, axis=0).T.astype(gm_ref.dtype)

    @pl.when(step == pl.num_programs(0) - 1)
    def _():
        pair = jnp.concatenate([nn(turned(logs[...]), weights[...]), total[...].T], axis=1)
        out[...] = pair.astype(out.dtype).reshape(out.shape)


def total_kernel(table, *refs):
    out = refs[-1]
    heads, hd = out.shape[0], out.shape[2]
    for h in range(heads):
        out[h, :hd, :] = sum(ref[h, :hd, :].astype(F32) for ref in refs[:-1]).astype(BF16)
        out[h, hd:, :] = thirds(sum(whole_row(ref[h, hd:, :]) for ref in refs[:-1]))


def spread_kernel(grp, others, closing, block_weight, total_weight, at, table, *refs):
    parts, totals, refs = refs[:grp], refs[grp : grp + others], refs[grp + others :]
    if closing:
        outs, grad, scratch = refs[:grp], refs[grp], refs[grp + 1]
    else:
        state_ref, norm_ref, outs = refs[0], refs[1], refs[2:]
    heads, hd = parts[0].shape[0], parts[0].shape[2]
    for h in range(heads):
        states = [ref[h, :hd, :].astype(F32) for ref in parts]
        norms = [whole_row(ref[h, hd:, :]) for ref in parts]
        others_state = [ref[h, :hd, :].astype(F32) for ref in totals]
        others_norm = [whole_row(ref[h, hd:, :]) for ref in totals]
        if closing:
            base, base_norm = jnp.zeros_like(states[0]), jnp.zeros_like(norms[0])
            scratch[...] = sum(states) + sum(others_state)
            rows = grad.shape[1]
            grad[h] = scratch[pl.ds(pl.multiple_of(table[at] * rows, rows), rows), :]
        else:
            base, base_norm = state_ref[h], norm_ref[pl.ds(h, 1), :]
        for i, (state, norm) in enumerate(zip(others_state, others_norm)):
            base = base + table[total_weight + i].astype(F32) * state
            base_norm = base_norm + table[total_weight + i].astype(F32) * norm
        for r, out in enumerate(outs):
            state, norm = base, base_norm
            for i in range(grp):
                if i != r:
                    state = state + table[block_weight + r * grp + i].astype(F32) * states[i]
                    norm = norm + table[block_weight + r * grp + i].astype(F32) * norms[i]
            out[h, :hd, :] = state.astype(BF16)
            out[h, hd:, :] = thirds(norm)


def close_kernel(pairs, singles, at, table, q_ref, k_ref, *refs):
    both, q_parts, k_parts = (
        refs[:pairs],
        refs[pairs : pairs + singles],
        refs[pairs + singles : pairs + 2 * singles],
    )
    for i, (own, parts, out) in enumerate(
        ((q_ref, q_parts, refs[-2]), (k_ref, k_parts, refs[-1]))
    ):
        rows, half = out.shape[1:]
        mine = pl.ds(pl.multiple_of(table[at] * rows, rows), rows)
        for h in range(own.shape[0]):
            total = own[h, mine, :].astype(F32)
            for ref in both:
                total = total + ref[i, h].astype(F32)
            for ref in parts:
                total = total + ref[h].astype(F32)
            for u in range(PAIR):
                out[h * PAIR + u] = total[:, u * half : (u + 1) * half]


def whole_call(kernel, outs, table, arrays, name, scratch=()):
    return pl.pallas_call(
        kernel,
        out_shape=outs,
        in_specs=[pl.BlockSpec(memory_space=SMEM)]
        + [pl.BlockSpec(memory_space=pltpu.VMEM)] * len(arrays),
        out_specs=[pl.BlockSpec(memory_space=pltpu.VMEM)] * len(outs),
        scratch_shapes=list(scratch),
        compiler_params=pltpu.CompilerParams(vmem_limit_bytes=LIMIT),
        cost_estimate=LITTLE,
        name=name,
    )(table, *arrays)


def after(value, *others):
    return lax.optimization_barrier((value, *others))[0]


def shards(
    query_rows, key_rows, value_rows, grad_out, query_map, key_map, prefix_state, prefix_norm
):
    ctx, fsdp = lax.axis_size("ctx"), lax.axis_size("fsdp")
    tok = query_rows.shape[0]
    heads, map_rows, half = query_map.shape
    hd = map_rows * fsdp
    kv_heads = key_rows.shape[1] // hd
    replicas = ctx // kv_heads
    part = BLK // tok
    grp = ctx // part
    mine = lax.axis_index("ctx")
    at, block, seq = mine % part, mine // part, lax.axis_index("fsdp")
    shifts, slots = range(part), range(grp)
    order = list(reversed(slots))
    grid = (heads // PAIR,)
    blocks_of = [[g * part + p for p in range(part)] for g in slots]

    def within(array):
        return lax.all_to_all(array, "ctx", 0, 0, axis_index_groups=blocks_of, tiled=True)

    def around(array, shift):
        return lax.ppermute(
            array, "ctx", [(d, d // part * part + (d + shift) % part) for d in range(ctx)]
        )

    def across(array, shift):
        return lax.ppermute(array, "ctx", [(d, (d + shift * part) % ctx) for d in range(ctx)])

    def along(array, shift):
        return lax.ppermute(array, "fsdp", [(d, (d + shift) % fsdp) for d in range(fsdp)])

    def apart(array, s, r):
        moves = [
            (d * fsdp + i, (d + s * part) % ctx * fsdp + (i + r) % fsdp)
            for d in range(ctx)
            for i in range(fsdp)
        ]
        return lax.ppermute(array, ("ctx", "fsdp"), moves)

    slot = [(block + s) % grp for s in slots]
    near = [(block - r) % grp for r in slots]
    far = [(seq - r) % fsdp for r in range(1, fsdp)]
    lists = {
        "seq": [seq],
        "owner": [slot[s] * part + p for s in slots for p in range(part)],
        "sent": [slot[s] * part + (at + r) % part for s in slots for r in shifts],
        "kv": [
            (slot[s] * part + (at + r) % part) // replicas for r in shifts for s in slots
        ],
        "sorted": [(at - r) % part for r in shifts],
        "near before": [b < a for a in near for b in near],
        "near after": [b > a for a in near for b in near],
        "far before": [other < seq for other in far],
        "far after": [other > seq for other in far],
    }
    base, values = {}, []
    for name, entries in lists.items():
        base[name] = len(values)
        values += entries
    table = jnp.stack([jnp.asarray(v, jnp.int32) for v in values])

    own_maps = jnp.concatenate((query_map, key_map), axis=-1)
    near_maps = jnp.stack([own_maps] + [across(own_maps, -s) for s in slots[1:]])
    kv_sent = pack(table, base["kv"], (key_rows, value_rows), part, grp, hd)
    kv = [kv_sent[0]] + [around(kv_sent[r], r) for r in shifts[1:]]
    maps = lax.all_gather(near_maps, "fsdp")

    rows = {}
    for s in order:
        sent = pack(
            after(table, near_maps, *kv),
            base["sent"] + s * part,
            (query_rows, grad_out),
            part,
            1,
            heads * hd,
        )
        rows[s] = [sent[0]] + [around(sent[r], r) for r in shifts[1:]]

    def piece_specs(column, count):
        return [pl.BlockSpec((tok, count * hd), lambda h, t: (0, column(h)))] * part

    def kv_specs(s):
        return piece_specs(lambda h: 2 * s, 1) + piece_specs(lambda h: 2 * s + 1, 1)

    def map_spec(s):
        return pl.BlockSpec((fsdp, None, PAIR, map_rows, 2 * half), lambda h, t: (0, s, h, 0, 0))

    def head_spec(*shape):
        return pl.BlockSpec((PAIR, *shape), lambda h, t: (h,) + (0,) * len(shape))

    def of(dtype, *shape):
        return jax.ShapeDtypeStruct(shape, dtype)

    ext_spec, ext_shape = head_spec(hd + EXT, hd), of(BF16, heads, hd + EXT, hd)
    gm_spec = pl.BlockSpec((1, hd, PAIR * half), lambda h, t: (h, 0, 0))
    gm_shape = of(BF16, heads // PAIR, hd, PAIR * half)
    dk_spec, dk_shape = head_spec(2 * half, BLK), of(F32, heads, 2 * half, BLK)
    dv_spec, dv_shape = pl.BlockSpec((hd, BLK), lambda h, t: (0, 0)), of(F32, hd, BLK)
    low, wide = pltpu.VMEM((BLK, hd), BF16), pltpu.VMEM((BLK, PAIR * hd), BF16)

    def call(kernel, outs, specs, out_specs, arrays, scratch, name, alias=(), limit=LIMIT):
        return pl.pallas_call(
            functools.partial(kernel, part, base["sorted"]),
            out_shape=outs,
            grid_spec=pltpu.PrefetchScalarGridSpec(
                num_scalar_prefetch=1,
                grid=grid,
                in_specs=specs,
                out_specs=out_specs,
                scratch_shapes=scratch,
            ),
            compiler_params=pltpu.CompilerParams(
                dimension_semantics=("arbitrary",), vmem_limit_bytes=limit
            ),
            cost_estimate=LITTLE,
            input_output_aliases=dict(alias),
            name=name,
        )(table, *arrays)

    def states_of(s):
        return call(
            state_kernel,
            [ext_shape],
            kv_specs(s) + [map_spec(s)],
            [ext_spec],
            [*kv, *kv, maps],
            [low, low],
            "states",
        )[0]

    def spread(parts, others, when, extra, closing):
        weights = [base["near " + when], base["far " + when], base["seq"]]
        result = whole_call(
            functools.partial(spread_kernel, grp, fsdp - 1, closing, *weights),
            [ext_shape] * grp + [of(F32, heads, map_rows, hd)] * closing,
            table,
            parts + others + extra,
            "spread",
            [pltpu.VMEM((hd, hd), F32)] * closing,
        )
        return [result[0]] + [across(result[s], -s) for s in slots[1:]], result[grp:]

    def around_all(total):
        return [along(total, r) for r in range(1, fsdp)]

    def totals_of(parts):
        return whole_call(total_kernel, [ext_shape], table, parts, "totals")[0]

    partial = {s: states_of(s) for s in order}
    parts = [after(partial[0], *rows[order[0]])] + [across(partial[s], s) for s in slots[1:]]
    others = around_all(totals_of(parts))
    state, _ = spread(parts, others, "before", [prefix_state, prefix_norm], False)

    def block_of(s):
        return call(
            block_kernel,
            [of(BF16, part, tok, heads * hd), dk_shape, dv_shape, ext_shape, gm_shape],
            kv_specs(s)
            + piece_specs(lambda h: h, PAIR)
            + piece_specs(lambda h: grid[0] + h, PAIR)
            + [map_spec(s), ext_spec],
            [
                pl.BlockSpec((part, tok, PAIR * hd), lambda h, t: (0, 0, h)),
                dk_spec,
                dv_spec,
                ext_spec,
                gm_spec,
            ],
            [*kv, *kv, *rows[s], *rows[s], maps, state[s]],
            [low, low, pltpu.VMEM((hd, BLK), BF16), wide, wide],
            "blocks",
            limit=LARGE,
        )

    def rows_for(array, device):
        pieces = array.reshape(*array.shape[:-2], fsdp, map_rows, array.shape[-1])
        return lax.dynamic_index_in_dim(pieces, device % fsdp, array.ndim - 2, keepdims=False)

    blocks, parts, q_maps = {}, {}, []
    for s in order:
        blocks[s] = block_of(s)
        parts[s] = across(blocks[s][3], s) if s else blocks[s][3]
    parts = [parts[s] for s in slots]
    total = totals_of(parts)
    for s in slots[1:]:
        late = after(blocks[s][4], total)
        q_maps += [apart(rows_for(late, seq + r), s, r) for r in range(fsdp)]
    others = around_all(total)
    suffix, (grad_prefix,) = spread(parts, others, "after", [], True)
    returned = {s: within(after(blocks[s][0], others[0])) for s in order if s}

    kv_type = BF16 if replicas == 1 else F32
    pairs = of(kv_type, part, tok, grp * 2 * hd)
    k_maps, both_maps, key_gm = [], [], {}
    for s in slots:
        begun = [] if s == 0 else [pairs]
        pairs, key_gm[s] = call(
            functools.partial(key_kernel, bool(begun)),
            [of(kv_type, *pairs.shape), gm_shape],
            kv_specs(s)
            + [map_spec(s), ext_spec, dk_spec, dv_spec]
            + [pl.BlockSpec(memory_space=pl.ANY)] * len(begun),
            [pl.BlockSpec((part, tok, 2 * hd), lambda h, t: (0, 0, s)), gm_spec],
            [*kv, *kv, maps, suffix[s], blocks[s][1], blocks[s][2], *begun],
            [
                low,
                low,
                pltpu.VMEM((hd, BLK), BF16),
                pltpu.VMEM((hd, BLK), F32),
                pltpu.VMEM((heads * half, BLK), BF16),
                pltpu.VMEM((heads * half, hd), BF16),
            ],
            "keys",
            {2 * part + 5: 0} if begun else {},
        )
        if s == 0:
            two = after(jnp.stack([blocks[s][4], key_gm[s]]), *suffix[1:], *q_maps)
            both_maps = [along(rows_for(two, seq + r), r) for r in range(1, fsdp)]
            returned[s] = within(after(blocks[s][0], key_gm[s]))
        else:
            k_maps += [apart(rows_for(key_gm[s], seq + r), s, r) for r in range(fsdp)]

    pairs = within(pairs)
    (grad_queries,) = unpack(table, base["owner"], [returned[s] for s in slots], 1, 1, heads * hd)
    grad_keys, grad_values = unpack(table, base["owner"], [pairs], grp, 2, hd)
    if replicas > 1:
        grad_keys, grad_values = (
            jnp.sum(a.reshape(tok, kv_heads, replicas, hd), axis=2)
            .astype(BF16)
            .reshape(tok, kv_heads * hd)
            for a in (grad_keys, grad_values)
        )
    query_map_grad, key_map_grad = whole_call(
        functools.partial(close_kernel, len(both_maps), len(q_maps), base["seq"]),
        [of(F32, heads, map_rows, half)] * 2,
        table,
        [blocks[0][4], key_gm[0]] + both_maps + q_maps + k_maps,
        "close",
    )
    return grad_queries, grad_keys, grad_values, query_map_grad, key_map_grad, grad_prefix


def solution(mesh):
    rows, maps = P(("fsdp", "ctx"), None), P("ctx", "fsdp", None)
    return jax.shard_map(
        shards,
        mesh=mesh,
        in_specs=(rows,) * 4 + (maps, maps, P("ctx", None, None), P("ctx", None)),
        out_specs=(rows,) * 3 + (maps,) * 3,
        check_vma=False,
    )
```

```python
import functools

import jax
import jax.numpy as jnp
from jax import lax
from jax.experimental import pallas as pl
from jax.experimental.pallas import tpu as pltpu
from jax.sharding import PartitionSpec as P

BLK = 512
TILE = 256
PAIR = 2
EXT = 16
LIMIT = 40 * 1024 * 1024
LARGE = 56 * 1024 * 1024

LITTLE = pl.CostEstimate(flops=1000, bytes_accessed=1000, transcendentals=0)

F32 = jnp.float32
BF16 = jnp.bfloat16
SMEM = pltpu.SMEM


def nn(left, right):
    return lax.dot_general(left, right, (((1,), (0,)), ((), ())), preferred_element_type=F32)


def nt(left, right):
    return lax.dot_general(left, right, (((1,), (1,)), ((), ())), preferred_element_type=F32)


def turned(array):
    return array.astype(F32).T.astype(array.dtype)


def column(row, width):
    n = row.shape[1]
    square = jnp.broadcast_to(row, (n, n)).T
    return jnp.concatenate([square] * (width // n), axis=1)


def thirds(row):
    rows = jnp.broadcast_to(row, (EXT, row.shape[1]))
    high = rows.astype(BF16).astype(F32)
    middle = (rows - high).astype(BF16).astype(F32)
    low = rows - high - middle
    place = lax.broadcasted_iota(jnp.int32, rows.shape, 0)
    picked = jnp.where(place == 0, high, jnp.where(place == 1, middle, low))
    return jnp.where(place < 3, picked, 0.0).astype(BF16)


def whole_row(block):
    return jnp.sum(block.astype(F32), axis=0, keepdims=True)


def weight_rows(ref, u):
    whole = jnp.concatenate([ref[i, u] for i in range(ref.shape[0])], axis=0)
    return turned(whole)


def features(weight, rows):
    logits = nt(weight, rows).astype(BF16).astype(F32)
    upper = jnp.exp(logits)
    lower = jnp.exp(-logits)
    upper = upper * (1.0 / jnp.sum(upper, axis=0, keepdims=True))
    lower = lower * (1.0 / jnp.sum(lower, axis=0, keepdims=True))
    return jnp.concatenate([upper, lower], axis=0)


def feature_back(feats, upstream):
    half = feats.shape[0] // 2
    weighted = feats * upstream
    first, second = weighted[:half], weighted[half:]
    first = first - feats[:half] * jnp.sum(first, axis=0, keepdims=True)
    second = second - feats[half:] * jnp.sum(second, axis=0, keepdims=True)
    return (first - second).astype(BF16)


def gather(table, base, refs, out):
    rows = refs[0].shape[0]
    for r, ref in enumerate(refs):
        out[pl.ds(pl.multiple_of(table[base + r] * rows, rows), rows), :] = ref[...]


def pack_kernel(columns, inputs, table, *refs):
    count = columns * inputs
    for r, out in enumerate(refs[-(len(refs) // (count + 1)) :]):
        width = out.shape[1] // count
        for i in range(count):
            out[:, i * width : (i + 1) * width] = refs[r * count + i][...]


def pack(table, base, sources, pieces, columns, width):
    rows = sources[0].shape[0]
    count = columns * len(sources)
    step = rows // 2

    def take(at):
        return pl.BlockSpec((step, width), lambda i, t: (i, t[base + at]))

    return pl.pallas_call(
        functools.partial(pack_kernel, columns, len(sources)),
        out_shape=[jax.ShapeDtypeStruct((rows, count * width), sources[0].dtype)] * pieces,
        grid_spec=pltpu.PrefetchScalarGridSpec(
            num_scalar_prefetch=1,
            grid=(rows // step,),
            in_specs=[
                take(r * columns + s)
                for r in range(pieces)
                for s in range(columns)
                for _ in sources
            ],
            out_specs=[pl.BlockSpec((step, count * width), lambda i, t: (i, 0))] * pieces,
        ),
        compiler_params=pltpu.CompilerParams(vmem_limit_bytes=LIMIT),
        cost_estimate=LITTLE,
        name="pack",
    )(table, *(list(sources) * (pieces * columns)))


def unpack_kernel(outputs, inner, base, table, *refs):
    sources, outs = refs[:-outputs], refs[-outputs:]
    for s, source in enumerate(sources):
        pieces = source.shape[0]
        width = source.shape[2] // (outputs * inner)
        for r in range(pieces):
            for j in range(inner):
                slot = s * inner + j
                at = table[base + slot * pieces + r] * width
                for i, out in enumerate(outs):
                    lanes = slice((j * outputs + i) * width, (j * outputs + i + 1) * width)
                    out[:, pl.ds(pl.multiple_of(at, width), width)] = source[r, :, lanes]


def unpack(table, base, sources, inner, outputs, width):
    pieces, rows = sources[0].shape[:2]
    total = len(sources) * inner * pieces * width
    step = rows // 2
    taken = pl.BlockSpec((pieces, step, inner * outputs * width), lambda i: (0, i, 0))
    return pl.pallas_call(
        functools.partial(unpack_kernel, outputs, inner, base),
        out_shape=[jax.ShapeDtypeStruct((rows, total), sources[0].dtype)] * outputs,
        grid=(rows // step,),
        in_specs=[pl.BlockSpec(memory_space=SMEM)] + [taken] * len(sources),
        out_specs=[pl.BlockSpec((step, total), lambda i: (i, 0))] * outputs,
        compiler_params=pltpu.CompilerParams(vmem_limit_bytes=LIMIT),
        cost_estimate=LITTLE,
        name="unpack",
    )(table, *sources)


def state_kernel(part, base, table, *refs):
    k_refs, v_refs, (w_ref, out, k_all, v_all) = refs[:part], refs[part : 2 * part], refs[2 * part :]
    hd = k_all.shape[1]

    @pl.when(pl.program_id(0) == 0)
    def _():
        gather(table, base, k_refs, k_all)
        gather(table, base, v_refs, v_all)

    for u in range(out.shape[0]):
        weight = weight_rows(w_ref, u)
        feats = features(weight[weight.shape[0] // 2 :], k_all[...]).astype(BF16)
        out[u, :hd, :] = nn(feats, v_all[...]).astype(BF16)
        ones = jnp.ones((EXT, feats.shape[1]), BF16)
        out[u, hd:, :] = thirds(nt(ones, feats)[:1])


def block_kernel(part, base, table, *refs):
    k_refs, v_refs = refs[:part], refs[part : 2 * part]
    q_refs, g_refs = refs[2 * part : 3 * part], refs[3 * part : 4 * part]
    w_ref, st_ref = refs[4 * part : 4 * part + 2]
    gq_ref, dk_ref, dv_ref, sx_ref, gm_ref, k_all, v_all, vt_all, q_all, g_all = refs[4 * part + 2 :]
    hd = k_all.shape[1]

    @pl.when(pl.program_id(0) == 0)
    def _():
        gather(table, base, k_refs, k_all)
        gather(table, base, v_refs, v_all)
        vt_all[...] = turned(v_all[...])
        dv_ref[...] = jnp.zeros_like(dv_ref)

    gather(table, base, q_refs, q_all)
    gather(table, base, g_refs, g_all)
    maps = []
    earlier = lax.broadcasted_iota(jnp.int32, (TILE, TILE), 0) <= lax.broadcasted_iota(
        jnp.int32, (TILE, TILE), 1
    )

    def causal(array, begin):
        masked = jnp.where(earlier, array[begin:], 0.0)
        return masked if begin == 0 else jnp.concatenate([array[:begin], masked], axis=0)

    for u in range(PAIR):
        weight = weight_rows(w_ref, u)
        half = weight.shape[0] // 2
        lanes = slice(u * hd, (u + 1) * hd)
        q_feat = features(weight[:half], q_all[:, lanes])
        k_low = features(weight[half:], k_all[...]).astype(BF16)
        q_low = q_feat.astype(BF16)
        k_turned = turned(k_low)
        state = st_ref[u, :hd, :]
        state_turned = turned(state)
        norm = column(whole_row(st_ref[u, hd:, :]), TILE)
        g_turned = g_all[:, lanes].astype(F32).T
        back = []
        dkey = [jnp.zeros((2 * half, TILE), F32) for _ in range(BLK // TILE)]
        dvalue = [jnp.zeros((hd, TILE), F32) for _ in range(BLK // TILE)]
        suffix = jnp.zeros((2 * half, hd), F32)
        suffix_norm = jnp.zeros((2 * half, 1), F32)
        for j in range(BLK // TILE):
            begin, end = j * TILE, (j + 1) * TILE
            own = q_low[:, begin:end]
            own_wide = own.astype(F32)
            scores = causal(nn(k_turned[:end], own), begin)
            scores_low = scores.astype(BF16)
            numerator = nn(state_turned, own) + nn(vt_all[:, :end], scores_low)
            denominator = jnp.sum(own_wide * norm, axis=0, keepdims=True) + jnp.sum(
                scores, axis=0, keepdims=True
            )
            inverse = 1.0 / denominator
            scaled = g_turned[:, begin:end] * inverse
            scaled_low = scaled.astype(BF16)
            norm_grad = -jnp.sum(scaled * (numerator * inverse), axis=0, keepdims=True)
            dscores = causal(nn(v_all[:end, :], scaled_low) + norm_grad, begin).astype(BF16)
            dquery = nn(state, scaled_low) + norm * norm_grad + nn(k_low[:, :end], dscores)
            back.append(feature_back(q_feat[:, begin:end], dquery))
            for i in range(j + 1):
                rows = slice(i * TILE, (i + 1) * TILE)
                dkey[i] = dkey[i] + nt(own, dscores[rows])
                dvalue[i] = dvalue[i] + nt(scaled_low, scores_low[rows])
            suffix = suffix + nt(own, scaled_low)
            suffix_norm = suffix_norm + jnp.sum(own_wide * norm_grad, axis=1, keepdims=True)
        dlog = jnp.concatenate(back, axis=1)
        grads = nn(turned(dlog), weight[:half]).astype(BF16)
        gq_ref[:, :, lanes] = grads.reshape(gq_ref.shape[0], -1, hd)
        maps.append(nn(dlog, q_all[:, lanes]))
        dk_ref[u] = jnp.concatenate(dkey, axis=1)
        dv_ref[...] += jnp.concatenate(dvalue, axis=1)
        sx_ref[u, :hd, :] = suffix.astype(BF16)
        sx_ref[u, hd:, :] = thirds(jnp.broadcast_to(suffix_norm, (2 * half, 2 * half)).T[:1])
    gm_ref[0] = jnp.concatenate(maps, axis=0).T.astype(gm_ref.dtype)


def key_kernel(begun, part, base, table, *refs):
    k_refs, v_refs = refs[:part], refs[part : 2 * part]
    w_ref, sx_ref, dk_ref, dv_ref = refs[2 * part : 2 * part + 4]
    out, gm_ref, k_all, v_all, vt_all, total, logs, weights = refs[2 * part + 4 + begun :]
    hd = k_all.shape[1]
    step = pl.program_id(0)

    @pl.when(step == 0)
    def _():
        gather(table, base, k_refs, k_all)
        gather(table, base, v_refs, v_all)
        vt_all[...] = turned(v_all[...])
        total[...] = dv_ref[...]

    maps = []
    for u in range(PAIR):
        weight = weight_rows(w_ref, u)
        half = weight.shape[0] // 2
        weight = weight[half:]
        feats = features(weight, k_all[...])
        suffix = sx_ref[u, :hd, :]
        norm = column(whole_row(sx_ref[u, hd:, :]), BLK)
        dlog = feature_back(feats, dk_ref[u] + nn(suffix, vt_all[...]) + norm)
        at = pl.ds(pl.multiple_of((step * PAIR + u) * half, half), half)
        logs[at, :] = dlog
        weights[at, :] = weight
        maps.append(nn(dlog, k_all[...]))
        total[...] += nn(turned(suffix), feats.astype(BF16))
    gm_ref[0] = jnp.concatenate(maps, axis=0).T.astype(gm_ref.dtype)

    @pl.when(step == pl.num_programs(0) - 1)
    def _():
        pair = jnp.concatenate([nn(turned(logs[...]), weights[...]), total[...].T], axis=1)
        out[...] = pair.astype(out.dtype).reshape(out.shape)


def total_kernel(table, *refs):
    out = refs[-1]
    heads, hd = out.shape[0], out.shape[2]
    for h in range(heads):
        out[h, :hd, :] = sum(ref[h, :hd, :].astype(F32) for ref in refs[:-1]).astype(BF16)
        out[h, hd:, :] = thirds(sum(whole_row(ref[h, hd:, :]) for ref in refs[:-1]))


def spread_kernel(grp, others, closing, block_weight, total_weight, at, table, *refs):
    parts, totals, refs = refs[:grp], refs[grp : grp + others], refs[grp + others :]
    if closing:
        outs, grad, scratch = refs[:grp], refs[grp], refs[grp + 1]
    else:
        state_ref, norm_ref, outs = refs[0], refs[1], refs[2:]
    heads, hd = parts[0].shape[0], parts[0].shape[2]
    for h in range(heads):
        states = [ref[h, :hd, :].astype(F32) for ref in parts]
        norms = [whole_row(ref[h, hd:, :]) for ref in parts]
        others_state = [ref[h, :hd, :].astype(F32) for ref in totals]
        others_norm = [whole_row(ref[h, hd:, :]) for ref in totals]
        if closing:
            base, base_norm = jnp.zeros_like(states[0]), jnp.zeros_like(norms[0])
            scratch[...] = sum(states) + sum(others_state)
            rows = grad.shape[1]
            grad[h] = scratch[pl.ds(pl.multiple_of(table[at] * rows, rows), rows), :]
        else:
            base, base_norm = state_ref[h], norm_ref[pl.ds(h, 1), :]
        for i, (state, norm) in enumerate(zip(others_state, others_norm)):
            base = base + table[total_weight + i].astype(F32) * state
            base_norm = base_norm + table[total_weight + i].astype(F32) * norm
        for r, out in enumerate(outs):
            state, norm = base, base_norm
            for i in range(grp):
                if i != r:
                    state = state + table[block_weight + r * grp + i].astype(F32) * states[i]
                    norm = norm + table[block_weight + r * grp + i].astype(F32) * norms[i]
            out[h, :hd, :] = state.astype(BF16)
            out[h, hd:, :] = thirds(norm)


def close_kernel(at, table, q_ref, k_ref, *refs):
    pieces, outs = refs[:-2], refs[-2:]
    for i, (own, out) in enumerate(zip((q_ref, k_ref), outs)):
        rows, half = out.shape[1:]
        mine = pl.ds(pl.multiple_of(table[at] * rows, rows), rows)
        for h in range(own.shape[0]):
            total = own[h, mine, :].astype(F32)
            for ref in pieces:
                total = total + ref[i, h].astype(F32)
            for u in range(PAIR):
                out[h * PAIR + u] = total[:, u * half : (u + 1) * half]


def whole_call(kernel, outs, table, arrays, name, scratch=()):
    return pl.pallas_call(
        kernel,
        out_shape=outs,
        in_specs=[pl.BlockSpec(memory_space=SMEM)]
        + [pl.BlockSpec(memory_space=pltpu.VMEM)] * len(arrays),
        out_specs=[pl.BlockSpec(memory_space=pltpu.VMEM)] * len(outs),
        scratch_shapes=list(scratch),
        compiler_params=pltpu.CompilerParams(vmem_limit_bytes=LIMIT),
        cost_estimate=LITTLE,
        name=name,
    )(table, *arrays)


def after(value, *others):
    return lax.optimization_barrier((value, *others))[0]


def shards(
    query_rows, key_rows, value_rows, grad_out, query_map, key_map, prefix_state, prefix_norm
):
    ctx, fsdp = lax.axis_size("ctx"), lax.axis_size("fsdp")
    tok = query_rows.shape[0]
    heads, map_rows, half = query_map.shape
    hd = map_rows * fsdp
    kv_heads = key_rows.shape[1] // hd
    replicas = ctx // kv_heads
    part = BLK // tok
    grp = ctx // part
    mine = lax.axis_index("ctx")
    at, block, seq = mine % part, mine // part, lax.axis_index("fsdp")
    shifts, slots = range(part), range(grp)
    order = list(reversed(slots))
    grid = (heads // PAIR,)
    blocks_of = [[g * part + p for p in range(part)] for g in slots]

    def within(array):
        return lax.all_to_all(array, "ctx", 0, 0, axis_index_groups=blocks_of, tiled=True)

    def around(array, shift):
        return lax.ppermute(
            array, "ctx", [(d, d // part * part + (d + shift) % part) for d in range(ctx)]
        )

    def across(array, shift):
        return lax.ppermute(array, "ctx", [(d, (d + shift * part) % ctx) for d in range(ctx)])

    def along(array, shift):
        return lax.ppermute(array, "fsdp", [(d, (d + shift) % fsdp) for d in range(fsdp)])

    def twin(array, bit):
        return lax.ppermute(array, "fsdp", [(d, d ^ bit) for d in range(fsdp)])

    def apart(array, s, r):
        moves = [
            (d * fsdp + i, (d + s * part) % ctx * fsdp + (i + r) % fsdp)
            for d in range(ctx)
            for i in range(fsdp)
        ]
        return lax.ppermute(array, ("ctx", "fsdp"), moves)

    slot = [(block + s) % grp for s in slots]
    near = [(block - r) % grp for r in slots]
    bits = [1 << i for i in range(fsdp.bit_length() - 1)]
    lists = {
        "seq": [seq],
        "owner": [slot[s] * part + p for s in slots for p in range(part)],
        "sent": [slot[s] * part + (at + r) % part for s in slots for r in shifts],
        "kv": [
            (slot[s] * part + (at + r) % part) // replicas for r in shifts for s in slots
        ],
        "sorted": [(at - r) % part for r in shifts],
        "near before": [b < a for a in near for b in near],
        "near after": [b > a for a in near for b in near],
        "far before": [(seq ^ bit) < seq for bit in bits],
        "far after": [(seq ^ bit) > seq for bit in bits],
    }
    base, values = {}, []
    for name, entries in lists.items():
        base[name] = len(values)
        values += entries
    table = jnp.stack([jnp.asarray(v, jnp.int32) for v in values])

    own_maps = jnp.concatenate((query_map, key_map), axis=-1)
    near_maps = jnp.stack([own_maps] + [across(own_maps, -s) for s in slots[1:]])
    kv_sent = pack(table, base["kv"], (key_rows, value_rows), part, grp, hd)
    kv = [kv_sent[0]] + [around(kv_sent[r], r) for r in shifts[1:]]
    maps = lax.all_gather(near_maps, "fsdp")

    def sent_rows(s, *earlier):
        sent = pack(
            after(table, *earlier),
            base["sent"] + s * part,
            (query_rows, grad_out),
            part,
            1,
            heads * hd,
        )
        return [sent[0]] + [around(sent[r], r) for r in shifts[1:]]

    def piece_specs(column, count):
        return [pl.BlockSpec((tok, count * hd), lambda h, t: (0, column(h)))] * part

    def kv_specs(s):
        return piece_specs(lambda h: 2 * s, 1) + piece_specs(lambda h: 2 * s + 1, 1)

    def map_spec(s):
        return pl.BlockSpec((fsdp, None, PAIR, map_rows, 2 * half), lambda h, t: (0, s, h, 0, 0))

    def head_spec(*shape):
        return pl.BlockSpec((PAIR, *shape), lambda h, t: (h,) + (0,) * len(shape))

    def of(dtype, *shape):
        return jax.ShapeDtypeStruct(shape, dtype)

    ext_spec, ext_shape = head_spec(hd + EXT, hd), of(BF16, heads, hd + EXT, hd)
    gm_spec = pl.BlockSpec((1, hd, PAIR * half), lambda h, t: (h, 0, 0))
    gm_shape = of(BF16, heads // PAIR, hd, PAIR * half)
    dk_spec, dk_shape = head_spec(2 * half, BLK), of(F32, heads, 2 * half, BLK)
    dv_spec, dv_shape = pl.BlockSpec((hd, BLK), lambda h, t: (0, 0)), of(F32, hd, BLK)
    low, wide = pltpu.VMEM((BLK, hd), BF16), pltpu.VMEM((BLK, PAIR * hd), BF16)

    def call(kernel, outs, specs, out_specs, arrays, scratch, name, alias=(), limit=LIMIT):
        return pl.pallas_call(
            functools.partial(kernel, part, base["sorted"]),
            out_shape=outs,
            grid_spec=pltpu.PrefetchScalarGridSpec(
                num_scalar_prefetch=1,
                grid=grid,
                in_specs=specs,
                out_specs=out_specs,
                scratch_shapes=scratch,
            ),
            compiler_params=pltpu.CompilerParams(
                dimension_semantics=("arbitrary",), vmem_limit_bytes=limit
            ),
            cost_estimate=LITTLE,
            input_output_aliases=dict(alias),
            name=name,
        )(table, *arrays)

    def states_of(s):
        return call(
            state_kernel,
            [ext_shape],
            kv_specs(s) + [map_spec(s)],
            [ext_spec],
            [*kv, *kv, maps],
            [low, low],
            "states",
        )[0]

    def spread(parts, others, when, extra, closing):
        weights = [base["near " + when], base["far " + when], base["seq"]]
        result = whole_call(
            functools.partial(spread_kernel, grp, len(bits), closing, *weights),
            [ext_shape] * grp + [of(F32, heads, map_rows, hd)] * closing,
            table,
            parts + others + extra,
            "spread",
            [pltpu.VMEM((hd, hd), F32)] * closing,
        )
        return [result[0]] + [across(result[s], -s) for s in slots[1:]], result[grp:]

    def totals_of(parts):
        return whole_call(total_kernel, [ext_shape], table, parts, "totals")[0]

    def around_all(total, waits=()):
        others = []
        for i, bit in enumerate(bits):
            if others:
                last = after(others[-1], waits[i - 1]) if i <= len(waits) else others[-1]
                total = totals_of([total, last])
            others.append(twin(total, bit))
        return others

    partial = {s: states_of(s) for s in order}
    parts = [partial[0]] + [across(partial[s], s) for s in slots[1:]]
    bulk = sent_rows(order[0], partial[order[0]])
    rows = {order[0]: bulk}
    parts[0] = after(parts[0], bulk[1])
    others = around_all(totals_of(parts), bulk[2:-1])
    others[-1] = after(others[-1], bulk[-1])
    state, _ = spread(parts, others, "before", [prefix_state, prefix_norm], False)
    for s in order[1:]:
        rows[s] = sent_rows(s, state[0])

    def block_of(s):
        return call(
            block_kernel,
            [of(BF16, part, tok, heads * hd), dk_shape, dv_shape, ext_shape, gm_shape],
            kv_specs(s)
            + piece_specs(lambda h: h, PAIR)
            + piece_specs(lambda h: grid[0] + h, PAIR)
            + [map_spec(s), ext_spec],
            [
                pl.BlockSpec((part, tok, PAIR * hd), lambda h, t: (0, 0, h)),
                dk_spec,
                dv_spec,
                ext_spec,
                gm_spec,
            ],
            [*kv, *kv, *rows[s], *rows[s], maps, state[s]],
            [low, low, pltpu.VMEM((hd, BLK), BF16), wide, wide],
            "blocks",
            limit=LARGE,
        )

    def rows_for(array, device):
        pieces = array.reshape(*array.shape[:-2], fsdp, map_rows, array.shape[-1])
        return lax.dynamic_index_in_dim(pieces, device % fsdp, array.ndim - 2, keepdims=False)

    blocks, parts = {}, {}
    for s in order:
        blocks[s] = block_of(s)
        parts[s] = across(blocks[s][3], s) if s else blocks[s][3]
    parts = [parts[s] for s in slots]
    total = totals_of(parts)
    others = around_all(total)
    suffix, (grad_prefix,) = spread(parts, others, "after", [], True)
    returned = {s: within(after(blocks[s][0], others[0])) for s in order if s}
    suffix[0] = after(suffix[0], *returned.values())

    kv_type = BF16 if replicas == 1 else F32
    pairs = of(kv_type, part, tok, grp * 2 * hd)
    moved, key_gm = [], {}
    for s in slots:
        begun = [] if s == 0 else [pairs]
        pairs, key_gm[s] = call(
            functools.partial(key_kernel, bool(begun)),
            [of(kv_type, *pairs.shape), gm_shape],
            kv_specs(s)
            + [map_spec(s), ext_spec, dk_spec, dv_spec]
            + [pl.BlockSpec(memory_space=pl.ANY)] * len(begun),
            [pl.BlockSpec((part, tok, 2 * hd), lambda h, t: (0, 0, s)), gm_spec],
            [*kv, *kv, maps, suffix[s], blocks[s][1], blocks[s][2], *begun],
            [
                low,
                low,
                pltpu.VMEM((hd, BLK), BF16),
                pltpu.VMEM((hd, BLK), F32),
                pltpu.VMEM((heads * half, BLK), BF16),
                pltpu.VMEM((heads * half, hd), BF16),
            ],
            "keys",
            {2 * part + 5: 0} if begun else {},
        )
        two = jnp.stack([blocks[s][4], key_gm[s]])
        if s:
            moved += [apart(rows_for(two, seq + r), s, r) for r in range(fsdp)]
        else:
            two = after(two, *suffix[1:])
            moved += [along(rows_for(two, seq + r), r) for r in range(1, fsdp)]
            returned[s] = within(after(blocks[s][0], key_gm[s]))

    pairs = within(after(pairs, returned[0]))
    (grad_queries,) = unpack(table, base["owner"], [returned[s] for s in slots], 1, 1, heads * hd)
    grad_keys, grad_values = unpack(table, base["owner"], [pairs], grp, 2, hd)
    if replicas > 1:
        grad_keys, grad_values = (
            jnp.sum(a.reshape(tok, kv_heads, replicas, hd), axis=2)
            .astype(BF16)
            .reshape(tok, kv_heads * hd)
            for a in (grad_keys, grad_values)
        )
    query_map_grad, key_map_grad = whole_call(
        functools.partial(close_kernel, base["seq"]),
        [of(F32, heads, map_rows, half)] * 2,
        table,
        [blocks[0][4], key_gm[0]] + moved,
        "close",
    )
    return grad_queries, grad_keys, grad_values, query_map_grad, key_map_grad, grad_prefix


def solution(mesh):
    rows, maps = P(("fsdp", "ctx"), None), P("ctx", "fsdp", None)
    return jax.shard_map(
        shards,
        mesh=mesh,
        in_specs=(rows,) * 4 + (maps, maps, P("ctx", None, None), P("ctx", None)),
        out_specs=(rows,) * 3 + (maps,) * 3,
        check_vma=False,
    )
```

```python
import functools

import jax
import jax.numpy as jnp
from jax import lax
from jax.experimental import pallas as pl
from jax.experimental.pallas import tpu as pltpu
from jax.sharding import PartitionSpec as P

BLK = 512
TILE = 256
PAIR = 2
EXT = 16
LIMIT = 40 * 1024 * 1024
LARGE = 56 * 1024 * 1024

LITTLE = pl.CostEstimate(flops=1000, bytes_accessed=1000, transcendentals=0)

F32 = jnp.float32
BF16 = jnp.bfloat16
SMEM = pltpu.SMEM


def nn(left, right):
    return lax.dot_general(left, right, (((1,), (0,)), ((), ())), preferred_element_type=F32)


def nt(left, right):
    return lax.dot_general(left, right, (((1,), (1,)), ((), ())), preferred_element_type=F32)


def turned(array):
    return array.astype(F32).T.astype(array.dtype)


def column(row, width):
    n = row.shape[1]
    square = jnp.broadcast_to(row, (n, n)).T
    return jnp.concatenate([square] * (width // n), axis=1)


def thirds(row):
    rows = jnp.broadcast_to(row, (EXT, row.shape[1]))
    high = rows.astype(BF16).astype(F32)
    middle = (rows - high).astype(BF16).astype(F32)
    low = rows - high - middle
    place = lax.broadcasted_iota(jnp.int32, rows.shape, 0)
    picked = jnp.where(place == 0, high, jnp.where(place == 1, middle, low))
    return jnp.where(place < 3, picked, 0.0).astype(BF16)


def whole_row(block):
    return jnp.sum(block.astype(F32), axis=0, keepdims=True)


def weight_rows(ref, u):
    whole = jnp.concatenate([ref[i, u] for i in range(ref.shape[0])], axis=0)
    return turned(whole)


def features(weight, rows):
    logits = nt(weight, rows).astype(BF16).astype(F32)
    upper = jnp.exp(logits)
    lower = jnp.exp(-logits)
    upper = upper * (1.0 / jnp.sum(upper, axis=0, keepdims=True))
    lower = lower * (1.0 / jnp.sum(lower, axis=0, keepdims=True))
    return jnp.concatenate([upper, lower], axis=0)


def feature_back(feats, upstream):
    half = feats.shape[0] // 2
    weighted = feats * upstream
    first, second = weighted[:half], weighted[half:]
    first = first - feats[:half] * jnp.sum(first, axis=0, keepdims=True)
    second = second - feats[half:] * jnp.sum(second, axis=0, keepdims=True)
    return (first - second).astype(BF16)


def gather(table, base, refs, out):
    rows = refs[0].shape[0]
    for r, ref in enumerate(refs):
        out[pl.ds(pl.multiple_of(table[base + r] * rows, rows), rows), :] = ref[...]


def pack_kernel(columns, inputs, table, *refs):
    count = columns * inputs
    for r, out in enumerate(refs[-(len(refs) // (count + 1)) :]):
        width = out.shape[1] // count
        for i in range(count):
            out[:, i * width : (i + 1) * width] = refs[r * count + i][...]


def pack(table, base, sources, pieces, columns, width):
    rows = sources[0].shape[0]
    count = columns * len(sources)
    step = rows // 2

    def take(at):
        return pl.BlockSpec((step, width), lambda i, t: (i, t[base + at]))

    return pl.pallas_call(
        functools.partial(pack_kernel, columns, len(sources)),
        out_shape=[jax.ShapeDtypeStruct((rows, count * width), sources[0].dtype)] * pieces,
        grid_spec=pltpu.PrefetchScalarGridSpec(
            num_scalar_prefetch=1,
            grid=(rows // step,),
            in_specs=[
                take(r * columns + s)
                for r in range(pieces)
                for s in range(columns)
                for _ in sources
            ],
            out_specs=[pl.BlockSpec((step, count * width), lambda i, t: (i, 0))] * pieces,
        ),
        compiler_params=pltpu.CompilerParams(vmem_limit_bytes=LIMIT),
        cost_estimate=LITTLE,
        name="pack",
    )(table, *(list(sources) * (pieces * columns)))


def unpack_kernel(outputs, inner, base, table, *refs):
    sources, outs = refs[:-outputs], refs[-outputs:]
    for s, source in enumerate(sources):
        pieces = source.shape[0]
        width = source.shape[2] // (outputs * inner)
        for r in range(pieces):
            for j in range(inner):
                slot = s * inner + j
                at = table[base + slot * pieces + r] * width
                for i, out in enumerate(outs):
                    lanes = slice((j * outputs + i) * width, (j * outputs + i + 1) * width)
                    out[:, pl.ds(pl.multiple_of(at, width), width)] = source[r, :, lanes]


def unpack(table, base, sources, inner, outputs, width):
    pieces, rows = sources[0].shape[:2]
    total = len(sources) * inner * pieces * width
    step = rows // 2
    taken = pl.BlockSpec((pieces, step, inner * outputs * width), lambda i: (0, i, 0))
    return pl.pallas_call(
        functools.partial(unpack_kernel, outputs, inner, base),
        out_shape=[jax.ShapeDtypeStruct((rows, total), sources[0].dtype)] * outputs,
        grid=(rows // step,),
        in_specs=[pl.BlockSpec(memory_space=SMEM)] + [taken] * len(sources),
        out_specs=[pl.BlockSpec((step, total), lambda i: (i, 0))] * outputs,
        compiler_params=pltpu.CompilerParams(vmem_limit_bytes=LIMIT),
        cost_estimate=LITTLE,
        name="unpack",
    )(table, *sources)


def state_kernel(part, base, table, *refs):
    k_refs, v_refs, (w_ref, out, k_all, v_all) = refs[:part], refs[part : 2 * part], refs[2 * part :]
    hd = k_all.shape[1]

    @pl.when(pl.program_id(0) == 0)
    def _():
        gather(table, base, k_refs, k_all)
        gather(table, base, v_refs, v_all)

    for u in range(out.shape[0]):
        weight = weight_rows(w_ref, u)
        feats = features(weight[weight.shape[0] // 2 :], k_all[...]).astype(BF16)
        out[u, :hd, :] = nn(feats, v_all[...]).astype(BF16)
        ones = jnp.ones((EXT, feats.shape[1]), BF16)
        out[u, hd:, :] = thirds(nt(ones, feats)[:1])


def block_kernel(part, base, table, *refs):
    k_refs, v_refs = refs[:part], refs[part : 2 * part]
    q_refs, g_refs = refs[2 * part : 3 * part], refs[3 * part : 4 * part]
    w_ref, st_ref = refs[4 * part : 4 * part + 2]
    gq_refs = refs[4 * part + 2 : 5 * part + 2]
    dk_ref, dv_ref, sx_ref, gm_ref, k_all, v_all, vt_all, q_all, g_all, gq_all = refs[5 * part + 2 :]
    hd = k_all.shape[1]

    @pl.when(pl.program_id(0) == 0)
    def _():
        gather(table, base, k_refs, k_all)
        gather(table, base, v_refs, v_all)
        vt_all[...] = turned(v_all[...])
        dv_ref[...] = jnp.zeros_like(dv_ref)

    gather(table, base, q_refs, q_all)
    gather(table, base, g_refs, g_all)
    maps = []
    earlier = lax.broadcasted_iota(jnp.int32, (TILE, TILE), 0) <= lax.broadcasted_iota(
        jnp.int32, (TILE, TILE), 1
    )

    def causal(array, begin):
        masked = jnp.where(earlier, array[begin:], 0.0)
        return masked if begin == 0 else jnp.concatenate([array[:begin], masked], axis=0)

    for u in range(PAIR):
        weight = weight_rows(w_ref, u)
        half = weight.shape[0] // 2
        lanes = slice(u * hd, (u + 1) * hd)
        q_feat = features(weight[:half], q_all[:, lanes])
        k_low = features(weight[half:], k_all[...]).astype(BF16)
        q_low = q_feat.astype(BF16)
        k_turned = turned(k_low)
        state = st_ref[u, :hd, :]
        state_turned = turned(state)
        norm = column(whole_row(st_ref[u, hd:, :]), TILE)
        g_turned = g_all[:, lanes].astype(F32).T
        back = []
        dkey = [jnp.zeros((2 * half, TILE), F32) for _ in range(BLK // TILE)]
        dvalue = [jnp.zeros((hd, TILE), F32) for _ in range(BLK // TILE)]
        suffix = jnp.zeros((2 * half, hd), F32)
        suffix_norm = jnp.zeros((2 * half, 1), F32)
        for j in range(BLK // TILE):
            begin, end = j * TILE, (j + 1) * TILE
            own = q_low[:, begin:end]
            own_wide = own.astype(F32)
            scores = causal(nn(k_turned[:end], own), begin)
            scores_low = scores.astype(BF16)
            numerator = nn(state_turned, own) + nn(vt_all[:, :end], scores_low)
            denominator = jnp.sum(own_wide * norm, axis=0, keepdims=True) + jnp.sum(
                scores, axis=0, keepdims=True
            )
            inverse = 1.0 / denominator
            scaled = g_turned[:, begin:end] * inverse
            scaled_low = scaled.astype(BF16)
            norm_grad = -jnp.sum(scaled * (numerator * inverse), axis=0, keepdims=True)
            dscores = causal(nn(v_all[:end, :], scaled_low) + norm_grad, begin).astype(BF16)
            dquery = nn(state, scaled_low) + norm * norm_grad + nn(k_low[:, :end], dscores)
            back.append(feature_back(q_feat[:, begin:end], dquery))
            for i in range(j + 1):
                rows = slice(i * TILE, (i + 1) * TILE)
                dkey[i] = dkey[i] + nt(own, dscores[rows])
                dvalue[i] = dvalue[i] + nt(scaled_low, scores_low[rows])
            suffix = suffix + nt(own, scaled_low)
            suffix_norm = suffix_norm + jnp.sum(own_wide * norm_grad, axis=1, keepdims=True)
        dlog = jnp.concatenate(back, axis=1)
        gq_all[:, lanes] = nn(turned(dlog), weight[:half]).astype(BF16)
        maps.append(nn(dlog, q_all[:, lanes]))
        dk_ref[u] = jnp.concatenate(dkey, axis=1)
        dv_ref[...] += jnp.concatenate(dvalue, axis=1)
        sx_ref[u, :hd, :] = suffix.astype(BF16)
        sx_ref[u, hd:, :] = thirds(jnp.broadcast_to(suffix_norm, (2 * half, 2 * half)).T[:1])
    gm_ref[0] = jnp.concatenate(maps, axis=0).T.astype(gm_ref.dtype)
    for r, ref in enumerate(gq_refs):
        rows = ref.shape[0]
        ref[...] = gq_all[pl.ds(pl.multiple_of(table[base + r] * rows, rows), rows), :]


def key_kernel(begun, part, base, table, *refs):
    k_refs, v_refs = refs[:part], refs[part : 2 * part]
    w_ref, sx_ref, dk_ref, dv_ref = refs[2 * part : 2 * part + 4]
    out, gm_ref, k_all, v_all, vt_all, total, logs, weights = refs[2 * part + 4 + begun :]
    hd = k_all.shape[1]
    step = pl.program_id(0)

    @pl.when(step == 0)
    def _():
        gather(table, base, k_refs, k_all)
        gather(table, base, v_refs, v_all)
        vt_all[...] = turned(v_all[...])
        total[...] = dv_ref[...]

    maps = []
    for u in range(PAIR):
        weight = weight_rows(w_ref, u)
        half = weight.shape[0] // 2
        weight = weight[half:]
        feats = features(weight, k_all[...])
        suffix = sx_ref[u, :hd, :]
        norm = column(whole_row(sx_ref[u, hd:, :]), BLK)
        dlog = feature_back(feats, dk_ref[u] + nn(suffix, vt_all[...]) + norm)
        at = pl.ds(pl.multiple_of((step * PAIR + u) * half, half), half)
        logs[at, :] = dlog
        weights[at, :] = weight
        maps.append(nn(dlog, k_all[...]))
        total[...] += nn(turned(suffix), feats.astype(BF16))
    gm_ref[0] = jnp.concatenate(maps, axis=0).T.astype(gm_ref.dtype)

    @pl.when(step == pl.num_programs(0) - 1)
    def _():
        pair = jnp.concatenate([nn(turned(logs[...]), weights[...]), total[...].T], axis=1)
        out[...] = pair.astype(out.dtype).reshape(out.shape)


def total_kernel(table, *refs):
    out = refs[-1]
    heads, hd = out.shape[0], out.shape[2]
    for h in range(heads):
        out[h, :hd, :] = sum(ref[h, :hd, :].astype(F32) for ref in refs[:-1]).astype(BF16)
        out[h, hd:, :] = thirds(sum(whole_row(ref[h, hd:, :]) for ref in refs[:-1]))


def spread_kernel(grp, others, closing, block_weight, total_weight, at, table, *refs):
    parts, totals, refs = refs[:grp], refs[grp : grp + others], refs[grp + others :]
    if closing:
        outs, grad, scratch = refs[:grp], refs[grp], refs[grp + 1]
    else:
        state_ref, norm_ref, outs = refs[0], refs[1], refs[2:]
    heads, hd = parts[0].shape[0], parts[0].shape[2]
    for h in range(heads):
        states = [ref[h, :hd, :].astype(F32) for ref in parts]
        norms = [whole_row(ref[h, hd:, :]) for ref in parts]
        others_state = [ref[h, :hd, :].astype(F32) for ref in totals]
        others_norm = [whole_row(ref[h, hd:, :]) for ref in totals]
        if closing:
            base, base_norm = jnp.zeros_like(states[0]), jnp.zeros_like(norms[0])
            scratch[...] = sum(states) + sum(others_state)
            rows = grad.shape[1]
            grad[h] = scratch[pl.ds(pl.multiple_of(table[at] * rows, rows), rows), :]
        else:
            base, base_norm = state_ref[h], norm_ref[pl.ds(h, 1), :]
        for i, (state, norm) in enumerate(zip(others_state, others_norm)):
            base = base + table[total_weight + i].astype(F32) * state
            base_norm = base_norm + table[total_weight + i].astype(F32) * norm
        for r, out in enumerate(outs):
            state, norm = base, base_norm
            for i in range(grp):
                if i != r:
                    state = state + table[block_weight + r * grp + i].astype(F32) * states[i]
                    norm = norm + table[block_weight + r * grp + i].astype(F32) * norms[i]
            out[h, :hd, :] = state.astype(BF16)
            out[h, hd:, :] = thirds(norm)


def close_kernel(at, table, q_ref, k_ref, *refs):
    pieces, outs = refs[:-2], refs[-2:]
    for i, (own, out) in enumerate(zip((q_ref, k_ref), outs)):
        rows, half = out.shape[1:]
        mine = pl.ds(pl.multiple_of(table[at] * rows, rows), rows)
        for h in range(own.shape[0]):
            total = own[h, mine, :].astype(F32)
            for ref in pieces:
                total = total + ref[i, h].astype(F32)
            for u in range(PAIR):
                out[h * PAIR + u] = total[:, u * half : (u + 1) * half]


def whole_call(kernel, outs, table, arrays, name, scratch=()):
    return pl.pallas_call(
        kernel,
        out_shape=outs,
        in_specs=[pl.BlockSpec(memory_space=SMEM)]
        + [pl.BlockSpec(memory_space=pltpu.VMEM)] * len(arrays),
        out_specs=[pl.BlockSpec(memory_space=pltpu.VMEM)] * len(outs),
        scratch_shapes=list(scratch),
        compiler_params=pltpu.CompilerParams(vmem_limit_bytes=LIMIT),
        cost_estimate=LITTLE,
        name=name,
    )(table, *arrays)


def after(value, *others):
    return lax.optimization_barrier((value, *others))[0]


def shards(
    query_rows, key_rows, value_rows, grad_out, query_map, key_map, prefix_state, prefix_norm
):
    ctx, fsdp = lax.axis_size("ctx"), lax.axis_size("fsdp")
    tok = query_rows.shape[0]
    heads, map_rows, half = query_map.shape
    hd = map_rows * fsdp
    kv_heads = key_rows.shape[1] // hd
    replicas = ctx // kv_heads
    part = BLK // tok
    grp = ctx // part
    mine = lax.axis_index("ctx")
    at, block, seq = mine % part, mine // part, lax.axis_index("fsdp")
    shifts, slots = range(part), range(grp)
    order = list(reversed(slots))
    grid = (heads // PAIR,)
    blocks_of = [[g * part + p for p in range(part)] for g in slots]

    def within(array):
        return lax.all_to_all(array, "ctx", 0, 0, axis_index_groups=blocks_of, tiled=True)

    def around(array, shift):
        return lax.ppermute(
            array, "ctx", [(d, d // part * part + (d + shift) % part) for d in range(ctx)]
        )

    def across(array, shift):
        return lax.ppermute(array, "ctx", [(d, (d + shift * part) % ctx) for d in range(ctx)])

    def along(array, shift):
        return lax.ppermute(array, "fsdp", [(d, (d + shift) % fsdp) for d in range(fsdp)])

    def twin(array, bit):
        return lax.ppermute(array, "fsdp", [(d, d ^ bit) for d in range(fsdp)])

    def apart(array, s, r):
        moves = [
            (d * fsdp + i, (d + s * part) % ctx * fsdp + (i + r) % fsdp)
            for d in range(ctx)
            for i in range(fsdp)
        ]
        return lax.ppermute(array, ("ctx", "fsdp"), moves)

    slot = [(block + s) % grp for s in slots]
    near = [(block - r) % grp for r in slots]
    bits = [1 << i for i in range(fsdp.bit_length() - 1)]
    lists = {
        "seq": [seq],
        "owner": [slot[s] * part + p for s in slots for p in range(part)],
        "sent": [slot[s] * part + (at + r) % part for s in slots for r in shifts],
        "back": [slot[s] * part + (at + r) % part for s in slots for r in shifts],
        "kv": [
            (slot[s] * part + (at + r) % part) // replicas for r in shifts for s in slots
        ],
        "sorted": [(at - r) % part for r in shifts],
        "near before": [b < a for a in near for b in near],
        "near after": [b > a for a in near for b in near],
        "far before": [(seq ^ bit) < seq for bit in bits],
        "far after": [(seq ^ bit) > seq for bit in bits],
    }
    base, values = {}, []
    for name, entries in lists.items():
        base[name] = len(values)
        values += entries
    table = jnp.stack([jnp.asarray(v, jnp.int32) for v in values])

    own_maps = jnp.concatenate((query_map, key_map), axis=-1)
    near_maps = jnp.stack([own_maps] + [across(own_maps, -s) for s in slots[1:]])
    kv_sent = pack(table, base["kv"], (key_rows, value_rows), part, grp, hd)
    kv = [kv_sent[0]] + [around(kv_sent[r], r) for r in shifts[1:]]
    maps = lax.all_gather(near_maps, "fsdp")

    def sent_rows(s, *earlier):
        sent = pack(
            after(table, *earlier),
            base["sent"] + s * part,
            (query_rows, grad_out),
            part,
            1,
            heads * hd,
        )
        return [sent[0]] + [around(sent[r], r) for r in shifts[1:]]

    def piece_specs(column, count):
        return [pl.BlockSpec((tok, count * hd), lambda h, t: (0, column(h)))] * part

    def kv_specs(s):
        return piece_specs(lambda h: 2 * s, 1) + piece_specs(lambda h: 2 * s + 1, 1)

    def map_spec(s):
        return pl.BlockSpec((fsdp, None, PAIR, map_rows, 2 * half), lambda h, t: (0, s, h, 0, 0))

    def head_spec(*shape):
        return pl.BlockSpec((PAIR, *shape), lambda h, t: (h,) + (0,) * len(shape))

    def of(dtype, *shape):
        return jax.ShapeDtypeStruct(shape, dtype)

    ext_spec, ext_shape = head_spec(hd + EXT, hd), of(BF16, heads, hd + EXT, hd)
    gm_spec = pl.BlockSpec((1, hd, PAIR * half), lambda h, t: (h, 0, 0))
    gm_shape = of(BF16, heads // PAIR, hd, PAIR * half)
    dk_spec, dk_shape = head_spec(2 * half, BLK), of(F32, heads, 2 * half, BLK)
    dv_spec, dv_shape = pl.BlockSpec((hd, BLK), lambda h, t: (0, 0)), of(F32, hd, BLK)
    low, wide = pltpu.VMEM((BLK, hd), BF16), pltpu.VMEM((BLK, PAIR * hd), BF16)

    def call(kernel, outs, specs, out_specs, arrays, scratch, name, alias=(), limit=LIMIT):
        return pl.pallas_call(
            functools.partial(kernel, part, base["sorted"]),
            out_shape=outs,
            grid_spec=pltpu.PrefetchScalarGridSpec(
                num_scalar_prefetch=1,
                grid=grid,
                in_specs=specs,
                out_specs=out_specs,
                scratch_shapes=scratch,
            ),
            compiler_params=pltpu.CompilerParams(
                dimension_semantics=("arbitrary",), vmem_limit_bytes=limit
            ),
            cost_estimate=LITTLE,
            input_output_aliases=dict(alias),
            name=name,
        )(table, *arrays)

    def states_of(s):
        return call(
            state_kernel,
            [ext_shape],
            kv_specs(s) + [map_spec(s)],
            [ext_spec],
            [*kv, *kv, maps],
            [low, low],
            "states",
        )[0]

    def spread(parts, others, when, extra, closing):
        weights = [base["near " + when], base["far " + when], base["seq"]]
        result = whole_call(
            functools.partial(spread_kernel, grp, len(bits), closing, *weights),
            [ext_shape] * grp + [of(F32, heads, map_rows, hd)] * closing,
            table,
            parts + others + extra,
            "spread",
            [pltpu.VMEM((hd, hd), F32)] * closing,
        )
        return [result[0]] + [across(result[s], -s) for s in slots[1:]], result[grp:]

    def totals_of(parts):
        return whole_call(total_kernel, [ext_shape], table, parts, "totals")[0]

    def around_all(total):
        others = []
        for bit in bits:
            total = totals_of([total, others[-1]]) if others else total
            others.append(twin(total, bit))
        return others

    partial = {s: states_of(s) for s in order}
    parts = [partial[0]] + [across(partial[s], s) for s in slots[1:]]
    rows = {order[0]: sent_rows(order[0], near_maps, *kv)}
    parts[0] = after(parts[0], *rows[order[0]])
    others = around_all(totals_of(parts))
    state, _ = spread(parts, others, "before", [prefix_state, prefix_norm], False)
    for s in order[1:]:
        rows[s] = sent_rows(s, state[0])

    def block_of(s):
        return call(
            block_kernel,
            [of(BF16, tok, heads * hd)] * part + [dk_shape, dv_shape, ext_shape, gm_shape],
            kv_specs(s)
            + piece_specs(lambda h: h, PAIR)
            + piece_specs(lambda h: grid[0] + h, PAIR)
            + [map_spec(s), ext_spec],
            piece_specs(lambda h: h, PAIR) + [dk_spec, dv_spec, ext_spec, gm_spec],
            [*kv, *kv, *rows[s], *rows[s], maps, state[s]],
            [low, low, pltpu.VMEM((hd, BLK), BF16), wide, wide, wide],
            "blocks",
            limit=LARGE,
        )

    def rows_for(array, device):
        pieces = array.reshape(*array.shape[:-2], fsdp, map_rows, array.shape[-1])
        return lax.dynamic_index_in_dim(pieces, device % fsdp, array.ndim - 2, keepdims=False)

    blocks, parts = {}, {}
    for s in order:
        result = block_of(s)
        blocks[s] = (result[:part], *result[part:])
        parts[s] = across(blocks[s][3], s) if s else blocks[s][3]
    parts = [parts[s] for s in slots]
    total = totals_of(parts)
    others = around_all(total)
    suffix, (grad_prefix,) = spread(parts, others, "after", [], True)
    def brought_back(s, begin):
        pieces = [after(piece, begin) for piece in blocks[s][0]]
        return [pieces[0]] + [around(pieces[r], -r) for r in shifts[1:]]

    returned = {s: brought_back(s, others[0]) for s in order if s}
    suffix[0] = after(suffix[0], *[piece for s in returned for piece in returned[s]])

    kv_type = BF16 if replicas == 1 else F32
    pairs = of(kv_type, part, tok, grp * 2 * hd)
    moved, key_gm = [], {}
    for s in slots:
        begun = [] if s == 0 else [pairs]
        pairs, key_gm[s] = call(
            functools.partial(key_kernel, bool(begun)),
            [of(kv_type, *pairs.shape), gm_shape],
            kv_specs(s)
            + [map_spec(s), ext_spec, dk_spec, dv_spec]
            + [pl.BlockSpec(memory_space=pl.ANY)] * len(begun),
            [pl.BlockSpec((part, tok, 2 * hd), lambda h, t: (0, 0, s)), gm_spec],
            [*kv, *kv, maps, suffix[s], blocks[s][1], blocks[s][2], *begun],
            [
                low,
                low,
                pltpu.VMEM((hd, BLK), BF16),
                pltpu.VMEM((hd, BLK), F32),
                pltpu.VMEM((heads * half, BLK), BF16),
                pltpu.VMEM((heads * half, hd), BF16),
            ],
            "keys",
            {2 * part + 5: 0} if begun else {},
        )
        two = jnp.stack([blocks[s][4], key_gm[s]])
        if s:
            moved += [apart(rows_for(two, seq + r), s, r) for r in range(fsdp)]
        else:
            two = after(two, *suffix[1:])
            moved += [along(rows_for(two, seq + r), r) for r in range(1, fsdp)]
            returned[s] = brought_back(s, key_gm[s])

    pairs = within(after(pairs, *returned[0]))
    back = [piece[None] for s in slots for piece in returned[s]]
    (grad_queries,) = unpack(table, base["back"], back, 1, 1, heads * hd)
    grad_keys, grad_values = unpack(table, base["owner"], [pairs], grp, 2, hd)
    if replicas > 1:
        grad_keys, grad_values = (
            jnp.sum(a.reshape(tok, kv_heads, replicas, hd), axis=2)
            .astype(BF16)
            .reshape(tok, kv_heads * hd)
            for a in (grad_keys, grad_values)
        )
    query_map_grad, key_map_grad = whole_call(
        functools.partial(close_kernel, base["seq"]),
        [of(F32, heads, map_rows, half)] * 2,
        table,
        [blocks[0][4], key_gm[0]] + moved,
        "close",
    )
    return grad_queries, grad_keys, grad_values, query_map_grad, key_map_grad, grad_prefix


def solution(mesh):
    rows, maps = P(("fsdp", "ctx"), None), P("ctx", "fsdp", None)
    return jax.shard_map(
        shards,
        mesh=mesh,
        in_specs=(rows,) * 4 + (maps, maps, P("ctx", None, None), P("ctx", None)),
        out_specs=(rows,) * 3 + (maps,) * 3,
        check_vma=False,
    )
```

```python
import functools

import jax
import jax.numpy as jnp
from jax import lax
from jax.experimental import pallas as pl
from jax.experimental.pallas import tpu as pltpu
from jax.sharding import PartitionSpec as P

BLK = 512
TILE = 256
PAIR = 2
EXT = 16
LIMIT = 40 * 1024 * 1024
LARGE = 56 * 1024 * 1024

LITTLE = pl.CostEstimate(flops=1000, bytes_accessed=1000, transcendentals=0)

F32 = jnp.float32
BF16 = jnp.bfloat16
SMEM = pltpu.SMEM


def nn(left, right):
    return lax.dot_general(left, right, (((1,), (0,)), ((), ())), preferred_element_type=F32)


def nt(left, right):
    return lax.dot_general(left, right, (((1,), (1,)), ((), ())), preferred_element_type=F32)


def turned(array):
    return array.T


def column(row, width):
    n = row.shape[1]
    square = jnp.broadcast_to(row, (n, n)).T
    return jnp.concatenate([square] * (width // n), axis=1)


def thirds(row):
    rows = jnp.broadcast_to(row, (EXT, row.shape[1]))
    high = rows.astype(BF16).astype(F32)
    middle = (rows - high).astype(BF16).astype(F32)
    low = rows - high - middle
    place = lax.broadcasted_iota(jnp.int32, rows.shape, 0)
    picked = jnp.where(place == 0, high, jnp.where(place == 1, middle, low))
    return jnp.where(place < 3, picked, 0.0).astype(BF16)


def whole_row(block):
    return jnp.sum(block.astype(F32), axis=0, keepdims=True)


def weight_rows(ref, u):
    whole = jnp.concatenate([ref[i, u] for i in range(ref.shape[0])], axis=0)
    return turned(whole)


def features(weight, rows):
    logits = nt(weight, rows).astype(BF16).astype(F32)
    upper = jnp.exp(logits)
    lower = jnp.exp(-logits)
    upper = upper * (1.0 / jnp.sum(upper, axis=0, keepdims=True))
    lower = lower * (1.0 / jnp.sum(lower, axis=0, keepdims=True))
    return jnp.concatenate([upper, lower], axis=0)


def feature_back(feats, upstream):
    half = feats.shape[0] // 2
    weighted = feats * upstream
    first, second = weighted[:half], weighted[half:]
    first = first - feats[:half] * jnp.sum(first, axis=0, keepdims=True)
    second = second - feats[half:] * jnp.sum(second, axis=0, keepdims=True)
    return (first - second).astype(BF16)


def gather(table, base, refs, out):
    rows = refs[0].shape[0]
    for r, ref in enumerate(refs):
        out[pl.ds(pl.multiple_of(table[base + r] * rows, rows), rows), :] = ref[...]


def pack_kernel(columns, inputs, table, *refs):
    count = columns * inputs
    for r, out in enumerate(refs[-(len(refs) // (count + 1)) :]):
        width = out.shape[1] // count
        for i in range(count):
            out[:, i * width : (i + 1) * width] = refs[r * count + i][...]


def pack(table, base, sources, pieces, columns, width):
    rows = sources[0].shape[0]
    count = columns * len(sources)
    step = rows // 2

    def take(at):
        return pl.BlockSpec((step, width), lambda i, t: (i, t[base + at]))

    return pl.pallas_call(
        functools.partial(pack_kernel, columns, len(sources)),
        out_shape=[jax.ShapeDtypeStruct((rows, count * width), sources[0].dtype)] * pieces,
        grid_spec=pltpu.PrefetchScalarGridSpec(
            num_scalar_prefetch=1,
            grid=(rows // step,),
            in_specs=[
                take(r * columns + s)
                for r in range(pieces)
                for s in range(columns)
                for _ in sources
            ],
            out_specs=[pl.BlockSpec((step, count * width), lambda i, t: (i, 0))] * pieces,
        ),
        compiler_params=pltpu.CompilerParams(vmem_limit_bytes=LIMIT),
        cost_estimate=LITTLE,
        name="pack",
    )(table, *(list(sources) * (pieces * columns)))


def unpack_kernel(outputs, inner, base, table, *refs):
    sources, outs = refs[:-outputs], refs[-outputs:]
    for s, source in enumerate(sources):
        pieces = source.shape[0]
        width = source.shape[2] // (outputs * inner)
        for r in range(pieces):
            for j in range(inner):
                slot = s * inner + j
                at = table[base + slot * pieces + r] * width
                for i, out in enumerate(outs):
                    lanes = slice((j * outputs + i) * width, (j * outputs + i + 1) * width)
                    out[:, pl.ds(pl.multiple_of(at, width), width)] = source[r, :, lanes]


def unpack(table, base, sources, inner, outputs, width):
    pieces, rows = sources[0].shape[:2]
    total = len(sources) * inner * pieces * width
    step = rows // 2
    taken = pl.BlockSpec((pieces, step, inner * outputs * width), lambda i: (0, i, 0))
    return pl.pallas_call(
        functools.partial(unpack_kernel, outputs, inner, base),
        out_shape=[jax.ShapeDtypeStruct((rows, total), sources[0].dtype)] * outputs,
        grid=(rows // step,),
        in_specs=[pl.BlockSpec(memory_space=SMEM)] + [taken] * len(sources),
        out_specs=[pl.BlockSpec((step, total), lambda i: (i, 0))] * outputs,
        compiler_params=pltpu.CompilerParams(vmem_limit_bytes=LIMIT),
        cost_estimate=LITTLE,
        name="unpack",
    )(table, *sources)


def state_kernel(part, base, table, *refs):
    k_refs, v_refs, (w_ref, out, k_all, v_all) = refs[:part], refs[part : 2 * part], refs[2 * part :]
    hd = k_all.shape[1]

    @pl.when(pl.program_id(0) == 0)
    def _():
        gather(table, base, k_refs, k_all)
        gather(table, base, v_refs, v_all)

    for u in range(out.shape[0]):
        weight = weight_rows(w_ref, u)
        feats = features(weight[weight.shape[0] // 2 :], k_all[...]).astype(BF16)
        out[u, :hd, :] = nn(feats, v_all[...]).astype(BF16)
        ones = jnp.ones((EXT, feats.shape[1]), BF16)
        out[u, hd:, :] = thirds(nt(ones, feats)[:1])


def block_kernel(part, base, table, *refs):
    k_refs, v_refs = refs[:part], refs[part : 2 * part]
    q_refs, g_refs = refs[2 * part : 3 * part], refs[3 * part : 4 * part]
    w_ref, st_ref = refs[4 * part : 4 * part + 2]
    gq_refs = refs[4 * part + 2 : 5 * part + 2]
    dk_ref, dv_ref, sx_ref, gm_ref, k_all, v_all, vt_all, q_all, g_all, gq_all = refs[5 * part + 2 :]
    hd = k_all.shape[1]

    @pl.when(pl.program_id(0) == 0)
    def _():
        gather(table, base, k_refs, k_all)
        gather(table, base, v_refs, v_all)
        vt_all[...] = turned(v_all[...])
        dv_ref[...] = jnp.zeros_like(dv_ref)

    gather(table, base, q_refs, q_all)
    gather(table, base, g_refs, g_all)
    maps = []
    earlier = lax.broadcasted_iota(jnp.int32, (TILE, TILE), 0) <= lax.broadcasted_iota(
        jnp.int32, (TILE, TILE), 1
    )

    def causal(array, begin):
        masked = jnp.where(earlier, array[begin:], 0.0)
        return masked if begin == 0 else jnp.concatenate([array[:begin], masked], axis=0)

    for u in range(PAIR):
        weight = weight_rows(w_ref, u)
        half = weight.shape[0] // 2
        lanes = slice(u * hd, (u + 1) * hd)
        q_feat = features(weight[:half], q_all[:, lanes])
        k_low = features(weight[half:], k_all[...]).astype(BF16)
        q_low = q_feat.astype(BF16)
        k_turned = turned(k_low)
        state = st_ref[u, :hd, :]
        state_turned = turned(state)
        norm = column(whole_row(st_ref[u, hd:, :]), TILE)
        g_turned = g_all[:, lanes].T.astype(F32)
        back = []
        dkey = [jnp.zeros((2 * half, TILE), F32) for _ in range(BLK // TILE)]
        dvalue = [jnp.zeros((hd, TILE), F32) for _ in range(BLK // TILE)]
        suffix = jnp.zeros((2 * half, hd), F32)
        suffix_norm = jnp.zeros((2 * half, 1), F32)
        for j in range(BLK // TILE):
            begin, end = j * TILE, (j + 1) * TILE
            own = q_low[:, begin:end]
            own_wide = own.astype(F32)
            scores = causal(nn(k_turned[:end], own), begin)
            scores_low = scores.astype(BF16)
            numerator = nn(state_turned, own) + nn(vt_all[:, :end], scores_low)
            denominator = jnp.sum(own_wide * norm, axis=0, keepdims=True) + jnp.sum(
                scores, axis=0, keepdims=True
            )
            inverse = 1.0 / denominator
            scaled = g_turned[:, begin:end] * inverse
            scaled_low = scaled.astype(BF16)
            norm_grad = -jnp.sum(scaled * (numerator * inverse), axis=0, keepdims=True)
            dscores = causal(nn(v_all[:end, :], scaled_low) + norm_grad, begin).astype(BF16)
            dquery = nn(state, scaled_low) + norm * norm_grad + nn(k_low[:, :end], dscores)
            back.append(feature_back(q_feat[:, begin:end], dquery))
            for i in range(j + 1):
                rows = slice(i * TILE, (i + 1) * TILE)
                dkey[i] = dkey[i] + nt(own, dscores[rows])
                dvalue[i] = dvalue[i] + nt(scaled_low, scores_low[rows])
            suffix = suffix + nt(own, scaled_low)
            suffix_norm = suffix_norm + jnp.sum(own_wide * norm_grad, axis=1, keepdims=True)
        dlog = jnp.concatenate(back, axis=1)
        gq_all[:, lanes] = nn(turned(dlog), weight[:half]).astype(BF16)
        maps.append(nn(dlog, q_all[:, lanes]))
        dk_ref[u] = jnp.concatenate(dkey, axis=1)
        dv_ref[...] += jnp.concatenate(dvalue, axis=1)
        sx_ref[u, :hd, :] = suffix.astype(BF16)
        sx_ref[u, hd:, :] = thirds(jnp.broadcast_to(suffix_norm, (2 * half, 2 * half)).T[:1])
    gm_ref[0] = jnp.concatenate(maps, axis=0).T.astype(gm_ref.dtype)
    for r, ref in enumerate(gq_refs):
        rows = ref.shape[0]
        ref[...] = gq_all[pl.ds(pl.multiple_of(table[base + r] * rows, rows), rows), :]


def key_kernel(begun, part, base, table, *refs):
    k_refs, v_refs = refs[:part], refs[part : 2 * part]
    w_ref, sx_ref, dk_ref, dv_ref = refs[2 * part : 2 * part + 4]
    out, gm_ref, k_all, v_all, vt_all, total, logs, weights = refs[2 * part + 4 + begun :]
    hd = k_all.shape[1]
    step = pl.program_id(0)

    @pl.when(step == 0)
    def _():
        gather(table, base, k_refs, k_all)
        gather(table, base, v_refs, v_all)
        vt_all[...] = turned(v_all[...])
        total[...] = dv_ref[...]

    maps = []
    for u in range(PAIR):
        weight = weight_rows(w_ref, u)
        half = weight.shape[0] // 2
        weight = weight[half:]
        feats = features(weight, k_all[...])
        suffix = sx_ref[u, :hd, :]
        norm = column(whole_row(sx_ref[u, hd:, :]), BLK)
        dlog = feature_back(feats, dk_ref[u] + nn(suffix, vt_all[...]) + norm)
        at = pl.ds(pl.multiple_of((step * PAIR + u) * half, half), half)
        logs[at, :] = dlog
        weights[at, :] = weight
        maps.append(nn(dlog, k_all[...]))
        total[...] += nn(turned(suffix), feats.astype(BF16))
    gm_ref[0] = jnp.concatenate(maps, axis=0).T.astype(gm_ref.dtype)

    @pl.when(step == pl.num_programs(0) - 1)
    def _():
        pair = jnp.concatenate([nn(turned(logs[...]), weights[...]), total[...].T], axis=1)
        out[...] = pair.astype(out.dtype).reshape(out.shape)


def total_kernel(table, *refs):
    out = refs[-1]
    heads, hd = out.shape[0], out.shape[2]
    for h in range(heads):
        out[h, :hd, :] = sum(ref[h, :hd, :].astype(F32) for ref in refs[:-1]).astype(BF16)
        out[h, hd:, :] = thirds(sum(whole_row(ref[h, hd:, :]) for ref in refs[:-1]))


def spread_kernel(grp, others, closing, block_weight, total_weight, at, table, *refs):
    parts, totals, refs = refs[:grp], refs[grp : grp + others], refs[grp + others :]
    if closing:
        outs, grad, scratch = refs[:grp], refs[grp], refs[grp + 1]
    else:
        state_ref, norm_ref, outs = refs[0], refs[1], refs[2:]
    heads, hd = parts[0].shape[0], parts[0].shape[2]
    for h in range(heads):
        states = [ref[h, :hd, :].astype(F32) for ref in parts]
        norms = [whole_row(ref[h, hd:, :]) for ref in parts]
        others_state = [ref[h, :hd, :].astype(F32) for ref in totals]
        others_norm = [whole_row(ref[h, hd:, :]) for ref in totals]
        if closing:
            base, base_norm = jnp.zeros_like(states[0]), jnp.zeros_like(norms[0])
            scratch[...] = sum(states) + sum(others_state)
            rows = grad.shape[1]
            grad[h] = scratch[pl.ds(pl.multiple_of(table[at] * rows, rows), rows), :]
        else:
            base, base_norm = state_ref[h], norm_ref[pl.ds(h, 1), :]
        for i, (state, norm) in enumerate(zip(others_state, others_norm)):
            base = base + table[total_weight + i].astype(F32) * state
            base_norm = base_norm + table[total_weight + i].astype(F32) * norm
        for r, out in enumerate(outs):
            state, norm = base, base_norm
            for i in range(grp):
                if i != r:
                    state = state + table[block_weight + r * grp + i].astype(F32) * states[i]
                    norm = norm + table[block_weight + r * grp + i].astype(F32) * norms[i]
            out[h, :hd, :] = state.astype(BF16)
            out[h, hd:, :] = thirds(norm)


def close_kernel(at, table, q_ref, k_ref, *refs):
    pieces, outs = refs[:-2], refs[-2:]
    for i, (own, out) in enumerate(zip((q_ref, k_ref), outs)):
        rows, half = out.shape[1:]
        mine = pl.ds(pl.multiple_of(table[at] * rows, rows), rows)
        for h in range(own.shape[0]):
            total = own[h, mine, :].astype(F32)
            for ref in pieces:
                total = total + ref[i, h].astype(F32)
            for u in range(PAIR):
                out[h * PAIR + u] = total[:, u * half : (u + 1) * half]


def whole_call(kernel, outs, table, arrays, name, scratch=()):
    return pl.pallas_call(
        kernel,
        out_shape=outs,
        in_specs=[pl.BlockSpec(memory_space=SMEM)]
        + [pl.BlockSpec(memory_space=pltpu.VMEM)] * len(arrays),
        out_specs=[pl.BlockSpec(memory_space=pltpu.VMEM)] * len(outs),
        scratch_shapes=list(scratch),
        compiler_params=pltpu.CompilerParams(vmem_limit_bytes=LIMIT),
        cost_estimate=LITTLE,
        name=name,
    )(table, *arrays)


def after(value, *others):
    return lax.optimization_barrier((value, *others))[0]


def shards(
    query_rows, key_rows, value_rows, grad_out, query_map, key_map, prefix_state, prefix_norm
):
    ctx, fsdp = lax.axis_size("ctx"), lax.axis_size("fsdp")
    tok = query_rows.shape[0]
    heads, map_rows, half = query_map.shape
    hd = map_rows * fsdp
    kv_heads = key_rows.shape[1] // hd
    replicas = ctx // kv_heads
    part = BLK // tok
    grp = ctx // part
    mine = lax.axis_index("ctx")
    at, block, seq = mine % part, mine // part, lax.axis_index("fsdp")
    shifts, slots = range(part), range(grp)
    order = list(reversed(slots))
    grid = (heads // PAIR,)
    blocks_of = [[g * part + p for p in range(part)] for g in slots]

    def within(array):
        return lax.all_to_all(array, "ctx", 0, 0, axis_index_groups=blocks_of, tiled=True)

    def around(array, shift):
        return lax.ppermute(
            array, "ctx", [(d, d // part * part + (d + shift) % part) for d in range(ctx)]
        )

    def across(array, shift):
        return lax.ppermute(array, "ctx", [(d, (d + shift * part) % ctx) for d in range(ctx)])

    def along(array, shift):
        return lax.ppermute(array, "fsdp", [(d, (d + shift) % fsdp) for d in range(fsdp)])

    def twin(array, bit):
        return lax.ppermute(array, "fsdp", [(d, d ^ bit) for d in range(fsdp)])

    def apart(array, s, r):
        moves = [
            (d * fsdp + i, (d + s * part) % ctx * fsdp + (i + r) % fsdp)
            for d in range(ctx)
            for i in range(fsdp)
        ]
        return lax.ppermute(array, ("ctx", "fsdp"), moves)

    slot = [(block + s) % grp for s in slots]
    near = [(block - r) % grp for r in slots]
    bits = [1 << i for i in range(fsdp.bit_length() - 1)]
    lists = {
        "seq": [seq],
        "owner": [slot[s] * part + p for s in slots for p in range(part)],
        "sent": [slot[s] * part + (at + r) % part for s in slots for r in shifts],
        "back": [slot[s] * part + (at + r) % part for s in slots for r in shifts],
        "kv": [
            (slot[s] * part + (at + r) % part) // replicas for r in shifts for s in slots
        ],
        "sorted": [(at - r) % part for r in shifts],
        "near before": [b < a for a in near for b in near],
        "near after": [b > a for a in near for b in near],
        "far before": [(seq ^ bit) < seq for bit in bits],
        "far after": [(seq ^ bit) > seq for bit in bits],
    }
    base, values = {}, []
    for name, entries in lists.items():
        base[name] = len(values)
        values += entries
    table = jnp.stack([jnp.asarray(v, jnp.int32) for v in values])

    own_maps = jnp.concatenate((query_map, key_map), axis=-1)
    near_maps = jnp.stack([own_maps] + [across(own_maps, -s) for s in slots[1:]])
    kv_sent = pack(table, base["kv"], (key_rows, value_rows), part, grp, hd)
    kv = [kv_sent[0]] + [around(kv_sent[r], r) for r in shifts[1:]]
    maps = lax.all_gather(near_maps, "fsdp")

    def sent_rows(s, *earlier):
        sent = pack(
            after(table, *earlier),
            base["sent"] + s * part,
            (query_rows, grad_out),
            part,
            1,
            heads * hd,
        )
        return [sent[0]] + [around(sent[r], r) for r in shifts[1:]]

    def piece_specs(column, count):
        return [pl.BlockSpec((tok, count * hd), lambda h, t: (0, column(h)))] * part

    def kv_specs(s):
        return piece_specs(lambda h: 2 * s, 1) + piece_specs(lambda h: 2 * s + 1, 1)

    def map_spec(s):
        return pl.BlockSpec((fsdp, None, PAIR, map_rows, 2 * half), lambda h, t: (0, s, h, 0, 0))

    def head_spec(*shape):
        return pl.BlockSpec((PAIR, *shape), lambda h, t: (h,) + (0,) * len(shape))

    def of(dtype, *shape):
        return jax.ShapeDtypeStruct(shape, dtype)

    ext_spec, ext_shape = head_spec(hd + EXT, hd), of(BF16, heads, hd + EXT, hd)
    gm_spec = pl.BlockSpec((1, hd, PAIR * half), lambda h, t: (h, 0, 0))
    gm_shape = of(BF16, heads // PAIR, hd, PAIR * half)
    dk_spec, dk_shape = head_spec(2 * half, BLK), of(F32, heads, 2 * half, BLK)
    dv_spec, dv_shape = pl.BlockSpec((hd, BLK), lambda h, t: (0, 0)), of(F32, hd, BLK)
    low, wide = pltpu.VMEM((BLK, hd), BF16), pltpu.VMEM((BLK, PAIR * hd), BF16)

    def call(kernel, outs, specs, out_specs, arrays, scratch, name, alias=(), limit=LIMIT):
        return pl.pallas_call(
            functools.partial(kernel, part, base["sorted"]),
            out_shape=outs,
            grid_spec=pltpu.PrefetchScalarGridSpec(
                num_scalar_prefetch=1,
                grid=grid,
                in_specs=specs,
                out_specs=out_specs,
                scratch_shapes=scratch,
            ),
            compiler_params=pltpu.CompilerParams(
                dimension_semantics=("arbitrary",), vmem_limit_bytes=limit
            ),
            cost_estimate=LITTLE,
            input_output_aliases=dict(alias),
            name=name,
        )(table, *arrays)

    def states_of(s):
        return call(
            state_kernel,
            [ext_shape],
            kv_specs(s) + [map_spec(s)],
            [ext_spec],
            [*kv, *kv, maps],
            [low, low],
            "states",
        )[0]

    def spread(parts, others, when, extra, closing):
        weights = [base["near " + when], base["far " + when], base["seq"]]
        result = whole_call(
            functools.partial(spread_kernel, grp, len(bits), closing, *weights),
            [ext_shape] * grp + [of(F32, heads, map_rows, hd)] * closing,
            table,
            parts + others + extra,
            "spread",
            [pltpu.VMEM((hd, hd), F32)] * closing,
        )
        return [result[0]] + [across(result[s], -s) for s in slots[1:]], result[grp:]

    def totals_of(parts):
        return whole_call(total_kernel, [ext_shape], table, parts, "totals")[0]

    def around_all(total):
        others = []
        for bit in bits:
            total = totals_of([total, others[-1]]) if others else total
            others.append(twin(total, bit))
        return others

    partial = {s: states_of(s) for s in order}
    parts = [partial[0]] + [across(partial[s], s) for s in slots[1:]]
    rows = {order[0]: sent_rows(order[0], partial[order[0]])}
    others = around_all(totals_of(parts))
    state, _ = spread(parts, others, "before", [prefix_state, prefix_norm], False)
    for s in order[1:]:
        rows[s] = sent_rows(s, state[0])

    def block_of(s):
        return call(
            block_kernel,
            [of(BF16, tok, heads * hd)] * part + [dk_shape, dv_shape, ext_shape, gm_shape],
            kv_specs(s)
            + piece_specs(lambda h: h, PAIR)
            + piece_specs(lambda h: grid[0] + h, PAIR)
            + [map_spec(s), ext_spec],
            piece_specs(lambda h: h, PAIR) + [dk_spec, dv_spec, ext_spec, gm_spec],
            [*kv, *kv, *rows[s], *rows[s], maps, state[s]],
            [low, low, pltpu.VMEM((hd, BLK), BF16), wide, wide, wide],
            "blocks",
            limit=LARGE,
        )

    def rows_for(array, device):
        pieces = array.reshape(*array.shape[:-2], fsdp, map_rows, array.shape[-1])
        return lax.dynamic_index_in_dim(pieces, device % fsdp, array.ndim - 2, keepdims=False)

    blocks, parts = {}, {}
    for s in order:
        result = block_of(s)
        blocks[s] = (result[:part], *result[part:])
        parts[s] = across(blocks[s][3], s) if s else blocks[s][3]
    parts = [parts[s] for s in slots]
    total = totals_of(parts)
    others = around_all(total)
    suffix, (grad_prefix,) = spread(parts, others, "after", [], True)
    def brought_back(s, begin):
        pieces = [after(piece, begin) for piece in blocks[s][0]]
        return [pieces[0]] + [around(pieces[r], -r) for r in shifts[1:]]

    returned = {s: brought_back(s, others[0]) for s in order if s}
    suffix[0] = after(suffix[0], *[piece for s in returned for piece in returned[s]])

    kv_type = BF16 if replicas == 1 else F32
    pairs = of(kv_type, part, tok, grp * 2 * hd)
    moved, key_gm = [], {}
    for s in slots:
        begun = [] if s == 0 else [pairs]
        pairs, key_gm[s] = call(
            functools.partial(key_kernel, bool(begun)),
            [of(kv_type, *pairs.shape), gm_shape],
            kv_specs(s)
            + [map_spec(s), ext_spec, dk_spec, dv_spec]
            + [pl.BlockSpec(memory_space=pl.ANY)] * len(begun),
            [pl.BlockSpec((part, tok, 2 * hd), lambda h, t: (0, 0, s)), gm_spec],
            [*kv, *kv, maps, suffix[s], blocks[s][1], blocks[s][2], *begun],
            [
                low,
                low,
                pltpu.VMEM((hd, BLK), BF16),
                pltpu.VMEM((hd, BLK), F32),
                pltpu.VMEM((heads * half, BLK), BF16),
                pltpu.VMEM((heads * half, hd), BF16),
            ],
            "keys",
            {2 * part + 5: 0} if begun else {},
        )
        two = jnp.stack([blocks[s][4], key_gm[s]])
        if s:
            moved += [apart(rows_for(two, seq + r), s, r) for r in range(fsdp)]
        else:
            two = after(two, *suffix[1:])
            moved += [along(rows_for(two, seq + r), r) for r in range(1, fsdp)]
            returned[s] = brought_back(s, key_gm[s])

    pairs = within(pairs)
    back = [piece[None] for s in slots for piece in returned[s]]
    (grad_queries,) = unpack(table, base["back"], back, 1, 1, heads * hd)
    grad_keys, grad_values = unpack(table, base["owner"], [pairs], grp, 2, hd)
    if replicas > 1:
        grad_keys, grad_values = (
            jnp.sum(a.reshape(tok, kv_heads, replicas, hd), axis=2)
            .astype(BF16)
            .reshape(tok, kv_heads * hd)
            for a in (grad_keys, grad_values)
        )
    query_map_grad, key_map_grad = whole_call(
        functools.partial(close_kernel, base["seq"]),
        [of(F32, heads, map_rows, half)] * 2,
        table,
        [blocks[0][4], key_gm[0]] + moved,
        "close",
    )
    return grad_queries, grad_keys, grad_values, query_map_grad, key_map_grad, grad_prefix


def solution(mesh):
    rows, maps = P(("fsdp", "ctx"), None), P("ctx", "fsdp", None)
    return jax.shard_map(
        shards,
        mesh=mesh,
        in_specs=(rows,) * 4 + (maps, maps, P("ctx", None, None), P("ctx", None)),
        out_specs=(rows,) * 3 + (maps,) * 3,
        check_vma=False,
    )
```

```python
import functools

import jax
import jax.numpy as jnp
from jax import lax
from jax.experimental import pallas as pl
from jax.experimental.pallas import tpu as pltpu
from jax.sharding import PartitionSpec as P

BLK = 512
TILE = 256
PAIR = 2
EXT = 16
LIMIT = 40 * 1024 * 1024
LARGE = 56 * 1024 * 1024

LITTLE = pl.CostEstimate(flops=1000, bytes_accessed=1000, transcendentals=0)

F32 = jnp.float32
BF16 = jnp.bfloat16
SMEM = pltpu.SMEM


def nn(left, right):
    return lax.dot_general(left, right, (((1,), (0,)), ((), ())), preferred_element_type=F32)


def nt(left, right):
    return lax.dot_general(left, right, (((1,), (1,)), ((), ())), preferred_element_type=F32)


def turned(array):
    return array.T


def column(row, width):
    n = row.shape[1]
    square = jnp.broadcast_to(row, (n, n)).T
    return jnp.concatenate([square] * (width // n), axis=1)


def thirds(row):
    rows = jnp.broadcast_to(row, (EXT, row.shape[1]))
    high = rows.astype(BF16).astype(F32)
    middle = (rows - high).astype(BF16).astype(F32)
    low = rows - high - middle
    place = lax.broadcasted_iota(jnp.int32, rows.shape, 0)
    picked = jnp.where(place == 0, high, jnp.where(place == 1, middle, low))
    return jnp.where(place < 3, picked, 0.0).astype(BF16)


def whole_row(block):
    return jnp.sum(block.astype(F32), axis=0, keepdims=True)


def weight_rows(ref, u):
    whole = jnp.concatenate([ref[i, u] for i in range(ref.shape[0])], axis=0)
    return turned(whole)


def features(weight, rows):
    logits = nt(weight, rows).astype(BF16).astype(F32)
    upper = jnp.exp(logits)
    lower = jnp.exp(-logits)
    upper = upper * (1.0 / jnp.sum(upper, axis=0, keepdims=True))
    lower = lower * (1.0 / jnp.sum(lower, axis=0, keepdims=True))
    return jnp.concatenate([upper, lower], axis=0)


def feature_back(feats, upstream):
    half = feats.shape[0] // 2
    weighted = feats * upstream
    first, second = weighted[:half], weighted[half:]
    first = first - feats[:half] * jnp.sum(first, axis=0, keepdims=True)
    second = second - feats[half:] * jnp.sum(second, axis=0, keepdims=True)
    return (first - second).astype(BF16)


def gather(table, base, refs, out):
    rows = refs[0].shape[0]
    for r, ref in enumerate(refs):
        out[pl.ds(pl.multiple_of(table[base + r] * rows, rows), rows), :] = ref[...]


def pack_kernel(columns, inputs, table, *refs):
    count = columns * inputs
    for r, out in enumerate(refs[-(len(refs) // (count + 1)) :]):
        width = out.shape[1] // count
        for i in range(count):
            out[:, i * width : (i + 1) * width] = refs[r * count + i][...]


def pack(table, base, sources, pieces, columns, width):
    rows = sources[0].shape[0]
    count = columns * len(sources)
    step = rows // 2

    def take(at):
        return pl.BlockSpec((step, width), lambda i, t: (i, t[base + at]))

    return pl.pallas_call(
        functools.partial(pack_kernel, columns, len(sources)),
        out_shape=[jax.ShapeDtypeStruct((rows, count * width), sources[0].dtype)] * pieces,
        grid_spec=pltpu.PrefetchScalarGridSpec(
            num_scalar_prefetch=1,
            grid=(rows // step,),
            in_specs=[
                take(r * columns + s)
                for r in range(pieces)
                for s in range(columns)
                for _ in sources
            ],
            out_specs=[pl.BlockSpec((step, count * width), lambda i, t: (i, 0))] * pieces,
        ),
        compiler_params=pltpu.CompilerParams(vmem_limit_bytes=LIMIT),
        cost_estimate=LITTLE,
        name="pack",
    )(table, *(list(sources) * (pieces * columns)))


def stack_kernel(table, *refs):
    sources, out = refs[:-1], refs[-1]
    width = sources[0].shape[1]
    for i, source in enumerate(sources):
        out[:, i * width : (i + 1) * width] = source[...]


def stacked(table, base, sources, pieces, width):
    rows = sources[0].shape[0]
    total = len(sources) * width
    return pl.pallas_call(
        stack_kernel,
        out_shape=jax.ShapeDtypeStruct((pieces, rows, total), sources[0].dtype),
        grid_spec=pltpu.PrefetchScalarGridSpec(
            num_scalar_prefetch=1,
            grid=(pieces,),
            in_specs=[pl.BlockSpec((rows, width), lambda i, t: (0, t[base + i]))] * len(sources),
            out_specs=pl.BlockSpec((None, rows, total), lambda i, t: (i, 0, 0)),
        ),
        compiler_params=pltpu.CompilerParams(vmem_limit_bytes=LIMIT),
        cost_estimate=LITTLE,
        name="stacked",
    )(table, *sources)


def unpack_kernel(outputs, inner, base, table, *refs):
    sources, outs = refs[:-outputs], refs[-outputs:]
    for s, source in enumerate(sources):
        pieces = source.shape[0]
        width = source.shape[2] // (outputs * inner)
        for r in range(pieces):
            for j in range(inner):
                slot = s * inner + j
                at = table[base + slot * pieces + r] * width
                for i, out in enumerate(outs):
                    lanes = slice((j * outputs + i) * width, (j * outputs + i + 1) * width)
                    out[:, pl.ds(pl.multiple_of(at, width), width)] = source[r, :, lanes]


def unpack(table, base, sources, inner, outputs, width):
    pieces, rows = sources[0].shape[:2]
    total = len(sources) * inner * pieces * width
    step = rows // 2
    taken = pl.BlockSpec((pieces, step, inner * outputs * width), lambda i: (0, i, 0))
    return pl.pallas_call(
        functools.partial(unpack_kernel, outputs, inner, base),
        out_shape=[jax.ShapeDtypeStruct((rows, total), sources[0].dtype)] * outputs,
        grid=(rows // step,),
        in_specs=[pl.BlockSpec(memory_space=SMEM)] + [taken] * len(sources),
        out_specs=[pl.BlockSpec((step, total), lambda i: (i, 0))] * outputs,
        compiler_params=pltpu.CompilerParams(vmem_limit_bytes=LIMIT),
        cost_estimate=LITTLE,
        name="unpack",
    )(table, *sources)


def state_kernel(part, base, table, *refs):
    k_refs, v_refs, (w_ref, out, k_all, v_all) = refs[:part], refs[part : 2 * part], refs[2 * part :]
    hd = k_all.shape[1]

    @pl.when(pl.program_id(0) == 0)
    def _():
        gather(table, base, k_refs, k_all)
        gather(table, base, v_refs, v_all)

    for u in range(out.shape[0]):
        weight = weight_rows(w_ref, u)
        feats = features(weight[weight.shape[0] // 2 :], k_all[...]).astype(BF16)
        out[u, :hd, :] = nn(feats, v_all[...]).astype(BF16)
        ones = jnp.ones((EXT, feats.shape[1]), BF16)
        out[u, hd:, :] = thirds(nt(ones, feats)[:1])


def block_kernel(part, base, table, *refs):
    k_refs, v_refs = refs[:part], refs[part : 2 * part]
    q_refs, g_refs = refs[2 * part : 3 * part], refs[3 * part : 4 * part]
    w_ref, st_ref = refs[4 * part : 4 * part + 2]
    gq_refs = refs[4 * part + 2 : 5 * part + 2]
    dk_ref, dv_ref, sx_ref, gm_ref, k_all, v_all, vt_all, q_all, g_all, gq_all = refs[5 * part + 2 :]
    hd = k_all.shape[1]

    @pl.when(pl.program_id(0) == 0)
    def _():
        gather(table, base, k_refs, k_all)
        gather(table, base, v_refs, v_all)
        vt_all[...] = turned(v_all[...])
        dv_ref[...] = jnp.zeros_like(dv_ref)

    gather(table, base, q_refs, q_all)
    gather(table, base, g_refs, g_all)
    maps = []
    earlier = lax.broadcasted_iota(jnp.int32, (TILE, TILE), 0) <= lax.broadcasted_iota(
        jnp.int32, (TILE, TILE), 1
    )

    def causal(array, begin):
        masked = jnp.where(earlier, array[begin:], 0.0)
        return masked if begin == 0 else jnp.concatenate([array[:begin], masked], axis=0)

    for u in range(PAIR):
        weight = weight_rows(w_ref, u)
        half = weight.shape[0] // 2
        lanes = slice(u * hd, (u + 1) * hd)
        q_feat = features(weight[:half], q_all[:, lanes])
        k_low = features(weight[half:], k_all[...]).astype(BF16)
        q_low = q_feat.astype(BF16)
        k_turned = turned(k_low)
        state = st_ref[u, :hd, :]
        state_turned = turned(state)
        norm = column(whole_row(st_ref[u, hd:, :]), TILE)
        g_turned = g_all[:, lanes].T.astype(F32)
        back = []
        dkey = [jnp.zeros((2 * half, TILE), F32) for _ in range(BLK // TILE)]
        dvalue = [jnp.zeros((hd, TILE), F32) for _ in range(BLK // TILE)]
        suffix = jnp.zeros((2 * half, hd), F32)
        suffix_norm = jnp.zeros((2 * half, 1), F32)
        for j in range(BLK // TILE):
            begin, end = j * TILE, (j + 1) * TILE
            own = q_low[:, begin:end]
            own_wide = own.astype(F32)
            scores = causal(nn(k_turned[:end], own), begin)
            scores_low = scores.astype(BF16)
            numerator = nn(state_turned, own) + nn(vt_all[:, :end], scores_low)
            denominator = jnp.sum(own_wide * norm, axis=0, keepdims=True) + jnp.sum(
                scores, axis=0, keepdims=True
            )
            inverse = 1.0 / denominator
            scaled = g_turned[:, begin:end] * inverse
            scaled_low = scaled.astype(BF16)
            norm_grad = -jnp.sum(scaled * (numerator * inverse), axis=0, keepdims=True)
            dscores = causal(nn(v_all[:end, :], scaled_low) + norm_grad, begin).astype(BF16)
            dquery = nn(state, scaled_low) + norm * norm_grad + nn(k_low[:, :end], dscores)
            back.append(feature_back(q_feat[:, begin:end], dquery))
            for i in range(j + 1):
                rows = slice(i * TILE, (i + 1) * TILE)
                dkey[i] = dkey[i] + nt(own, dscores[rows])
                dvalue[i] = dvalue[i] + nt(scaled_low, scores_low[rows])
            suffix = suffix + nt(own, scaled_low)
            suffix_norm = suffix_norm + jnp.sum(own_wide * norm_grad, axis=1, keepdims=True)
        dlog = jnp.concatenate(back, axis=1)
        gq_all[:, lanes] = nn(turned(dlog), weight[:half]).astype(BF16)
        maps.append(nn(dlog, q_all[:, lanes]))
        dk_ref[u] = jnp.concatenate(dkey, axis=1)
        dv_ref[...] += jnp.concatenate(dvalue, axis=1)
        sx_ref[u, :hd, :] = suffix.astype(BF16)
        sx_ref[u, hd:, :] = thirds(jnp.broadcast_to(suffix_norm, (2 * half, 2 * half)).T[:1])
    gm_ref[0] = jnp.concatenate(maps, axis=0).T.astype(gm_ref.dtype)
    for r, ref in enumerate(gq_refs):
        rows = ref.shape[0]
        ref[...] = gq_all[pl.ds(pl.multiple_of(table[base + r] * rows, rows), rows), :]


def key_kernel(begun, part, base, table, *refs):
    k_refs, v_refs = refs[:part], refs[part : 2 * part]
    w_ref, sx_ref, dk_ref, dv_ref = refs[2 * part : 2 * part + 4]
    out, gm_ref, k_all, v_all, vt_all, total, logs, weights = refs[2 * part + 4 + begun :]
    hd = k_all.shape[1]
    step = pl.program_id(0)

    @pl.when(step == 0)
    def _():
        gather(table, base, k_refs, k_all)
        gather(table, base, v_refs, v_all)
        vt_all[...] = turned(v_all[...])
        total[...] = dv_ref[...]

    maps = []
    for u in range(PAIR):
        weight = weight_rows(w_ref, u)
        half = weight.shape[0] // 2
        weight = weight[half:]
        feats = features(weight, k_all[...])
        suffix = sx_ref[u, :hd, :]
        norm = column(whole_row(sx_ref[u, hd:, :]), BLK)
        dlog = feature_back(feats, dk_ref[u] + nn(suffix, vt_all[...]) + norm)
        at = pl.ds(pl.multiple_of((step * PAIR + u) * half, half), half)
        logs[at, :] = dlog
        weights[at, :] = weight
        maps.append(nn(dlog, k_all[...]))
        total[...] += nn(turned(suffix), feats.astype(BF16))
    gm_ref[0] = jnp.concatenate(maps, axis=0).T.astype(gm_ref.dtype)

    @pl.when(step == pl.num_programs(0) - 1)
    def _():
        pair = jnp.concatenate([nn(turned(logs[...]), weights[...]), total[...].T], axis=1)
        out[...] = pair.astype(out.dtype).reshape(out.shape)


def total_kernel(table, *refs):
    out = refs[-1]
    heads, hd = out.shape[0], out.shape[2]
    for h in range(heads):
        out[h, :hd, :] = sum(ref[h, :hd, :].astype(F32) for ref in refs[:-1]).astype(BF16)
        out[h, hd:, :] = thirds(sum(whole_row(ref[h, hd:, :]) for ref in refs[:-1]))


def spread_kernel(grp, others, closing, block_weight, total_weight, at, table, *refs):
    parts, totals, refs = refs[:grp], refs[grp : grp + others], refs[grp + others :]
    if closing:
        outs, grad, scratch = refs[:grp], refs[grp], refs[grp + 1]
    else:
        state_ref, norm_ref, outs = refs[0], refs[1], refs[2:]
    heads, hd = parts[0].shape[0], parts[0].shape[2]
    for h in range(heads):
        states = [ref[h, :hd, :].astype(F32) for ref in parts]
        norms = [whole_row(ref[h, hd:, :]) for ref in parts]
        others_state = [ref[h, :hd, :].astype(F32) for ref in totals]
        others_norm = [whole_row(ref[h, hd:, :]) for ref in totals]
        if closing:
            base, base_norm = jnp.zeros_like(states[0]), jnp.zeros_like(norms[0])
            scratch[...] = sum(states) + sum(others_state)
            rows = grad.shape[1]
            grad[h] = scratch[pl.ds(pl.multiple_of(table[at] * rows, rows), rows), :]
        else:
            base, base_norm = state_ref[h], norm_ref[pl.ds(h, 1), :]
        for i, (state, norm) in enumerate(zip(others_state, others_norm)):
            base = base + table[total_weight + i].astype(F32) * state
            base_norm = base_norm + table[total_weight + i].astype(F32) * norm
        for r, out in enumerate(outs):
            state, norm = base, base_norm
            for i in range(grp):
                if i != r:
                    state = state + table[block_weight + r * grp + i].astype(F32) * states[i]
                    norm = norm + table[block_weight + r * grp + i].astype(F32) * norms[i]
            out[h, :hd, :] = state.astype(BF16)
            out[h, hd:, :] = thirds(norm)


def close_kernel(at, table, q_ref, k_ref, *refs):
    pieces, outs = refs[:-2], refs[-2:]
    for i, (own, out) in enumerate(zip((q_ref, k_ref), outs)):
        rows, half = out.shape[1:]
        mine = pl.ds(pl.multiple_of(table[at] * rows, rows), rows)
        for h in range(own.shape[0]):
            total = own[h, mine, :].astype(F32)
            for ref in pieces:
                total = total + ref[i, h].astype(F32)
            for u in range(PAIR):
                out[h * PAIR + u] = total[:, u * half : (u + 1) * half]


def whole_call(kernel, outs, table, arrays, name, scratch=()):
    return pl.pallas_call(
        kernel,
        out_shape=outs,
        in_specs=[pl.BlockSpec(memory_space=SMEM)]
        + [pl.BlockSpec(memory_space=pltpu.VMEM)] * len(arrays),
        out_specs=[pl.BlockSpec(memory_space=pltpu.VMEM)] * len(outs),
        scratch_shapes=list(scratch),
        compiler_params=pltpu.CompilerParams(vmem_limit_bytes=LIMIT),
        cost_estimate=LITTLE,
        name=name,
    )(table, *arrays)


def after(value, *others):
    return lax.optimization_barrier((value, *others))[0]


def shards(
    query_rows, key_rows, value_rows, grad_out, query_map, key_map, prefix_state, prefix_norm
):
    ctx, fsdp = lax.axis_size("ctx"), lax.axis_size("fsdp")
    tok = query_rows.shape[0]
    heads, map_rows, half = query_map.shape
    hd = map_rows * fsdp
    kv_heads = key_rows.shape[1] // hd
    replicas = ctx // kv_heads
    part = BLK // tok
    grp = ctx // part
    mine = lax.axis_index("ctx")
    at, block, seq = mine % part, mine // part, lax.axis_index("fsdp")
    shifts, slots = range(part), range(grp)
    order = list(reversed(slots))
    grid = (heads // PAIR,)
    blocks_of = [[g * part + p for p in range(part)] for g in slots]

    def within(array):
        return lax.all_to_all(array, "ctx", 0, 0, axis_index_groups=blocks_of, tiled=True)

    def around(array, shift):
        return lax.ppermute(
            array, "ctx", [(d, d // part * part + (d + shift) % part) for d in range(ctx)]
        )

    def across(array, shift):
        return lax.ppermute(array, "ctx", [(d, (d + shift * part) % ctx) for d in range(ctx)])

    def along(array, shift):
        return lax.ppermute(array, "fsdp", [(d, (d + shift) % fsdp) for d in range(fsdp)])

    def twin(array, bit):
        return lax.ppermute(array, "fsdp", [(d, d ^ bit) for d in range(fsdp)])

    def apart(array, s, r):
        moves = [
            (d * fsdp + i, (d + s * part) % ctx * fsdp + (i + r) % fsdp)
            for d in range(ctx)
            for i in range(fsdp)
        ]
        return lax.ppermute(array, ("ctx", "fsdp"), moves)

    slot = [(block + s) % grp for s in slots]
    near = [(block - r) % grp for r in slots]
    bits = [1 << i for i in range(fsdp.bit_length() - 1)]
    lists = {
        "seq": [seq],
        "owner": [slot[s] * part + p for s in slots for p in range(part)],
        "sent": [slot[s] * part + (at + r) % part for s in slots for r in shifts],
        "back": [slot[s] * part + (at + r) % part for s in slots for r in shifts],
        "kv": [
            (slot[s] * part + (at + r) % part) // replicas for r in shifts for s in slots
        ],
        "sorted": [(at - r) % part for r in shifts],
        "near before": [b < a for a in near for b in near],
        "near after": [b > a for a in near for b in near],
        "far before": [(seq ^ bit) < seq for bit in bits],
        "far after": [(seq ^ bit) > seq for bit in bits],
    }
    base, values = {}, []
    for name, entries in lists.items():
        base[name] = len(values)
        values += entries
    table = jnp.stack([jnp.asarray(v, jnp.int32) for v in values])

    own_maps = jnp.concatenate((query_map, key_map), axis=-1)
    near_maps = jnp.stack([own_maps] + [across(own_maps, -s) for s in slots[1:]])
    kv_sent = pack(table, base["kv"], (key_rows, value_rows), part, grp, hd)
    kv = [kv_sent[0]] + [around(kv_sent[r], r) for r in shifts[1:]]
    maps = lax.all_gather(near_maps, "fsdp")

    def sent_rows(s, *earlier):
        sent = pack(
            after(table, *earlier),
            base["sent"] + s * part,
            (query_rows, grad_out),
            part,
            1,
            heads * hd,
        )
        return [sent[0]] + [around(sent[r], r) for r in shifts[1:]]

    def piece_specs(column, count):
        return [pl.BlockSpec((tok, count * hd), lambda h, t: (0, column(h)))] * part

    def kv_specs(s):
        return piece_specs(lambda h: 2 * s, 1) + piece_specs(lambda h: 2 * s + 1, 1)

    def map_spec(s):
        return pl.BlockSpec((fsdp, None, PAIR, map_rows, 2 * half), lambda h, t: (0, s, h, 0, 0))

    def head_spec(*shape):
        return pl.BlockSpec((PAIR, *shape), lambda h, t: (h,) + (0,) * len(shape))

    def of(dtype, *shape):
        return jax.ShapeDtypeStruct(shape, dtype)

    ext_spec, ext_shape = head_spec(hd + EXT, hd), of(BF16, heads, hd + EXT, hd)
    gm_spec = pl.BlockSpec((1, hd, PAIR * half), lambda h, t: (h, 0, 0))
    gm_shape = of(BF16, heads // PAIR, hd, PAIR * half)
    dk_spec, dk_shape = head_spec(2 * half, BLK), of(F32, heads, 2 * half, BLK)
    dv_spec, dv_shape = pl.BlockSpec((hd, BLK), lambda h, t: (0, 0)), of(F32, hd, BLK)
    low, wide = pltpu.VMEM((BLK, hd), BF16), pltpu.VMEM((BLK, PAIR * hd), BF16)

    def call(kernel, outs, specs, out_specs, arrays, scratch, name, alias=(), limit=LIMIT):
        return pl.pallas_call(
            functools.partial(kernel, part, base["sorted"]),
            out_shape=outs,
            grid_spec=pltpu.PrefetchScalarGridSpec(
                num_scalar_prefetch=1,
                grid=grid,
                in_specs=specs,
                out_specs=out_specs,
                scratch_shapes=scratch,
            ),
            compiler_params=pltpu.CompilerParams(
                dimension_semantics=("arbitrary",), vmem_limit_bytes=limit
            ),
            cost_estimate=LITTLE,
            input_output_aliases=dict(alias),
            name=name,
        )(table, *arrays)

    def states_of(s):
        return call(
            state_kernel,
            [ext_shape],
            kv_specs(s) + [map_spec(s)],
            [ext_spec],
            [*kv, *kv, maps],
            [low, low],
            "states",
        )[0]

    def spread(parts, others, when, extra, closing):
        weights = [base["near " + when], base["far " + when], base["seq"]]
        result = whole_call(
            functools.partial(spread_kernel, grp, len(bits), closing, *weights),
            [ext_shape] * grp + [of(F32, heads, map_rows, hd)] * closing,
            table,
            parts + others + extra,
            "spread",
            [pltpu.VMEM((hd, hd), F32)] * closing,
        )
        return [result[0]] + [across(result[s], -s) for s in slots[1:]], result[grp:]

    def totals_of(parts):
        return whole_call(total_kernel, [ext_shape], table, parts, "totals")[0]

    def around_all(total):
        others = []
        for bit in bits:
            total = totals_of([total, others[-1]]) if others else total
            others.append(twin(total, bit))
        return others

    partial = {s: states_of(s) for s in order}
    parts = [partial[0]] + [across(partial[s], s) for s in slots[1:]]
    bulk = stacked(
        after(table, partial[0]),
        base["owner"] + order[0] * part,
        (query_rows, grad_out),
        part,
        heads * hd,
    )
    bulk = lax.all_to_all(bulk, "ctx", 0, 0, axis_index_groups=blocks_of, tiled=True)
    rows = {order[0]: [bulk] * part}
    others = around_all(totals_of(parts))
    state, _ = spread(parts, others, "before", [prefix_state, prefix_norm], False)
    for s in order[1:]:
        rows[s] = sent_rows(s, state[0])

    def row_specs(s, column):
        if rows[s][0].ndim == 2:
            return piece_specs(column, PAIR)

        def spec(r):
            return pl.BlockSpec(
                (None, tok, PAIR * hd), lambda h, t: (t[base["sorted"] + r], 0, column(h))
            )

        return [spec(r) for r in shifts]

    def block_of(s):
        return call(
            block_kernel,
            [of(BF16, tok, heads * hd)] * part + [dk_shape, dv_shape, ext_shape, gm_shape],
            kv_specs(s)
            + row_specs(s, lambda h: h)
            + row_specs(s, lambda h: grid[0] + h)
            + [map_spec(s), ext_spec],
            piece_specs(lambda h: h, PAIR) + [dk_spec, dv_spec, ext_spec, gm_spec],
            [*kv, *kv, *rows[s], *rows[s], maps, state[s]],
            [low, low, pltpu.VMEM((hd, BLK), BF16), wide, wide, wide],
            "blocks",
            limit=LARGE,
        )

    def rows_for(array, device):
        pieces = array.reshape(*array.shape[:-2], fsdp, map_rows, array.shape[-1])
        return lax.dynamic_index_in_dim(pieces, device % fsdp, array.ndim - 2, keepdims=False)

    blocks, parts = {}, {}
    for s in order:
        result = block_of(s)
        blocks[s] = (result[:part], *result[part:])
        parts[s] = across(blocks[s][3], s) if s else blocks[s][3]
    parts = [parts[s] for s in slots]
    total = totals_of(parts)
    others = around_all(total)
    suffix, (grad_prefix,) = spread(parts, others, "after", [], True)
    def brought_back(s, begin):
        pieces = [after(piece, begin) for piece in blocks[s][0]]
        return [pieces[0]] + [around(pieces[r], -r) for r in shifts[1:]]

    returned = {s: brought_back(s, others[0]) for s in order if s}
    suffix[0] = after(suffix[0], *[piece for s in returned for piece in returned[s]])

    kv_type = BF16 if replicas == 1 else F32
    pairs = of(kv_type, part, tok, grp * 2 * hd)
    moved, key_gm = [], {}
    for s in slots:
        begun = [] if s == 0 else [pairs]
        pairs, key_gm[s] = call(
            functools.partial(key_kernel, bool(begun)),
            [of(kv_type, *pairs.shape), gm_shape],
            kv_specs(s)
            + [map_spec(s), ext_spec, dk_spec, dv_spec]
            + [pl.BlockSpec(memory_space=pl.ANY)] * len(begun),
            [pl.BlockSpec((part, tok, 2 * hd), lambda h, t: (0, 0, s)), gm_spec],
            [*kv, *kv, maps, suffix[s], blocks[s][1], blocks[s][2], *begun],
            [
                low,
                low,
                pltpu.VMEM((hd, BLK), BF16),
                pltpu.VMEM((hd, BLK), F32),
                pltpu.VMEM((heads * half, BLK), BF16),
                pltpu.VMEM((heads * half, hd), BF16),
            ],
            "keys",
            {2 * part + 5: 0} if begun else {},
        )
        two = jnp.stack([blocks[s][4], key_gm[s]])
        if s:
            two = after(two, *returned[0])
            moved += [apart(rows_for(two, seq + r), s, r) for r in range(fsdp)]
        else:
            two = after(two, *suffix[1:])
            moved += [along(rows_for(two, seq + r), r) for r in range(1, fsdp)]
            returned[s] = brought_back(s, key_gm[s])

    pairs = within(pairs)
    back = [piece[None] for s in slots for piece in returned[s]]
    (grad_queries,) = unpack(table, base["back"], back, 1, 1, heads * hd)
    grad_keys, grad_values = unpack(table, base["owner"], [pairs], grp, 2, hd)
    if replicas > 1:
        grad_keys, grad_values = (
            jnp.sum(a.reshape(tok, kv_heads, replicas, hd), axis=2)
            .astype(BF16)
            .reshape(tok, kv_heads * hd)
            for a in (grad_keys, grad_values)
        )
    query_map_grad, key_map_grad = whole_call(
        functools.partial(close_kernel, base["seq"]),
        [of(F32, heads, map_rows, half)] * 2,
        table,
        [blocks[0][4], key_gm[0]] + moved,
        "close",
    )
    return grad_queries, grad_keys, grad_values, query_map_grad, key_map_grad, grad_prefix


def solution(mesh):
    rows, maps = P(("fsdp", "ctx"), None), P("ctx", "fsdp", None)
    return jax.shard_map(
        shards,
        mesh=mesh,
        in_specs=(rows,) * 4 + (maps, maps, P("ctx", None, None), P("ctx", None)),
        out_specs=(rows,) * 3 + (maps,) * 3,
        check_vma=False,
    )
```

```python
import functools

import jax
import jax.numpy as jnp
from jax import lax
from jax.experimental import pallas as pl
from jax.experimental.pallas import tpu as pltpu
from jax.sharding import PartitionSpec as P

BLK = 512
TILE = 256
PAIR = 2
EXT = 16
LIMIT = 40 * 1024 * 1024
LARGE = 56 * 1024 * 1024

LITTLE = pl.CostEstimate(flops=1000, bytes_accessed=1000, transcendentals=0)

F32 = jnp.float32
BF16 = jnp.bfloat16
SMEM = pltpu.SMEM


def nn(left, right):
    return lax.dot_general(left, right, (((1,), (0,)), ((), ())), preferred_element_type=F32)


def nt(left, right):
    return lax.dot_general(left, right, (((1,), (1,)), ((), ())), preferred_element_type=F32)


def turned(array):
    return array.T


def column(row, width):
    n = row.shape[1]
    square = jnp.broadcast_to(row, (n, n)).T
    return jnp.concatenate([square] * (width // n), axis=1)


def thirds(row):
    rows = jnp.broadcast_to(row, (EXT, row.shape[1]))
    high = rows.astype(BF16).astype(F32)
    middle = (rows - high).astype(BF16).astype(F32)
    low = rows - high - middle
    place = lax.broadcasted_iota(jnp.int32, rows.shape, 0)
    picked = jnp.where(place == 0, high, jnp.where(place == 1, middle, low))
    return jnp.where(place < 3, picked, 0.0).astype(BF16)


def whole_row(block):
    return jnp.sum(block.astype(F32), axis=0, keepdims=True)


def weight_rows(ref, u):
    whole = jnp.concatenate([ref[i, u] for i in range(ref.shape[0])], axis=0)
    return turned(whole)


def features(weight, rows):
    logits = nt(weight, rows).astype(BF16).astype(F32)
    upper = jnp.exp(logits)
    lower = jnp.exp(-logits)
    upper = upper * (1.0 / jnp.sum(upper, axis=0, keepdims=True))
    lower = lower * (1.0 / jnp.sum(lower, axis=0, keepdims=True))
    return jnp.concatenate([upper, lower], axis=0)


def feature_back(feats, upstream):
    half = feats.shape[0] // 2
    weighted = feats * upstream
    first, second = weighted[:half], weighted[half:]
    first = first - feats[:half] * jnp.sum(first, axis=0, keepdims=True)
    second = second - feats[half:] * jnp.sum(second, axis=0, keepdims=True)
    return (first - second).astype(BF16)


def gather(table, base, refs, out):
    rows = refs[0].shape[0]
    for r, ref in enumerate(refs):
        out[pl.ds(pl.multiple_of(table[base + r] * rows, rows), rows), :] = ref[...]


def pack_kernel(columns, inputs, table, *refs):
    count = columns * inputs
    for r, out in enumerate(refs[-(len(refs) // (count + 1)) :]):
        width = out.shape[1] // count
        for i in range(count):
            out[:, i * width : (i + 1) * width] = refs[r * count + i][...]


def pack(table, base, sources, pieces, columns, width):
    rows = sources[0].shape[0]
    count = columns * len(sources)
    step = rows // 2

    def take(at):
        return pl.BlockSpec((step, width), lambda i, t: (i, t[base + at]))

    return pl.pallas_call(
        functools.partial(pack_kernel, columns, len(sources)),
        out_shape=[jax.ShapeDtypeStruct((rows, count * width), sources[0].dtype)] * pieces,
        grid_spec=pltpu.PrefetchScalarGridSpec(
            num_scalar_prefetch=1,
            grid=(rows // step,),
            in_specs=[
                take(r * columns + s)
                for r in range(pieces)
                for s in range(columns)
                for _ in sources
            ],
            out_specs=[pl.BlockSpec((step, count * width), lambda i, t: (i, 0))] * pieces,
        ),
        compiler_params=pltpu.CompilerParams(vmem_limit_bytes=LIMIT),
        cost_estimate=LITTLE,
        name="pack",
    )(table, *(list(sources) * (pieces * columns)))


def stack_kernel(table, *refs):
    sources, out = refs[:-1], refs[-1]
    width = sources[0].shape[1]
    for i, source in enumerate(sources):
        out[:, i * width : (i + 1) * width] = source[...]


def stacked(table, base, sources, pieces, width):
    rows = sources[0].shape[0]
    total = len(sources) * width
    return pl.pallas_call(
        stack_kernel,
        out_shape=jax.ShapeDtypeStruct((pieces, rows, total), sources[0].dtype),
        grid_spec=pltpu.PrefetchScalarGridSpec(
            num_scalar_prefetch=1,
            grid=(pieces,),
            in_specs=[pl.BlockSpec((rows, width), lambda i, t: (0, t[base + i]))] * len(sources),
            out_specs=pl.BlockSpec((None, rows, total), lambda i, t: (i, 0, 0)),
        ),
        compiler_params=pltpu.CompilerParams(vmem_limit_bytes=LIMIT),
        cost_estimate=LITTLE,
        name="stacked",
    )(table, *sources)


def unpack_kernel(outputs, inner, base, table, *refs):
    sources, outs = refs[:-outputs], refs[-outputs:]
    for s, source in enumerate(sources):
        pieces = source.shape[0]
        width = source.shape[2] // (outputs * inner)
        for r in range(pieces):
            for j in range(inner):
                slot = s * inner + j
                at = table[base + slot * pieces + r] * width
                for i, out in enumerate(outs):
                    lanes = slice((j * outputs + i) * width, (j * outputs + i + 1) * width)
                    out[:, pl.ds(pl.multiple_of(at, width), width)] = source[r, :, lanes]


def unpack(table, base, sources, inner, outputs, width):
    pieces, rows = sources[0].shape[:2]
    total = len(sources) * inner * pieces * width
    step = rows // 2
    taken = pl.BlockSpec((pieces, step, inner * outputs * width), lambda i: (0, i, 0))
    return pl.pallas_call(
        functools.partial(unpack_kernel, outputs, inner, base),
        out_shape=[jax.ShapeDtypeStruct((rows, total), sources[0].dtype)] * outputs,
        grid=(rows // step,),
        in_specs=[pl.BlockSpec(memory_space=SMEM)] + [taken] * len(sources),
        out_specs=[pl.BlockSpec((step, total), lambda i: (i, 0))] * outputs,
        compiler_params=pltpu.CompilerParams(vmem_limit_bytes=LIMIT),
        cost_estimate=LITTLE,
        name="unpack",
    )(table, *sources)


def state_kernel(part, base, table, *refs):
    k_refs, v_refs, (w_ref, out, k_all, v_all) = refs[:part], refs[part : 2 * part], refs[2 * part :]
    hd = k_all.shape[1]

    @pl.when(pl.program_id(0) == 0)
    def _():
        gather(table, base, k_refs, k_all)
        gather(table, base, v_refs, v_all)

    for u in range(out.shape[0]):
        weight = weight_rows(w_ref, u)
        feats = features(weight[weight.shape[0] // 2 :], k_all[...]).astype(BF16)
        out[u, :hd, :] = nn(feats, v_all[...]).astype(BF16)
        ones = jnp.ones((EXT, feats.shape[1]), BF16)
        out[u, hd:, :] = thirds(nt(ones, feats)[:1])


def block_kernel(part, base, table, *refs):
    k_refs, v_refs = refs[:part], refs[part : 2 * part]
    q_refs, g_refs = refs[2 * part : 3 * part], refs[3 * part : 4 * part]
    w_ref, st_ref = refs[4 * part : 4 * part + 2]
    gq_refs = refs[4 * part + 2 : 5 * part + 2]
    dk_ref, dv_ref, sx_ref, gm_ref, k_all, v_all, vt_all, q_all, g_all, gq_all = refs[5 * part + 2 :]
    hd = k_all.shape[1]

    @pl.when(pl.program_id(0) == 0)
    def _():
        gather(table, base, k_refs, k_all)
        gather(table, base, v_refs, v_all)
        vt_all[...] = turned(v_all[...])
        dv_ref[...] = jnp.zeros_like(dv_ref)

    gather(table, base, q_refs, q_all)
    gather(table, base, g_refs, g_all)
    maps = []
    earlier = lax.broadcasted_iota(jnp.int32, (TILE, TILE), 0) <= lax.broadcasted_iota(
        jnp.int32, (TILE, TILE), 1
    )

    def causal(array, begin):
        masked = jnp.where(earlier, array[begin:], 0.0)
        return masked if begin == 0 else jnp.concatenate([array[:begin], masked], axis=0)

    for u in range(PAIR):
        weight = weight_rows(w_ref, u)
        half = weight.shape[0] // 2
        lanes = slice(u * hd, (u + 1) * hd)
        q_feat = features(weight[:half], q_all[:, lanes])
        k_low = features(weight[half:], k_all[...]).astype(BF16)
        q_low = q_feat.astype(BF16)
        k_turned = turned(k_low)
        state = st_ref[u, :hd, :]
        state_turned = turned(state)
        norm = column(whole_row(st_ref[u, hd:, :]), TILE)
        g_turned = g_all[:, lanes].T.astype(F32)
        back = []
        dkey = [jnp.zeros((2 * half, TILE), F32) for _ in range(BLK // TILE)]
        dvalue = [jnp.zeros((hd, TILE), F32) for _ in range(BLK // TILE)]
        suffix = jnp.zeros((2 * half, hd), F32)
        suffix_norm = jnp.zeros((2 * half, 1), F32)
        for j in range(BLK // TILE):
            begin, end = j * TILE, (j + 1) * TILE
            own = q_low[:, begin:end]
            own_wide = own.astype(F32)
            scores = causal(nn(k_turned[:end], own), begin)
            scores_low = scores.astype(BF16)
            numerator = nn(state_turned, own) + nn(vt_all[:, :end], scores_low)
            denominator = jnp.sum(own_wide * norm, axis=0, keepdims=True) + jnp.sum(
                scores, axis=0, keepdims=True
            )
            inverse = 1.0 / denominator
            scaled = g_turned[:, begin:end] * inverse
            scaled_low = scaled.astype(BF16)
            norm_grad = -jnp.sum(scaled * (numerator * inverse), axis=0, keepdims=True)
            dscores = causal(nn(v_all[:end, :], scaled_low) + norm_grad, begin).astype(BF16)
            dquery = nn(state, scaled_low) + norm * norm_grad + nn(k_low[:, :end], dscores)
            back.append(feature_back(q_feat[:, begin:end], dquery))
            for i in range(j + 1):
                rows = slice(i * TILE, (i + 1) * TILE)
                dkey[i] = dkey[i] + nt(own, dscores[rows])
                dvalue[i] = dvalue[i] + nt(scaled_low, scores_low[rows])
            suffix = suffix + nt(own, scaled_low)
            suffix_norm = suffix_norm + jnp.sum(own_wide * norm_grad, axis=1, keepdims=True)
        dlog = jnp.concatenate(back, axis=1)
        gq_all[:, lanes] = nn(turned(dlog), weight[:half]).astype(BF16)
        maps.append(nn(dlog, q_all[:, lanes]))
        dk_ref[u] = jnp.concatenate(dkey, axis=1)
        dv_ref[...] += jnp.concatenate(dvalue, axis=1)
        sx_ref[u, :hd, :] = suffix.astype(BF16)
        sx_ref[u, hd:, :] = thirds(jnp.broadcast_to(suffix_norm, (2 * half, 2 * half)).T[:1])
    gm_ref[0] = jnp.concatenate(maps, axis=0).T.astype(gm_ref.dtype)
    for r, ref in enumerate(gq_refs):
        rows = ref.shape[0]
        ref[...] = gq_all[pl.ds(pl.multiple_of(table[base + r] * rows, rows), rows), :]


def key_kernel(begun, part, base, table, *refs):
    k_refs, v_refs = refs[:part], refs[part : 2 * part]
    w_ref, sx_ref, dk_ref, dv_ref = refs[2 * part : 2 * part + 4]
    out, gm_ref, k_all, v_all, vt_all, total, logs, weights = refs[2 * part + 4 + begun :]
    hd = k_all.shape[1]
    step = pl.program_id(0)

    @pl.when(step == 0)
    def _():
        gather(table, base, k_refs, k_all)
        gather(table, base, v_refs, v_all)
        vt_all[...] = turned(v_all[...])
        total[...] = dv_ref[...]

    maps = []
    for u in range(PAIR):
        weight = weight_rows(w_ref, u)
        half = weight.shape[0] // 2
        weight = weight[half:]
        feats = features(weight, k_all[...])
        suffix = sx_ref[u, :hd, :]
        norm = column(whole_row(sx_ref[u, hd:, :]), BLK)
        dlog = feature_back(feats, dk_ref[u] + nn(suffix, vt_all[...]) + norm)
        at = pl.ds(pl.multiple_of((step * PAIR + u) * half, half), half)
        logs[at, :] = dlog
        weights[at, :] = weight
        maps.append(nn(dlog, k_all[...]))
        total[...] += nn(turned(suffix), feats.astype(BF16))
    gm_ref[0] = jnp.concatenate(maps, axis=0).T.astype(gm_ref.dtype)

    @pl.when(step == pl.num_programs(0) - 1)
    def _():
        pair = jnp.concatenate([nn(turned(logs[...]), weights[...]), total[...].T], axis=1)
        out[...] = pair.astype(out.dtype).reshape(out.shape)


def total_kernel(table, *refs):
    out = refs[-1]
    heads, hd = out.shape[0], out.shape[2]
    for h in range(heads):
        out[h, :hd, :] = sum(ref[h, :hd, :].astype(F32) for ref in refs[:-1]).astype(BF16)
        out[h, hd:, :] = thirds(sum(whole_row(ref[h, hd:, :]) for ref in refs[:-1]))


def spread_kernel(grp, others, closing, block_weight, total_weight, at, table, *refs):
    parts, totals, refs = refs[:grp], refs[grp : grp + others], refs[grp + others :]
    if closing:
        outs, grad, scratch = refs[:grp], refs[grp], refs[grp + 1]
    else:
        state_ref, norm_ref, outs = refs[0], refs[1], refs[2:]
    heads, hd = parts[0].shape[0], parts[0].shape[2]
    for h in range(heads):
        states = [ref[h, :hd, :].astype(F32) for ref in parts]
        norms = [whole_row(ref[h, hd:, :]) for ref in parts]
        others_state = [ref[h, :hd, :].astype(F32) for ref in totals]
        others_norm = [whole_row(ref[h, hd:, :]) for ref in totals]
        if closing:
            base, base_norm = jnp.zeros_like(states[0]), jnp.zeros_like(norms[0])
            scratch[...] = sum(states) + sum(others_state)
            rows = grad.shape[1]
            grad[h] = scratch[pl.ds(pl.multiple_of(table[at] * rows, rows), rows), :]
        else:
            base, base_norm = state_ref[h], norm_ref[pl.ds(h, 1), :]
        for i, (state, norm) in enumerate(zip(others_state, others_norm)):
            base = base + table[total_weight + i].astype(F32) * state
            base_norm = base_norm + table[total_weight + i].astype(F32) * norm
        for r, out in enumerate(outs):
            state, norm = base, base_norm
            for i in range(grp):
                if i != r:
                    state = state + table[block_weight + r * grp + i].astype(F32) * states[i]
                    norm = norm + table[block_weight + r * grp + i].astype(F32) * norms[i]
            out[h, :hd, :] = state.astype(BF16)
            out[h, hd:, :] = thirds(norm)


def close_kernel(at, table, q_ref, k_ref, *refs):
    pieces, outs = refs[:-2], refs[-2:]
    for i, (own, out) in enumerate(zip((q_ref, k_ref), outs)):
        rows, half = out.shape[1:]
        mine = pl.ds(pl.multiple_of(table[at] * rows, rows), rows)
        for h in range(own.shape[0]):
            total = own[h, mine, :].astype(F32)
            for ref in pieces:
                total = total + ref[i, h].astype(F32)
            for u in range(PAIR):
                out[h * PAIR + u] = total[:, u * half : (u + 1) * half]


def whole_call(kernel, outs, table, arrays, name, scratch=()):
    return pl.pallas_call(
        kernel,
        out_shape=outs,
        in_specs=[pl.BlockSpec(memory_space=SMEM)]
        + [pl.BlockSpec(memory_space=pltpu.VMEM)] * len(arrays),
        out_specs=[pl.BlockSpec(memory_space=pltpu.VMEM)] * len(outs),
        scratch_shapes=list(scratch),
        compiler_params=pltpu.CompilerParams(vmem_limit_bytes=LIMIT),
        cost_estimate=LITTLE,
        name=name,
    )(table, *arrays)


def after(value, *others):
    return lax.optimization_barrier((value, *others))[0]


def shards(
    query_rows, key_rows, value_rows, grad_out, query_map, key_map, prefix_state, prefix_norm
):
    ctx, fsdp = lax.axis_size("ctx"), lax.axis_size("fsdp")
    tok = query_rows.shape[0]
    heads, map_rows, half = query_map.shape
    hd = map_rows * fsdp
    kv_heads = key_rows.shape[1] // hd
    replicas = ctx // kv_heads
    part = BLK // tok
    grp = ctx // part
    mine = lax.axis_index("ctx")
    at, block, seq = mine % part, mine // part, lax.axis_index("fsdp")
    shifts, slots = range(part), range(grp)
    order = list(reversed(slots))
    grid = (heads // PAIR,)
    blocks_of = [[g * part + p for p in range(part)] for g in slots]

    def within(array):
        return lax.all_to_all(array, "ctx", 0, 0, axis_index_groups=blocks_of, tiled=True)

    def around(array, shift):
        return lax.ppermute(
            array, "ctx", [(d, d // part * part + (d + shift) % part) for d in range(ctx)]
        )

    def across(array, shift):
        return lax.ppermute(array, "ctx", [(d, (d + shift * part) % ctx) for d in range(ctx)])

    def along(array, shift):
        return lax.ppermute(array, "fsdp", [(d, (d + shift) % fsdp) for d in range(fsdp)])

    def twin(array, bit):
        return lax.ppermute(array, "fsdp", [(d, d ^ bit) for d in range(fsdp)])

    def apart(array, s, r):
        moves = [
            (d * fsdp + i, (d + s * part) % ctx * fsdp + (i + r) % fsdp)
            for d in range(ctx)
            for i in range(fsdp)
        ]
        return lax.ppermute(array, ("ctx", "fsdp"), moves)

    slot = [(block + s) % grp for s in slots]
    near = [(block - r) % grp for r in slots]
    bits = [1 << i for i in range(fsdp.bit_length() - 1)]
    lists = {
        "seq": [seq],
        "owner": [slot[s] * part + p for s in slots for p in range(part)],
        "sent": [slot[s] * part + (at + r) % part for s in slots for r in shifts],
        "back": [slot[s] * part + (at + r) % part for s in slots for r in shifts],
        "kv": [
            (slot[s] * part + (at + r) % part) // replicas for r in shifts for s in slots
        ],
        "sorted": [(at - r) % part for r in shifts],
        "near before": [b < a for a in near for b in near],
        "near after": [b > a for a in near for b in near],
        "far before": [(seq ^ bit) < seq for bit in bits],
        "far after": [(seq ^ bit) > seq for bit in bits],
    }
    base, values = {}, []
    for name, entries in lists.items():
        base[name] = len(values)
        values += entries
    table = jnp.stack([jnp.asarray(v, jnp.int32) for v in values])

    own_maps = jnp.concatenate((query_map, key_map), axis=-1)
    near_maps = jnp.stack([own_maps] + [across(own_maps, -s) for s in slots[1:]])
    kv_sent = pack(table, base["kv"], (key_rows, value_rows), part, grp, hd)
    kv = [kv_sent[0]] + [around(kv_sent[r], r) for r in shifts[1:]]
    maps = lax.all_gather(near_maps, "fsdp")

    def sent_rows(s, *earlier):
        sent = pack(
            after(table, *earlier),
            base["sent"] + s * part,
            (query_rows, grad_out),
            part,
            1,
            heads * hd,
        )
        return [sent[0]] + [around(sent[r], r) for r in shifts[1:]]

    def piece_specs(column, count):
        return [pl.BlockSpec((tok, count * hd), lambda h, t: (0, column(h)))] * part

    def kv_specs(s):
        return piece_specs(lambda h: 2 * s, 1) + piece_specs(lambda h: 2 * s + 1, 1)

    def map_spec(s):
        return pl.BlockSpec((fsdp, None, PAIR, map_rows, 2 * half), lambda h, t: (0, s, h, 0, 0))

    def head_spec(*shape):
        return pl.BlockSpec((PAIR, *shape), lambda h, t: (h,) + (0,) * len(shape))

    def of(dtype, *shape):
        return jax.ShapeDtypeStruct(shape, dtype)

    ext_spec, ext_shape = head_spec(hd + EXT, hd), of(BF16, heads, hd + EXT, hd)
    gm_spec = pl.BlockSpec((1, hd, PAIR * half), lambda h, t: (h, 0, 0))
    gm_shape = of(BF16, heads // PAIR, hd, PAIR * half)
    dk_spec, dk_shape = head_spec(2 * half, BLK), of(F32, heads, 2 * half, BLK)
    dv_spec, dv_shape = pl.BlockSpec((hd, BLK), lambda h, t: (0, 0)), of(F32, hd, BLK)
    low, wide = pltpu.VMEM((BLK, hd), BF16), pltpu.VMEM((BLK, PAIR * hd), BF16)

    def call(kernel, outs, specs, out_specs, arrays, scratch, name, alias=(), limit=LIMIT):
        return pl.pallas_call(
            functools.partial(kernel, part, base["sorted"]),
            out_shape=outs,
            grid_spec=pltpu.PrefetchScalarGridSpec(
                num_scalar_prefetch=1,
                grid=grid,
                in_specs=specs,
                out_specs=out_specs,
                scratch_shapes=scratch,
            ),
            compiler_params=pltpu.CompilerParams(
                dimension_semantics=("arbitrary",), vmem_limit_bytes=limit
            ),
            cost_estimate=LITTLE,
            input_output_aliases=dict(alias),
            name=name,
        )(table, *arrays)

    def states_of(s, maps):
        return call(
            state_kernel,
            [ext_shape],
            kv_specs(s) + [map_spec(s)],
            [ext_spec],
            [*kv, *kv, maps],
            [low, low],
            "states",
        )[0]

    def spread(parts, others, when, extra, closing):
        weights = [base["near " + when], base["far " + when], base["seq"]]
        result = whole_call(
            functools.partial(spread_kernel, grp, len(bits), closing, *weights),
            [ext_shape] * grp + [of(F32, heads, map_rows, hd)] * closing,
            table,
            parts + others + extra,
            "spread",
            [pltpu.VMEM((hd, hd), F32)] * closing,
        )
        return [result[0]] + [across(result[s], -s) for s in slots[1:]], result[grp:]

    def totals_of(parts):
        return whole_call(total_kernel, [ext_shape], table, parts, "totals")[0]

    def around_all(total):
        others = []
        for bit in bits:
            total = totals_of([total, others[-1]]) if others else total
            others.append(twin(total, bit))
        return others

    partial = {}
    for s in order:
        partial[s] = states_of(s, after(maps, *partial.values()))
    parts = [partial[0]] + [across(partial[s], s) for s in slots[1:]]
    bulk = stacked(
        after(table, partial[0]),
        base["owner"] + order[0] * part,
        (query_rows, grad_out),
        part,
        heads * hd,
    )
    bulk = lax.all_to_all(bulk, "ctx", 0, 0, axis_index_groups=blocks_of, tiled=True)
    rows = {order[0]: [bulk] * part}
    others = around_all(totals_of(parts))
    state, _ = spread(parts, others, "before", [prefix_state, prefix_norm], False)
    for s in order[1:]:
        rows[s] = sent_rows(s, state[0])

    def row_specs(s, column):
        if rows[s][0].ndim == 2:
            return piece_specs(column, PAIR)

        def spec(r):
            return pl.BlockSpec(
                (None, tok, PAIR * hd), lambda h, t: (t[base["sorted"] + r], 0, column(h))
            )

        return [spec(r) for r in shifts]

    def block_of(s):
        return call(
            block_kernel,
            [of(BF16, tok, heads * hd)] * part + [dk_shape, dv_shape, ext_shape, gm_shape],
            kv_specs(s)
            + row_specs(s, lambda h: h)
            + row_specs(s, lambda h: grid[0] + h)
            + [map_spec(s), ext_spec],
            piece_specs(lambda h: h, PAIR) + [dk_spec, dv_spec, ext_spec, gm_spec],
            [*kv, *kv, *rows[s], *rows[s], maps, state[s]],
            [low, low, pltpu.VMEM((hd, BLK), BF16), wide, wide, wide],
            "blocks",
            limit=LARGE,
        )

    def rows_for(array, device):
        pieces = array.reshape(*array.shape[:-2], fsdp, map_rows, array.shape[-1])
        return lax.dynamic_index_in_dim(pieces, device % fsdp, array.ndim - 2, keepdims=False)

    blocks, parts = {}, {}
    for s in order:
        result = block_of(s)
        blocks[s] = (result[:part], *result[part:])
        parts[s] = across(blocks[s][3], s) if s else blocks[s][3]
    parts = [parts[s] for s in slots]
    total = totals_of(parts)
    others = around_all(total)
    suffix, (grad_prefix,) = spread(parts, others, "after", [], True)
    def brought_back(s, begin):
        pieces = [after(piece, begin) for piece in blocks[s][0]]
        return [pieces[0]] + [around(pieces[r], -r) for r in shifts[1:]]

    returned = {s: brought_back(s, others[0]) for s in order if s}
    suffix[0] = after(suffix[0], *[piece for s in returned for piece in returned[s]])

    kv_type = BF16 if replicas == 1 else F32
    pairs = of(kv_type, part, tok, grp * 2 * hd)
    moved, key_gm = [], {}
    for s in slots:
        begun = [] if s == 0 else [pairs]
        pairs, key_gm[s] = call(
            functools.partial(key_kernel, bool(begun)),
            [of(kv_type, *pairs.shape), gm_shape],
            kv_specs(s)
            + [map_spec(s), ext_spec, dk_spec, dv_spec]
            + [pl.BlockSpec(memory_space=pl.ANY)] * len(begun),
            [pl.BlockSpec((part, tok, 2 * hd), lambda h, t: (0, 0, s)), gm_spec],
            [*kv, *kv, maps, suffix[s], blocks[s][1], blocks[s][2], *begun],
            [
                low,
                low,
                pltpu.VMEM((hd, BLK), BF16),
                pltpu.VMEM((hd, BLK), F32),
                pltpu.VMEM((heads * half, BLK), BF16),
                pltpu.VMEM((heads * half, hd), BF16),
            ],
            "keys",
            {2 * part + 5: 0} if begun else {},
        )
        two = jnp.stack([blocks[s][4], key_gm[s]])
        if s:
            moved += [apart(rows_for(two, seq + r), s, r) for r in range(fsdp)]
        else:
            two = after(two, *suffix[1:])
            moved += [along(rows_for(two, seq + r), r) for r in range(1, fsdp)]
            returned[s] = brought_back(s, key_gm[s])

    pairs = within(after(pairs, *returned[0]))
    back = [piece[None] for s in slots for piece in returned[s]]
    (grad_queries,) = unpack(table, base["back"], back, 1, 1, heads * hd)
    grad_keys, grad_values = unpack(table, base["owner"], [pairs], grp, 2, hd)
    if replicas > 1:
        grad_keys, grad_values = (
            jnp.sum(a.reshape(tok, kv_heads, replicas, hd), axis=2)
            .astype(BF16)
            .reshape(tok, kv_heads * hd)
            for a in (grad_keys, grad_values)
        )
    query_map_grad, key_map_grad = whole_call(
        functools.partial(close_kernel, base["seq"]),
        [of(F32, heads, map_rows, half)] * 2,
        table,
        [blocks[0][4], key_gm[0]] + moved,
        "close",
    )
    return grad_queries, grad_keys, grad_values, query_map_grad, key_map_grad, grad_prefix


def solution(mesh):
    rows, maps = P(("fsdp", "ctx"), None), P("ctx", "fsdp", None)
    return jax.shard_map(
        shards,
        mesh=mesh,
        in_specs=(rows,) * 4 + (maps, maps, P("ctx", None, None), P("ctx", None)),
        out_specs=(rows,) * 3 + (maps,) * 3,
        check_vma=False,
    )
```

```python
import functools

import jax
import jax.numpy as jnp
from jax import lax
from jax.experimental import pallas as pl
from jax.experimental.pallas import tpu as pltpu
from jax.sharding import PartitionSpec as P

BLK = 512
TILE = 256
PAIR = 2
EXT = 16
LIMIT = 40 * 1024 * 1024
LARGE = 56 * 1024 * 1024

LITTLE = pl.CostEstimate(flops=1000, bytes_accessed=1000, transcendentals=0)

F32 = jnp.float32
BF16 = jnp.bfloat16
SMEM = pltpu.SMEM


def nn(left, right):
    return lax.dot_general(left, right, (((1,), (0,)), ((), ())), preferred_element_type=F32)


def nt(left, right):
    return lax.dot_general(left, right, (((1,), (1,)), ((), ())), preferred_element_type=F32)


def turned(array):
    return array.T


def column(row, width):
    n = row.shape[1]
    square = jnp.broadcast_to(row, (n, n)).T
    return jnp.concatenate([square] * (width // n), axis=1)


def thirds(row):
    rows = jnp.broadcast_to(row, (EXT, row.shape[1]))
    high = rows.astype(BF16).astype(F32)
    middle = (rows - high).astype(BF16).astype(F32)
    low = rows - high - middle
    place = lax.broadcasted_iota(jnp.int32, rows.shape, 0)
    picked = jnp.where(place == 0, high, jnp.where(place == 1, middle, low))
    return jnp.where(place < 3, picked, 0.0).astype(BF16)


def whole_row(block):
    return jnp.sum(block.astype(F32), axis=0, keepdims=True)


def weight_rows(ref, u):
    whole = jnp.concatenate([ref[i, u] for i in range(ref.shape[0])], axis=0)
    return turned(whole)


def features(weight, rows):
    logits = nt(weight, rows).astype(BF16).astype(F32)
    upper = jnp.exp(logits)
    lower = jnp.exp(-logits)
    upper = upper * (1.0 / jnp.sum(upper, axis=0, keepdims=True))
    lower = lower * (1.0 / jnp.sum(lower, axis=0, keepdims=True))
    return jnp.concatenate([upper, lower], axis=0)


def feature_back(feats, upstream):
    half = feats.shape[0] // 2
    weighted = feats * upstream
    first, second = weighted[:half], weighted[half:]
    first = first - feats[:half] * jnp.sum(first, axis=0, keepdims=True)
    second = second - feats[half:] * jnp.sum(second, axis=0, keepdims=True)
    return (first - second).astype(BF16)


def gather(table, base, refs, out):
    rows = refs[0].shape[0]
    for r, ref in enumerate(refs):
        out[pl.ds(pl.multiple_of(table[base + r] * rows, rows), rows), :] = ref[...]


def pack_kernel(columns, inputs, table, *refs):
    count = columns * inputs
    for r, out in enumerate(refs[-(len(refs) // (count + 1)) :]):
        width = out.shape[1] // count
        for i in range(count):
            out[:, i * width : (i + 1) * width] = refs[r * count + i][...]


def pack(table, base, sources, pieces, columns, width):
    rows = sources[0].shape[0]
    count = columns * len(sources)
    step = rows // 2

    def take(at):
        return pl.BlockSpec((step, width), lambda i, t: (i, t[base + at]))

    return pl.pallas_call(
        functools.partial(pack_kernel, columns, len(sources)),
        out_shape=[jax.ShapeDtypeStruct((rows, count * width), sources[0].dtype)] * pieces,
        grid_spec=pltpu.PrefetchScalarGridSpec(
            num_scalar_prefetch=1,
            grid=(rows // step,),
            in_specs=[
                take(r * columns + s)
                for r in range(pieces)
                for s in range(columns)
                for _ in sources
            ],
            out_specs=[pl.BlockSpec((step, count * width), lambda i, t: (i, 0))] * pieces,
        ),
        compiler_params=pltpu.CompilerParams(vmem_limit_bytes=LIMIT),
        cost_estimate=LITTLE,
        name="pack",
    )(table, *(list(sources) * (pieces * columns)))


def unpack_kernel(outputs, inner, base, table, *refs):
    sources, outs = refs[:-outputs], refs[-outputs:]
    for s, source in enumerate(sources):
        pieces = source.shape[0]
        width = source.shape[2] // (outputs * inner)
        for r in range(pieces):
            for j in range(inner):
                slot = s * inner + j
                at = table[base + slot * pieces + r] * width
                for i, out in enumerate(outs):
                    lanes = slice((j * outputs + i) * width, (j * outputs + i + 1) * width)
                    out[:, pl.ds(pl.multiple_of(at, width), width)] = source[r, :, lanes]


def unpack(table, base, sources, inner, outputs, width):
    pieces, rows = sources[0].shape[:2]
    total = len(sources) * inner * pieces * width
    step = rows // 2
    taken = pl.BlockSpec((pieces, step, inner * outputs * width), lambda i: (0, i, 0))
    return pl.pallas_call(
        functools.partial(unpack_kernel, outputs, inner, base),
        out_shape=[jax.ShapeDtypeStruct((rows, total), sources[0].dtype)] * outputs,
        grid=(rows // step,),
        in_specs=[pl.BlockSpec(memory_space=SMEM)] + [taken] * len(sources),
        out_specs=[pl.BlockSpec((step, total), lambda i: (i, 0))] * outputs,
        compiler_params=pltpu.CompilerParams(vmem_limit_bytes=LIMIT),
        cost_estimate=LITTLE,
        name="unpack",
    )(table, *sources)


def state_kernel(part, base, table, *refs):
    k_refs, v_refs, (w_ref, out, k_all, v_all) = refs[:part], refs[part : 2 * part], refs[2 * part :]
    hd = k_all.shape[1]

    @pl.when(pl.program_id(0) == 0)
    def _():
        gather(table, base, k_refs, k_all)
        gather(table, base, v_refs, v_all)

    ones = jnp.ones((EXT, k_all.shape[0]), BF16)
    weights = [weight_rows(w_ref, u) for u in range(PAIR)]
    feats = [features(w[w.shape[0] // 2 :], k_all[...]).astype(BF16) for w in weights]
    for u in range(PAIR):
        out[u, :hd, :] = nn(feats[u], v_all[...]).astype(BF16)
        out[u, hd:, :] = thirds(nt(ones, feats[u])[:1])


def block_kernel(part, base, table, *refs):
    k_refs, v_refs = refs[:part], refs[part : 2 * part]
    q_refs, g_refs = refs[2 * part : 3 * part], refs[3 * part : 4 * part]
    w_ref, st_ref = refs[4 * part : 4 * part + 2]
    gq_refs = refs[4 * part + 2 : 5 * part + 2]
    dk_ref, dv_ref, sx_ref, gm_ref, k_all, v_all, vt_all, q_all, g_all, gq_all = refs[5 * part + 2 :]
    hd = k_all.shape[1]

    @pl.when(pl.program_id(0) == 0)
    def _():
        gather(table, base, k_refs, k_all)
        gather(table, base, v_refs, v_all)
        vt_all[...] = turned(v_all[...])
        dv_ref[...] = jnp.zeros_like(dv_ref)

    gather(table, base, q_refs, q_all)
    gather(table, base, g_refs, g_all)
    maps = []
    earlier = lax.broadcasted_iota(jnp.int32, (TILE, TILE), 0) <= lax.broadcasted_iota(
        jnp.int32, (TILE, TILE), 1
    )

    def causal(array, begin):
        masked = jnp.where(earlier, array[begin:], 0.0)
        return masked if begin == 0 else jnp.concatenate([array[:begin], masked], axis=0)

    heads = range(PAIR)
    lanes = [slice(u * hd, (u + 1) * hd) for u in heads]
    weight = [weight_rows(w_ref, u) for u in heads]
    half = weight[0].shape[0] // 2
    q_feat = [features(weight[u][:half], q_all[:, lanes[u]]) for u in heads]
    k_low = [features(weight[u][half:], k_all[...]).astype(BF16) for u in heads]
    q_low = [q_feat[u].astype(BF16) for u in heads]
    k_turned = [turned(k_low[u]) for u in heads]
    state = [st_ref[u, :hd, :] for u in heads]
    state_turned = [turned(state[u]) for u in heads]
    norm = [column(whole_row(st_ref[u, hd:, :]), TILE) for u in heads]
    g_turned = [g_all[:, lanes[u]].T for u in heads]
    back = [[] for u in heads]
    dkey = [[jnp.zeros((2 * half, TILE), F32) for _ in range(BLK // TILE)] for u in heads]
    dvalue = [[jnp.zeros((hd, TILE), F32) for _ in range(BLK // TILE)] for u in heads]
    suffix = [jnp.zeros((2 * half, hd), F32) for u in heads]
    suffix_norm = [jnp.zeros((2 * half, 1), F32) for u in heads]
    for j in range(BLK // TILE):
        begin, end = j * TILE, (j + 1) * TILE
        own = [q_low[u][:, begin:end] for u in heads]
        scores = [causal(nn(k_turned[u][:end], own[u]), begin) for u in heads]
        scores_low = [scores[u].astype(BF16) for u in heads]
        inverse = [
            1.0
            / (
                jnp.sum(own[u].astype(F32) * norm[u], axis=0, keepdims=True)
                + jnp.sum(scores[u], axis=0, keepdims=True)
            )
            for u in heads
        ]
        scaled = [g_turned[u][:, begin:end].astype(F32) * inverse[u] for u in heads]
        scaled_low = [scaled[u].astype(BF16) for u in heads]
        numerator = [
            nn(state_turned[u], own[u]) + nn(vt_all[:, :end], scores_low[u]) for u in heads
        ]
        products = [nn(v_all[:end, :], scaled_low[u]) for u in heads]
        norm_grad = [
            -jnp.sum(scaled[u] * (numerator[u] * inverse[u]), axis=0, keepdims=True)
            for u in heads
        ]
        dscores = [causal(products[u] + norm_grad[u], begin).astype(BF16) for u in heads]
        dquery = [
            nn(state[u], scaled_low[u])
            + norm[u] * norm_grad[u]
            + nn(k_low[u][:, :end], dscores[u])
            for u in heads
        ]
        for u in heads:
            back[u].append(feature_back(q_feat[u][:, begin:end], dquery[u]))
            for i in range(j + 1):
                rows = slice(i * TILE, (i + 1) * TILE)
                dkey[u][i] = dkey[u][i] + nt(own[u], dscores[u][rows])
                dvalue[u][i] = dvalue[u][i] + nt(scaled_low[u], scores_low[u][rows])
            suffix[u] = suffix[u] + nt(own[u], scaled_low[u])
            suffix_norm[u] = suffix_norm[u] + jnp.sum(
                own[u].astype(F32) * norm_grad[u], axis=1, keepdims=True
            )
    for u in heads:
        dlog = jnp.concatenate(back[u], axis=1)
        gq_all[:, lanes[u]] = nn(turned(dlog), weight[u][:half]).astype(BF16)
        maps.append(nn(dlog, q_all[:, lanes[u]]))
        dk_ref[u] = jnp.concatenate(dkey[u], axis=1)
        dv_ref[...] += jnp.concatenate(dvalue[u], axis=1)
        sx_ref[u, :hd, :] = suffix[u].astype(BF16)
        sx_ref[u, hd:, :] = thirds(jnp.broadcast_to(suffix_norm[u], (2 * half, 2 * half)).T[:1])
    gm_ref[0] = jnp.concatenate(maps, axis=0).T.astype(gm_ref.dtype)
    for r, ref in enumerate(gq_refs):
        rows = ref.shape[0]
        ref[...] = gq_all[pl.ds(pl.multiple_of(table[base + r] * rows, rows), rows), :]


def key_kernel(begun, part, base, table, *refs):
    k_refs, v_refs = refs[:part], refs[part : 2 * part]
    w_ref, sx_ref, dk_ref, dv_ref = refs[2 * part : 2 * part + 4]
    out, gm_ref, k_all, v_all, vt_all, total, logs, weights = refs[2 * part + 4 + begun :]
    hd = k_all.shape[1]
    step = pl.program_id(0)

    @pl.when(step == 0)
    def _():
        gather(table, base, k_refs, k_all)
        gather(table, base, v_refs, v_all)
        vt_all[...] = turned(v_all[...])
        total[...] = dv_ref[...]

    heads = range(PAIR)
    weight = [weight_rows(w_ref, u) for u in heads]
    half = weight[0].shape[0] // 2
    feats = [features(weight[u][half:], k_all[...]) for u in heads]
    suffix = [sx_ref[u, :hd, :] for u in heads]
    upstream = [
        dk_ref[u] + nn(suffix[u], vt_all[...]) + column(whole_row(sx_ref[u, hd:, :]), BLK)
        for u in heads
    ]
    dlog = [feature_back(feats[u], upstream[u]) for u in heads]
    maps = [nn(dlog[u], k_all[...]) for u in heads]
    for u in heads:
        at = pl.ds(pl.multiple_of((step * PAIR + u) * half, half), half)
        logs[at, :] = dlog[u]
        weights[at, :] = weight[u][half:]
    total[...] += sum(nn(turned(suffix[u]), feats[u].astype(BF16)) for u in heads)
    gm_ref[0] = jnp.concatenate(maps, axis=0).T.astype(gm_ref.dtype)

    @pl.when(step == pl.num_programs(0) - 1)
    def _():
        pair = jnp.concatenate([nn(turned(logs[...]), weights[...]), total[...].T], axis=1)
        out[...] = pair.astype(out.dtype).reshape(out.shape)


def total_kernel(table, *refs):
    out = refs[-1]
    heads, hd = out.shape[0], out.shape[2]
    for h in range(heads):
        out[h, :hd, :] = sum(ref[h, :hd, :].astype(F32) for ref in refs[:-1]).astype(BF16)
        out[h, hd:, :] = thirds(sum(whole_row(ref[h, hd:, :]) for ref in refs[:-1]))


def spread_kernel(grp, others, closing, block_weight, total_weight, at, table, *refs):
    parts, totals, refs = refs[:grp], refs[grp : grp + others], refs[grp + others :]
    if closing:
        outs, grad, scratch = refs[:grp], refs[grp], refs[grp + 1]
    else:
        state_ref, norm_ref, outs = refs[0], refs[1], refs[2:]
    heads, hd = parts[0].shape[0], parts[0].shape[2]
    for h in range(heads):
        states = [ref[h, :hd, :].astype(F32) for ref in parts]
        norms = [whole_row(ref[h, hd:, :]) for ref in parts]
        others_state = [ref[h, :hd, :].astype(F32) for ref in totals]
        others_norm = [whole_row(ref[h, hd:, :]) for ref in totals]
        if closing:
            base, base_norm = jnp.zeros_like(states[0]), jnp.zeros_like(norms[0])
            scratch[...] = sum(states) + sum(others_state)
            rows = grad.shape[1]
            grad[h] = scratch[pl.ds(pl.multiple_of(table[at] * rows, rows), rows), :]
        else:
            base, base_norm = state_ref[h], norm_ref[pl.ds(h, 1), :]
        for i, (state, norm) in enumerate(zip(others_state, others_norm)):
            base = base + table[total_weight + i].astype(F32) * state
            base_norm = base_norm + table[total_weight + i].astype(F32) * norm
        for r, out in enumerate(outs):
            state, norm = base, base_norm
            for i in range(grp):
                if i != r:
                    state = state + table[block_weight + r * grp + i].astype(F32) * states[i]
                    norm = norm + table[block_weight + r * grp + i].astype(F32) * norms[i]
            out[h, :hd, :] = state.astype(BF16)
            out[h, hd:, :] = thirds(norm)


def close_kernel(at, table, q_ref, k_ref, *refs):
    pieces, outs = refs[:-2], refs[-2:]
    for i, (own, out) in enumerate(zip((q_ref, k_ref), outs)):
        rows, half = out.shape[1:]
        mine = pl.ds(pl.multiple_of(table[at] * rows, rows), rows)
        for h in range(own.shape[0]):
            total = own[h, mine, :].astype(F32)
            for ref in pieces:
                total = total + ref[i, h].astype(F32)
            for u in range(PAIR):
                out[h * PAIR + u] = total[:, u * half : (u + 1) * half]


def whole_call(kernel, outs, table, arrays, name, scratch=()):
    return pl.pallas_call(
        kernel,
        out_shape=outs,
        in_specs=[pl.BlockSpec(memory_space=SMEM)]
        + [pl.BlockSpec(memory_space=pltpu.VMEM)] * len(arrays),
        out_specs=[pl.BlockSpec(memory_space=pltpu.VMEM)] * len(outs),
        scratch_shapes=list(scratch),
        compiler_params=pltpu.CompilerParams(vmem_limit_bytes=LIMIT),
        cost_estimate=LITTLE,
        name=name,
    )(table, *arrays)


def after(value, *others):
    return lax.optimization_barrier((value, *others))[0]


def shards(
    query_rows, key_rows, value_rows, grad_out, query_map, key_map, prefix_state, prefix_norm
):
    ctx, fsdp = lax.axis_size("ctx"), lax.axis_size("fsdp")
    tok = query_rows.shape[0]
    heads, map_rows, half = query_map.shape
    hd = map_rows * fsdp
    kv_heads = key_rows.shape[1] // hd
    replicas = ctx // kv_heads
    part = BLK // tok
    grp = ctx // part
    mine = lax.axis_index("ctx")
    at, block, seq = mine % part, mine // part, lax.axis_index("fsdp")
    shifts, slots = range(part), range(grp)
    order = list(reversed(slots))
    grid = (heads // PAIR,)
    blocks_of = [[g * part + p for p in range(part)] for g in slots]

    def within(array):
        return lax.all_to_all(array, "ctx", 0, 0, axis_index_groups=blocks_of, tiled=True)

    def around(array, shift):
        return lax.ppermute(
            array, "ctx", [(d, d // part * part + (d + shift) % part) for d in range(ctx)]
        )

    def across(array, shift):
        return lax.ppermute(array, "ctx", [(d, (d + shift * part) % ctx) for d in range(ctx)])

    def along(array, shift):
        return lax.ppermute(array, "fsdp", [(d, (d + shift) % fsdp) for d in range(fsdp)])

    def twin(array, bit):
        return lax.ppermute(array, "fsdp", [(d, d ^ bit) for d in range(fsdp)])

    def apart(array, s, r):
        moves = [
            (d * fsdp + i, (d + s * part) % ctx * fsdp + (i + r) % fsdp)
            for d in range(ctx)
            for i in range(fsdp)
        ]
        return lax.ppermute(array, ("ctx", "fsdp"), moves)

    slot = [(block + s) % grp for s in slots]
    near = [(block - r) % grp for r in slots]
    bits = [1 << i for i in range(fsdp.bit_length() - 1)]
    lists = {
        "seq": [seq],
        "owner": [slot[s] * part + p for s in slots for p in range(part)],
        "sent": [slot[s] * part + (at + r) % part for s in slots for r in shifts],
        "back": [slot[s] * part + (at + r) % part for s in slots for r in shifts],
        "kv": [
            (slot[s] * part + (at + r) % part) // replicas for r in shifts for s in slots
        ],
        "sorted": [(at - r) % part for r in shifts],
        "near before": [b < a for a in near for b in near],
        "near after": [b > a for a in near for b in near],
        "far before": [(seq ^ bit) < seq for bit in bits],
        "far after": [(seq ^ bit) > seq for bit in bits],
    }
    base, values = {}, []
    for name, entries in lists.items():
        base[name] = len(values)
        values += entries
    table = jnp.stack([jnp.asarray(v, jnp.int32) for v in values])

    own_maps = jnp.concatenate((query_map, key_map), axis=-1)
    near_maps = jnp.stack([own_maps] + [across(own_maps, -s) for s in slots[1:]])
    kv_sent = pack(table, base["kv"], (key_rows, value_rows), part, grp, hd)
    kv = [kv_sent[0]] + [around(kv_sent[r], r) for r in shifts[1:]]
    maps = lax.all_gather(near_maps, "fsdp")

    def sent_rows(s, *earlier):
        sent = pack(
            after(table, *earlier),
            base["sent"] + s * part,
            (query_rows, grad_out),
            part,
            1,
            heads * hd,
        )
        return [sent[0]] + [around(sent[r], r) for r in shifts[1:]]

    def piece_specs(column, count):
        return [pl.BlockSpec((tok, count * hd), lambda h, t: (0, column(h)))] * part

    def kv_specs(s):
        return piece_specs(lambda h: 2 * s, 1) + piece_specs(lambda h: 2 * s + 1, 1)

    def map_spec(s):
        return pl.BlockSpec((fsdp, None, PAIR, map_rows, 2 * half), lambda h, t: (0, s, h, 0, 0))

    def head_spec(*shape):
        return pl.BlockSpec((PAIR, *shape), lambda h, t: (h,) + (0,) * len(shape))

    def of(dtype, *shape):
        return jax.ShapeDtypeStruct(shape, dtype)

    ext_spec, ext_shape = head_spec(hd + EXT, hd), of(BF16, heads, hd + EXT, hd)
    gm_spec = pl.BlockSpec((1, hd, PAIR * half), lambda h, t: (h, 0, 0))
    gm_shape = of(BF16, heads // PAIR, hd, PAIR * half)
    dk_spec, dk_shape = head_spec(2 * half, BLK), of(F32, heads, 2 * half, BLK)
    dv_spec, dv_shape = pl.BlockSpec((hd, BLK), lambda h, t: (0, 0)), of(F32, hd, BLK)
    low, wide = pltpu.VMEM((BLK, hd), BF16), pltpu.VMEM((BLK, PAIR * hd), BF16)

    def call(kernel, outs, specs, out_specs, arrays, scratch, name, alias=(), limit=LIMIT):
        return pl.pallas_call(
            functools.partial(kernel, part, base["sorted"]),
            out_shape=outs,
            grid_spec=pltpu.PrefetchScalarGridSpec(
                num_scalar_prefetch=1,
                grid=grid,
                in_specs=specs,
                out_specs=out_specs,
                scratch_shapes=scratch,
            ),
            compiler_params=pltpu.CompilerParams(
                dimension_semantics=("arbitrary",), vmem_limit_bytes=limit
            ),
            cost_estimate=LITTLE,
            input_output_aliases=dict(alias),
            name=name,
        )(table, *arrays)

    def states_of(s):
        return call(
            state_kernel,
            [ext_shape],
            kv_specs(s) + [map_spec(s)],
            [ext_spec],
            [*kv, *kv, maps],
            [low, low],
            "states",
        )[0]

    def spread(parts, others, when, extra, closing):
        weights = [base["near " + when], base["far " + when], base["seq"]]
        result = whole_call(
            functools.partial(spread_kernel, grp, len(bits), closing, *weights),
            [ext_shape] * grp + [of(F32, heads, map_rows, hd)] * closing,
            table,
            parts + others + extra,
            "spread",
            [pltpu.VMEM((hd, hd), F32)] * closing,
        )
        return [result[0]] + [across(result[s], -s) for s in slots[1:]], result[grp:]

    def totals_of(parts):
        return whole_call(total_kernel, [ext_shape], table, parts, "totals")[0]

    def around_all(total):
        others = []
        for bit in bits:
            total = totals_of([total, others[-1]]) if others else total
            others.append(twin(total, bit))
        return others

    partial = {s: states_of(s) for s in order}
    parts = [partial[0]] + [across(partial[s], s) for s in slots[1:]]
    rows = {order[0]: sent_rows(order[0], near_maps, *kv)}
    parts[0] = after(parts[0], *rows[order[0]])
    others = around_all(totals_of(parts))
    state, _ = spread(parts, others, "before", [prefix_state, prefix_norm], False)
    for s in order[1:]:
        rows[s] = sent_rows(s, state[0])

    def block_of(s):
        return call(
            block_kernel,
            [of(BF16, tok, heads * hd)] * part + [dk_shape, dv_shape, ext_shape, gm_shape],
            kv_specs(s)
            + piece_specs(lambda h: h, PAIR)
            + piece_specs(lambda h: grid[0] + h, PAIR)
            + [map_spec(s), ext_spec],
            piece_specs(lambda h: h, PAIR) + [dk_spec, dv_spec, ext_spec, gm_spec],
            [*kv, *kv, *rows[s], *rows[s], maps, state[s]],
            [low, low, pltpu.VMEM((hd, BLK), BF16), wide, wide, wide],
            "blocks",
            limit=LARGE,
        )

    def rows_for(array, device):
        pieces = array.reshape(*array.shape[:-2], fsdp, map_rows, array.shape[-1])
        return lax.dynamic_index_in_dim(pieces, device % fsdp, array.ndim - 2, keepdims=False)

    blocks, parts = {}, {}
    for s in order:
        result = block_of(s)
        blocks[s] = (result[:part], *result[part:])
        parts[s] = across(blocks[s][3], s) if s else blocks[s][3]
    parts = [parts[s] for s in slots]
    total = totals_of(parts)
    others = around_all(total)
    suffix, (grad_prefix,) = spread(parts, others, "after", [], True)
    def brought_back(s, begin):
        pieces = [after(piece, begin) for piece in blocks[s][0]]
        return [pieces[0]] + [around(pieces[r], -r) for r in shifts[1:]]

    returned = {s: brought_back(s, others[0]) for s in order if s}
    suffix[0] = after(suffix[0], *[piece for s in returned for piece in returned[s]])

    kv_type = BF16 if replicas == 1 else F32
    pairs = of(kv_type, part, tok, grp * 2 * hd)
    moved, key_gm = [], {}
    for s in slots:
        begun = [] if s == 0 else [pairs]
        pairs, key_gm[s] = call(
            functools.partial(key_kernel, bool(begun)),
            [of(kv_type, *pairs.shape), gm_shape],
            kv_specs(s)
            + [map_spec(s), ext_spec, dk_spec, dv_spec]
            + [pl.BlockSpec(memory_space=pl.ANY)] * len(begun),
            [pl.BlockSpec((part, tok, 2 * hd), lambda h, t: (0, 0, s)), gm_spec],
            [*kv, *kv, maps, suffix[s], blocks[s][1], blocks[s][2], *begun],
            [
                low,
                low,
                pltpu.VMEM((hd, BLK), BF16),
                pltpu.VMEM((hd, BLK), F32),
                pltpu.VMEM((heads * half, BLK), BF16),
                pltpu.VMEM((heads * half, hd), BF16),
            ],
            "keys",
            {2 * part + 5: 0} if begun else {},
        )
        two = jnp.stack([blocks[s][4], key_gm[s]])
        if s:
            moved += [apart(rows_for(two, seq + r), s, r) for r in range(fsdp)]
        else:
            two = after(two, *suffix[1:])
            moved += [along(rows_for(two, seq + r), r) for r in range(1, fsdp)]
            returned[s] = brought_back(s, key_gm[s])

    pairs = within(after(pairs, *returned[0]))
    back = [piece[None] for s in slots for piece in returned[s]]
    (grad_queries,) = unpack(table, base["back"], back, 1, 1, heads * hd)
    grad_keys, grad_values = unpack(table, base["owner"], [pairs], grp, 2, hd)
    if replicas > 1:
        grad_keys, grad_values = (
            jnp.sum(a.reshape(tok, kv_heads, replicas, hd), axis=2)
            .astype(BF16)
            .reshape(tok, kv_heads * hd)
            for a in (grad_keys, grad_values)
        )
    query_map_grad, key_map_grad = whole_call(
        functools.partial(close_kernel, base["seq"]),
        [of(F32, heads, map_rows, half)] * 2,
        table,
        [blocks[0][4], key_gm[0]] + moved,
        "close",
    )
    return grad_queries, grad_keys, grad_values, query_map_grad, key_map_grad, grad_prefix


def solution(mesh):
    rows, maps = P(("fsdp", "ctx"), None), P("ctx", "fsdp", None)
    return jax.shard_map(
        shards,
        mesh=mesh,
        in_specs=(rows,) * 4 + (maps, maps, P("ctx", None, None), P("ctx", None)),
        out_specs=(rows,) * 3 + (maps,) * 3,
        check_vma=False,
    )
```

```python
import functools

import jax
import jax.numpy as jnp
from jax import lax
from jax.experimental import pallas as pl
from jax.experimental.pallas import tpu as pltpu
from jax.sharding import PartitionSpec as P

BLK = 512
TILE = 256
PAIR = 2
EXT = 16
LIMIT = 40 * 1024 * 1024
LARGE = 56 * 1024 * 1024

LITTLE = pl.CostEstimate(flops=1000, bytes_accessed=1000, transcendentals=0)

F32 = jnp.float32
BF16 = jnp.bfloat16
SMEM = pltpu.SMEM


def nn(left, right):
    return lax.dot_general(left, right, (((1,), (0,)), ((), ())), preferred_element_type=F32)


def nt(left, right):
    return lax.dot_general(left, right, (((1,), (1,)), ((), ())), preferred_element_type=F32)


def turned(array):
    return array.T


def column(row, width):
    n = row.shape[1]
    square = jnp.broadcast_to(row, (n, n)).T
    return jnp.concatenate([square] * (width // n), axis=1)


def thirds(row):
    rows = jnp.broadcast_to(row, (EXT, row.shape[1]))
    high = rows.astype(BF16).astype(F32)
    middle = (rows - high).astype(BF16).astype(F32)
    low = rows - high - middle
    place = lax.broadcasted_iota(jnp.int32, rows.shape, 0)
    picked = jnp.where(place == 0, high, jnp.where(place == 1, middle, low))
    return jnp.where(place < 3, picked, 0.0).astype(BF16)


def whole_row(block):
    return jnp.sum(block.astype(F32), axis=0, keepdims=True)


def weight_rows(ref, u):
    whole = jnp.concatenate([ref[i, u] for i in range(ref.shape[0])], axis=0)
    return turned(whole)


def features(weight, rows):
    logits = nt(weight, rows).astype(BF16).astype(F32)
    upper = jnp.exp(logits)
    lower = jnp.exp(-logits)
    upper = upper * (1.0 / jnp.sum(upper, axis=0, keepdims=True))
    lower = lower * (1.0 / jnp.sum(lower, axis=0, keepdims=True))
    return jnp.concatenate([upper, lower], axis=0)


def feature_back(feats, upstream):
    half = feats.shape[0] // 2
    weighted = feats * upstream
    first, second = weighted[:half], weighted[half:]
    first = first - feats[:half] * jnp.sum(first, axis=0, keepdims=True)
    second = second - feats[half:] * jnp.sum(second, axis=0, keepdims=True)
    return (first - second).astype(BF16)


def gather(table, base, refs, out):
    rows = refs[0].shape[0]
    for r, ref in enumerate(refs):
        out[pl.ds(pl.multiple_of(table[base + r] * rows, rows), rows), :] = ref[...]


def pack_kernel(columns, inputs, table, *refs):
    count = columns * inputs
    for r, out in enumerate(refs[-(len(refs) // (count + 1)) :]):
        width = out.shape[1] // count
        for i in range(count):
            out[:, i * width : (i + 1) * width] = refs[r * count + i][...]


def pack(table, base, sources, pieces, columns, width):
    rows = sources[0].shape[0]
    count = columns * len(sources)
    step = rows // 2

    def take(at):
        return pl.BlockSpec((step, width), lambda i, t: (i, t[base + at]))

    return pl.pallas_call(
        functools.partial(pack_kernel, columns, len(sources)),
        out_shape=[jax.ShapeDtypeStruct((rows, count * width), sources[0].dtype)] * pieces,
        grid_spec=pltpu.PrefetchScalarGridSpec(
            num_scalar_prefetch=1,
            grid=(rows // step,),
            in_specs=[
                take(r * columns + s)
                for r in range(pieces)
                for s in range(columns)
                for _ in sources
            ],
            out_specs=[pl.BlockSpec((step, count * width), lambda i, t: (i, 0))] * pieces,
        ),
        compiler_params=pltpu.CompilerParams(vmem_limit_bytes=LIMIT),
        cost_estimate=LITTLE,
        name="pack",
    )(table, *(list(sources) * (pieces * columns)))


def unpack_kernel(outputs, inner, base, table, *refs):
    sources, outs = refs[:-outputs], refs[-outputs:]
    for s, source in enumerate(sources):
        pieces = source.shape[0]
        width = source.shape[2] // (outputs * inner)
        for r in range(pieces):
            for j in range(inner):
                slot = s * inner + j
                at = table[base + slot * pieces + r] * width
                for i, out in enumerate(outs):
                    lanes = slice((j * outputs + i) * width, (j * outputs + i + 1) * width)
                    out[:, pl.ds(pl.multiple_of(at, width), width)] = source[r, :, lanes]


def unpack(table, base, sources, inner, outputs, width):
    pieces, rows = sources[0].shape[:2]
    total = len(sources) * inner * pieces * width
    step = rows // 2
    taken = pl.BlockSpec((pieces, step, inner * outputs * width), lambda i: (0, i, 0))
    return pl.pallas_call(
        functools.partial(unpack_kernel, outputs, inner, base),
        out_shape=[jax.ShapeDtypeStruct((rows, total), sources[0].dtype)] * outputs,
        grid=(rows // step,),
        in_specs=[pl.BlockSpec(memory_space=SMEM)] + [taken] * len(sources),
        out_specs=[pl.BlockSpec((step, total), lambda i: (i, 0))] * outputs,
        compiler_params=pltpu.CompilerParams(vmem_limit_bytes=LIMIT),
        cost_estimate=LITTLE,
        name="unpack",
    )(table, *sources)


def state_kernel(part, base, table, *refs):
    k_refs, v_refs, (w_ref, out, k_all, v_all) = refs[:part], refs[part : 2 * part], refs[2 * part :]
    hd = k_all.shape[1]

    @pl.when(pl.program_id(0) == 0)
    def _():
        gather(table, base, k_refs, k_all)
        gather(table, base, v_refs, v_all)

    ones = jnp.ones((EXT, k_all.shape[0]), BF16)
    weights = [weight_rows(w_ref, u) for u in range(PAIR)]
    feats = [features(w[w.shape[0] // 2 :], k_all[...]).astype(BF16) for w in weights]
    for u in range(PAIR):
        out[u, :hd, :] = nn(feats[u], v_all[...]).astype(BF16)
        out[u, hd:, :] = thirds(nt(ones, feats[u])[:1])


def block_kernel(part, base, table, *refs):
    k_refs, v_refs = refs[:part], refs[part : 2 * part]
    q_refs, g_refs = refs[2 * part : 3 * part], refs[3 * part : 4 * part]
    w_ref, st_ref = refs[4 * part : 4 * part + 2]
    gq_refs = refs[4 * part + 2 : 5 * part + 2]
    dk_ref, dv_ref, sx_ref, gm_ref, k_all, v_all, vt_all, q_all, g_all, gq_all = refs[5 * part + 2 :]
    hd = k_all.shape[1]

    @pl.when(pl.program_id(0) == 0)
    def _():
        gather(table, base, k_refs, k_all)
        gather(table, base, v_refs, v_all)
        vt_all[...] = turned(v_all[...])
        dv_ref[...] = jnp.zeros_like(dv_ref)

    gather(table, base, q_refs, q_all)
    gather(table, base, g_refs, g_all)
    maps = []
    earlier = lax.broadcasted_iota(jnp.int32, (TILE, TILE), 0) <= lax.broadcasted_iota(
        jnp.int32, (TILE, TILE), 1
    )

    def causal(array, begin):
        masked = jnp.where(earlier, array[begin:], 0.0)
        return masked if begin == 0 else jnp.concatenate([array[:begin], masked], axis=0)

    heads = range(PAIR)
    lanes = [slice(u * hd, (u + 1) * hd) for u in heads]
    weight = [weight_rows(w_ref, u) for u in heads]
    half = weight[0].shape[0] // 2
    q_feat = [features(weight[u][:half], q_all[:, lanes[u]]) for u in heads]
    k_low = [features(weight[u][half:], k_all[...]).astype(BF16) for u in heads]
    q_low = [q_feat[u].astype(BF16) for u in heads]
    k_turned = [turned(k_low[u]) for u in heads]
    state = [st_ref[u, :hd, :] for u in heads]
    state_turned = [turned(state[u]) for u in heads]
    norm = [column(whole_row(st_ref[u, hd:, :]), TILE) for u in heads]
    g_turned = [g_all[:, lanes[u]].T for u in heads]
    back = [[] for u in heads]
    dkey = [[jnp.zeros((2 * half, TILE), F32) for _ in range(BLK // TILE)] for u in heads]
    dvalue = [[jnp.zeros((hd, TILE), F32) for _ in range(BLK // TILE)] for u in heads]
    suffix = [jnp.zeros((2 * half, hd), F32) for u in heads]
    suffix_norm = [jnp.zeros((2 * half, 1), F32) for u in heads]
    for j in range(BLK // TILE):
        begin, end = j * TILE, (j + 1) * TILE
        own = [q_low[u][:, begin:end] for u in heads]
        scores = [causal(nn(k_turned[u][:end], own[u]), begin) for u in heads]
        scores_low = [scores[u].astype(BF16) for u in heads]
        inverse = [
            1.0
            / (
                jnp.sum(own[u].astype(F32) * norm[u], axis=0, keepdims=True)
                + jnp.sum(scores[u], axis=0, keepdims=True)
            )
            for u in heads
        ]
        scaled = [g_turned[u][:, begin:end].astype(F32) * inverse[u] for u in heads]
        scaled_low = [scaled[u].astype(BF16) for u in heads]
        numerator = [
            nn(state_turned[u], own[u]) + nn(vt_all[:, :end], scores_low[u]) for u in heads
        ]
        products = [nn(v_all[:end, :], scaled_low[u]) for u in heads]
        norm_grad = [
            -jnp.sum(scaled[u] * (numerator[u] * inverse[u]), axis=0, keepdims=True)
            for u in heads
        ]
        dscores = [causal(products[u] + norm_grad[u], begin).astype(BF16) for u in heads]
        dquery = [
            nn(state[u], scaled_low[u])
            + norm[u] * norm_grad[u]
            + nn(k_low[u][:, :end], dscores[u])
            for u in heads
        ]
        for u in heads:
            back[u].append(feature_back(q_feat[u][:, begin:end], dquery[u]))
            for i in range(j + 1):
                rows = slice(i * TILE, (i + 1) * TILE)
                dkey[u][i] = dkey[u][i] + nt(own[u], dscores[u][rows])
                dvalue[u][i] = dvalue[u][i] + nt(scaled_low[u], scores_low[u][rows])
            suffix[u] = suffix[u] + nt(own[u], scaled_low[u])
            suffix_norm[u] = suffix_norm[u] + jnp.sum(
                own[u].astype(F32) * norm_grad[u], axis=1, keepdims=True
            )
    for u in heads:
        dlog = jnp.concatenate(back[u], axis=1)
        gq_all[:, lanes[u]] = nn(turned(dlog), weight[u][:half]).astype(BF16)
        maps.append(nn(dlog, q_all[:, lanes[u]]))
        dk_ref[u] = jnp.concatenate(dkey[u], axis=1)
        dv_ref[...] += jnp.concatenate(dvalue[u], axis=1)
        sx_ref[u, :hd, :] = suffix[u].astype(BF16)
        sx_ref[u, hd:, :] = thirds(jnp.broadcast_to(suffix_norm[u], (2 * half, 2 * half)).T[:1])
    gm_ref[0] = jnp.concatenate(maps, axis=0).T.astype(gm_ref.dtype)
    for r, ref in enumerate(gq_refs):
        rows = ref.shape[0]
        ref[...] = gq_all[pl.ds(pl.multiple_of(table[base + r] * rows, rows), rows), :]


def key_kernel(begun, part, base, table, *refs):
    k_refs, v_refs = refs[:part], refs[part : 2 * part]
    w_ref, sx_ref, dk_ref, dv_ref = refs[2 * part : 2 * part + 4]
    out, gm_ref, k_all, v_all, vt_all, total, logs, weights = refs[2 * part + 4 + begun :]
    hd = k_all.shape[1]
    step = pl.program_id(0)

    @pl.when(step == 0)
    def _():
        gather(table, base, k_refs, k_all)
        gather(table, base, v_refs, v_all)
        vt_all[...] = turned(v_all[...])
        total[...] = dv_ref[...]

    heads = range(PAIR)
    weight = [weight_rows(w_ref, u) for u in heads]
    half = weight[0].shape[0] // 2
    feats = [features(weight[u][half:], k_all[...]) for u in heads]
    suffix = [sx_ref[u, :hd, :] for u in heads]
    upstream = [
        dk_ref[u] + nn(suffix[u], vt_all[...]) + column(whole_row(sx_ref[u, hd:, :]), BLK)
        for u in heads
    ]
    dlog = [feature_back(feats[u], upstream[u]) for u in heads]
    maps = [nn(dlog[u], k_all[...]) for u in heads]
    for u in heads:
        at = pl.ds(pl.multiple_of((step * PAIR + u) * half, half), half)
        logs[at, :] = dlog[u]
        weights[at, :] = weight[u][half:]
    total[...] += sum(nn(turned(suffix[u]), feats[u].astype(BF16)) for u in heads)
    gm_ref[0] = jnp.concatenate(maps, axis=0).T.astype(gm_ref.dtype)

    @pl.when(step == pl.num_programs(0) - 1)
    def _():
        pair = jnp.concatenate([nn(turned(logs[...]), weights[...]), total[...].T], axis=1)
        out[...] = pair.astype(out.dtype).reshape(out.shape)


def total_kernel(table, *refs):
    out = refs[-1]
    heads, hd = out.shape[0], out.shape[2]
    for h in range(heads):
        out[h, :hd, :] = sum(ref[h, :hd, :].astype(F32) for ref in refs[:-1]).astype(BF16)
        out[h, hd:, :] = thirds(sum(whole_row(ref[h, hd:, :]) for ref in refs[:-1]))


def spread_kernel(grp, others, closing, block_weight, total_weight, at, table, *refs):
    parts, totals, refs = refs[:grp], refs[grp : grp + others], refs[grp + others :]
    if closing:
        outs, grad, scratch = refs[:grp], refs[grp], refs[grp + 1]
    else:
        state_ref, norm_ref, outs = refs[0], refs[1], refs[2:]
    heads, hd = parts[0].shape[0], parts[0].shape[2]
    for h in range(heads):
        states = [ref[h, :hd, :].astype(F32) for ref in parts]
        norms = [whole_row(ref[h, hd:, :]) for ref in parts]
        others_state = [ref[h, :hd, :].astype(F32) for ref in totals]
        others_norm = [whole_row(ref[h, hd:, :]) for ref in totals]
        if closing:
            base, base_norm = jnp.zeros_like(states[0]), jnp.zeros_like(norms[0])
            scratch[...] = sum(states) + sum(others_state)
            rows = grad.shape[1]
            grad[h] = scratch[pl.ds(pl.multiple_of(table[at] * rows, rows), rows), :]
        else:
            base, base_norm = state_ref[h], norm_ref[pl.ds(h, 1), :]
        for i, (state, norm) in enumerate(zip(others_state, others_norm)):
            base = base + table[total_weight + i].astype(F32) * state
            base_norm = base_norm + table[total_weight + i].astype(F32) * norm
        for r, out in enumerate(outs):
            state, norm = base, base_norm
            for i in range(grp):
                if i != r:
                    state = state + table[block_weight + r * grp + i].astype(F32) * states[i]
                    norm = norm + table[block_weight + r * grp + i].astype(F32) * norms[i]
            out[h, :hd, :] = state.astype(BF16)
            out[h, hd:, :] = thirds(norm)


def close_kernel(at, table, q_ref, k_ref, *refs):
    pieces, outs = refs[:-2], refs[-2:]
    for i, (own, out) in enumerate(zip((q_ref, k_ref), outs)):
        rows, half = out.shape[1:]
        mine = pl.ds(pl.multiple_of(table[at] * rows, rows), rows)
        for h in range(own.shape[0]):
            total = own[h, mine, :].astype(F32)
            for ref in pieces:
                total = total + ref[i, h].astype(F32)
            for u in range(PAIR):
                out[h * PAIR + u] = total[:, u * half : (u + 1) * half]


def whole_call(kernel, outs, table, arrays, name, scratch=()):
    return pl.pallas_call(
        kernel,
        out_shape=outs,
        in_specs=[pl.BlockSpec(memory_space=SMEM)]
        + [pl.BlockSpec(memory_space=pltpu.VMEM)] * len(arrays),
        out_specs=[pl.BlockSpec(memory_space=pltpu.VMEM)] * len(outs),
        scratch_shapes=list(scratch),
        compiler_params=pltpu.CompilerParams(vmem_limit_bytes=LIMIT),
        cost_estimate=LITTLE,
        name=name,
    )(table, *arrays)


def after(value, *others):
    return lax.optimization_barrier((value, *others))[0]


def shards(
    query_rows, key_rows, value_rows, grad_out, query_map, key_map, prefix_state, prefix_norm
):
    ctx, fsdp = lax.axis_size("ctx"), lax.axis_size("fsdp")
    tok = query_rows.shape[0]
    heads, map_rows, half = query_map.shape
    hd = map_rows * fsdp
    kv_heads = key_rows.shape[1] // hd
    replicas = ctx // kv_heads
    part = BLK // tok
    grp = ctx // part
    mine = lax.axis_index("ctx")
    at, block, seq = mine % part, mine // part, lax.axis_index("fsdp")
    shifts, slots = range(part), range(grp)
    order = list(reversed(slots))
    grid = (heads // PAIR,)
    blocks_of = [[g * part + p for p in range(part)] for g in slots]

    def within(array):
        return lax.all_to_all(array, "ctx", 0, 0, axis_index_groups=blocks_of, tiled=True)

    def around(array, shift):
        return lax.ppermute(
            array, "ctx", [(d, d // part * part + (d + shift) % part) for d in range(ctx)]
        )

    def across(array, shift):
        return lax.ppermute(array, "ctx", [(d, (d + shift * part) % ctx) for d in range(ctx)])

    def along(array, shift):
        return lax.ppermute(array, "fsdp", [(d, (d + shift) % fsdp) for d in range(fsdp)])

    def twin(array, bit):
        return lax.ppermute(array, "fsdp", [(d, d ^ bit) for d in range(fsdp)])

    def apart(array, s, r):
        moves = [
            (d * fsdp + i, (d + s * part) % ctx * fsdp + (i + r) % fsdp)
            for d in range(ctx)
            for i in range(fsdp)
        ]
        return lax.ppermute(array, ("ctx", "fsdp"), moves)

    slot = [(block + s) % grp for s in slots]
    near = [(block - r) % grp for r in slots]
    bits = [1 << i for i in range(fsdp.bit_length() - 1)]
    lists = {
        "seq": [seq],
        "owner": [slot[s] * part + p for s in slots for p in range(part)],
        "sent": [slot[s] * part + (at + r) % part for s in slots for r in shifts],
        "back": [slot[s] * part + (at + r) % part for s in slots for r in shifts],
        "kv": [
            (slot[s] * part + (at + r) % part) // replicas for r in shifts for s in slots
        ],
        "sorted": [(at - r) % part for r in shifts],
        "near before": [b < a for a in near for b in near],
        "near after": [b > a for a in near for b in near],
        "far before": [(seq ^ bit) < seq for bit in bits],
        "far after": [(seq ^ bit) > seq for bit in bits],
    }
    base, values = {}, []
    for name, entries in lists.items():
        base[name] = len(values)
        values += entries
    table = jnp.stack([jnp.asarray(v, jnp.int32) for v in values])

    own_maps = jnp.concatenate((query_map, key_map), axis=-1)
    near_maps = jnp.stack([own_maps] + [across(own_maps, -s) for s in slots[1:]])
    kv_sent = pack(table, base["kv"], (key_rows, value_rows), part, grp, hd)
    kv = [kv_sent[0]] + [around(kv_sent[r], r) for r in shifts[1:]]
    maps = lax.all_gather(near_maps, "fsdp")

    def sent_rows(s, *earlier):
        sent = pack(
            after(table, *earlier),
            base["sent"] + s * part,
            (query_rows, grad_out),
            part,
            1,
            heads * hd,
        )
        return [sent[0]] + [around(sent[r], r) for r in shifts[1:]]

    def piece_specs(column, count):
        return [pl.BlockSpec((tok, count * hd), lambda h, t: (0, column(h)))] * part

    def kv_specs(s):
        return piece_specs(lambda h: 2 * s, 1) + piece_specs(lambda h: 2 * s + 1, 1)

    def map_spec(s):
        return pl.BlockSpec((fsdp, None, PAIR, map_rows, 2 * half), lambda h, t: (0, s, h, 0, 0))

    def head_spec(*shape):
        return pl.BlockSpec((PAIR, *shape), lambda h, t: (h,) + (0,) * len(shape))

    def of(dtype, *shape):
        return jax.ShapeDtypeStruct(shape, dtype)

    ext_spec, ext_shape = head_spec(hd + EXT, hd), of(BF16, heads, hd + EXT, hd)
    gm_spec = pl.BlockSpec((1, hd, PAIR * half), lambda h, t: (h, 0, 0))
    gm_shape = of(BF16, heads // PAIR, hd, PAIR * half)
    dk_spec, dk_shape = head_spec(2 * half, BLK), of(F32, heads, 2 * half, BLK)
    dv_spec, dv_shape = pl.BlockSpec((hd, BLK), lambda h, t: (0, 0)), of(F32, hd, BLK)
    low, wide = pltpu.VMEM((BLK, hd), BF16), pltpu.VMEM((BLK, PAIR * hd), BF16)

    def call(kernel, outs, specs, out_specs, arrays, scratch, name, alias=(), limit=LIMIT):
        return pl.pallas_call(
            functools.partial(kernel, part, base["sorted"]),
            out_shape=outs,
            grid_spec=pltpu.PrefetchScalarGridSpec(
                num_scalar_prefetch=1,
                grid=grid,
                in_specs=specs,
                out_specs=out_specs,
                scratch_shapes=scratch,
            ),
            compiler_params=pltpu.CompilerParams(
                dimension_semantics=("arbitrary",), vmem_limit_bytes=limit
            ),
            cost_estimate=LITTLE,
            input_output_aliases=dict(alias),
            name=name,
        )(table, *arrays)

    def states_of(s):
        return call(
            state_kernel,
            [ext_shape],
            kv_specs(s) + [map_spec(s)],
            [ext_spec],
            [*kv, *kv, maps],
            [low, low],
            "states",
        )[0]

    def spread(parts, others, when, extra, closing):
        weights = [base["near " + when], base["far " + when], base["seq"]]
        result = whole_call(
            functools.partial(spread_kernel, grp, len(bits), closing, *weights),
            [ext_shape] * grp + [of(F32, heads, map_rows, hd)] * closing,
            table,
            parts + others + extra,
            "spread",
            [pltpu.VMEM((hd, hd), F32)] * closing,
        )
        return [result[0]] + [across(result[s], -s) for s in slots[1:]], result[grp:]

    def totals_of(parts):
        return whole_call(total_kernel, [ext_shape], table, parts, "totals")[0]

    def around_all(total):
        others = []
        for bit in bits:
            total = totals_of([total, others[-1]]) if others else total
            others.append(twin(total, bit))
        return others

    partial = {s: states_of(s) for s in order}
    parts = [partial[0]] + [across(partial[s], s) for s in slots[1:]]
    rows = {order[0]: sent_rows(order[0], near_maps, *kv)}
    parts[0] = after(parts[0], *rows[order[0]])
    others = around_all(totals_of(parts))
    state, _ = spread(parts, others, "before", [prefix_state, prefix_norm], False)
    for s in order[1:]:
        rows[s] = sent_rows(s, state[0])

    def block_of(s):
        return call(
            block_kernel,
            [of(BF16, tok, heads * hd)] * part + [dk_shape, dv_shape, ext_shape, gm_shape],
            kv_specs(s)
            + piece_specs(lambda h: h, PAIR)
            + piece_specs(lambda h: grid[0] + h, PAIR)
            + [map_spec(s), ext_spec],
            piece_specs(lambda h: h, PAIR) + [dk_spec, dv_spec, ext_spec, gm_spec],
            [*kv, *kv, *rows[s], *rows[s], maps, state[s]],
            [low, low, pltpu.VMEM((hd, BLK), BF16), wide, wide, wide],
            "blocks",
            limit=LARGE,
        )

    def rows_for(array, device):
        pieces = array.reshape(*array.shape[:-2], fsdp, map_rows, array.shape[-1])
        return lax.dynamic_index_in_dim(pieces, device % fsdp, array.ndim - 2, keepdims=False)

    blocks, parts = {}, {}
    for s in order:
        result = block_of(s)
        blocks[s] = (result[:part], *result[part:])
        parts[s] = across(blocks[s][3], s) if s else blocks[s][3]
    parts = [parts[s] for s in slots]
    total = totals_of(parts)
    others = around_all(total)
    suffix, (grad_prefix,) = spread(parts, others, "after", [], True)
    def brought_back(s, *begin):
        pieces = [after(piece, *begin) for piece in blocks[s][0]]
        return [pieces[0]] + [around(pieces[r], -r) for r in shifts[1:]]

    returned = {s: brought_back(s, others[0]) for s in order if s}
    earlier = [piece for s in returned for piece in returned[s]]

    kv_type = BF16 if replicas == 1 else F32
    pairs = of(kv_type, part, tok, grp * 2 * hd)
    moved, key_gm = [], {}
    for s in slots:
        begun = [] if s == 0 else [pairs]
        pairs, key_gm[s] = call(
            functools.partial(key_kernel, bool(begun)),
            [of(kv_type, *pairs.shape), gm_shape],
            kv_specs(s)
            + [map_spec(s), ext_spec, dk_spec, dv_spec]
            + [pl.BlockSpec(memory_space=pl.ANY)] * len(begun),
            [pl.BlockSpec((part, tok, 2 * hd), lambda h, t: (0, 0, s)), gm_spec],
            [*kv, *kv, maps, suffix[s], blocks[s][1], blocks[s][2], *begun],
            [
                low,
                low,
                pltpu.VMEM((hd, BLK), BF16),
                pltpu.VMEM((hd, BLK), F32),
                pltpu.VMEM((heads * half, BLK), BF16),
                pltpu.VMEM((heads * half, hd), BF16),
            ],
            "keys",
            {2 * part + 5: 0} if begun else {},
        )
        two = jnp.stack([blocks[s][4], key_gm[s]])
        if s:
            moved += [apart(rows_for(two, seq + r), s, r) for r in range(fsdp)]
        else:
            two = after(two, *suffix[1:])
            moved += [along(rows_for(two, seq + r), r) for r in range(1, fsdp)]
            returned[s] = brought_back(s, key_gm[s], *earlier)

    pairs = within(after(pairs, *returned[0]))
    back = [piece[None] for s in slots for piece in returned[s]]
    (grad_queries,) = unpack(table, base["back"], back, 1, 1, heads * hd)
    grad_keys, grad_values = unpack(table, base["owner"], [pairs], grp, 2, hd)
    if replicas > 1:
        grad_keys, grad_values = (
            jnp.sum(a.reshape(tok, kv_heads, replicas, hd), axis=2)
            .astype(BF16)
            .reshape(tok, kv_heads * hd)
            for a in (grad_keys, grad_values)
        )
    query_map_grad, key_map_grad = whole_call(
        functools.partial(close_kernel, base["seq"]),
        [of(F32, heads, map_rows, half)] * 2,
        table,
        [blocks[0][4], key_gm[0]] + moved,
        "close",
    )
    return grad_queries, grad_keys, grad_values, query_map_grad, key_map_grad, grad_prefix


def solution(mesh):
    rows, maps = P(("fsdp", "ctx"), None), P("ctx", "fsdp", None)
    return jax.shard_map(
        shards,
        mesh=mesh,
        in_specs=(rows,) * 4 + (maps, maps, P("ctx", None, None), P("ctx", None)),
        out_specs=(rows,) * 3 + (maps,) * 3,
        check_vma=False,
    )
```

```python
import functools

import jax
import jax.numpy as jnp
from jax import lax
from jax.experimental import pallas as pl
from jax.experimental.pallas import tpu as pltpu
from jax.sharding import PartitionSpec as P

BLK = 512
TILE = 256
PAIR = 2
EXT = 16
LIMIT = 40 * 1024 * 1024
LARGE = 56 * 1024 * 1024

LITTLE = pl.CostEstimate(flops=1000, bytes_accessed=1000, transcendentals=0)

F32 = jnp.float32
BF16 = jnp.bfloat16
SMEM = pltpu.SMEM


def nn(left, right):
    return lax.dot_general(left, right, (((1,), (0,)), ((), ())), preferred_element_type=F32)


def nt(left, right):
    return lax.dot_general(left, right, (((1,), (1,)), ((), ())), preferred_element_type=F32)


def turned(array):
    return array.T


def column(row, width):
    n = row.shape[1]
    square = jnp.broadcast_to(row, (n, n)).T
    return jnp.concatenate([square] * (width // n), axis=1)


def thirds(row):
    rows = jnp.broadcast_to(row, (EXT, row.shape[1]))
    high = rows.astype(BF16).astype(F32)
    middle = (rows - high).astype(BF16).astype(F32)
    low = rows - high - middle
    place = lax.broadcasted_iota(jnp.int32, rows.shape, 0)
    picked = jnp.where(place == 0, high, jnp.where(place == 1, middle, low))
    return jnp.where(place < 3, picked, 0.0).astype(BF16)


def whole_row(block):
    return jnp.sum(block.astype(F32), axis=0, keepdims=True)


def weight_rows(ref, u):
    whole = jnp.concatenate([ref[i, u] for i in range(ref.shape[0])], axis=0)
    return turned(whole)


def features(weight, rows):
    logits = nt(weight, rows).astype(BF16).astype(F32)
    upper = jnp.exp(logits)
    lower = jnp.exp(-logits)
    upper = upper * (1.0 / jnp.sum(upper, axis=0, keepdims=True))
    lower = lower * (1.0 / jnp.sum(lower, axis=0, keepdims=True))
    return jnp.concatenate([upper, lower], axis=0)


def feature_back(feats, upstream):
    half = feats.shape[0] // 2
    weighted = feats * upstream
    first, second = weighted[:half], weighted[half:]
    first = first - feats[:half] * jnp.sum(first, axis=0, keepdims=True)
    second = second - feats[half:] * jnp.sum(second, axis=0, keepdims=True)
    return (first - second).astype(BF16)


def gather(table, base, refs, out):
    rows = refs[0].shape[0]
    for r, ref in enumerate(refs):
        out[pl.ds(pl.multiple_of(table[base + r] * rows, rows), rows), :] = ref[...]


def pack_kernel(columns, inputs, table, *refs):
    count = columns * inputs
    for r, out in enumerate(refs[-(len(refs) // (count + 1)) :]):
        width = out.shape[1] // count
        for i in range(count):
            out[:, i * width : (i + 1) * width] = refs[r * count + i][...]


def pack(table, base, sources, pieces, columns, width):
    rows = sources[0].shape[0]
    count = columns * len(sources)
    step = rows // 2

    def take(at):
        return pl.BlockSpec((step, width), lambda i, t: (i, t[base + at]))

    return pl.pallas_call(
        functools.partial(pack_kernel, columns, len(sources)),
        out_shape=[jax.ShapeDtypeStruct((rows, count * width), sources[0].dtype)] * pieces,
        grid_spec=pltpu.PrefetchScalarGridSpec(
            num_scalar_prefetch=1,
            grid=(rows // step,),
            in_specs=[
                take(r * columns + s)
                for r in range(pieces)
                for s in range(columns)
                for _ in sources
            ],
            out_specs=[pl.BlockSpec((step, count * width), lambda i, t: (i, 0))] * pieces,
        ),
        compiler_params=pltpu.CompilerParams(vmem_limit_bytes=LIMIT),
        cost_estimate=LITTLE,
        name="pack",
    )(table, *(list(sources) * (pieces * columns)))


def unpack_kernel(outputs, inner, base, table, *refs):
    sources, outs = refs[:-outputs], refs[-outputs:]
    for s, source in enumerate(sources):
        pieces = source.shape[0]
        width = source.shape[2] // (outputs * inner)
        for r in range(pieces):
            for j in range(inner):
                slot = s * inner + j
                at = table[base + slot * pieces + r] * width
                for i, out in enumerate(outs):
                    lanes = slice((j * outputs + i) * width, (j * outputs + i + 1) * width)
                    out[:, pl.ds(pl.multiple_of(at, width), width)] = source[r, :, lanes]


def unpack(table, base, sources, inner, outputs, width):
    pieces, rows = sources[0].shape[:2]
    total = len(sources) * inner * pieces * width
    step = rows // 2
    taken = pl.BlockSpec((pieces, step, inner * outputs * width), lambda i: (0, i, 0))
    return pl.pallas_call(
        functools.partial(unpack_kernel, outputs, inner, base),
        out_shape=[jax.ShapeDtypeStruct((rows, total), sources[0].dtype)] * outputs,
        grid=(rows // step,),
        in_specs=[pl.BlockSpec(memory_space=SMEM)] + [taken] * len(sources),
        out_specs=[pl.BlockSpec((step, total), lambda i: (i, 0))] * outputs,
        compiler_params=pltpu.CompilerParams(vmem_limit_bytes=LIMIT),
        cost_estimate=LITTLE,
        name="unpack",
    )(table, *sources)


def state_kernel(part, base, table, *refs):
    k_refs, v_refs, (w_ref, out, k_all, v_all) = refs[:part], refs[part : 2 * part], refs[2 * part :]
    hd = k_all.shape[1]

    @pl.when(pl.program_id(0) == 0)
    def _():
        gather(table, base, k_refs, k_all)
        gather(table, base, v_refs, v_all)

    ones = jnp.ones((EXT, k_all.shape[0]), BF16)
    weights = [weight_rows(w_ref, u) for u in range(PAIR)]
    feats = [features(w[w.shape[0] // 2 :], k_all[...]).astype(BF16) for w in weights]
    for u in range(PAIR):
        out[u, :hd, :] = nn(feats[u], v_all[...]).astype(BF16)
        out[u, hd:, :] = thirds(nt(ones, feats[u])[:1])


def block_kernel(part, base, table, *refs):
    k_refs, v_refs = refs[:part], refs[part : 2 * part]
    q_refs, g_refs = refs[2 * part : 3 * part], refs[3 * part : 4 * part]
    w_ref, st_ref = refs[4 * part : 4 * part + 2]
    gq_refs = refs[4 * part + 2 : 5 * part + 2]
    dk_ref, dv_ref, sx_ref, gm_ref, k_all, v_all, vt_all, q_all, g_all, gq_all = refs[5 * part + 2 :]
    hd = k_all.shape[1]

    @pl.when(pl.program_id(0) == 0)
    def _():
        gather(table, base, k_refs, k_all)
        gather(table, base, v_refs, v_all)
        vt_all[...] = turned(v_all[...])
        dv_ref[...] = jnp.zeros_like(dv_ref)

    gather(table, base, q_refs, q_all)
    gather(table, base, g_refs, g_all)
    maps = []
    earlier = lax.broadcasted_iota(jnp.int32, (TILE, TILE), 0) <= lax.broadcasted_iota(
        jnp.int32, (TILE, TILE), 1
    )

    def causal(array, begin):
        masked = jnp.where(earlier, array[begin:], 0.0)
        return masked if begin == 0 else jnp.concatenate([array[:begin], masked], axis=0)

    heads = range(PAIR)
    lanes = [slice(u * hd, (u + 1) * hd) for u in heads]
    weight = [weight_rows(w_ref, u) for u in heads]
    half = weight[0].shape[0] // 2
    q_feat = [features(weight[u][:half], q_all[:, lanes[u]]) for u in heads]
    k_low = [features(weight[u][half:], k_all[...]).astype(BF16) for u in heads]
    q_low = [q_feat[u].astype(BF16) for u in heads]
    k_turned = [turned(k_low[u]) for u in heads]
    state = [st_ref[u, :hd, :] for u in heads]
    state_turned = [turned(state[u]) for u in heads]
    norm = [column(whole_row(st_ref[u, hd:, :]), TILE) for u in heads]
    g_turned = [g_all[:, lanes[u]].T for u in heads]
    back = [[] for u in heads]
    dkey = [[jnp.zeros((2 * half, TILE), F32) for _ in range(BLK // TILE)] for u in heads]
    dvalue = [[jnp.zeros((hd, TILE), F32) for _ in range(BLK // TILE)] for u in heads]
    suffix = [jnp.zeros((2 * half, hd), F32) for u in heads]
    suffix_norm = [jnp.zeros((2 * half, 1), F32) for u in heads]
    chains = [(u, j) for j in range(BLK // TILE) for u in heads]
    tile = {(u, j): slice(j * TILE, (j + 1) * TILE) for u, j in chains}
    own = {c: q_low[c[0]][:, tile[c]] for c in chains}
    scores = {c: causal(nn(k_turned[c[0]][: tile[c].stop], own[c]), tile[c].start) for c in chains}
    scores_low = {c: scores[c].astype(BF16) for c in chains}
    inverse = {
        c: 1.0
        / (
            jnp.sum(own[c].astype(F32) * norm[c[0]], axis=0, keepdims=True)
            + jnp.sum(scores[c], axis=0, keepdims=True)
        )
        for c in chains
    }
    scaled = {c: g_turned[c[0]][:, tile[c]].astype(F32) * inverse[c] for c in chains}
    scaled_low = {c: scaled[c].astype(BF16) for c in chains}
    numerator = {
        c: nn(state_turned[c[0]], own[c]) + nn(vt_all[:, : tile[c].stop], scores_low[c])
        for c in chains
    }
    products = {c: nn(v_all[: tile[c].stop, :], scaled_low[c]) for c in chains}
    norm_grad = {
        c: -jnp.sum(scaled[c] * (numerator[c] * inverse[c]), axis=0, keepdims=True)
        for c in chains
    }
    dscores = {
        c: causal(products[c] + norm_grad[c], tile[c].start).astype(BF16) for c in chains
    }
    dquery = {
        c: nn(state[c[0]], scaled_low[c])
        + norm[c[0]] * norm_grad[c]
        + nn(k_low[c[0]][:, : tile[c].stop], dscores[c])
        for c in chains
    }
    for c in chains:
        u, j = c
        back[u].append(feature_back(q_feat[u][:, tile[c]], dquery[c]))
        for i in range(j + 1):
            rows = slice(i * TILE, (i + 1) * TILE)
            dkey[u][i] = dkey[u][i] + nt(own[c], dscores[c][rows])
            dvalue[u][i] = dvalue[u][i] + nt(scaled_low[c], scores_low[c][rows])
        suffix[u] = suffix[u] + nt(own[c], scaled_low[c])
        suffix_norm[u] = suffix_norm[u] + jnp.sum(
            own[c].astype(F32) * norm_grad[c], axis=1, keepdims=True
        )
    for u in heads:
        dlog = jnp.concatenate(back[u], axis=1)
        gq_all[:, lanes[u]] = nn(turned(dlog), weight[u][:half]).astype(BF16)
        maps.append(nn(dlog, q_all[:, lanes[u]]))
        dk_ref[u] = jnp.concatenate(dkey[u], axis=1)
        dv_ref[...] += jnp.concatenate(dvalue[u], axis=1)
        sx_ref[u, :hd, :] = suffix[u].astype(BF16)
        sx_ref[u, hd:, :] = thirds(jnp.broadcast_to(suffix_norm[u], (2 * half, 2 * half)).T[:1])
    gm_ref[0] = jnp.concatenate(maps, axis=0).T.astype(gm_ref.dtype)
    for r, ref in enumerate(gq_refs):
        rows = ref.shape[0]
        ref[...] = gq_all[pl.ds(pl.multiple_of(table[base + r] * rows, rows), rows), :]


def key_kernel(begun, part, base, table, *refs):
    k_refs, v_refs = refs[:part], refs[part : 2 * part]
    w_ref, sx_ref, dk_ref, dv_ref = refs[2 * part : 2 * part + 4]
    out, gm_ref, k_all, v_all, vt_all, total, logs, weights = refs[2 * part + 4 + begun :]
    hd = k_all.shape[1]
    step = pl.program_id(0)

    @pl.when(step == 0)
    def _():
        gather(table, base, k_refs, k_all)
        gather(table, base, v_refs, v_all)
        vt_all[...] = turned(v_all[...])
        total[...] = dv_ref[...]

    heads = range(PAIR)
    weight = [weight_rows(w_ref, u) for u in heads]
    half = weight[0].shape[0] // 2
    feats = [features(weight[u][half:], k_all[...]) for u in heads]
    suffix = [sx_ref[u, :hd, :] for u in heads]
    upstream = [
        dk_ref[u] + nn(suffix[u], vt_all[...]) + column(whole_row(sx_ref[u, hd:, :]), BLK)
        for u in heads
    ]
    dlog = [feature_back(feats[u], upstream[u]) for u in heads]
    maps = [nn(dlog[u], k_all[...]) for u in heads]
    for u in heads:
        at = pl.ds(pl.multiple_of((step * PAIR + u) * half, half), half)
        logs[at, :] = dlog[u]
        weights[at, :] = weight[u][half:]
    total[...] += sum(nn(turned(suffix[u]), feats[u].astype(BF16)) for u in heads)
    gm_ref[0] = jnp.concatenate(maps, axis=0).T.astype(gm_ref.dtype)

    @pl.when(step == pl.num_programs(0) - 1)
    def _():
        pair = jnp.concatenate([nn(turned(logs[...]), weights[...]), total[...].T], axis=1)
        out[...] = pair.astype(out.dtype).reshape(out.shape)


def total_kernel(table, *refs):
    out = refs[-1]
    heads, hd = out.shape[0], out.shape[2]
    for h in range(heads):
        out[h, :hd, :] = sum(ref[h, :hd, :].astype(F32) for ref in refs[:-1]).astype(BF16)
        out[h, hd:, :] = thirds(sum(whole_row(ref[h, hd:, :]) for ref in refs[:-1]))


def spread_kernel(grp, others, closing, block_weight, total_weight, at, table, *refs):
    parts, totals, refs = refs[:grp], refs[grp : grp + others], refs[grp + others :]
    if closing:
        outs, grad, scratch = refs[:grp], refs[grp], refs[grp + 1]
    else:
        state_ref, norm_ref, outs = refs[0], refs[1], refs[2:]
    heads, hd = parts[0].shape[0], parts[0].shape[2]
    for h in range(heads):
        states = [ref[h, :hd, :].astype(F32) for ref in parts]
        norms = [whole_row(ref[h, hd:, :]) for ref in parts]
        others_state = [ref[h, :hd, :].astype(F32) for ref in totals]
        others_norm = [whole_row(ref[h, hd:, :]) for ref in totals]
        if closing:
            base, base_norm = jnp.zeros_like(states[0]), jnp.zeros_like(norms[0])
            scratch[...] = sum(states) + sum(others_state)
            rows = grad.shape[1]
            grad[h] = scratch[pl.ds(pl.multiple_of(table[at] * rows, rows), rows), :]
        else:
            base, base_norm = state_ref[h], norm_ref[pl.ds(h, 1), :]
        for i, (state, norm) in enumerate(zip(others_state, others_norm)):
            base = base + table[total_weight + i].astype(F32) * state
            base_norm = base_norm + table[total_weight + i].astype(F32) * norm
        for r, out in enumerate(outs):
            state, norm = base, base_norm
            for i in range(grp):
                if i != r:
                    state = state + table[block_weight + r * grp + i].astype(F32) * states[i]
                    norm = norm + table[block_weight + r * grp + i].astype(F32) * norms[i]
            out[h, :hd, :] = state.astype(BF16)
            out[h, hd:, :] = thirds(norm)


def close_kernel(at, table, q_ref, k_ref, *refs):
    pieces, outs = refs[:-2], refs[-2:]
    for i, (own, out) in enumerate(zip((q_ref, k_ref), outs)):
        rows, half = out.shape[1:]
        mine = pl.ds(pl.multiple_of(table[at] * rows, rows), rows)
        for h in range(own.shape[0]):
            total = own[h, mine, :].astype(F32)
            for ref in pieces:
                total = total + ref[i, h].astype(F32)
            for u in range(PAIR):
                out[h * PAIR + u] = total[:, u * half : (u + 1) * half]


def whole_call(kernel, outs, table, arrays, name, scratch=()):
    return pl.pallas_call(
        kernel,
        out_shape=outs,
        in_specs=[pl.BlockSpec(memory_space=SMEM)]
        + [pl.BlockSpec(memory_space=pltpu.VMEM)] * len(arrays),
        out_specs=[pl.BlockSpec(memory_space=pltpu.VMEM)] * len(outs),
        scratch_shapes=list(scratch),
        compiler_params=pltpu.CompilerParams(vmem_limit_bytes=LIMIT),
        cost_estimate=LITTLE,
        name=name,
    )(table, *arrays)


def after(value, *others):
    return lax.optimization_barrier((value, *others))[0]


def shards(
    query_rows, key_rows, value_rows, grad_out, query_map, key_map, prefix_state, prefix_norm
):
    ctx, fsdp = lax.axis_size("ctx"), lax.axis_size("fsdp")
    tok = query_rows.shape[0]
    heads, map_rows, half = query_map.shape
    hd = map_rows * fsdp
    kv_heads = key_rows.shape[1] // hd
    replicas = ctx // kv_heads
    part = BLK // tok
    grp = ctx // part
    mine = lax.axis_index("ctx")
    at, block, seq = mine % part, mine // part, lax.axis_index("fsdp")
    shifts, slots = range(part), range(grp)
    order = list(reversed(slots))
    grid = (heads // PAIR,)
    blocks_of = [[g * part + p for p in range(part)] for g in slots]

    def within(array):
        return lax.all_to_all(array, "ctx", 0, 0, axis_index_groups=blocks_of, tiled=True)

    def around(array, shift):
        return lax.ppermute(
            array, "ctx", [(d, d // part * part + (d + shift) % part) for d in range(ctx)]
        )

    def across(array, shift):
        return lax.ppermute(array, "ctx", [(d, (d + shift * part) % ctx) for d in range(ctx)])

    def along(array, shift):
        return lax.ppermute(array, "fsdp", [(d, (d + shift) % fsdp) for d in range(fsdp)])

    def twin(array, bit):
        return lax.ppermute(array, "fsdp", [(d, d ^ bit) for d in range(fsdp)])

    def apart(array, s, r):
        moves = [
            (d * fsdp + i, (d + s * part) % ctx * fsdp + (i + r) % fsdp)
            for d in range(ctx)
            for i in range(fsdp)
        ]
        return lax.ppermute(array, ("ctx", "fsdp"), moves)

    slot = [(block + s) % grp for s in slots]
    near = [(block - r) % grp for r in slots]
    bits = [1 << i for i in range(fsdp.bit_length() - 1)]
    lists = {
        "seq": [seq],
        "owner": [slot[s] * part + p for s in slots for p in range(part)],
        "sent": [slot[s] * part + (at + r) % part for s in slots for r in shifts],
        "back": [slot[s] * part + (at + r) % part for s in slots for r in shifts],
        "kv": [
            (slot[s] * part + (at + r) % part) // replicas for r in shifts for s in slots
        ],
        "sorted": [(at - r) % part for r in shifts],
        "near before": [b < a for a in near for b in near],
        "near after": [b > a for a in near for b in near],
        "far before": [(seq ^ bit) < seq for bit in bits],
        "far after": [(seq ^ bit) > seq for bit in bits],
    }
    base, values = {}, []
    for name, entries in lists.items():
        base[name] = len(values)
        values += entries
    table = jnp.stack([jnp.asarray(v, jnp.int32) for v in values])

    own_maps = jnp.concatenate((query_map, key_map), axis=-1)
    near_maps = jnp.stack([own_maps] + [across(own_maps, -s) for s in slots[1:]])
    kv_sent = pack(table, base["kv"], (key_rows, value_rows), part, grp, hd)
    kv = [kv_sent[0]] + [around(kv_sent[r], r) for r in shifts[1:]]
    maps = lax.all_gather(near_maps, "fsdp")

    def sent_rows(s, *earlier):
        sent = pack(
            after(table, *earlier),
            base["sent"] + s * part,
            (query_rows, grad_out),
            part,
            1,
            heads * hd,
        )
        return [sent[0]] + [around(sent[r], r) for r in shifts[1:]]

    def piece_specs(column, count):
        return [pl.BlockSpec((tok, count * hd), lambda h, t: (0, column(h)))] * part

    def kv_specs(s):
        return piece_specs(lambda h: 2 * s, 1) + piece_specs(lambda h: 2 * s + 1, 1)

    def map_spec(s):
        return pl.BlockSpec((fsdp, None, PAIR, map_rows, 2 * half), lambda h, t: (0, s, h, 0, 0))

    def head_spec(*shape):
        return pl.BlockSpec((PAIR, *shape), lambda h, t: (h,) + (0,) * len(shape))

    def of(dtype, *shape):
        return jax.ShapeDtypeStruct(shape, dtype)

    ext_spec, ext_shape = head_spec(hd + EXT, hd), of(BF16, heads, hd + EXT, hd)
    gm_spec = pl.BlockSpec((1, hd, PAIR * half), lambda h, t: (h, 0, 0))
    gm_shape = of(BF16, heads // PAIR, hd, PAIR * half)
    dk_spec, dk_shape = head_spec(2 * half, BLK), of(F32, heads, 2 * half, BLK)
    dv_spec, dv_shape = pl.BlockSpec((hd, BLK), lambda h, t: (0, 0)), of(F32, hd, BLK)
    low, wide = pltpu.VMEM((BLK, hd), BF16), pltpu.VMEM((BLK, PAIR * hd), BF16)

    def call(kernel, outs, specs, out_specs, arrays, scratch, name, alias=(), limit=LIMIT):
        return pl.pallas_call(
            functools.partial(kernel, part, base["sorted"]),
            out_shape=outs,
            grid_spec=pltpu.PrefetchScalarGridSpec(
                num_scalar_prefetch=1,
                grid=grid,
                in_specs=specs,
                out_specs=out_specs,
                scratch_shapes=scratch,
            ),
            compiler_params=pltpu.CompilerParams(
                dimension_semantics=("arbitrary",), vmem_limit_bytes=limit
            ),
            cost_estimate=LITTLE,
            input_output_aliases=dict(alias),
            name=name,
        )(table, *arrays)

    def states_of(s):
        return call(
            state_kernel,
            [ext_shape],
            kv_specs(s) + [map_spec(s)],
            [ext_spec],
            [*kv, *kv, maps],
            [low, low],
            "states",
        )[0]

    def spread(parts, others, when, extra, closing):
        weights = [base["near " + when], base["far " + when], base["seq"]]
        result = whole_call(
            functools.partial(spread_kernel, grp, len(bits), closing, *weights),
            [ext_shape] * grp + [of(F32, heads, map_rows, hd)] * closing,
            table,
            parts + others + extra,
            "spread",
            [pltpu.VMEM((hd, hd), F32)] * closing,
        )
        return [result[0]] + [across(result[s], -s) for s in slots[1:]], result[grp:]

    def totals_of(parts):
        return whole_call(total_kernel, [ext_shape], table, parts, "totals")[0]

    def around_all(total):
        others = []
        for bit in bits:
            total = totals_of([total, others[-1]]) if others else total
            others.append(twin(total, bit))
        return others

    partial = {s: states_of(s) for s in order}
    parts = [partial[0]] + [across(partial[s], s) for s in slots[1:]]
    rows = {order[0]: sent_rows(order[0], near_maps, *kv)}
    parts[0] = after(parts[0], *rows[order[0]])
    others = around_all(totals_of(parts))
    state, _ = spread(parts, others, "before", [prefix_state, prefix_norm], False)
    for s in order[1:]:
        rows[s] = sent_rows(s, state[0])

    def block_of(s):
        return call(
            block_kernel,
            [of(BF16, tok, heads * hd)] * part + [dk_shape, dv_shape, ext_shape, gm_shape],
            kv_specs(s)
            + piece_specs(lambda h: h, PAIR)
            + piece_specs(lambda h: grid[0] + h, PAIR)
            + [map_spec(s), ext_spec],
            piece_specs(lambda h: h, PAIR) + [dk_spec, dv_spec, ext_spec, gm_spec],
            [*kv, *kv, *rows[s], *rows[s], maps, state[s]],
            [low, low, pltpu.VMEM((hd, BLK), BF16), wide, wide, wide],
            "blocks",
            limit=LARGE,
        )

    def rows_for(array, device):
        pieces = array.reshape(*array.shape[:-2], fsdp, map_rows, array.shape[-1])
        return lax.dynamic_index_in_dim(pieces, device % fsdp, array.ndim - 2, keepdims=False)

    blocks, parts = {}, {}
    for s in order:
        result = block_of(s)
        blocks[s] = (result[:part], *result[part:])
        parts[s] = across(blocks[s][3], s) if s else blocks[s][3]
    parts = [parts[s] for s in slots]
    total = totals_of(parts)
    others = around_all(total)
    suffix, (grad_prefix,) = spread(parts, others, "after", [], True)
    def brought_back(s, *begin):
        pieces = [after(piece, *begin) for piece in blocks[s][0]]
        return [pieces[0]] + [around(pieces[r], -r) for r in shifts[1:]]

    returned = {s: brought_back(s, others[0]) for s in order if s}
    earlier = [piece for s in returned for piece in returned[s]]

    kv_type = BF16 if replicas == 1 else F32
    pairs = of(kv_type, part, tok, grp * 2 * hd)
    moved, key_gm = [], {}
    for s in slots:
        begun = [] if s == 0 else [pairs]
        pairs, key_gm[s] = call(
            functools.partial(key_kernel, bool(begun)),
            [of(kv_type, *pairs.shape), gm_shape],
            kv_specs(s)
            + [map_spec(s), ext_spec, dk_spec, dv_spec]
            + [pl.BlockSpec(memory_space=pl.ANY)] * len(begun),
            [pl.BlockSpec((part, tok, 2 * hd), lambda h, t: (0, 0, s)), gm_spec],
            [*kv, *kv, maps, suffix[s], blocks[s][1], blocks[s][2], *begun],
            [
                low,
                low,
                pltpu.VMEM((hd, BLK), BF16),
                pltpu.VMEM((hd, BLK), F32),
                pltpu.VMEM((heads * half, BLK), BF16),
                pltpu.VMEM((heads * half, hd), BF16),
            ],
            "keys",
            {2 * part + 5: 0} if begun else {},
        )
        two = jnp.stack([blocks[s][4], key_gm[s]])
        if s:
            moved += [apart(rows_for(two, seq + r), s, r) for r in range(fsdp)]
        else:
            two = after(two, *suffix[1:])
            moved += [along(rows_for(two, seq + r), r) for r in range(1, fsdp)]
            returned[s] = brought_back(s, key_gm[s], *earlier)

    pairs = within(after(pairs, *returned[0]))
    back = [piece[None] for s in slots for piece in returned[s]]
    (grad_queries,) = unpack(table, base["back"], back, 1, 1, heads * hd)
    grad_keys, grad_values = unpack(table, base["owner"], [pairs], grp, 2, hd)
    if replicas > 1:
        grad_keys, grad_values = (
            jnp.sum(a.reshape(tok, kv_heads, replicas, hd), axis=2)
            .astype(BF16)
            .reshape(tok, kv_heads * hd)
            for a in (grad_keys, grad_values)
        )
    query_map_grad, key_map_grad = whole_call(
        functools.partial(close_kernel, base["seq"]),
        [of(F32, heads, map_rows, half)] * 2,
        table,
        [blocks[0][4], key_gm[0]] + moved,
        "close",
    )
    return grad_queries, grad_keys, grad_values, query_map_grad, key_map_grad, grad_prefix


def solution(mesh):
    rows, maps = P(("fsdp", "ctx"), None), P("ctx", "fsdp", None)
    return jax.shard_map(
        shards,
        mesh=mesh,
        in_specs=(rows,) * 4 + (maps, maps, P("ctx", None, None), P("ctx", None)),
        out_specs=(rows,) * 3 + (maps,) * 3,
        check_vma=False,
    )
```

```python
import functools

import jax
import jax.numpy as jnp
from jax import lax
from jax.experimental import pallas as pl
from jax.experimental.pallas import tpu as pltpu
from jax.sharding import PartitionSpec as P

BLK = 512
TILE = 256
PAIR = 2
EXT = 16
LIMIT = 40 * 1024 * 1024
LARGE = 56 * 1024 * 1024

LITTLE = pl.CostEstimate(flops=1000, bytes_accessed=1000, transcendentals=0)

F32 = jnp.float32
BF16 = jnp.bfloat16
SMEM = pltpu.SMEM


def nn(left, right):
    return lax.dot_general(left, right, (((1,), (0,)), ((), ())), preferred_element_type=F32)


def nt(left, right):
    return lax.dot_general(left, right, (((1,), (1,)), ((), ())), preferred_element_type=F32)


def turned(array):
    return array.T


def column(row, width):
    n = row.shape[1]
    square = jnp.broadcast_to(row, (n, n)).T
    return jnp.concatenate([square] * (width // n), axis=1)


def thirds(row):
    rows = jnp.broadcast_to(row, (EXT, row.shape[1]))
    high = rows.astype(BF16).astype(F32)
    middle = (rows - high).astype(BF16).astype(F32)
    low = rows - high - middle
    place = lax.broadcasted_iota(jnp.int32, rows.shape, 0)
    picked = jnp.where(place == 0, high, jnp.where(place == 1, middle, low))
    return jnp.where(place < 3, picked, 0.0).astype(BF16)


def whole_row(block):
    return jnp.sum(block.astype(F32), axis=0, keepdims=True)


def weight_rows(ref, u):
    whole = jnp.concatenate([ref[i, u] for i in range(ref.shape[0])], axis=0)
    return turned(whole)


def features(weight, rows):
    logits = nt(weight, rows).astype(BF16).astype(F32)
    upper = jnp.exp(logits)
    lower = jnp.exp(-logits)
    upper = upper * (1.0 / jnp.sum(upper, axis=0, keepdims=True))
    lower = lower * (1.0 / jnp.sum(lower, axis=0, keepdims=True))
    return jnp.concatenate([upper, lower], axis=0)


def feature_back(feats, upstream):
    half = feats.shape[0] // 2
    weighted = feats * upstream
    first, second = weighted[:half], weighted[half:]
    first = first - feats[:half] * jnp.sum(first, axis=0, keepdims=True)
    second = second - feats[half:] * jnp.sum(second, axis=0, keepdims=True)
    return (first - second).astype(BF16)


def gather(table, base, refs, out):
    rows = refs[0].shape[0]
    for r, ref in enumerate(refs):
        out[pl.ds(pl.multiple_of(table[base + r] * rows, rows), rows), :] = ref[...]


def pack_kernel(columns, inputs, table, *refs):
    count = columns * inputs
    for r, out in enumerate(refs[-(len(refs) // (count + 1)) :]):
        width = out.shape[1] // count
        for i in range(count):
            out[:, i * width : (i + 1) * width] = refs[r * count + i][...]


def pack(table, base, sources, pieces, columns, width):
    rows = sources[0].shape[0]
    count = columns * len(sources)
    step = rows // 2

    def take(at):
        return pl.BlockSpec((step, width), lambda i, t: (i, t[base + at]))

    return pl.pallas_call(
        functools.partial(pack_kernel, columns, len(sources)),
        out_shape=[jax.ShapeDtypeStruct((rows, count * width), sources[0].dtype)] * pieces,
        grid_spec=pltpu.PrefetchScalarGridSpec(
            num_scalar_prefetch=1,
            grid=(rows // step,),
            in_specs=[
                take(r * columns + s)
                for r in range(pieces)
                for s in range(columns)
                for _ in sources
            ],
            out_specs=[pl.BlockSpec((step, count * width), lambda i, t: (i, 0))] * pieces,
        ),
        compiler_params=pltpu.CompilerParams(vmem_limit_bytes=LIMIT),
        cost_estimate=LITTLE,
        name="pack",
    )(table, *(list(sources) * (pieces * columns)))


def unpack_kernel(outputs, inner, base, table, *refs):
    sources, outs = refs[:-outputs], refs[-outputs:]
    for s, source in enumerate(sources):
        pieces = source.shape[0]
        width = source.shape[2] // (outputs * inner)
        for r in range(pieces):
            for j in range(inner):
                slot = s * inner + j
                at = table[base + slot * pieces + r] * width
                for i, out in enumerate(outs):
                    lanes = slice((j * outputs + i) * width, (j * outputs + i + 1) * width)
                    out[:, pl.ds(pl.multiple_of(at, width), width)] = source[r, :, lanes]


def unpack(table, base, sources, inner, outputs, width):
    pieces, rows = sources[0].shape[:2]
    total = len(sources) * inner * pieces * width
    step = rows // 2
    taken = pl.BlockSpec((pieces, step, inner * outputs * width), lambda i: (0, i, 0))
    return pl.pallas_call(
        functools.partial(unpack_kernel, outputs, inner, base),
        out_shape=[jax.ShapeDtypeStruct((rows, total), sources[0].dtype)] * outputs,
        grid=(rows // step,),
        in_specs=[pl.BlockSpec(memory_space=SMEM)] + [taken] * len(sources),
        out_specs=[pl.BlockSpec((step, total), lambda i: (i, 0))] * outputs,
        compiler_params=pltpu.CompilerParams(vmem_limit_bytes=LIMIT),
        cost_estimate=LITTLE,
        name="unpack",
    )(table, *sources)


def state_kernel(part, base, table, *refs):
    k_refs, v_refs, (w_ref, out, k_all, v_all) = refs[:part], refs[part : 2 * part], refs[2 * part :]
    hd = k_all.shape[1]

    @pl.when(pl.program_id(0) == 0)
    def _():
        gather(table, base, k_refs, k_all)
        gather(table, base, v_refs, v_all)

    ones = jnp.ones((EXT, k_all.shape[0]), BF16)
    weights = [weight_rows(w_ref, u) for u in range(PAIR)]
    feats = [features(w[w.shape[0] // 2 :], k_all[...]).astype(BF16) for w in weights]
    for u in range(PAIR):
        out[u, :hd, :] = nn(feats[u], v_all[...]).astype(BF16)
        out[u, hd:, :] = thirds(nt(ones, feats[u])[:1])


def block_kernel(part, base, table, *refs):
    k_refs, v_refs = refs[:part], refs[part : 2 * part]
    q_refs, g_refs = refs[2 * part : 3 * part], refs[3 * part : 4 * part]
    w_ref, st_ref = refs[4 * part : 4 * part + 2]
    gq_refs = refs[4 * part + 2 : 5 * part + 2]
    dk_ref, dv_ref, sx_ref, gm_ref, k_all, v_all, vt_all, q_all, g_all, gq_all = refs[5 * part + 2 :]
    hd = k_all.shape[1]

    @pl.when(pl.program_id(0) == 0)
    def _():
        gather(table, base, k_refs, k_all)
        gather(table, base, v_refs, v_all)
        vt_all[...] = turned(v_all[...])
        dv_ref[...] = jnp.zeros_like(dv_ref)

    gather(table, base, q_refs, q_all)
    gather(table, base, g_refs, g_all)
    maps = []
    earlier = lax.broadcasted_iota(jnp.int32, (TILE, TILE), 0) <= lax.broadcasted_iota(
        jnp.int32, (TILE, TILE), 1
    )

    def causal(array, begin):
        masked = jnp.where(earlier, array[begin:], 0.0)
        return masked if begin == 0 else jnp.concatenate([array[:begin], masked], axis=0)

    heads = range(PAIR)
    lanes = [slice(u * hd, (u + 1) * hd) for u in heads]
    weight = [weight_rows(w_ref, u) for u in heads]
    half = weight[0].shape[0] // 2
    q_feat = [features(weight[u][:half], q_all[:, lanes[u]]) for u in heads]
    k_low = [features(weight[u][half:], k_all[...]).astype(BF16) for u in heads]
    q_low = [q_feat[u].astype(BF16) for u in heads]
    k_turned = [turned(k_low[u]) for u in heads]
    state = [st_ref[u, :hd, :] for u in heads]
    state_turned = [turned(state[u]) for u in heads]
    norm = [column(whole_row(st_ref[u, hd:, :]), TILE) for u in heads]
    g_turned = [g_all[:, lanes[u]].T for u in heads]
    back = [[] for u in heads]
    dkey = [[jnp.zeros((2 * half, TILE), F32) for _ in range(BLK // TILE)] for u in heads]
    dvalue = [[jnp.zeros((hd, TILE), F32) for _ in range(BLK // TILE)] for u in heads]
    suffix = [jnp.zeros((2 * half, hd), F32) for u in heads]
    suffix_norm = [jnp.zeros((2 * half, 1), F32) for u in heads]
    chains = [(u, j) for j in range(BLK // TILE) for u in heads]
    tile = {(u, j): slice(j * TILE, (j + 1) * TILE) for u, j in chains}
    own = {c: q_low[c[0]][:, tile[c]] for c in chains}
    scores = {c: causal(nn(k_turned[c[0]][: tile[c].stop], own[c]), tile[c].start) for c in chains}
    scores_low = {c: scores[c].astype(BF16) for c in chains}
    inverse = {
        c: 1.0
        / (
            jnp.sum(own[c].astype(F32) * norm[c[0]], axis=0, keepdims=True)
            + jnp.sum(scores[c], axis=0, keepdims=True)
        )
        for c in chains
    }
    scaled = {c: g_turned[c[0]][:, tile[c]].astype(F32) * inverse[c] for c in chains}
    scaled_low = {c: scaled[c].astype(BF16) for c in chains}
    numerator = {
        c: nn(state_turned[c[0]], own[c]) + nn(vt_all[:, : tile[c].stop], scores_low[c])
        for c in chains
    }
    products = {c: nn(v_all[: tile[c].stop, :], scaled_low[c]) for c in chains}
    norm_grad = {
        c: -jnp.sum(scaled[c] * (numerator[c] * inverse[c]), axis=0, keepdims=True)
        for c in chains
    }
    dscores = {
        c: causal(products[c] + norm_grad[c], tile[c].start).astype(BF16) for c in chains
    }
    dquery = {
        c: nn(state[c[0]], scaled_low[c])
        + norm[c[0]] * norm_grad[c]
        + nn(k_low[c[0]][:, : tile[c].stop], dscores[c])
        for c in chains
    }
    for c in chains:
        u, j = c
        back[u].append(feature_back(q_feat[u][:, tile[c]], dquery[c]))
        for i in range(j + 1):
            rows = slice(i * TILE, (i + 1) * TILE)
            dkey[u][i] = dkey[u][i] + nt(own[c], dscores[c][rows])
            dvalue[u][i] = dvalue[u][i] + nt(scaled_low[c], scores_low[c][rows])
        suffix[u] = suffix[u] + nt(own[c], scaled_low[c])
        suffix_norm[u] = suffix_norm[u] + jnp.sum(
            own[c].astype(F32) * norm_grad[c], axis=1, keepdims=True
        )
    for u in heads:
        dlog = jnp.concatenate(back[u], axis=1)
        gq_all[:, lanes[u]] = nn(turned(dlog), weight[u][:half]).astype(BF16)
        maps.append(nn(dlog, q_all[:, lanes[u]]))
        dk_ref[u] = jnp.concatenate(dkey[u], axis=1)
        dv_ref[...] += jnp.concatenate(dvalue[u], axis=1)
        sx_ref[u, :hd, :] = suffix[u].astype(BF16)
        sx_ref[u, hd:, :] = thirds(jnp.broadcast_to(suffix_norm[u], (2 * half, 2 * half)).T[:1])
    gm_ref[0] = jnp.concatenate(maps, axis=0).T.astype(gm_ref.dtype)
    for r, ref in enumerate(gq_refs):
        rows = ref.shape[0]
        ref[...] = gq_all[pl.ds(pl.multiple_of(table[base + r] * rows, rows), rows), :]


def key_kernel(begun, part, base, table, *refs):
    k_refs, v_refs = refs[:part], refs[part : 2 * part]
    w_ref, sx_ref, dk_ref, dv_ref = refs[2 * part : 2 * part + 4]
    out, gm_ref, k_all, v_all, vt_all, total, logs, weights = refs[2 * part + 4 + begun :]
    hd = k_all.shape[1]
    step = pl.program_id(0)

    @pl.when(step == 0)
    def _():
        gather(table, base, k_refs, k_all)
        gather(table, base, v_refs, v_all)
        vt_all[...] = turned(v_all[...])
        total[...] = dv_ref[...]

    heads = range(PAIR)
    weight = [weight_rows(w_ref, u) for u in heads]
    half = weight[0].shape[0] // 2
    feats = [features(weight[u][half:], k_all[...]) for u in heads]
    suffix = [sx_ref[u, :hd, :] for u in heads]
    upstream = [
        dk_ref[u] + nn(suffix[u], vt_all[...]) + column(whole_row(sx_ref[u, hd:, :]), BLK)
        for u in heads
    ]
    dlog = [feature_back(feats[u], upstream[u]) for u in heads]
    maps = [nn(dlog[u], k_all[...]) for u in heads]
    for u in heads:
        at = pl.ds(pl.multiple_of((step * PAIR + u) * half, half), half)
        logs[at, :] = dlog[u]
        weights[at, :] = weight[u][half:]
    total[...] += sum(nn(turned(suffix[u]), feats[u].astype(BF16)) for u in heads)
    gm_ref[0] = jnp.concatenate(maps, axis=0).T.astype(gm_ref.dtype)

    @pl.when(step == pl.num_programs(0) - 1)
    def _():
        pair = jnp.concatenate([nn(turned(logs[...]), weights[...]), total[...].T], axis=1)
        out[...] = pair.astype(out.dtype).reshape(out.shape)


def total_kernel(table, *refs):
    out = refs[-1]
    heads, hd = out.shape[0], out.shape[2]
    for h in range(heads):
        out[h, :hd, :] = sum(ref[h, :hd, :].astype(F32) for ref in refs[:-1]).astype(BF16)
        out[h, hd:, :] = thirds(sum(whole_row(ref[h, hd:, :]) for ref in refs[:-1]))


def spread_kernel(grp, others, closing, block_weight, total_weight, at, table, *refs):
    parts, totals, refs = refs[:grp], refs[grp : grp + others], refs[grp + others :]
    if closing:
        outs, grad, scratch = refs[:grp], refs[grp], refs[grp + 1]
    else:
        state_ref, norm_ref, outs = refs[0], refs[1], refs[2:]
    heads, hd = parts[0].shape[0], parts[0].shape[2]
    for h in range(heads):
        states = [ref[h, :hd, :].astype(F32) for ref in parts]
        norms = [whole_row(ref[h, hd:, :]) for ref in parts]
        others_state = [ref[h, :hd, :].astype(F32) for ref in totals]
        others_norm = [whole_row(ref[h, hd:, :]) for ref in totals]
        if closing:
            base, base_norm = jnp.zeros_like(states[0]), jnp.zeros_like(norms[0])
            scratch[...] = sum(states) + sum(others_state)
            rows = grad.shape[1]
            grad[h] = scratch[pl.ds(pl.multiple_of(table[at] * rows, rows), rows), :]
        else:
            base, base_norm = state_ref[h], norm_ref[pl.ds(h, 1), :]
        for i, (state, norm) in enumerate(zip(others_state, others_norm)):
            base = base + table[total_weight + i].astype(F32) * state
            base_norm = base_norm + table[total_weight + i].astype(F32) * norm
        for r, out in enumerate(outs):
            state, norm = base, base_norm
            for i in range(grp):
                if i != r:
                    state = state + table[block_weight + r * grp + i].astype(F32) * states[i]
                    norm = norm + table[block_weight + r * grp + i].astype(F32) * norms[i]
            out[h, :hd, :] = state.astype(BF16)
            out[h, hd:, :] = thirds(norm)


def close_kernel(at, table, q_ref, k_ref, *refs):
    pieces, outs = refs[:-2], refs[-2:]
    for i, (own, out) in enumerate(zip((q_ref, k_ref), outs)):
        rows, half = out.shape[1:]
        mine = pl.ds(pl.multiple_of(table[at] * rows, rows), rows)
        for h in range(own.shape[0]):
            total = own[h, mine, :].astype(F32)
            for ref in pieces:
                total = total + ref[i, h].astype(F32)
            for u in range(PAIR):
                out[h * PAIR + u] = total[:, u * half : (u + 1) * half]


def whole_call(kernel, outs, table, arrays, name, scratch=()):
    return pl.pallas_call(
        kernel,
        out_shape=outs,
        in_specs=[pl.BlockSpec(memory_space=SMEM)]
        + [pl.BlockSpec(memory_space=pltpu.VMEM)] * len(arrays),
        out_specs=[pl.BlockSpec(memory_space=pltpu.VMEM)] * len(outs),
        scratch_shapes=list(scratch),
        compiler_params=pltpu.CompilerParams(vmem_limit_bytes=LIMIT),
        cost_estimate=LITTLE,
        name=name,
    )(table, *arrays)


def after(value, *others):
    return lax.optimization_barrier((value, *others))[0]


def shards(
    query_rows, key_rows, value_rows, grad_out, query_map, key_map, prefix_state, prefix_norm
):
    ctx, fsdp = lax.axis_size("ctx"), lax.axis_size("fsdp")
    tok = query_rows.shape[0]
    heads, map_rows, half = query_map.shape
    hd = map_rows * fsdp
    kv_heads = key_rows.shape[1] // hd
    replicas = ctx // kv_heads
    part = BLK // tok
    grp = ctx // part
    mine = lax.axis_index("ctx")
    at, block, seq = mine % part, mine // part, lax.axis_index("fsdp")
    shifts, slots = range(part), range(grp)
    order = list(reversed(slots))
    grid = (heads // PAIR,)
    blocks_of = [[g * part + p for p in range(part)] for g in slots]

    def within(array):
        return lax.all_to_all(array, "ctx", 0, 0, axis_index_groups=blocks_of, tiled=True)

    def around(array, shift):
        return lax.ppermute(
            array, "ctx", [(d, d // part * part + (d + shift) % part) for d in range(ctx)]
        )

    def across(array, shift):
        return lax.ppermute(array, "ctx", [(d, (d + shift * part) % ctx) for d in range(ctx)])

    def along(array, shift):
        return lax.ppermute(array, "fsdp", [(d, (d + shift) % fsdp) for d in range(fsdp)])

    def twin(array, bit):
        return lax.ppermute(array, "fsdp", [(d, d ^ bit) for d in range(fsdp)])

    def apart(array, s, r):
        moves = [
            (d * fsdp + i, (d + s * part) % ctx * fsdp + (i + r) % fsdp)
            for d in range(ctx)
            for i in range(fsdp)
        ]
        return lax.ppermute(array, ("ctx", "fsdp"), moves)

    slot = [(block + s) % grp for s in slots]
    near = [(block - r) % grp for r in slots]
    bits = [1 << i for i in range(fsdp.bit_length() - 1)]
    lists = {
        "seq": [seq],
        "owner": [slot[s] * part + p for s in slots for p in range(part)],
        "sent": [slot[s] * part + (at + r) % part for s in slots for r in shifts],
        "back": [slot[s] * part + (at + r) % part for s in slots for r in shifts],
        "kv": [
            (slot[s] * part + (at + r) % part) // replicas for r in shifts for s in slots
        ],
        "sorted": [(at - r) % part for r in shifts],
        "near before": [b < a for a in near for b in near],
        "near after": [b > a for a in near for b in near],
        "far before": [(seq ^ bit) < seq for bit in bits],
        "far after": [(seq ^ bit) > seq for bit in bits],
    }
    base, values = {}, []
    for name, entries in lists.items():
        base[name] = len(values)
        values += entries
    table = jnp.stack([jnp.asarray(v, jnp.int32) for v in values])

    own_maps = jnp.concatenate((query_map, key_map), axis=-1)
    near_maps = jnp.stack([own_maps] + [across(own_maps, -s) for s in slots[1:]])
    kv_sent = pack(table, base["kv"], (key_rows, value_rows), part, grp, hd)
    kv = [kv_sent[0]] + [around(kv_sent[r], r) for r in shifts[1:]]
    maps = lax.all_gather(near_maps, "fsdp")

    def packed_rows(s, *earlier):
        return pack(
            after(table, *earlier),
            base["sent"] + s * part,
            (query_rows, grad_out),
            part,
            1,
            heads * hd,
        )

    def sent_rows(sent, *begin):
        return [sent[0]] + [around(after(sent[r], *begin), r) for r in shifts[1:]]

    def piece_specs(column, count):
        return [pl.BlockSpec((tok, count * hd), lambda h, t: (0, column(h)))] * part

    def kv_specs(s):
        return piece_specs(lambda h: 2 * s, 1) + piece_specs(lambda h: 2 * s + 1, 1)

    def map_spec(s):
        return pl.BlockSpec((fsdp, None, PAIR, map_rows, 2 * half), lambda h, t: (0, s, h, 0, 0))

    def head_spec(*shape):
        return pl.BlockSpec((PAIR, *shape), lambda h, t: (h,) + (0,) * len(shape))

    def of(dtype, *shape):
        return jax.ShapeDtypeStruct(shape, dtype)

    ext_spec, ext_shape = head_spec(hd + EXT, hd), of(BF16, heads, hd + EXT, hd)
    gm_spec = pl.BlockSpec((1, hd, PAIR * half), lambda h, t: (h, 0, 0))
    gm_shape = of(BF16, heads // PAIR, hd, PAIR * half)
    dk_spec, dk_shape = head_spec(2 * half, BLK), of(F32, heads, 2 * half, BLK)
    dv_spec, dv_shape = pl.BlockSpec((hd, BLK), lambda h, t: (0, 0)), of(F32, hd, BLK)
    low, wide = pltpu.VMEM((BLK, hd), BF16), pltpu.VMEM((BLK, PAIR * hd), BF16)

    def call(kernel, outs, specs, out_specs, arrays, scratch, name, alias=(), limit=LIMIT):
        return pl.pallas_call(
            functools.partial(kernel, part, base["sorted"]),
            out_shape=outs,
            grid_spec=pltpu.PrefetchScalarGridSpec(
                num_scalar_prefetch=1,
                grid=grid,
                in_specs=specs,
                out_specs=out_specs,
                scratch_shapes=scratch,
            ),
            compiler_params=pltpu.CompilerParams(
                dimension_semantics=("arbitrary",), vmem_limit_bytes=limit
            ),
            cost_estimate=LITTLE,
            input_output_aliases=dict(alias),
            name=name,
        )(table, *arrays)

    def states_of(s):
        return call(
            state_kernel,
            [ext_shape],
            kv_specs(s) + [map_spec(s)],
            [ext_spec],
            [*kv, *kv, maps],
            [low, low],
            "states",
        )[0]

    def spread(parts, others, when, extra, closing):
        weights = [base["near " + when], base["far " + when], base["seq"]]
        result = whole_call(
            functools.partial(spread_kernel, grp, len(bits), closing, *weights),
            [ext_shape] * grp + [of(F32, heads, map_rows, hd)] * closing,
            table,
            parts + others + extra,
            "spread",
            [pltpu.VMEM((hd, hd), F32)] * closing,
        )
        return [result[0]] + [across(result[s], -s) for s in slots[1:]], result[grp:]

    def totals_of(parts):
        return whole_call(total_kernel, [ext_shape], table, parts, "totals")[0]

    def around_all(total):
        others = []
        for bit in bits:
            total = totals_of([total, others[-1]]) if others else total
            others.append(twin(total, bit))
        return others

    partial = {s: states_of(s) for s in order}
    parts = [partial[0]] + [across(partial[s], s) for s in slots[1:]]
    rows = {order[0]: sent_rows(packed_rows(order[0], near_maps, *kv), near_maps)}
    parts[0] = after(parts[0], *rows[order[0]])
    others = around_all(totals_of(parts))
    packed = {s: packed_rows(s, others[0]) for s in order[1:]}
    others[-1] = after(others[-1], *[packed[s][0] for s in packed])
    state, _ = spread(parts, others, "before", [prefix_state, prefix_norm], False)
    for s in order[1:]:
        rows[s] = sent_rows(packed[s], state[0])

    def block_of(s):
        return call(
            block_kernel,
            [of(BF16, tok, heads * hd)] * part + [dk_shape, dv_shape, ext_shape, gm_shape],
            kv_specs(s)
            + piece_specs(lambda h: h, PAIR)
            + piece_specs(lambda h: grid[0] + h, PAIR)
            + [map_spec(s), ext_spec],
            piece_specs(lambda h: h, PAIR) + [dk_spec, dv_spec, ext_spec, gm_spec],
            [*kv, *kv, *rows[s], *rows[s], maps, state[s]],
            [low, low, pltpu.VMEM((hd, BLK), BF16), wide, wide, wide],
            "blocks",
            limit=LARGE,
        )

    def rows_for(array, device):
        pieces = array.reshape(*array.shape[:-2], fsdp, map_rows, array.shape[-1])
        return lax.dynamic_index_in_dim(pieces, device % fsdp, array.ndim - 2, keepdims=False)

    blocks, parts = {}, {}
    for s in order:
        result = block_of(s)
        blocks[s] = (result[:part], *result[part:])
        parts[s] = across(blocks[s][3], s) if s else blocks[s][3]
    parts = [parts[s] for s in slots]
    total = totals_of(parts)
    others = around_all(total)
    suffix, (grad_prefix,) = spread(parts, others, "after", [], True)
    def brought_back(s, *begin):
        pieces = [after(piece, *begin) for piece in blocks[s][0]]
        return [pieces[0]] + [around(pieces[r], -r) for r in shifts[1:]]

    returned = {s: brought_back(s, others[0]) for s in order if s}
    earlier = [piece for s in returned for piece in returned[s]]

    kv_type = BF16 if replicas == 1 else F32
    pairs = of(kv_type, part, tok, grp * 2 * hd)
    moved, key_gm = [], {}
    for s in slots:
        begun = [] if s == 0 else [pairs]
        pairs, key_gm[s] = call(
            functools.partial(key_kernel, bool(begun)),
            [of(kv_type, *pairs.shape), gm_shape],
            kv_specs(s)
            + [map_spec(s), ext_spec, dk_spec, dv_spec]
            + [pl.BlockSpec(memory_space=pl.ANY)] * len(begun),
            [pl.BlockSpec((part, tok, 2 * hd), lambda h, t: (0, 0, s)), gm_spec],
            [*kv, *kv, maps, suffix[s], blocks[s][1], blocks[s][2], *begun],
            [
                low,
                low,
                pltpu.VMEM((hd, BLK), BF16),
                pltpu.VMEM((hd, BLK), F32),
                pltpu.VMEM((heads * half, BLK), BF16),
                pltpu.VMEM((heads * half, hd), BF16),
            ],
            "keys",
            {2 * part + 5: 0} if begun else {},
        )
        two = jnp.stack([blocks[s][4], key_gm[s]])
        if s:
            moved += [apart(rows_for(two, seq + r), s, r) for r in range(fsdp)]
        else:
            two = after(two, *suffix[1:])
            moved += [along(rows_for(two, seq + r), r) for r in range(1, fsdp)]
            returned[s] = brought_back(s, key_gm[s], *earlier)

    pairs = within(after(pairs, *returned[0]))
    back = [piece[None] for s in slots for piece in returned[s]]
    (grad_queries,) = unpack(table, base["back"], back, 1, 1, heads * hd)
    grad_keys, grad_values = unpack(table, base["owner"], [pairs], grp, 2, hd)
    if replicas > 1:
        grad_keys, grad_values = (
            jnp.sum(a.reshape(tok, kv_heads, replicas, hd), axis=2)
            .astype(BF16)
            .reshape(tok, kv_heads * hd)
            for a in (grad_keys, grad_values)
        )
    query_map_grad, key_map_grad = whole_call(
        functools.partial(close_kernel, base["seq"]),
        [of(F32, heads, map_rows, half)] * 2,
        table,
        [blocks[0][4], key_gm[0]] + moved,
        "close",
    )
    return grad_queries, grad_keys, grad_values, query_map_grad, key_map_grad, grad_prefix


def solution(mesh):
    rows, maps = P(("fsdp", "ctx"), None), P("ctx", "fsdp", None)
    return jax.shard_map(
        shards,
        mesh=mesh,
        in_specs=(rows,) * 4 + (maps, maps, P("ctx", None, None), P("ctx", None)),
        out_specs=(rows,) * 3 + (maps,) * 3,
        check_vma=False,
    )
```

```python
import functools

import jax
import jax.numpy as jnp
from jax import lax
from jax.experimental import pallas as pl
from jax.experimental.pallas import tpu as pltpu
from jax.sharding import PartitionSpec as P

BLK = 512
TILE = 256
PAIR = 2
EXT = 16
LIMIT = 40 * 1024 * 1024
LARGE = 56 * 1024 * 1024

LITTLE = pl.CostEstimate(flops=1000, bytes_accessed=1000, transcendentals=0)

F32 = jnp.float32
BF16 = jnp.bfloat16
SMEM = pltpu.SMEM


def nn(left, right):
    return lax.dot_general(left, right, (((1,), (0,)), ((), ())), preferred_element_type=F32)


def nt(left, right):
    return lax.dot_general(left, right, (((1,), (1,)), ((), ())), preferred_element_type=F32)


def turned(array):
    return array.T


def column(row, width):
    n = row.shape[1]
    square = jnp.broadcast_to(row, (n, n)).T
    return jnp.concatenate([square] * (width // n), axis=1)


def thirds(row):
    rows = jnp.broadcast_to(row, (EXT, row.shape[1]))
    high = rows.astype(BF16).astype(F32)
    middle = (rows - high).astype(BF16).astype(F32)
    low = rows - high - middle
    place = lax.broadcasted_iota(jnp.int32, rows.shape, 0)
    picked = jnp.where(place == 0, high, jnp.where(place == 1, middle, low))
    return jnp.where(place < 3, picked, 0.0).astype(BF16)


def whole_row(block):
    return jnp.sum(block.astype(F32), axis=0, keepdims=True)


def weight_rows(ref, u):
    whole = jnp.concatenate([ref[i, u] for i in range(ref.shape[0])], axis=0)
    return turned(whole)


def features(weight, rows):
    logits = nt(weight, rows).astype(BF16).astype(F32)
    upper = jnp.exp(logits)
    lower = jnp.exp(-logits)
    upper = upper * (1.0 / jnp.sum(upper, axis=0, keepdims=True))
    lower = lower * (1.0 / jnp.sum(lower, axis=0, keepdims=True))
    return jnp.concatenate([upper, lower], axis=0)


def feature_back(feats, upstream):
    half = feats.shape[0] // 2
    weighted = feats * upstream
    first, second = weighted[:half], weighted[half:]
    first = first - feats[:half] * jnp.sum(first, axis=0, keepdims=True)
    second = second - feats[half:] * jnp.sum(second, axis=0, keepdims=True)
    return (first - second).astype(BF16)


def gather(table, base, refs, out):
    rows = refs[0].shape[0]
    for r, ref in enumerate(refs):
        out[pl.ds(pl.multiple_of(table[base + r] * rows, rows), rows), :] = ref[...]


def pack_kernel(columns, inputs, table, *refs):
    count = columns * inputs
    for r, out in enumerate(refs[-(len(refs) // (count + 1)) :]):
        width = out.shape[1] // count
        for i in range(count):
            out[:, i * width : (i + 1) * width] = refs[r * count + i][...]


def pack(table, base, sources, pieces, columns, width):
    rows = sources[0].shape[0]
    count = columns * len(sources)
    step = rows // 2

    def take(at):
        return pl.BlockSpec((step, width), lambda i, t: (i, t[base + at]))

    return pl.pallas_call(
        functools.partial(pack_kernel, columns, len(sources)),
        out_shape=[jax.ShapeDtypeStruct((rows, count * width), sources[0].dtype)] * pieces,
        grid_spec=pltpu.PrefetchScalarGridSpec(
            num_scalar_prefetch=1,
            grid=(rows // step,),
            in_specs=[
                take(r * columns + s)
                for r in range(pieces)
                for s in range(columns)
                for _ in sources
            ],
            out_specs=[pl.BlockSpec((step, count * width), lambda i, t: (i, 0))] * pieces,
        ),
        compiler_params=pltpu.CompilerParams(vmem_limit_bytes=LIMIT),
        cost_estimate=LITTLE,
        name="pack",
    )(table, *(list(sources) * (pieces * columns)))


def unpack_kernel(outputs, inner, base, table, *refs):
    sources, outs = refs[:-outputs], refs[-outputs:]
    for s, source in enumerate(sources):
        pieces = source.shape[0]
        width = source.shape[2] // (outputs * inner)
        for r in range(pieces):
            for j in range(inner):
                slot = s * inner + j
                at = table[base + slot * pieces + r] * width
                for i, out in enumerate(outs):
                    lanes = slice((j * outputs + i) * width, (j * outputs + i + 1) * width)
                    out[:, pl.ds(pl.multiple_of(at, width), width)] = source[r, :, lanes]


def unpack(table, base, sources, inner, outputs, width):
    pieces, rows = sources[0].shape[:2]
    total = len(sources) * inner * pieces * width
    step = rows // 2
    taken = pl.BlockSpec((pieces, step, inner * outputs * width), lambda i: (0, i, 0))
    return pl.pallas_call(
        functools.partial(unpack_kernel, outputs, inner, base),
        out_shape=[jax.ShapeDtypeStruct((rows, total), sources[0].dtype)] * outputs,
        grid=(rows // step,),
        in_specs=[pl.BlockSpec(memory_space=SMEM)] + [taken] * len(sources),
        out_specs=[pl.BlockSpec((step, total), lambda i: (i, 0))] * outputs,
        compiler_params=pltpu.CompilerParams(vmem_limit_bytes=LIMIT),
        cost_estimate=LITTLE,
        name="unpack",
    )(table, *sources)


def state_kernel(part, base, table, *refs):
    k_refs, v_refs, (w_ref, out, k_all, v_all) = refs[:part], refs[part : 2 * part], refs[2 * part :]
    hd = k_all.shape[1]

    @pl.when(pl.program_id(0) == 0)
    def _():
        gather(table, base, k_refs, k_all)
        gather(table, base, v_refs, v_all)

    ones = jnp.ones((EXT, k_all.shape[0]), BF16)
    weights = [weight_rows(w_ref, u) for u in range(PAIR)]
    feats = [features(w[w.shape[0] // 2 :], k_all[...]).astype(BF16) for w in weights]
    for u in range(PAIR):
        out[u, :hd, :] = nn(feats[u], v_all[...]).astype(BF16)
        out[u, hd:, :] = thirds(nt(ones, feats[u])[:1])


def block_kernel(part, base, table, *refs):
    k_refs, v_refs = refs[:part], refs[part : 2 * part]
    q_refs, g_refs = refs[2 * part : 3 * part], refs[3 * part : 4 * part]
    w_ref, st_ref = refs[4 * part : 4 * part + 2]
    gq_refs = refs[4 * part + 2 : 5 * part + 2]
    dk_ref, dv_ref, sx_ref, gm_ref, k_all, v_all, vt_all, q_all, g_all, gq_all = refs[5 * part + 2 :]
    hd = k_all.shape[1]

    @pl.when(pl.program_id(0) == 0)
    def _():
        gather(table, base, k_refs, k_all)
        gather(table, base, v_refs, v_all)
        vt_all[...] = turned(v_all[...])
        dv_ref[...] = jnp.zeros_like(dv_ref)

    gather(table, base, q_refs, q_all)
    gather(table, base, g_refs, g_all)
    maps = []
    earlier = lax.broadcasted_iota(jnp.int32, (TILE, TILE), 0) <= lax.broadcasted_iota(
        jnp.int32, (TILE, TILE), 1
    )

    def causal(array, begin):
        masked = jnp.where(earlier, array[begin:], 0.0)
        return masked if begin == 0 else jnp.concatenate([array[:begin], masked], axis=0)

    heads = range(PAIR)
    lanes = [slice(u * hd, (u + 1) * hd) for u in heads]
    weight = [weight_rows(w_ref, u) for u in heads]
    half = weight[0].shape[0] // 2
    q_feat = [features(weight[u][:half], q_all[:, lanes[u]]) for u in heads]
    k_low = [features(weight[u][half:], k_all[...]).astype(BF16) for u in heads]
    q_low = [q_feat[u].astype(BF16) for u in heads]
    k_turned = [turned(k_low[u]) for u in heads]
    state = [st_ref[u, :hd, :] for u in heads]
    state_turned = [turned(state[u]) for u in heads]
    norm = [column(whole_row(st_ref[u, hd:, :]), TILE) for u in heads]
    g_turned = [g_all[:, lanes[u]].T for u in heads]
    back = [[] for u in heads]
    dkey = [[jnp.zeros((2 * half, TILE), F32) for _ in range(BLK // TILE)] for u in heads]
    dvalue = [[jnp.zeros((hd, TILE), F32) for _ in range(BLK // TILE)] for u in heads]
    suffix = [jnp.zeros((2 * half, hd), F32) for u in heads]
    suffix_norm = [jnp.zeros((2 * half, 1), F32) for u in heads]
    chains = [(u, j) for j in range(BLK // TILE) for u in heads]
    tile = {(u, j): slice(j * TILE, (j + 1) * TILE) for u, j in chains}
    own = {c: q_low[c[0]][:, tile[c]] for c in chains}
    scores = {c: causal(nn(k_turned[c[0]][: tile[c].stop], own[c]), tile[c].start) for c in chains}
    scores_low = {c: scores[c].astype(BF16) for c in chains}
    inverse = {
        c: 1.0
        / (
            jnp.sum(own[c].astype(F32) * norm[c[0]], axis=0, keepdims=True)
            + jnp.sum(scores[c], axis=0, keepdims=True)
        )
        for c in chains
    }
    scaled = {c: g_turned[c[0]][:, tile[c]].astype(F32) * inverse[c] for c in chains}
    scaled_low = {c: scaled[c].astype(BF16) for c in chains}
    numerator = {
        c: nn(state_turned[c[0]], own[c]) + nn(vt_all[:, : tile[c].stop], scores_low[c])
        for c in chains
    }
    products = {c: nn(v_all[: tile[c].stop, :], scaled_low[c]) for c in chains}
    norm_grad = {
        c: -jnp.sum(scaled[c] * (numerator[c] * inverse[c]), axis=0, keepdims=True)
        for c in chains
    }
    dscores = {
        c: causal(products[c] + norm_grad[c], tile[c].start).astype(BF16) for c in chains
    }
    dquery = {
        c: nn(state[c[0]], scaled_low[c])
        + norm[c[0]] * norm_grad[c]
        + nn(k_low[c[0]][:, : tile[c].stop], dscores[c])
        for c in chains
    }
    for c in chains:
        u, j = c
        back[u].append(feature_back(q_feat[u][:, tile[c]], dquery[c]))
        for i in range(j + 1):
            rows = slice(i * TILE, (i + 1) * TILE)
            dkey[u][i] = dkey[u][i] + nt(own[c], dscores[c][rows])
            dvalue[u][i] = dvalue[u][i] + nt(scaled_low[c], scores_low[c][rows])
        suffix[u] = suffix[u] + nt(own[c], scaled_low[c])
        suffix_norm[u] = suffix_norm[u] + jnp.sum(
            own[c].astype(F32) * norm_grad[c], axis=1, keepdims=True
        )
    for u in heads:
        dlog = jnp.concatenate(back[u], axis=1)
        gq_all[:, lanes[u]] = nn(turned(dlog), weight[u][:half]).astype(BF16)
        maps.append(nn(dlog, q_all[:, lanes[u]]))
        dk_ref[u] = jnp.concatenate(dkey[u], axis=1)
        dv_ref[...] += jnp.concatenate(dvalue[u], axis=1)
        sx_ref[u, :hd, :] = suffix[u].astype(BF16)
        sx_ref[u, hd:, :] = thirds(jnp.broadcast_to(suffix_norm[u], (2 * half, 2 * half)).T[:1])
    gm_ref[0] = jnp.concatenate(maps, axis=0).T.astype(gm_ref.dtype)
    for r, ref in enumerate(gq_refs):
        rows = ref.shape[0]
        ref[...] = gq_all[pl.ds(pl.multiple_of(table[base + r] * rows, rows), rows), :]


def key_kernel(begun, part, base, table, *refs):
    k_refs, v_refs = refs[:part], refs[part : 2 * part]
    w_ref, sx_ref, dk_ref, dv_ref = refs[2 * part : 2 * part + 4]
    out, gm_ref, k_all, v_all, vt_all, total, logs, weights = refs[2 * part + 4 + begun :]
    hd = k_all.shape[1]
    step = pl.program_id(0)

    @pl.when(step == 0)
    def _():
        gather(table, base, k_refs, k_all)
        gather(table, base, v_refs, v_all)
        vt_all[...] = turned(v_all[...])
        total[...] = dv_ref[...]

    heads = range(PAIR)
    weight = [weight_rows(w_ref, u) for u in heads]
    half = weight[0].shape[0] // 2
    feats = [features(weight[u][half:], k_all[...]) for u in heads]
    suffix = [sx_ref[u, :hd, :] for u in heads]
    upstream = [
        dk_ref[u] + nn(suffix[u], vt_all[...]) + column(whole_row(sx_ref[u, hd:, :]), BLK)
        for u in heads
    ]
    dlog = [feature_back(feats[u], upstream[u]) for u in heads]
    maps = [nn(dlog[u], k_all[...]) for u in heads]
    for u in heads:
        at = pl.ds(pl.multiple_of((step * PAIR + u) * half, half), half)
        logs[at, :] = dlog[u]
        weights[at, :] = weight[u][half:]
    total[...] += sum(nn(turned(suffix[u]), feats[u].astype(BF16)) for u in heads)
    gm_ref[0] = jnp.concatenate(maps, axis=0).T.astype(gm_ref.dtype)

    @pl.when(step == pl.num_programs(0) - 1)
    def _():
        pair = jnp.concatenate([nn(turned(logs[...]), weights[...]), total[...].T], axis=1)
        out[...] = pair.astype(out.dtype).reshape(out.shape)


def total_kernel(table, *refs):
    out = refs[-1]
    heads, hd = out.shape[0], out.shape[2]
    for h in range(heads):
        out[h, :hd, :] = sum(ref[h, :hd, :].astype(F32) for ref in refs[:-1]).astype(BF16)
        out[h, hd:, :] = thirds(sum(whole_row(ref[h, hd:, :]) for ref in refs[:-1]))


def spread_kernel(grp, others, closing, block_weight, total_weight, at, table, *refs):
    parts, totals, refs = refs[:grp], refs[grp : grp + others], refs[grp + others :]
    if closing:
        outs, grad, scratch = refs[:grp], refs[grp], refs[grp + 1]
    else:
        state_ref, norm_ref, outs = refs[0], refs[1], refs[2:]
    heads, hd = parts[0].shape[0], parts[0].shape[2]
    for h in range(heads):
        states = [ref[h, :hd, :].astype(F32) for ref in parts]
        norms = [whole_row(ref[h, hd:, :]) for ref in parts]
        others_state = [ref[h, :hd, :].astype(F32) for ref in totals]
        others_norm = [whole_row(ref[h, hd:, :]) for ref in totals]
        if closing:
            base, base_norm = jnp.zeros_like(states[0]), jnp.zeros_like(norms[0])
            scratch[...] = sum(states) + sum(others_state)
            rows = grad.shape[1]
            grad[h] = scratch[pl.ds(pl.multiple_of(table[at] * rows, rows), rows), :]
        else:
            base, base_norm = state_ref[h], norm_ref[pl.ds(h, 1), :]
        for i, (state, norm) in enumerate(zip(others_state, others_norm)):
            base = base + table[total_weight + i].astype(F32) * state
            base_norm = base_norm + table[total_weight + i].astype(F32) * norm
        for r, out in enumerate(outs):
            state, norm = base, base_norm
            for i in range(grp):
                if i != r:
                    state = state + table[block_weight + r * grp + i].astype(F32) * states[i]
                    norm = norm + table[block_weight + r * grp + i].astype(F32) * norms[i]
            out[h, :hd, :] = state.astype(BF16)
            out[h, hd:, :] = thirds(norm)


def close_kernel(at, table, q_ref, k_ref, *refs):
    pieces, outs = refs[:-2], refs[-2:]
    for i, (own, out) in enumerate(zip((q_ref, k_ref), outs)):
        rows, half = out.shape[1:]
        mine = pl.ds(pl.multiple_of(table[at] * rows, rows), rows)
        for h in range(own.shape[0]):
            total = own[h, mine, :].astype(F32)
            for ref in pieces:
                total = total + ref[i, h].astype(F32)
            for u in range(PAIR):
                out[h * PAIR + u] = total[:, u * half : (u + 1) * half]


def whole_call(kernel, outs, table, arrays, name, scratch=()):
    return pl.pallas_call(
        kernel,
        out_shape=outs,
        in_specs=[pl.BlockSpec(memory_space=SMEM)]
        + [pl.BlockSpec(memory_space=pltpu.VMEM)] * len(arrays),
        out_specs=[pl.BlockSpec(memory_space=pltpu.VMEM)] * len(outs),
        scratch_shapes=list(scratch),
        compiler_params=pltpu.CompilerParams(vmem_limit_bytes=LIMIT),
        cost_estimate=LITTLE,
        name=name,
    )(table, *arrays)


def after(value, *others):
    return lax.optimization_barrier((value, *others))[0]


def shards(
    query_rows, key_rows, value_rows, grad_out, query_map, key_map, prefix_state, prefix_norm
):
    ctx, fsdp = lax.axis_size("ctx"), lax.axis_size("fsdp")
    tok = query_rows.shape[0]
    heads, map_rows, half = query_map.shape
    hd = map_rows * fsdp
    kv_heads = key_rows.shape[1] // hd
    replicas = ctx // kv_heads
    part = BLK // tok
    grp = ctx // part
    mine = lax.axis_index("ctx")
    at, block, seq = mine % part, mine // part, lax.axis_index("fsdp")
    shifts, slots = range(part), range(grp)
    order = list(reversed(slots))
    grid = (heads // PAIR,)
    blocks_of = [[g * part + p for p in range(part)] for g in slots]

    def within(array):
        return lax.all_to_all(array, "ctx", 0, 0, axis_index_groups=blocks_of, tiled=True)

    def around(array, shift):
        return lax.ppermute(
            array, "ctx", [(d, d // part * part + (d + shift) % part) for d in range(ctx)]
        )

    def across(array, shift):
        return lax.ppermute(array, "ctx", [(d, (d + shift * part) % ctx) for d in range(ctx)])

    def along(array, shift):
        return lax.ppermute(array, "fsdp", [(d, (d + shift) % fsdp) for d in range(fsdp)])

    def twin(array, bit):
        return lax.ppermute(array, "fsdp", [(d, d ^ bit) for d in range(fsdp)])

    def apart(array, s, r):
        moves = [
            (d * fsdp + i, (d + s * part) % ctx * fsdp + (i + r) % fsdp)
            for d in range(ctx)
            for i in range(fsdp)
        ]
        return lax.ppermute(array, ("ctx", "fsdp"), moves)

    slot = [(block + s) % grp for s in slots]
    near = [(block - r) % grp for r in slots]
    bits = [1 << i for i in range(fsdp.bit_length() - 1)]
    lists = {
        "seq": [seq],
        "owner": [slot[s] * part + p for s in slots for p in range(part)],
        "sent": [slot[s] * part + (at + r) % part for s in slots for r in shifts],
        "back": [slot[s] * part + (at + r) % part for s in slots for r in shifts],
        "kv": [
            (slot[s] * part + (at + r) % part) // replicas for r in shifts for s in slots
        ],
        "sorted": [(at - r) % part for r in shifts],
        "near before": [b < a for a in near for b in near],
        "near after": [b > a for a in near for b in near],
        "far before": [(seq ^ bit) < seq for bit in bits],
        "far after": [(seq ^ bit) > seq for bit in bits],
    }
    base, values = {}, []
    for name, entries in lists.items():
        base[name] = len(values)
        values += entries
    table = jnp.stack([jnp.asarray(v, jnp.int32) for v in values])

    own_maps = jnp.concatenate((query_map, key_map), axis=-1)
    near_maps = jnp.stack([own_maps] + [across(own_maps, -s) for s in slots[1:]])
    kv_sent = pack(table, base["kv"], (key_rows, value_rows), part, grp, hd)
    kv = [kv_sent[0]] + [around(kv_sent[r], r) for r in shifts[1:]]
    maps = lax.all_gather(near_maps, "fsdp")

    def packed_rows(s, *earlier):
        return pack(
            after(table, *earlier),
            base["sent"] + s * part,
            (query_rows, grad_out),
            part,
            1,
            heads * hd,
        )

    def sent_rows(sent, *begin):
        return [sent[0]] + [around(after(sent[r], *begin), r) for r in shifts[1:]]

    def piece_specs(column, count):
        return [pl.BlockSpec((tok, count * hd), lambda h, t: (0, column(h)))] * part

    def kv_specs(s):
        return piece_specs(lambda h: 2 * s, 1) + piece_specs(lambda h: 2 * s + 1, 1)

    def map_spec(s):
        return pl.BlockSpec((fsdp, None, PAIR, map_rows, 2 * half), lambda h, t: (0, s, h, 0, 0))

    def head_spec(*shape):
        return pl.BlockSpec((PAIR, *shape), lambda h, t: (h,) + (0,) * len(shape))

    def of(dtype, *shape):
        return jax.ShapeDtypeStruct(shape, dtype)

    ext_spec, ext_shape = head_spec(hd + EXT, hd), of(BF16, heads, hd + EXT, hd)
    gm_spec = pl.BlockSpec((1, hd, PAIR * half), lambda h, t: (h, 0, 0))
    gm_shape = of(BF16, heads // PAIR, hd, PAIR * half)
    dk_spec, dk_shape = head_spec(2 * half, BLK), of(F32, heads, 2 * half, BLK)
    dv_spec, dv_shape = pl.BlockSpec((hd, BLK), lambda h, t: (0, 0)), of(F32, hd, BLK)
    low, wide = pltpu.VMEM((BLK, hd), BF16), pltpu.VMEM((BLK, PAIR * hd), BF16)

    def call(kernel, outs, specs, out_specs, arrays, scratch, name, alias=(), limit=LIMIT):
        return pl.pallas_call(
            functools.partial(kernel, part, base["sorted"]),
            out_shape=outs,
            grid_spec=pltpu.PrefetchScalarGridSpec(
                num_scalar_prefetch=1,
                grid=grid,
                in_specs=specs,
                out_specs=out_specs,
                scratch_shapes=scratch,
            ),
            compiler_params=pltpu.CompilerParams(
                dimension_semantics=("arbitrary",), vmem_limit_bytes=limit
            ),
            cost_estimate=LITTLE,
            input_output_aliases=dict(alias),
            name=name,
        )(table, *arrays)

    def states_of(s):
        return call(
            state_kernel,
            [ext_shape],
            kv_specs(s) + [map_spec(s)],
            [ext_spec],
            [*kv, *kv, maps],
            [low, low],
            "states",
        )[0]

    def spread(parts, others, when, extra, closing):
        weights = [base["near " + when], base["far " + when], base["seq"]]
        result = whole_call(
            functools.partial(spread_kernel, grp, len(bits), closing, *weights),
            [ext_shape] * grp + [of(F32, heads, map_rows, hd)] * closing,
            table,
            parts + others + extra,
            "spread",
            [pltpu.VMEM((hd, hd), F32)] * closing,
        )
        return [result[0]] + [across(result[s], -s) for s in slots[1:]], result[grp:]

    def totals_of(parts):
        return whole_call(total_kernel, [ext_shape], table, parts, "totals")[0]

    def around_all(total):
        others = []
        for bit in bits:
            total = totals_of([total, others[-1]]) if others else total
            others.append(twin(total, bit))
        return others

    partial = {s: states_of(s) for s in order}
    parts = [partial[0]] + [across(partial[s], s) for s in slots[1:]]
    rows = {order[0]: sent_rows(packed_rows(order[0], near_maps, *kv), near_maps)}
    parts[0] = after(parts[0], *rows[order[0]])
    others = around_all(totals_of(parts))
    packed = {s: packed_rows(s, others[0]) for s in order[1:]}
    others[-1] = after(others[-1], *[packed[s][0] for s in packed])
    state, _ = spread(parts, others, "before", [prefix_state, prefix_norm], False)
    for s in order[1:]:
        rows[s] = sent_rows(packed[s], state[0])

    def block_of(s):
        return call(
            block_kernel,
            [of(BF16, tok, heads * hd)] * part + [dk_shape, dv_shape, ext_shape, gm_shape],
            kv_specs(s)
            + piece_specs(lambda h: h, PAIR)
            + piece_specs(lambda h: grid[0] + h, PAIR)
            + [map_spec(s), ext_spec],
            piece_specs(lambda h: h, PAIR) + [dk_spec, dv_spec, ext_spec, gm_spec],
            [*kv, *kv, *rows[s], *rows[s], maps, state[s]],
            [low, low, pltpu.VMEM((hd, BLK), BF16), wide, wide, wide],
            "blocks",
            limit=LARGE,
        )

    def rows_for(array, device):
        pieces = array.reshape(*array.shape[:-2], fsdp, map_rows, array.shape[-1])
        return lax.dynamic_index_in_dim(pieces, device % fsdp, array.ndim - 2, keepdims=False)

    blocks, parts = {}, {}
    for s in order:
        result = block_of(s)
        blocks[s] = (result[:part], *result[part:])
        parts[s] = across(blocks[s][3], s) if s else blocks[s][3]
    parts = [parts[s] for s in slots]
    total = totals_of(parts)
    others = around_all(total)
    suffix, (grad_prefix,) = spread(parts, others, "after", [], True)
    def brought_back(s, *begin):
        pieces = [after(piece, *begin) for piece in blocks[s][0]]
        return [pieces[0]] + [around(pieces[r], -r) for r in shifts[1:]]

    returned = {s: brought_back(s, others[0]) for s in order if s}
    earlier = [piece for s in returned for piece in returned[s]]

    kv_type = BF16 if replicas == 1 else F32
    pairs = of(kv_type, part, tok, grp * 2 * hd)
    moved, key_gm = [], {}
    for s in slots:
        begun = [] if s == 0 else [pairs]
        suffix[s] = after(suffix[s], *moved)
        pairs, key_gm[s] = call(
            functools.partial(key_kernel, bool(begun)),
            [of(kv_type, *pairs.shape), gm_shape],
            kv_specs(s)
            + [map_spec(s), ext_spec, dk_spec, dv_spec]
            + [pl.BlockSpec(memory_space=pl.ANY)] * len(begun),
            [pl.BlockSpec((part, tok, 2 * hd), lambda h, t: (0, 0, s)), gm_spec],
            [*kv, *kv, maps, suffix[s], blocks[s][1], blocks[s][2], *begun],
            [
                low,
                low,
                pltpu.VMEM((hd, BLK), BF16),
                pltpu.VMEM((hd, BLK), F32),
                pltpu.VMEM((heads * half, BLK), BF16),
                pltpu.VMEM((heads * half, hd), BF16),
            ],
            "keys",
            {2 * part + 5: 0} if begun else {},
        )
        two = jnp.stack([blocks[s][4], key_gm[s]])
        if s:
            moved += [apart(rows_for(two, seq + r), s, r) for r in range(fsdp)]
        else:
            moved += [along(rows_for(two, seq + r), r) for r in range(1, fsdp)]
            returned[s] = brought_back(s, key_gm[s], *earlier)

    pairs = within(after(pairs, *returned[0]))
    back = [piece[None] for s in slots for piece in returned[s]]
    (grad_queries,) = unpack(table, base["back"], back, 1, 1, heads * hd)
    grad_keys, grad_values = unpack(table, base["owner"], [pairs], grp, 2, hd)
    if replicas > 1:
        grad_keys, grad_values = (
            jnp.sum(a.reshape(tok, kv_heads, replicas, hd), axis=2)
            .astype(BF16)
            .reshape(tok, kv_heads * hd)
            for a in (grad_keys, grad_values)
        )
    query_map_grad, key_map_grad = whole_call(
        functools.partial(close_kernel, base["seq"]),
        [of(F32, heads, map_rows, half)] * 2,
        table,
        [blocks[0][4], key_gm[0]] + moved,
        "close",
    )
    return grad_queries, grad_keys, grad_values, query_map_grad, key_map_grad, grad_prefix


def solution(mesh):
    rows, maps = P(("fsdp", "ctx"), None), P("ctx", "fsdp", None)
    return jax.shard_map(
        shards,
        mesh=mesh,
        in_specs=(rows,) * 4 + (maps, maps, P("ctx", None, None), P("ctx", None)),
        out_specs=(rows,) * 3 + (maps,) * 3,
        check_vma=False,
    )
```
